32 devices in a mesh: grp: 8 (over y, x, core), dp: 4 (over z).
Axes of the slice: x: 2, y: 2, z: 4, core: 2. Of those that a mesh axis runs over, the one named last changes fastest.
Arguments:
- latents: bfloat16 [64, 256, 1152], P(('grp', 'dp')), may hold values from -6 to 6
- cotangent: bfloat16 [64, 256, 1152], P(('grp', 'dp')), may hold values from -6 to 6
- bands: int32 [64], P(('grp', 'dp')), may hold values from 0 to 15
- labels: int32 [64], P(('grp', 'dp')), may hold values from 0 to 999
- kept: int32 [64, 128], P(('grp', 'dp')), may hold values from 0 to 255, as said below
- band_counts: int32 [8], P('grp'), may hold values from 1 to 8, as said below
- time_table: bfloat16 [16, 1152], P(None, 'grp'), may hold values from -6 to 6
- class_table: bfloat16 [1000, 1152], P(None, 'grp'), may hold values from -6 to 6
- w_ada: bfloat16 [1152, 6912], P(None, 'grp'), may hold values from -0.1875 to 0.1875
- b_ada: bfloat16 [6912], P('grp'), may hold values from -3 to 3
- w_qkv: bfloat16 [1152, 3456], P(None, 'grp'), may hold values from -0.1875 to 0.1875
- qv_bias: bfloat16 [2304], P('grp'), may hold values from -2 to 2
- w_proj: bfloat16 [1152, 1152], P('grp'), may hold values from -0.75 to 0.75
- b_proj: bfloat16 [1152], P('grp'), may hold values from -2 to 2
- w_fc1: bfloat16 [1152, 4608], P(None, 'grp'), may hold values from -0.1875 to 0.1875
- b_fc1: bfloat16 [4608], P('grp'), may hold values from -2 to 2
- w_fc2: bfloat16 [4608, 1152], P('grp'), may hold values from -0.1875 to 0.1875
- b_fc2: bfloat16 [1152], P('grp'), may hold values from -2 to 2
Outputs:
- block_out: bfloat16 [64, 256, 1152], P(('grp', 'dp'))
- latents_grad: bfloat16 [64, 256, 1152], P(('grp', 'dp'))
- time_table_grad: float32 [16, 1152], P(None, 'grp')
- class_table_grad: float32 [1000, 1152], P(None, 'grp')
- w_ada_grad: float32 [1152, 6912], P(None, 'grp')
- b_ada_grad: float32 [6912], P('grp')
- w_qkv_grad: float32 [1152, 3456], P(None, 'grp')
- qv_bias_grad: float32 [2304], P('grp')
- w_proj_grad: float32 [1152, 1152], P('grp')
- b_proj_grad: float32 [1152], P('grp')
- w_fc1_grad: float32 [1152, 4608], P(None, 'grp')
- b_fc1_grad: float32 [4608], P('grp')
- w_fc2_grad: float32 [4608, 1152], P('grp')
- b_fc2_grad: float32 [1152], P('grp')
The draws below stay inside these ranges and needn't reach their ends.
Inputs may be any that keep to these rules, and one draw needn't show every extreme that they name: `kept`: each row holds 128 different token positions in rising order. `band_counts`: some group has all 8 slots in use; slots below a group's count are in use.
All inputs are finite; a program needn't handle non-finite values.
Results may differ from the reference program's by a relative error of at most 0.018.
The reference program's roundings to bfloat16 on the way count: a program that leaves them out, or rounds other values in their place, can miss the bound.
Values may be sent and summed in bfloat16 or wider, within the bound.
A program may use at most 320 MiB of HBM per device.

```python
import math
import jax
import jax.numpy as jnp
from jax import lax

D = 1152
HEADS = 16
HEAD_DIM = 72
FF = 4608
CLASSES = 1000
SEQ = 256
BANDS = 16
KEEP = 128
GROUP_SLOTS = 8
GROUPS = 8
SAMPLES = 64


def draw_kept(key, part):
    key = jax.random.fold_in(key, 12)
    scores = jax.random.randint(key, (SAMPLES, SEQ), 0, 2 ** 20)
    keyed = scores * SEQ + jnp.arange(SEQ, dtype=jnp.int32)[None, :]
    order = jnp.argsort(keyed, axis=-1, stable=True)
    return jnp.sort(order[:, :KEEP], axis=-1).astype(jnp.int32)


def draw_band_counts(key, part):
    key = jax.random.fold_in(key, 11)
    first, second = jax.random.split(key)
    counts = jax.random.randint(first, (GROUPS,), 1, GROUP_SLOTS + 1)
    full = jax.random.randint(second, (), 0, GROUPS)
    counts = jnp.where(jnp.arange(GROUPS, dtype=jnp.int32) == full, GROUP_SLOTS, counts)
    return counts.astype(jnp.int32)


def set_ends(values, rng, least, high):
    extent = values.shape
    place = [jax.random.randint(jax.random.fold_in(rng, axis), (), 0, extent[axis]) for axis in range(len(extent))]
    values = values.at[tuple(place)].set(least)
    longest = extent.index(max(extent))
    place[longest] = (place[longest] + 1) % extent[longest]
    return values.at[tuple(place)].set(high)


def shard_levels(rng, shape, cuts, least, largest):
    loudness = 1.0
    for dim, blocks in cuts:
        steps = jax.random.uniform(jax.random.fold_in(jax.random.fold_in(rng, 6), dim), (blocks,), jnp.float32, least / len(cuts), largest / len(cuts))
        loudness = loudness * jnp.repeat(jnp.exp(steps), shape[dim] // blocks).reshape((-1,) + (1,) * (len(shape) - 1 - dim))
    return loudness


def noise(stream_key, extent, deviation, bound, cuts=(), kind=jnp.bfloat16):
    array = jax.random.normal(stream_key, extent, jnp.float32) * deviation
    if len(cuts) > 0:
        array = shard_levels(stream_key, extent, cuts, -0.22, 0.18) * array
    return jnp.clip(array, min=-bound, max=bound).astype(kind)


def setup_inputs(seed: int = 0) -> dict:
    seeds = jax.random.split(jax.random.key(seed), 19)
    latents = noise(seeds[0], (SAMPLES, SEQ, D), 1.0, 6.0, ((0, 32),))
    cotangent = noise(seeds[1], (SAMPLES, SEQ, D), 1.0, 6.0, ((0, 32),))
    bands = set_ends(jax.random.randint(seeds[2], (SAMPLES,), 0, BANDS), jax.random.fold_in(seeds[2], 1), 0, BANDS - 1).astype(jnp.int32)
    labels = set_ends(jax.random.randint(seeds[3], (SAMPLES,), 0, CLASSES), jax.random.fold_in(seeds[3], 1), 0, CLASSES - 1).astype(jnp.int32)
    kept = draw_kept(jax.random.fold_in(seeds[18], 71), 0)
    band_counts = draw_band_counts(jax.random.fold_in(seeds[18], 71), 0)
    time_table = noise(seeds[6], (BANDS, D), 1.0, 6.0, ((1, 8),))
    class_table = noise(seeds[7], (CLASSES, D), 1.0, 6.0, ((1, 8),))
    w_ada = noise(seeds[8], (D, 6 * D), D ** -0.5, 0.1875, ((1, 8),))
    b_ada = noise(seeds[9], (6 * D,), 0.5, 3.0, ((0, 8),))
    w_qkv = noise(seeds[10], (D, 3 * D), D ** -0.5, 0.1875, ((1, 8),))
    qv_bias = noise(seeds[11], (2 * D,), 0.3, 2.0, ((0, 8),))
    w_proj = noise(seeds[12], (D, D), (D // 16) ** -0.5, 0.75, ((0, 8),))
    b_proj = noise(seeds[13], (D,), 0.3, 2.0, ((0, 8),))
    w_fc1 = noise(seeds[14], (D, FF), D ** -0.5, 0.1875, ((1, 8),))
    b_fc1 = noise(seeds[15], (FF,), 0.3, 2.0, ((0, 8),))
    w_fc2 = noise(seeds[16], (FF, D), (FF // 4) ** -0.5, 0.1875, ((0, 8),))
    b_fc2 = noise(seeds[17], (D,), 0.3, 2.0, ((0, 8),))
    return dict(latents=latents, cotangent=cotangent, bands=bands, labels=labels, kept=kept, band_counts=band_counts, time_table=time_table, class_table=class_table, w_ada=w_ada, b_ada=b_ada, w_qkv=w_qkv, qv_bias=qv_bias, w_proj=w_proj, b_proj=b_proj, w_fc1=w_fc1, b_fc1=b_fc1, w_fc2=w_fc2, b_fc2=b_fc2)


EPS = 1e-06
HIGH = lax.Precision.HIGHEST

@jax.custom_vjp
def low(v):
    return lax.optimization_barrier(v.astype(jnp.bfloat16)).astype(jnp.float32)

@jax.custom_vjp
def low_back(v):
    return v

def low_keep(v):
    return (low(v), None)

def low_pass(kept, grad):
    return (grad,)

def back_keep(v):
    return (v, None)

def back_low(kept, grad):
    return (low(grad),)
low.defvjp(low_keep, low_pass)
low_back.defvjp(back_keep, back_low)

def modulate(values, shift, scale):
    mean = lax.optimization_barrier(jnp.mean(values, -1, keepdims=True))
    cent = values - mean
    var = lax.optimization_barrier(jnp.mean(cent * cent, -1, keepdims=True))
    return cent * lax.rsqrt(var + EPS) * (1.0 + scale[:, None, :]) + shift[:, None, :]

def matmul(a, b):
    return jnp.einsum('btd,de->bte', a, b, precision=HIGH)

def block(weights, tokens, cond):
    w_ada, b_ada, w_qkv, qv_bias, w_proj, b_proj, w_fc1, b_fc1, w_fc2, b_fc2 = weights
    count, length = (tokens.shape[0], tokens.shape[1])
    cvec = low(jax.nn.silu(cond))
    mod = low_back(jnp.dot(cvec, w_ada, precision=HIGH) + b_ada)
    shift1, scale1, gate1, shift2, scale2, gate2 = jnp.split(mod, 6, -1)
    h1 = low(modulate(tokens, shift1, scale1))
    bias = jnp.concatenate([qv_bias[:D], jnp.zeros((D,), jnp.float32), qv_bias[D:]])
    qkv = low(low_back(matmul(h1, w_qkv) + bias))
    query = qkv[..., :D].reshape(count, length, HEADS, HEAD_DIM)
    keys = qkv[..., D:2 * D].reshape(count, length, HEADS, HEAD_DIM)
    values = qkv[..., 2 * D:].reshape(count, length, HEADS, HEAD_DIM)
    scores = low_back(jnp.einsum('bqhd,bkhd->bhqk', query, keys, precision=HIGH) * HEAD_DIM ** (-0.5))
    probs = low(jax.nn.softmax(scores, -1))
    att = jnp.einsum('bhqk,bkhd->bqhd', probs, values, precision=HIGH).reshape(count, length, D)
    att = low(low_back(att))
    proj = low_back(matmul(att, w_proj) + b_proj)
    mixed = tokens + gate1[:, None, :] * proj
    h2 = low(modulate(mixed, shift2, scale2))
    pre = low_back(matmul(h2, w_fc1) + b_fc1)
    act = low(jax.nn.gelu(pre, approximate=True))
    mlp = low_back(matmul(act, w_fc2) + b_fc2)
    return mixed + gate2[:, None, :] * mlp

def reference(latents, cotangent, bands, labels, kept, band_counts, time_table, class_table, w_ada, b_ada, w_qkv, qv_bias, w_proj, b_proj, w_fc1, b_fc1, w_fc2, b_fc2):
    params = tuple((a.astype(jnp.float32) for a in (time_table, class_table, w_ada, b_ada, w_qkv, qv_bias, w_proj, b_proj, w_fc1, b_fc1, w_fc2, b_fc2)))
    samples = latents.shape[0]
    group_slots = samples // band_counts.shape[0]
    sample_ids = jnp.arange(samples, dtype=jnp.int32)
    count = band_counts[sample_ids // group_slots]
    weight = jnp.where(sample_ids % group_slots < count, 1.0, 0.0).astype(jnp.float32) / count.astype(jnp.float32)
    per = math.gcd(samples, 16)
    blocks = samples // per

    def forward(params, full):
        time_tab, class_tab = (params[0], params[1])
        rest = params[2:]

        def one(pieces):
            part, band_part, label_part, kept_part = pieces
            cond = time_tab[band_part] + class_tab[label_part]
            tokens = jnp.take_along_axis(part, kept_part[:, :, None], 1)
            result = block(rest, tokens, cond)
            rows = jnp.arange(per, dtype=jnp.int32)[:, None]
            return part.at[rows, kept_part].set(result)
        outs = lax.map(jax.checkpoint(one), (full.reshape(blocks, per, SEQ, D), bands.reshape(blocks, per), labels.reshape(blocks, per), kept.reshape(blocks, per, KEEP)))
        return outs.reshape(samples, SEQ, D)
    result, pull = jax.vjp(forward, params, latents.astype(jnp.float32))
    grads, input_grad = pull(weight[:, None, None] * cotangent.astype(jnp.float32))
    return (result.astype(jnp.bfloat16), input_grad.astype(jnp.bfloat16), grads[0], grads[1], grads[2], grads[3], grads[4], grads[5], grads[6], grads[7], grads[8], grads[9], grads[10], grads[11])
```

```python
import functools

import jax
import jax.numpy as jnp
from jax import lax
from jax.experimental import pallas as pl
from jax.experimental.pallas import tpu as pltpu
from jax.sharding import PartitionSpec as P

HEADS = 16
HEAD_DIM = 72


EPS = 1e-06
HIGH = lax.Precision.HIGHEST


def modulate(values, shift, scale):
    mean = jnp.mean(values, -1, keepdims=True)
    cent = values - mean
    var = jnp.mean(cent * cent, -1, keepdims=True)
    return cent * lax.rsqrt(var + EPS) * (1.0 + scale[:, None, :]) + shift[:, None, :]


def product(left, right):
    return jnp.einsum("btd,de->bte", left, right, preferred_element_type=jnp.float32)


def weight_term(left, right):
    return jnp.einsum("btd,bte->de", left, right, preferred_element_type=jnp.float32)


def core(weights, tokens, mod):
    w_qkv, qv_bias, w_proj, b_proj, w_fc1, b_fc1, w_fc2, b_fc2 = weights
    count, length, width = tokens.shape
    shift1, scale1, gate1, shift2, scale2, gate2 = jnp.split(mod, 6, -1)
    h1 = modulate(tokens, shift1, scale1).astype(jnp.bfloat16)
    bias = jnp.concatenate(
        [
            qv_bias[:width].astype(jnp.float32),
            jnp.zeros((width,), jnp.float32),
            qv_bias[width:].astype(jnp.float32),
        ]
    )
    qkv = (product(h1, w_qkv) + bias).astype(jnp.bfloat16)
    query = qkv[..., :width].reshape(count, length, HEADS, HEAD_DIM)
    keys = qkv[..., width : 2 * width].reshape(count, length, HEADS, HEAD_DIM)
    values = qkv[..., 2 * width :].reshape(count, length, HEADS, HEAD_DIM)
    scores = jnp.einsum(
        "bqhd,bkhd->bhqk", query, keys, preferred_element_type=jnp.float32
    ) * HEAD_DIM ** (-0.5)
    total = jax.scipy.special.logsumexp(scores, axis=-1, keepdims=True)
    probs_full = jnp.exp(scores - total)
    probs = probs_full.astype(jnp.bfloat16)
    att = (
        jnp.einsum("bhqk,bkhd->bqhd", probs, values, preferred_element_type=jnp.float32)
        .reshape(count, length, width)
        .astype(jnp.bfloat16)
    )
    proj = product(att, w_proj) + b_proj.astype(jnp.float32)
    mixed = tokens + gate1[:, None, :] * proj
    h2 = modulate(mixed, shift2, scale2).astype(jnp.bfloat16)
    pre = product(h2, w_fc1) + b_fc1.astype(jnp.float32)
    act = jax.nn.gelu(pre, approximate=True).astype(jnp.bfloat16)
    mlp = product(act, w_fc2) + b_fc2.astype(jnp.float32)
    result = mixed + gate2[:, None, :] * mlp
    saved = (h1, query, keys, values, probs_full, probs, att, proj, mixed, h2, pre, act, mlp)
    return (result, saved)


def body(
    latents,
    cotangent,
    bands,
    labels,
    kept,
    band_counts,
    time_table,
    class_table,
    w_ada,
    b_ada,
    w_qkv,
    qv_bias,
    w_proj,
    b_proj,
    w_fc1,
    b_fc1,
    w_fc2,
    b_fc2,
):
    gathered = (
        lax.all_gather(time_table, "grp", axis=1, tiled=True),
        lax.all_gather(class_table, "grp", axis=1, tiled=True),
        lax.all_gather(w_ada, "grp", axis=1, tiled=True),
        lax.all_gather(b_ada, "grp", axis=0, tiled=True),
        lax.all_gather(w_qkv, "grp", axis=1, tiled=True),
        lax.all_gather(qv_bias, "grp", axis=0, tiled=True),
        lax.all_gather(w_proj, "grp", axis=0, tiled=True),
        lax.all_gather(b_proj, "grp", axis=0, tiled=True),
        lax.all_gather(w_fc1, "grp", axis=1, tiled=True),
        lax.all_gather(b_fc1, "grp", axis=0, tiled=True),
        lax.all_gather(w_fc2, "grp", axis=0, tiled=True),
        lax.all_gather(b_fc2, "grp", axis=0, tiled=True),
    )
    time_full, class_full, ada_full, ada_bias = (gathered[0], gathered[1], gathered[2], gathered[3])
    samples = latents.shape[0]
    width = latents.shape[2]
    slot = lax.axis_index("dp") * samples + jnp.arange(samples, dtype=jnp.int32)
    group_count = band_counts[0]
    weight = jnp.where(slot < group_count, 1.0, 0.0).astype(jnp.float32) / group_count.astype(
        jnp.float32
    )
    band_hot = (bands[:, None] == jnp.arange(time_full.shape[0], dtype=jnp.int32)[None, :]).astype(
        jnp.float32
    )
    class_hot = (
        labels[:, None] == jnp.arange(class_full.shape[0], dtype=jnp.int32)[None, :]
    ).astype(jnp.float32)
    cond = jnp.dot(band_hot, time_full.astype(jnp.float32), precision=HIGH) + jnp.dot(
        class_hot, class_full.astype(jnp.float32), precision=HIGH
    )
    cvec = jax.nn.silu(cond).astype(jnp.bfloat16)
    mod = jnp.dot(cvec, ada_full, preferred_element_type=jnp.float32) + ada_bias.astype(jnp.float32)
    rows = jnp.arange(samples, dtype=jnp.int32)[:, None]
    tokens = jnp.take_along_axis(latents, kept[:, :, None], 1).astype(jnp.float32)
    result, unused = core(tuple(gathered[4:]), tokens, mod)
    block_out = latents.at[rows, kept].set(result.astype(jnp.bfloat16))
    fetched = (
        lax.all_gather(w_ada, "grp", axis=1, tiled=True),
        lax.all_gather(w_qkv, "grp", axis=1, tiled=True),
        lax.all_gather(qv_bias, "grp", axis=0, tiled=True),
        lax.all_gather(w_proj, "grp", axis=0, tiled=True),
        lax.all_gather(b_proj, "grp", axis=0, tiled=True),
        lax.all_gather(w_fc1, "grp", axis=1, tiled=True),
        lax.all_gather(b_fc1, "grp", axis=0, tiled=True),
        lax.all_gather(w_fc2, "grp", axis=0, tiled=True),
        lax.all_gather(b_fc2, "grp", axis=0, tiled=True),
    )
    ada_full = fetched[0]
    back = tuple(fetched[1:])
    qkv_full, unused_bias, proj_full, unused_pbias, fc1_full, unused_b1, fc2_full, unused_b2 = back
    result, saved = core(back, tokens, mod)
    h1, query, keys, values, probs_full, probs, att, proj, mixed, h2, pre, act, mlp = saved
    shift1, scale1, gate1, shift2, scale2, gate2 = jnp.split(mod, 6, -1)
    weighted = cotangent.astype(jnp.float32) * weight[:, None, None]
    grad_out = jnp.take_along_axis(weighted, kept[:, :, None], 1)
    grad_mlp = (gate2[:, None, :] * grad_out).astype(jnp.bfloat16)
    grad_gate2 = jnp.sum(grad_out * mlp, 1)
    fc2_grad = weight_term(act, grad_mlp)
    fc2_bias_grad = jnp.sum(grad_mlp.astype(jnp.float32), (0, 1))
    grad_act = jnp.einsum("bte,de->btd", grad_mlp, fc2_full, preferred_element_type=jnp.float32)
    unused_pre, gelu_back = jax.vjp(lambda value: jax.nn.gelu(value, approximate=True), pre)
    grad_pre = gelu_back(grad_act)[0].astype(jnp.bfloat16)
    fc1_grad = weight_term(h2, grad_pre)
    fc1_bias_grad = jnp.sum(grad_pre.astype(jnp.float32), (0, 1))
    grad_h2 = jnp.einsum("bte,de->btd", grad_pre, fc1_full, preferred_element_type=jnp.float32)
    unused_h2, norm_back = jax.vjp(modulate, mixed, shift2, scale2)
    grad_mixed, grad_shift2, grad_scale2 = norm_back(grad_h2)
    grad_mixed = grad_mixed + grad_out
    grad_proj = (gate1[:, None, :] * grad_mixed).astype(jnp.bfloat16)
    grad_gate1 = jnp.sum(grad_mixed * proj, 1)
    proj_grad = weight_term(att, grad_proj)
    proj_bias_grad = jnp.sum(grad_proj.astype(jnp.float32), (0, 1))
    grad_att = jnp.einsum(
        "bte,de->btd", grad_proj, proj_full, preferred_element_type=jnp.float32
    ).astype(jnp.bfloat16)
    grad_heads = grad_att.reshape(query.shape)
    grad_values = jnp.einsum(
        "bhqk,bqhd->bkhd", probs, grad_heads, preferred_element_type=jnp.float32
    )
    grad_probs = jnp.einsum(
        "bqhd,bkhd->bhqk", grad_heads, values, preferred_element_type=jnp.float32
    )
    grad_scores = probs_full * (grad_probs - jnp.sum(grad_probs * probs_full, -1, keepdims=True))
    grad_scores = grad_scores.astype(jnp.bfloat16)
    grad_query = jnp.einsum(
        "bhqk,bkhd->bqhd", grad_scores, keys, preferred_element_type=jnp.float32
    ) * HEAD_DIM ** (-0.5)
    grad_keys = jnp.einsum(
        "bhqk,bqhd->bkhd", grad_scores, query, preferred_element_type=jnp.float32
    ) * HEAD_DIM ** (-0.5)
    count, length = (tokens.shape[0], tokens.shape[1])
    grad_qkv = jnp.concatenate(
        [
            grad_query.reshape(count, length, width),
            grad_keys.reshape(count, length, width),
            grad_values.reshape(count, length, width),
        ],
        -1,
    ).astype(jnp.bfloat16)
    qkv_grad = weight_term(h1, grad_qkv)
    qkv_sums = jnp.sum(grad_qkv.astype(jnp.float32), (0, 1))
    qv_bias_grad = jnp.concatenate([qkv_sums[:width], qkv_sums[2 * width :]])
    grad_h1 = jnp.einsum("bte,de->btd", grad_qkv, qkv_full, preferred_element_type=jnp.float32)
    unused_h1, first_back = jax.vjp(modulate, tokens, shift1, scale1)
    grad_tokens, grad_shift1, grad_scale1 = first_back(grad_h1)
    grad_tokens = grad_tokens + grad_mixed
    latents_grad = weighted.at[rows, kept].set(grad_tokens).astype(jnp.bfloat16)
    grad_mod = jnp.concatenate(
        [grad_shift1, grad_scale1, grad_gate1, grad_shift2, grad_scale2, grad_gate2], -1
    ).astype(jnp.bfloat16)
    ada_grad = jnp.dot(cvec.T, grad_mod, preferred_element_type=jnp.float32)
    ada_bias_grad = jnp.sum(grad_mod.astype(jnp.float32), 0)
    grad_cvec = jnp.dot(grad_mod, ada_full.T, preferred_element_type=jnp.float32)
    unused_cond, silu_back = jax.vjp(jax.nn.silu, cond)
    grad_cond = silu_back(grad_cvec)[0]
    time_grad = jnp.dot(band_hot.T, grad_cond, precision=HIGH)
    class_grad = jnp.dot(class_hot.T, grad_cond, precision=HIGH)
    shares = (
        lax.psum_scatter(time_grad, "grp", scatter_dimension=1, tiled=True),
        lax.psum_scatter(class_grad, "grp", scatter_dimension=1, tiled=True),
        lax.psum_scatter(ada_grad, "grp", scatter_dimension=1, tiled=True),
        lax.psum_scatter(ada_bias_grad, "grp", scatter_dimension=0, tiled=True),
        lax.psum_scatter(qkv_grad, "grp", scatter_dimension=1, tiled=True),
        lax.psum_scatter(qv_bias_grad, "grp", scatter_dimension=0, tiled=True),
        lax.psum_scatter(proj_grad, "grp", scatter_dimension=0, tiled=True),
        lax.psum_scatter(proj_bias_grad, "grp", scatter_dimension=0, tiled=True),
        lax.psum_scatter(fc1_grad, "grp", scatter_dimension=1, tiled=True),
        lax.psum_scatter(fc1_bias_grad, "grp", scatter_dimension=0, tiled=True),
        lax.psum_scatter(fc2_grad, "grp", scatter_dimension=0, tiled=True),
        lax.psum_scatter(fc2_bias_grad, "grp", scatter_dimension=0, tiled=True),
    )
    totals = (
        lax.psum(shares[0].astype(jnp.bfloat16), "dp").astype(jnp.float32),
        lax.psum(shares[1].astype(jnp.bfloat16), "dp").astype(jnp.float32),
        lax.psum(shares[2].astype(jnp.bfloat16), "dp").astype(jnp.float32),
        lax.psum(shares[3].astype(jnp.bfloat16), "dp").astype(jnp.float32),
        lax.psum(shares[4].astype(jnp.bfloat16), "dp").astype(jnp.float32),
        lax.psum(shares[5].astype(jnp.bfloat16), "dp").astype(jnp.float32),
        lax.psum(shares[6].astype(jnp.bfloat16), "dp").astype(jnp.float32),
        lax.psum(shares[7].astype(jnp.bfloat16), "dp").astype(jnp.float32),
        lax.psum(shares[8].astype(jnp.bfloat16), "dp").astype(jnp.float32),
        lax.psum(shares[9].astype(jnp.bfloat16), "dp").astype(jnp.float32),
        lax.psum(shares[10].astype(jnp.bfloat16), "dp").astype(jnp.float32),
        lax.psum(shares[11].astype(jnp.bfloat16), "dp").astype(jnp.float32),
    )
    return (
        block_out,
        latents_grad,
        totals[0],
        totals[1],
        totals[2],
        totals[3],
        totals[4],
        totals[5],
        totals[6],
        totals[7],
        totals[8],
        totals[9],
        totals[10],
        totals[11],
    )


MESH = pl.DeviceIdType.MESH
F32 = jnp.float32
BF16 = jnp.bfloat16
GELU_A = 0.7978845608028654
GELU_B = 0.044715


def dot(left, right, dims):
    return lax.dot_general(left, right, ((dims[:1], dims[1:]), ((), ())), preferred_element_type=F32)


class Place:
    def __init__(self):
        self.g = lax.axis_index("grp")
        self.z = lax.axis_index("dp")
        self.c = self.g % 2
        self.x = (self.g // 2) % 2
        self.y = self.g // 4

    def block(self, dc, dx, dy):
        c = 1 - self.c if dc else self.c
        x = 1 - self.x if dx else self.x
        y = 1 - self.y if dy else self.y
        return y * 4 + x * 2 + c

    def device(self, dc, dx, dy):
        return (self.block(dc, dx, dy), self.z)


RELATIVE = [(r & 1, (r >> 1) & 1, r >> 2) for r in range(8)]


class Wire:
    def __init__(self, send, recv):
        self.send, self.recv, self.used = send, recv, 0

    def take(self, count):
        first = self.used
        self.used += count
        return first

    def copy(self, number, src, dst, device):
        return pltpu.make_async_remote_copy(
            src_ref=src,
            dst_ref=dst,
            send_sem=self.send.at[number],
            recv_sem=self.recv.at[number],
            device_id=device,
            device_id_type=MESH,
        )


def halves(rows):
    cut = rows // 32 * 16
    return pl.ds(0, cut), pl.ds(cut, rows - cut)


def greet(devices):
    barrier = pltpu.get_barrier_semaphore()
    for device in devices:
        pl.semaphore_signal(barrier, inc=1, device_id=device, device_id_type=MESH)
    pl.semaphore_wait(barrier, len(devices))


def plane(place):
    return [place.device(*rel) for rel in RELATIVE[1:]]


class Gather:
    def __init__(self, place, wire, buf):
        self.p, self.w, self.buf = place, wire, buf
        self.first = wire.take(8)
        self.parts = halves(buf.shape[1])

    def make(self, number, block, device, part=None):
        ref = self.buf.at[block]
        if part is not None:
            ref = self.buf.at[block, self.parts[part]]
        return self.w.copy(self.first + number, ref, ref, device)

    def copies(self):
        p = self.p
        own, xb, yb, db = p.g, p.block(0, 1, 0), p.block(0, 0, 1), p.block(0, 1, 1)
        xd, yd, sd = p.device(0, 1, 0), p.device(0, 0, 1), p.device(1, 0, 0)
        return [
            self.make(0, own, xd),
            self.make(1, own, yd),
            self.make(2, own, sd),
            self.make(3, xb, yd, 0),
            self.make(4, xb, sd),
            self.make(5, yb, xd, 1),
            self.make(6, yb, sd),
            self.make(7, db, sd),
        ]

    def start(self):
        self.c = self.copies()
        for number in (0, 1, 2):
            self.c[number].start()

    def neighbours(self):
        self.c[0].wait_recv()
        self.c[3].start()
        self.c[4].start()
        self.c[1].wait_recv()
        self.c[5].start()
        self.c[6].start()

    def far(self):
        self.c[3].wait_recv()
        self.c[5].wait_recv()
        self.c[7].start()

    def wait_sib(self):
        self.c[2].wait_recv()

    def wait_sib_neighbours(self):
        self.c[4].wait_recv()
        self.c[6].wait_recv()

    def wait_sib_far(self):
        self.c[7].wait_recv()

    def finish(self):
        for copy in self.c:
            copy.wait_send()


class Scatter:
    def __init__(self, place, wire, buf, r1, r2, r3):
        self.p, self.w, self.buf = place, wire, buf
        self.r1, self.r2, self.r3 = r1, r2, r3
        self.parts = halves(buf.shape[1])
        self.first = wire.take(10)
        p = place
        self.sib = [p.block(1, q & 1, q >> 1) for q in range(4)]
        self.mine = [p.block(0, q & 1, q >> 1) for q in range(4)]
        xd, yd, sd = p.device(0, 1, 0), p.device(0, 0, 1), p.device(1, 0, 0)
        f, w = self.first, wire
        lo, hi = self.parts
        self.s1 = [w.copy(f + q, buf.at[self.sib[q]], r1.at[q], sd) for q in range(4)]
        self.s2 = [
            w.copy(f + 4, buf.at[self.mine[3], lo], r2.at[0, pl.ds(0, lo.size)], xd),
            w.copy(f + 5, buf.at[self.mine[3], hi], r2.at[1, pl.ds(0, hi.size)], yd),
        ]
        self.s3 = [
            w.copy(f + 6, buf.at[self.mine[1], lo], r3.at[0, lo], xd),
            w.copy(f + 7, buf.at[self.mine[1], hi], r3.at[0, hi], xd),
            w.copy(f + 8, buf.at[self.mine[2], lo], r3.at[1, lo], yd),
            w.copy(f + 9, buf.at[self.mine[2], hi], r3.at[1, hi], yd),
        ]

    def send_sib(self, q):
        self.s1[q].start()

    def add_sib(self, q):
        self.s1[q].wait_recv()
        add_into(self.buf.at[self.mine[q]], self.r1.at[q])

    def send_far(self):
        self.add_sib(3)
        self.s2[0].start()
        self.s2[1].start()

    def send_near(self):
        self.add_sib(1)
        self.s3[0].start()
        self.add_sib(2)
        self.s3[3].start()

    def relay(self):
        lo, hi = self.parts
        self.s2[1].wait_recv()
        add_into(self.buf.at[self.mine[1], hi], self.r2.at[1, pl.ds(0, hi.size)])
        self.s3[1].start()
        self.s2[0].wait_recv()
        add_into(self.buf.at[self.mine[2], lo], self.r2.at[0, pl.ds(0, lo.size)])
        self.s3[2].start()
        self.add_sib(0)

    def result(self, out):
        for copy in self.s3:
            copy.wait_recv()
        rows = self.buf.shape[1]
        step = 16

        @pl.loop(0, rows // step)
        def _(i):
            at = pl.ds(pl.multiple_of(i * step, step), step)
            total = self.buf[self.mine[0], at].astype(F32) + self.r3[0, at].astype(F32) + self.r3[1, at].astype(F32)
            out[at] = total.astype(out.dtype)

    def finish(self):
        for copy in self.s1 + self.s2 + self.s3:
            copy.wait_send()


def add_into(ref, other):
    step = 16

    @pl.loop(0, ref.shape[0] // step)
    def _(i):
        at = pl.ds(pl.multiple_of(i * step, step), step)
        ref[at] = (ref[at].astype(F32) + other[at].astype(F32)).astype(ref.dtype)


def scatter_scratch(rows, width):
    return [
        pltpu.VMEM((4, rows, width), BF16),
        pltpu.VMEM((2, halves(rows)[1].size, width), BF16),
        pltpu.VMEM((2, rows, width), BF16),
    ]


def to_all(place, wire, make):
    first = wire.take(7)
    copies = []
    for number, rel in enumerate(RELATIVE[1:]):
        src, dst = make(rel)
        copies.append(wire.copy(first + number, src, dst, place.device(*rel)))
        copies[-1].start()
    return copies


def wait_recv(copies):
    for copy in copies:
        copy.wait_recv()


def wait_send(copies):
    for copy in copies:
        copy.wait_send()


def params(collective_id):
    return pltpu.CompilerParams(
        collective_id=collective_id, has_side_effects=True, vmem_limit_bytes=60 * 2**20
    )


VMEM = pl.BlockSpec(memory_space=pltpu.VMEM)


def front_kernel(samples, w_ref, ids_ref, class_ref, time_ref, ada_ref, bias_ref, w_all, cond_all, mod_in, ids_all, mod_out, send, recv):
    p = Place()
    wire = Wire(send, recv)
    greet(plane(p))
    g = p.g
    ids_all[g] = ids_ref[...]
    ids_copies = to_all(p, wire, lambda rel: (ids_ref, ids_all.at[g]))
    w_all[g] = w_ref[...]
    gather = Gather(p, wire, w_all)
    gather.start()
    wait_recv(ids_copies)
    labels = jnp.concatenate([ids_all[j, 0:samples, 0:1] for j in range(8)], 0)
    bands = jnp.concatenate([ids_all[j, 0:samples, 1:2] for j in range(8)], 0)

    def pick(ids, table):
        rows = ids.shape[0]
        lanes = lax.broadcasted_iota(jnp.int32, (rows, table.shape[0]), 1).astype(F32)
        hot = jnp.where(lanes == ids, 1.0, 0.0).astype(BF16)
        return jnp.dot(hot, table[...], preferred_element_type=F32)

    cond = pick(bands, time_ref) + pick(labels, class_ref)
    cond_all[g] = cond
    cond_copies = to_all(p, wire, lambda rel: (cond_all.at[g], cond_all.at[g]))
    wait_recv(cond_copies)
    depth = class_ref.shape[1]
    mod = jnp.zeros((cond.shape[0], ada_ref.shape[1]), F32) + bias_ref[...]
    for j in range(8):
        part = cond_all[j]
        vec = (part * jax.nn.sigmoid(part)).astype(BF16)
        mod = mod + jnp.dot(vec, ada_ref[j * depth : (j + 1) * depth, :], preferred_element_type=F32)
    mod_out[...] = jnp.zeros_like(mod_out)
    for j in range(8):
        mod_out[j, 0:samples, :] = mod[samples * j : samples * (j + 1), :]
    mod_in[g] = mod_out[g]
    mod_copies = to_all(p, wire, lambda rel: (mod_out.at[p.block(*rel)], mod_in.at[g]))
    wait_recv(mod_copies)
    gather.neighbours()
    gather.far()
    gather.wait_sib()
    gather.wait_sib_neighbours()
    gather.wait_sib_far()
    gather.finish()
    for copies in (ids_copies, cond_copies, mod_copies):
        wait_send(copies)


def front(samples, w, ids, class_table, time_table, w_ada, b_ada):
    rows = 8 * samples
    return pl.pallas_call(
        functools.partial(front_kernel, samples),
        out_shape=[
            jax.ShapeDtypeStruct((8,) + w.shape, BF16),
            jax.ShapeDtypeStruct((8, rows, class_table.shape[1]), F32),
            jax.ShapeDtypeStruct((8, 8, w_ada.shape[1]), F32),
        ],
        in_specs=[VMEM] * 6,
        out_specs=[VMEM] * 3,
        scratch_shapes=[
            pltpu.VMEM((8,) + ids.shape, F32),
            pltpu.VMEM((8, 8, w_ada.shape[1]), F32),
            pltpu.SemaphoreType.DMA((29,)),
            pltpu.SemaphoreType.DMA((29,)),
        ],
        compiler_params=params(1),
    )(w, ids, class_table, time_table, w_ada, b_ada)


def gelu_parts(pre):
    square = pre * pre
    inner = jnp.tanh(GELU_A * pre * (1.0 + GELU_B * square))
    act = 0.5 * pre * (1.0 + inner)
    slope = 0.5 * (1.0 + inner) + 0.5 * pre * (1.0 - inner * inner) * (GELU_A * (1.0 + 3.0 * GELU_B * square))
    return act, slope


def mlp_kernel(h2_ref, dm_ref, h1_ref, w1_ref, b1_ref, w2_ref, dh2_out, mlp_out, g1_out, g2_out, gb1_out, h1_all,
               h2_all, dm_all, act, dpre, pbuf, p1, p2, p3, qbuf, q1, q2, q3, acc, send, recv):
    p = Place()
    wire = Wire(send, recv)
    greet(plane(p))
    g = p.g
    h2_all[g] = h2_ref[...]
    dm_all[g] = dm_ref[...]
    h1_all[g] = h1_ref[...]
    gathers = [Gather(p, wire, buf) for buf in (h2_all, dm_all, h1_all)]
    main, back, other = gathers
    for gather in gathers:
        gather.start()
    sums = Scatter(p, wire, pbuf, p1, p2, p3)
    outs = Scatter(p, wire, qbuf, q1, q2, q3)
    gb1_out[...] = jnp.zeros_like(gb1_out)

    def units(block):
        pre = jnp.dot(h2_all[block], w1_ref[...], preferred_element_type=F32) + b1_ref[...]
        value, slope = gelu_parts(pre)
        act[block] = value.astype(BF16)
        low = (dot(dm_all[block], w2_ref[...], (1, 1)) * slope).astype(BF16)
        dpre[block] = low
        gb1_out[...] += jnp.sum(low.astype(F32), 0, keepdims=True)
        pbuf[block] = dot(low, w1_ref[...], (1, 1)).astype(BF16)

    def block_of(t):
        dc = jnp.where((t == 1) | (t == 4) | (t == 5) | (t == 7), 1, 0)
        dx = jnp.where((t == 2) | (t == 4) | (t >= 6), 1, 0)
        dy = jnp.where((t == 3) | (t >= 5), 1, 0)
        c, x, y = (p.c + dc) % 2, (p.x + dx) % 2, (p.y + dy) % 2
        return y * 4 + x * 2 + c

    @pl.loop(0, 8)
    def _(t):
        @pl.when(t == 1)
        def _():
            main.wait_sib()
            back.wait_sib()

        @pl.when(t == 2)
        def _():
            main.neighbours()
            back.neighbours()
            other.neighbours()

        @pl.when(t == 4)
        def _():
            main.wait_sib_neighbours()
            back.wait_sib_neighbours()

        @pl.when(t == 6)
        def _():
            main.far()
            back.far()

        @pl.when(t == 7)
        def _():
            main.wait_sib_far()
            back.wait_sib_far()

        units(block_of(t))
        for at, q in ((1, 0), (4, 1), (5, 2), (7, 3)):

            @pl.when(t == at)
            def _(q=q):
                sums.send_sib(q)

    sums.send_far()
    sums.send_near()

    @pl.loop(0, 8)
    def _(t):
        block = block_of(7 - t)
        qbuf[block] = jnp.dot(act[block], w2_ref[...], preferred_element_type=F32).astype(BF16)
        for at, q in ((1, 0), (4, 1), (5, 2), (7, 3)):

            @pl.when(t == 7 - at)
            def _(q=q):
                outs.send_sib(q)

    sums.relay()
    outs.send_far()
    outs.send_near()
    for left, right, out in ((dpre, h2_all, g1_out), (act, dm_all, g2_out)):
        acc[...] = jnp.zeros_like(acc)

        @pl.loop(0, 8)
        def _(block, left=left, right=right):
            acc[...] += dot(left[block], right[block], (0, 0))

        out[...] = acc[...].astype(BF16)
    outs.relay()
    sums.result(dh2_out)
    outs.result(mlp_out)
    other.far()
    other.wait_sib()
    other.wait_sib_neighbours()
    other.wait_sib_far()
    for piece in gathers + [sums, outs]:
        piece.finish()


def mlp_layer(h2, dm, h1, w1, b1, w2):
    rows, width = h2.shape
    hidden = w1.shape[1]
    return pl.pallas_call(
        mlp_kernel,
        out_shape=[
            jax.ShapeDtypeStruct((rows, width), F32),
            jax.ShapeDtypeStruct((rows, width), F32),
            jax.ShapeDtypeStruct((hidden, width), BF16),
            jax.ShapeDtypeStruct((hidden, width), BF16),
            jax.ShapeDtypeStruct((1, hidden), F32),
            jax.ShapeDtypeStruct((8, rows, width), BF16),
        ],
        in_specs=[VMEM] * 6,
        out_specs=[VMEM] * 6,
        scratch_shapes=[
            pltpu.VMEM((8, rows, width), BF16),
            pltpu.VMEM((8, rows, width), BF16),
            pltpu.VMEM((8, rows, hidden), BF16),
            pltpu.VMEM((8, rows, hidden), BF16),
            pltpu.VMEM((8, rows, width), BF16),
            *scatter_scratch(rows, width),
            pltpu.VMEM((8, rows, width), BF16),
            *scatter_scratch(rows, width),
            pltpu.VMEM((hidden, width), F32),
            pltpu.SemaphoreType.DMA((44,)),
            pltpu.SemaphoreType.DMA((44,)),
        ],
        compiler_params=params(2),
    )(h2, dm, h1, w1, b1, w2)


def swap_kernel(dq_ref, proj_ref, small_ref, dq_all, proj_out, small_all, pbuf, p1, p2, p3, send, recv):
    p = Place()
    wire = Wire(send, recv)
    greet(plane(p))
    g = p.g
    small_all[g] = small_ref[...]
    small = to_all(p, wire, lambda rel: (small_ref, small_all.at[g]))
    sums = Scatter(p, wire, pbuf, p1, p2, p3)
    pbuf[...] = proj_ref[...]
    for q in (3, 1, 2, 0):
        sums.send_sib(q)
    dq_all[g] = dq_ref[g]
    moves = to_all(p, wire, lambda rel: (dq_ref.at[p.block(*rel)], dq_all.at[g]))
    sums.send_far()
    sums.send_near()
    sums.relay()
    sums.result(proj_out)
    wait_recv(small)
    wait_recv(moves)
    sums.finish()
    wait_send(small)
    wait_send(moves)


def swap(dq, proj, small):
    rows, width = proj.shape[1:]
    return pl.pallas_call(
        swap_kernel,
        out_shape=[
            jax.ShapeDtypeStruct(dq.shape, BF16),
            jax.ShapeDtypeStruct((rows, width), BF16),
            jax.ShapeDtypeStruct((8,) + small.shape, F32),
        ],
        in_specs=[VMEM] * 3,
        out_specs=[VMEM] * 3,
        scratch_shapes=[
            pltpu.VMEM((8, rows, width), BF16),
            *scatter_scratch(rows, width),
            pltpu.SemaphoreType.DMA((24,)),
            pltpu.SemaphoreType.DMA((24,)),
        ],
        compiler_params=params(3),
    )(dq, proj, small)


CHUNK = 144


def last_kernel(planes, g1_ref, g2_ref, gq_ref, gp_ref, dc_ref, cond_ref, small_ref, out, dcond_all, small_all,
                from_end, middle, from_middle, dc_in, send, recv):
    p = Place()
    wire = Wire(send, recv)
    others = [(p.g, (p.z + k) % planes) for k in range(1, planes)]
    greet(plane(p) + others)
    g, z = p.g, p.z
    small_all[z] = small_ref[...]
    first = wire.take(planes - 1)
    small = []
    for k, device in enumerate(others):
        small.append(wire.copy(first + k, small_ref, small_all.at[z], device))
        small[-1].start()
    dc_in[g] = dc_ref[g]
    dcs = to_all(p, wire, lambda rel: (dc_ref.at[p.block(*rel)], dc_in.at[g]))

    sources = []
    for ref in (g1_ref, g2_ref, gq_ref, gp_ref):
        for start in range(0, ref.shape[0], CHUNK):
            sources.append(ref.at[pl.ds(start, CHUNK)])
    count = len(sources)
    up = wire.take(count)
    across = wire.take(count)
    down = wire.take(count)
    inner = 1 + z // 3
    outer = (z - 1) * 3
    partner = 3 - z
    at_end = (z == 0) | (z == planes - 1)
    ups = [wire.copy(up + k, sources[k], from_end.at[k], (g, inner)) for k in range(count)]
    acrosses = [wire.copy(across + k, middle.at[k], from_middle.at[k], (g, partner)) for k in range(count)]
    downs = [wire.copy(down + k, out.at[k], out.at[k], (g, outer)) for k in range(count)]

    @pl.when(at_end)
    def _():
        for k in range(count):
            ups[k].start()

    def total():
        wait_recv(dcs)
        vec = dc_in[0]
        for j in range(1, 8):
            vec = vec + dc_in[j]
        cond = cond_ref[...]
        gate = jax.nn.sigmoid(cond)
        dcond_all[z] = vec * (gate * (1.0 + cond * (1.0 - gate)))

    total()
    first = wire.take(planes - 1)
    conds = []
    for k, device in enumerate(others):
        conds.append(wire.copy(first + k, dcond_all.at[z], dcond_all.at[z], device))
        conds[-1].start()

    step = 16

    def settle(k):
        acrosses[k].wait_recv()

        @pl.loop(0, CHUNK // step)
        def _(i):
            at = pl.ds(pl.multiple_of(i * step, step), step)
            out[k, at] = (middle[k, at].astype(F32) + from_middle[k, at].astype(F32)).astype(BF16)

        downs[k].start()

    @pl.when(jnp.logical_not(at_end))
    def _():
        for k in range(count):
            ups[k].wait_recv()

            @pl.loop(0, CHUNK // step)
            def _(i):
                at = pl.ds(pl.multiple_of(i * step, step), step)
                middle[k, at] = (sources[k][at].astype(F32) + from_end[k, at].astype(F32)).astype(BF16)

            acrosses[k].start()
            if k > 0:
                settle(k - 1)
        settle(count - 1)
        for k in range(count):
            acrosses[k].wait_send()
            downs[k].wait_send()

    @pl.when(at_end)
    def _():
        for k in range(count):
            downs[k].wait_recv()
            ups[k].wait_send()

    wait_recv(small)
    wait_recv(conds)
    wait_send(small)
    wait_send(conds)
    wait_send(dcs)


def last(planes, g1, g2, gq, gp, dc, cond, small):
    count = (g1.shape[0] + g2.shape[0] + gq.shape[0] + gp.shape[0]) // CHUNK
    width = g1.shape[1]
    buf = pltpu.VMEM((count, CHUNK, width), BF16)
    sems = 2 * (planes - 1) + 7 + 3 * count
    return pl.pallas_call(
        functools.partial(last_kernel, planes),
        out_shape=[
            jax.ShapeDtypeStruct((count, CHUNK, width), BF16),
            jax.ShapeDtypeStruct((planes,) + cond.shape, F32),
            jax.ShapeDtypeStruct((planes,) + small.shape, F32),
        ],
        in_specs=[VMEM] * 7,
        out_specs=[VMEM] * 3,
        scratch_shapes=[
            buf,
            buf,
            buf,
            pltpu.VMEM(dc.shape, F32),
            pltpu.SemaphoreType.DMA((sems,)),
            pltpu.SemaphoreType.DMA((sems,)),
        ],
        compiler_params=params(4),
    )(g1, g2, gq, gp, dc, cond, small)


def plane_body(planes, latents, cotangent, bands, labels, kept, band_counts, time_table, class_table, w_ada, b_ada, w_qkv,
               qv_bias, w_proj, b_proj, w_fc1, b_fc1, w_fc2, b_fc2):
    samples, length, width = latents.shape
    keep = kept.shape[1]
    g = lax.axis_index("grp")
    wq = w_qkv.shape[1]
    wp = w_proj.shape[0]

    pair = jnp.stack([labels, bands], 1).astype(F32)
    ids = jnp.zeros((8, 128), F32).at[:samples, :2].set(pair)
    packed = jnp.concatenate([w_qkv.T, w_proj], 0)
    packed_all, cond_all, mod_in = front(samples, packed, ids, class_table, time_table, w_ada, b_ada.astype(F32)[None])
    qkv_t = packed_all[:, :wq].reshape(-1, width)
    proj_full = packed_all[:, wq:].reshape(-1, width)
    mod = mod_in[:, :samples].transpose(1, 0, 2).reshape(samples, -1)
    shift1, scale1, gate1, shift2, scale2, gate2 = jnp.split(mod, 6, -1)
    vectors = jnp.concatenate([qv_bias, b_proj, b_fc2]).astype(F32)
    vectors_all = lax.all_gather(vectors, "grp", axis=0)
    qv = vectors_all[:, : qv_bias.shape[0]].reshape(-1)
    bias_proj = vectors_all[:, qv_bias.shape[0] : qv_bias.shape[0] + b_proj.shape[0]].reshape(-1)
    bias_fc2 = vectors_all[:, qv_bias.shape[0] + b_proj.shape[0] :].reshape(-1)

    slot = lax.axis_index("dp") * samples + jnp.arange(samples, dtype=jnp.int32)
    group_count = band_counts[0]
    weight = jnp.where(slot < group_count, 1.0, 0.0).astype(F32) / group_count.astype(F32)
    hot = (kept[:, :, None] == jnp.arange(length, dtype=jnp.int32)[None, None, :]).astype(BF16)
    tokens = jnp.einsum("bks,bsd->bkd", hot, latents, preferred_element_type=F32)
    grad_out = jnp.einsum("bks,bsd->bkd", hot, cotangent, preferred_element_type=F32) * weight[:, None, None]
    is_kept = jnp.any(hot > 0, 1)[:, :, None]

    h1 = modulate(tokens, shift1, scale1).astype(BF16)
    bias = jnp.concatenate([qv[:width], jnp.zeros((width,), F32), qv[width:]])
    qkv = (jnp.einsum("btd,ed->bte", h1, qkv_t, preferred_element_type=F32) + bias).astype(BF16)
    query = qkv[..., :width].reshape(samples, keep, HEADS, HEAD_DIM)
    keys = qkv[..., width : 2 * width].reshape(samples, keep, HEADS, HEAD_DIM)
    values = qkv[..., 2 * width :].reshape(samples, keep, HEADS, HEAD_DIM)
    scores = jnp.einsum("bqhd,bkhd->bhqk", query, keys, preferred_element_type=F32) * HEAD_DIM ** (-0.5)
    probs_full = jax.nn.softmax(scores, -1)
    probs = probs_full.astype(BF16)
    att = (
        jnp.einsum("bhqk,bkhd->bqhd", probs, values, preferred_element_type=F32)
        .reshape(samples, keep, width)
        .astype(BF16)
    )
    proj = product(att, proj_full) + bias_proj
    mixed = tokens + gate1[:, None, :] * proj
    h2 = modulate(mixed, shift2, scale2).astype(BF16)
    grad_mlp = (gate2[:, None, :] * grad_out).astype(BF16)

    rows = samples * keep
    flat = lambda v: v.reshape(rows, v.shape[-1])
    grad_h2, mlp, fc1_grad, fc2_grad, fc1_sums, h1_all = mlp_layer(
        flat(h2), flat(grad_mlp), flat(h1), w_fc1, b_fc1.astype(F32)[None], w_fc2
    )
    grad_h2 = grad_h2.reshape(samples, keep, width)
    mlp = mlp.reshape(samples, keep, width) + bias_fc2
    result = mixed + gate2[:, None, :] * mlp
    spread = lambda v: jnp.einsum("bks,bkd->bsd", hot, v.astype(BF16), preferred_element_type=F32).astype(BF16)
    block_out = jnp.where(is_kept, spread(result), latents)

    grad_gate2 = jnp.sum(grad_out * mlp, 1)
    unused_h2, norm_back = jax.vjp(modulate, mixed, shift2, scale2)
    grad_mixed, grad_shift2, grad_scale2 = norm_back(grad_h2)
    grad_mixed = grad_mixed + grad_out
    grad_proj = (gate1[:, None, :] * grad_mixed).astype(BF16)
    grad_gate1 = jnp.sum(grad_mixed * proj, 1)
    proj_grad = weight_term(att, grad_proj).astype(BF16)

    grad_att = jnp.einsum("bte,de->btd", grad_proj, proj_full, preferred_element_type=F32).astype(BF16)
    grad_heads = grad_att.reshape(query.shape)
    grad_values = jnp.einsum("bhqk,bqhd->bkhd", probs, grad_heads, preferred_element_type=F32)
    grad_probs = jnp.einsum("bqhd,bkhd->bhqk", grad_heads, values, preferred_element_type=F32)
    grad_scores = probs_full * (grad_probs - jnp.sum(grad_probs * probs_full, -1, keepdims=True))
    grad_scores = grad_scores.astype(BF16)
    grad_query = jnp.einsum("bhqk,bkhd->bqhd", grad_scores, keys, preferred_element_type=F32) * HEAD_DIM ** (-0.5)
    grad_keys = jnp.einsum("bhqk,bqhd->bkhd", grad_scores, query, preferred_element_type=F32) * HEAD_DIM ** (-0.5)
    grad_qkv = jnp.concatenate(
        [v.reshape(samples, keep, width) for v in (grad_query, grad_keys, grad_values)], -1
    ).astype(BF16)
    grad_h1 = jnp.einsum("bte,ed->btd", grad_qkv, qkv_t, preferred_element_type=F32)
    unused_h1, first_back = jax.vjp(modulate, tokens, shift1, scale1)
    grad_tokens, grad_shift1, grad_scale1 = first_back(grad_h1)
    grad_tokens = grad_tokens + grad_mixed
    weighted = (cotangent.astype(F32) * weight[:, None, None]).astype(BF16)
    latents_grad = jnp.where(is_kept, spread(grad_tokens), weighted)

    grad_mod = jnp.stack([grad_shift1, grad_scale1, grad_gate1, grad_shift2, grad_scale2, grad_gate2], 1)
    grad_mod = grad_mod.astype(BF16).astype(F32)
    qkv_sums = jnp.sum(grad_qkv.astype(F32), (0, 1))
    sums = jnp.concatenate(
        [qkv_sums, jnp.sum(grad_proj.astype(F32), (0, 1)), jnp.sum(grad_mlp.astype(F32), (0, 1))]
    ).reshape(5, width)
    small = jnp.concatenate([grad_mod.reshape(samples * 6, width), sums], 0)
    small = jnp.pad(small, ((0, -small.shape[0] % 8), (0, 0)))
    grad_cols = flat(grad_qkv).T.reshape(8, wq, rows)
    grad_cols_all, proj_sum, small_all = swap(grad_cols, proj_grad.reshape(8, wp, width), small)
    qkv_grad = jnp.einsum("jer,jrd->ed", grad_cols_all, h1_all, preferred_element_type=F32).astype(BF16)
    mod_all = small_all[:, : samples * 6].reshape(8 * samples, 6 * width)
    mod_cols = w_ada.shape[1]
    mod_part = lax.dynamic_slice_in_dim(mod_all, g * mod_cols, mod_cols, 1).astype(BF16)
    grad_cvec = jnp.einsum("se,de->sd", mod_part, w_ada, preferred_element_type=F32)
    cols = class_table.shape[1]
    grad_cvec = grad_cvec.reshape(8 * samples, 8, cols).transpose(1, 0, 2)
    sums = jnp.sum(small_all[:, samples * 6 : samples * 6 + 5], 0)
    qv_sums = jnp.concatenate([sums[0], sums[2]])
    part = lambda v, size: lax.dynamic_slice_in_dim(v, g * size, size, 0)
    cond = lax.dynamic_index_in_dim(cond_all, g, 0, False)
    cvec = jax.nn.silu(cond_all).astype(BF16).astype(F32).transpose(1, 0, 2).reshape(8 * samples, width)
    flat_sums = jnp.concatenate(
        [part(qv_sums, qv_bias.shape[0]), part(sums[3], b_proj.shape[0]), part(sums[4], b_fc2.shape[0]), fc1_sums[0]]
    )
    flat_sums = jnp.pad(flat_sums, (0, 8 * width - flat_sums.shape[0])).reshape(8, width)
    pad_cols = -mod_cols % 128
    mod_pad = jnp.pad(mod_part.astype(F32), ((0, 0), (0, width - mod_cols)))
    id_rows = jnp.zeros((8, width), F32)
    ids_here = jnp.stack([labels, bands], 0).astype(F32)
    table_ids = lax.all_gather(ids_here, ("grp", "dp"), axis=0)
    packed_small = jnp.concatenate([cvec, mod_pad, flat_sums], 0)

    totals, dcond_all, small_z = last(
        planes, fc1_grad, fc2_grad, qkv_grad, proj_sum, grad_cvec, cond, packed_small
    )
    totals = totals.reshape(-1, width)
    hidden = w_fc1.shape[1]
    at = 0
    pieces = []
    for size in (hidden, hidden, wq, wp):
        pieces.append(totals[at : at + size].astype(F32))
        at += size
    per = 8 * samples
    cvec_z = small_z[:, :per].reshape(planes * per, width).astype(BF16)
    mod_z = small_z[:, per : 2 * per, :mod_cols].reshape(planes * per, mod_cols).astype(BF16)
    ada_grad = jnp.einsum("sd,se->de", cvec_z, mod_z, preferred_element_type=F32)
    ada_bias_grad = jnp.sum(mod_z.astype(F32), 0)
    flat_z = jnp.sum(small_z[:, 2 * per :], 0).reshape(-1)
    bounds = [0]
    for size in (qv_bias.shape[0], b_proj.shape[0], b_fc2.shape[0], hidden):
        bounds.append(bounds[-1] + size)
    qv_grad, bp_grad, b2_grad, b1_grad = (flat_z[bounds[i] : bounds[i + 1]] for i in range(4))
    ids_z = table_ids.reshape(8, planes, 2, samples).transpose(2, 1, 0, 3).reshape(2, planes * per)
    dcond = dcond_all.reshape(planes * per, cols)
    hot_class = (jnp.arange(class_table.shape[0], dtype=F32)[:, None] == ids_z[0][None, :]).astype(F32)
    hot_time = (jnp.arange(time_table.shape[0], dtype=F32)[:, None] == ids_z[1][None, :]).astype(F32)
    time_grad = jnp.dot(hot_time, dcond, precision=HIGH)
    class_grad = jnp.dot(hot_class, dcond, precision=HIGH)
    return (
        block_out,
        latents_grad,
        time_grad,
        class_grad,
        ada_grad,
        ada_bias_grad,
        pieces[2].T,
        qv_grad,
        pieces[3],
        bp_grad,
        pieces[0].T,
        b1_grad,
        pieces[1],
        b2_grad,
    )


def solution(mesh):
    planes = mesh.shape["dp"]
    small = mesh.shape["grp"] == 8 and planes == 4
    return jax.shard_map(
        functools.partial(plane_body, planes) if small else body,
        mesh=mesh,
        in_specs=(
            P(("grp", "dp"), None, None),
            P(("grp", "dp"), None, None),
            P(("grp", "dp")),
            P(("grp", "dp")),
            P(("grp", "dp"), None),
            P("grp"),
            P(None, "grp"),
            P(None, "grp"),
            P(None, "grp"),
            P("grp"),
            P(None, "grp"),
            P("grp"),
            P("grp", None),
            P("grp"),
            P(None, "grp"),
            P("grp"),
            P("grp", None),
            P("grp"),
        ),
        out_specs=(
            P(("grp", "dp"), None, None),
            P(("grp", "dp"), None, None),
            P(None, "grp"),
            P(None, "grp"),
            P(None, "grp"),
            P("grp"),
            P(None, "grp"),
            P("grp"),
            P("grp", None),
            P("grp"),
            P(None, "grp"),
            P("grp"),
            P("grp", None),
            P("grp"),
        ),
        check_vma=False,
    )
```

```python
import functools

import jax
import jax.numpy as jnp
from jax import lax
from jax.experimental import pallas as pl
from jax.experimental.pallas import tpu as pltpu
from jax.sharding import PartitionSpec as P

HEADS = 16
HEAD_DIM = 72


EPS = 1e-06
HIGH = lax.Precision.HIGHEST


def modulate(values, shift, scale):
    mean = jnp.mean(values, -1, keepdims=True)
    cent = values - mean
    var = jnp.mean(cent * cent, -1, keepdims=True)
    return cent * lax.rsqrt(var + EPS) * (1.0 + scale[:, None, :]) + shift[:, None, :]


def product(left, right):
    return jnp.einsum("btd,de->bte", left, right, preferred_element_type=jnp.float32)


def weight_term(left, right):
    return jnp.einsum("btd,bte->de", left, right, preferred_element_type=jnp.float32)


def core(weights, tokens, mod):
    w_qkv, qv_bias, w_proj, b_proj, w_fc1, b_fc1, w_fc2, b_fc2 = weights
    count, length, width = tokens.shape
    shift1, scale1, gate1, shift2, scale2, gate2 = jnp.split(mod, 6, -1)
    h1 = modulate(tokens, shift1, scale1).astype(jnp.bfloat16)
    bias = jnp.concatenate(
        [
            qv_bias[:width].astype(jnp.float32),
            jnp.zeros((width,), jnp.float32),
            qv_bias[width:].astype(jnp.float32),
        ]
    )
    qkv = (product(h1, w_qkv) + bias).astype(jnp.bfloat16)
    query = qkv[..., :width].reshape(count, length, HEADS, HEAD_DIM)
    keys = qkv[..., width : 2 * width].reshape(count, length, HEADS, HEAD_DIM)
    values = qkv[..., 2 * width :].reshape(count, length, HEADS, HEAD_DIM)
    scores = jnp.einsum(
        "bqhd,bkhd->bhqk", query, keys, preferred_element_type=jnp.float32
    ) * HEAD_DIM ** (-0.5)
    total = jax.scipy.special.logsumexp(scores, axis=-1, keepdims=True)
    probs_full = jnp.exp(scores - total)
    probs = probs_full.astype(jnp.bfloat16)
    att = (
        jnp.einsum("bhqk,bkhd->bqhd", probs, values, preferred_element_type=jnp.float32)
        .reshape(count, length, width)
        .astype(jnp.bfloat16)
    )
    proj = product(att, w_proj) + b_proj.astype(jnp.float32)
    mixed = tokens + gate1[:, None, :] * proj
    h2 = modulate(mixed, shift2, scale2).astype(jnp.bfloat16)
    pre = product(h2, w_fc1) + b_fc1.astype(jnp.float32)
    act = jax.nn.gelu(pre, approximate=True).astype(jnp.bfloat16)
    mlp = product(act, w_fc2) + b_fc2.astype(jnp.float32)
    result = mixed + gate2[:, None, :] * mlp
    saved = (h1, query, keys, values, probs_full, probs, att, proj, mixed, h2, pre, act, mlp)
    return (result, saved)


def body(
    latents,
    cotangent,
    bands,
    labels,
    kept,
    band_counts,
    time_table,
    class_table,
    w_ada,
    b_ada,
    w_qkv,
    qv_bias,
    w_proj,
    b_proj,
    w_fc1,
    b_fc1,
    w_fc2,
    b_fc2,
):
    gathered = (
        lax.all_gather(time_table, "grp", axis=1, tiled=True),
        lax.all_gather(class_table, "grp", axis=1, tiled=True),
        lax.all_gather(w_ada, "grp", axis=1, tiled=True),
        lax.all_gather(b_ada, "grp", axis=0, tiled=True),
        lax.all_gather(w_qkv, "grp", axis=1, tiled=True),
        lax.all_gather(qv_bias, "grp", axis=0, tiled=True),
        lax.all_gather(w_proj, "grp", axis=0, tiled=True),
        lax.all_gather(b_proj, "grp", axis=0, tiled=True),
        lax.all_gather(w_fc1, "grp", axis=1, tiled=True),
        lax.all_gather(b_fc1, "grp", axis=0, tiled=True),
        lax.all_gather(w_fc2, "grp", axis=0, tiled=True),
        lax.all_gather(b_fc2, "grp", axis=0, tiled=True),
    )
    time_full, class_full, ada_full, ada_bias = (gathered[0], gathered[1], gathered[2], gathered[3])
    samples = latents.shape[0]
    width = latents.shape[2]
    slot = lax.axis_index("dp") * samples + jnp.arange(samples, dtype=jnp.int32)
    group_count = band_counts[0]
    weight = jnp.where(slot < group_count, 1.0, 0.0).astype(jnp.float32) / group_count.astype(
        jnp.float32
    )
    band_hot = (bands[:, None] == jnp.arange(time_full.shape[0], dtype=jnp.int32)[None, :]).astype(
        jnp.float32
    )
    class_hot = (
        labels[:, None] == jnp.arange(class_full.shape[0], dtype=jnp.int32)[None, :]
    ).astype(jnp.float32)
    cond = jnp.dot(band_hot, time_full.astype(jnp.float32), precision=HIGH) + jnp.dot(
        class_hot, class_full.astype(jnp.float32), precision=HIGH
    )
    cvec = jax.nn.silu(cond).astype(jnp.bfloat16)
    mod = jnp.dot(cvec, ada_full, preferred_element_type=jnp.float32) + ada_bias.astype(jnp.float32)
    rows = jnp.arange(samples, dtype=jnp.int32)[:, None]
    tokens = jnp.take_along_axis(latents, kept[:, :, None], 1).astype(jnp.float32)
    result, unused = core(tuple(gathered[4:]), tokens, mod)
    block_out = latents.at[rows, kept].set(result.astype(jnp.bfloat16))
    fetched = (
        lax.all_gather(w_ada, "grp", axis=1, tiled=True),
        lax.all_gather(w_qkv, "grp", axis=1, tiled=True),
        lax.all_gather(qv_bias, "grp", axis=0, tiled=True),
        lax.all_gather(w_proj, "grp", axis=0, tiled=True),
        lax.all_gather(b_proj, "grp", axis=0, tiled=True),
        lax.all_gather(w_fc1, "grp", axis=1, tiled=True),
        lax.all_gather(b_fc1, "grp", axis=0, tiled=True),
        lax.all_gather(w_fc2, "grp", axis=0, tiled=True),
        lax.all_gather(b_fc2, "grp", axis=0, tiled=True),
    )
    ada_full = fetched[0]
    back = tuple(fetched[1:])
    qkv_full, unused_bias, proj_full, unused_pbias, fc1_full, unused_b1, fc2_full, unused_b2 = back
    result, saved = core(back, tokens, mod)
    h1, query, keys, values, probs_full, probs, att, proj, mixed, h2, pre, act, mlp = saved
    shift1, scale1, gate1, shift2, scale2, gate2 = jnp.split(mod, 6, -1)
    weighted = cotangent.astype(jnp.float32) * weight[:, None, None]
    grad_out = jnp.take_along_axis(weighted, kept[:, :, None], 1)
    grad_mlp = (gate2[:, None, :] * grad_out).astype(jnp.bfloat16)
    grad_gate2 = jnp.sum(grad_out * mlp, 1)
    fc2_grad = weight_term(act, grad_mlp)
    fc2_bias_grad = jnp.sum(grad_mlp.astype(jnp.float32), (0, 1))
    grad_act = jnp.einsum("bte,de->btd", grad_mlp, fc2_full, preferred_element_type=jnp.float32)
    unused_pre, gelu_back = jax.vjp(lambda value: jax.nn.gelu(value, approximate=True), pre)
    grad_pre = gelu_back(grad_act)[0].astype(jnp.bfloat16)
    fc1_grad = weight_term(h2, grad_pre)
    fc1_bias_grad = jnp.sum(grad_pre.astype(jnp.float32), (0, 1))
    grad_h2 = jnp.einsum("bte,de->btd", grad_pre, fc1_full, preferred_element_type=jnp.float32)
    unused_h2, norm_back = jax.vjp(modulate, mixed, shift2, scale2)
    grad_mixed, grad_shift2, grad_scale2 = norm_back(grad_h2)
    grad_mixed = grad_mixed + grad_out
    grad_proj = (gate1[:, None, :] * grad_mixed).astype(jnp.bfloat16)
    grad_gate1 = jnp.sum(grad_mixed * proj, 1)
    proj_grad = weight_term(att, grad_proj)
    proj_bias_grad = jnp.sum(grad_proj.astype(jnp.float32), (0, 1))
    grad_att = jnp.einsum(
        "bte,de->btd", grad_proj, proj_full, preferred_element_type=jnp.float32
    ).astype(jnp.bfloat16)
    grad_heads = grad_att.reshape(query.shape)
    grad_values = jnp.einsum(
        "bhqk,bqhd->bkhd", probs, grad_heads, preferred_element_type=jnp.float32
    )
    grad_probs = jnp.einsum(
        "bqhd,bkhd->bhqk", grad_heads, values, preferred_element_type=jnp.float32
    )
    grad_scores = probs_full * (grad_probs - jnp.sum(grad_probs * probs_full, -1, keepdims=True))
    grad_scores = grad_scores.astype(jnp.bfloat16)
    grad_query = jnp.einsum(
        "bhqk,bkhd->bqhd", grad_scores, keys, preferred_element_type=jnp.float32
    ) * HEAD_DIM ** (-0.5)
    grad_keys = jnp.einsum(
        "bhqk,bqhd->bkhd", grad_scores, query, preferred_element_type=jnp.float32
    ) * HEAD_DIM ** (-0.5)
    count, length = (tokens.shape[0], tokens.shape[1])
    grad_qkv = jnp.concatenate(
        [
            grad_query.reshape(count, length, width),
            grad_keys.reshape(count, length, width),
            grad_values.reshape(count, length, width),
        ],
        -1,
    ).astype(jnp.bfloat16)
    qkv_grad = weight_term(h1, grad_qkv)
    qkv_sums = jnp.sum(grad_qkv.astype(jnp.float32), (0, 1))
    qv_bias_grad = jnp.concatenate([qkv_sums[:width], qkv_sums[2 * width :]])
    grad_h1 = jnp.einsum("bte,de->btd", grad_qkv, qkv_full, preferred_element_type=jnp.float32)
    unused_h1, first_back = jax.vjp(modulate, tokens, shift1, scale1)
    grad_tokens, grad_shift1, grad_scale1 = first_back(grad_h1)
    grad_tokens = grad_tokens + grad_mixed
    latents_grad = weighted.at[rows, kept].set(grad_tokens).astype(jnp.bfloat16)
    grad_mod = jnp.concatenate(
        [grad_shift1, grad_scale1, grad_gate1, grad_shift2, grad_scale2, grad_gate2], -1
    ).astype(jnp.bfloat16)
    ada_grad = jnp.dot(cvec.T, grad_mod, preferred_element_type=jnp.float32)
    ada_bias_grad = jnp.sum(grad_mod.astype(jnp.float32), 0)
    grad_cvec = jnp.dot(grad_mod, ada_full.T, preferred_element_type=jnp.float32)
    unused_cond, silu_back = jax.vjp(jax.nn.silu, cond)
    grad_cond = silu_back(grad_cvec)[0]
    time_grad = jnp.dot(band_hot.T, grad_cond, precision=HIGH)
    class_grad = jnp.dot(class_hot.T, grad_cond, precision=HIGH)
    shares = (
        lax.psum_scatter(time_grad, "grp", scatter_dimension=1, tiled=True),
        lax.psum_scatter(class_grad, "grp", scatter_dimension=1, tiled=True),
        lax.psum_scatter(ada_grad, "grp", scatter_dimension=1, tiled=True),
        lax.psum_scatter(ada_bias_grad, "grp", scatter_dimension=0, tiled=True),
        lax.psum_scatter(qkv_grad, "grp", scatter_dimension=1, tiled=True),
        lax.psum_scatter(qv_bias_grad, "grp", scatter_dimension=0, tiled=True),
        lax.psum_scatter(proj_grad, "grp", scatter_dimension=0, tiled=True),
        lax.psum_scatter(proj_bias_grad, "grp", scatter_dimension=0, tiled=True),
        lax.psum_scatter(fc1_grad, "grp", scatter_dimension=1, tiled=True),
        lax.psum_scatter(fc1_bias_grad, "grp", scatter_dimension=0, tiled=True),
        lax.psum_scatter(fc2_grad, "grp", scatter_dimension=0, tiled=True),
        lax.psum_scatter(fc2_bias_grad, "grp", scatter_dimension=0, tiled=True),
    )
    totals = (
        lax.psum(shares[0].astype(jnp.bfloat16), "dp").astype(jnp.float32),
        lax.psum(shares[1].astype(jnp.bfloat16), "dp").astype(jnp.float32),
        lax.psum(shares[2].astype(jnp.bfloat16), "dp").astype(jnp.float32),
        lax.psum(shares[3].astype(jnp.bfloat16), "dp").astype(jnp.float32),
        lax.psum(shares[4].astype(jnp.bfloat16), "dp").astype(jnp.float32),
        lax.psum(shares[5].astype(jnp.bfloat16), "dp").astype(jnp.float32),
        lax.psum(shares[6].astype(jnp.bfloat16), "dp").astype(jnp.float32),
        lax.psum(shares[7].astype(jnp.bfloat16), "dp").astype(jnp.float32),
        lax.psum(shares[8].astype(jnp.bfloat16), "dp").astype(jnp.float32),
        lax.psum(shares[9].astype(jnp.bfloat16), "dp").astype(jnp.float32),
        lax.psum(shares[10].astype(jnp.bfloat16), "dp").astype(jnp.float32),
        lax.psum(shares[11].astype(jnp.bfloat16), "dp").astype(jnp.float32),
    )
    return (
        block_out,
        latents_grad,
        totals[0],
        totals[1],
        totals[2],
        totals[3],
        totals[4],
        totals[5],
        totals[6],
        totals[7],
        totals[8],
        totals[9],
        totals[10],
        totals[11],
    )


MESH = pl.DeviceIdType.MESH
F32 = jnp.float32
BF16 = jnp.bfloat16
GELU_A = 0.7978845608028654
GELU_B = 0.044715


def dot(left, right, dims):
    return lax.dot_general(left, right, ((dims[:1], dims[1:]), ((), ())), preferred_element_type=F32)


class Place:
    def __init__(self):
        self.g = lax.axis_index("grp")
        self.z = lax.axis_index("dp")
        self.c = self.g % 2
        self.x = (self.g // 2) % 2
        self.y = self.g // 4

    def block(self, dc, dx, dy):
        c = 1 - self.c if dc else self.c
        x = 1 - self.x if dx else self.x
        y = 1 - self.y if dy else self.y
        return y * 4 + x * 2 + c

    def device(self, dc, dx, dy):
        return (self.block(dc, dx, dy), self.z)


RELATIVE = [(r & 1, (r >> 1) & 1, r >> 2) for r in range(8)]


class Wire:
    def __init__(self, send, recv):
        self.send, self.recv, self.used = send, recv, 0

    def take(self, count):
        first = self.used
        self.used += count
        return first

    def copy(self, number, src, dst, device):
        return pltpu.make_async_remote_copy(
            src_ref=src,
            dst_ref=dst,
            send_sem=self.send.at[number],
            recv_sem=self.recv.at[number],
            device_id=device,
            device_id_type=MESH,
        )


def halves(rows):
    cut = rows // 32 * 16
    return pl.ds(0, cut), pl.ds(cut, rows - cut)


def greet(devices):
    barrier = pltpu.get_barrier_semaphore()
    for device in devices:
        pl.semaphore_signal(barrier, inc=1, device_id=device, device_id_type=MESH)
    pl.semaphore_wait(barrier, len(devices))


def plane(place):
    return [place.device(*rel) for rel in RELATIVE[1:]]


class Gather:
    def __init__(self, place, wire, buf):
        self.p, self.w, self.buf = place, wire, buf
        self.first = wire.take(8)
        self.parts = halves(buf.shape[1])
        self.c = self.copies()

    def make(self, number, block, device, part=None):
        ref = self.buf.at[block]
        if part is not None:
            ref = self.buf.at[block, self.parts[part]]
        return self.w.copy(self.first + number, ref, ref, device)

    def copies(self):
        p = self.p
        own, xb, yb, db = p.g, p.block(0, 1, 0), p.block(0, 0, 1), p.block(0, 1, 1)
        xd, yd, sd = p.device(0, 1, 0), p.device(0, 0, 1), p.device(1, 0, 0)
        return [
            self.make(0, own, xd),
            self.make(1, own, yd),
            self.make(2, own, sd),
            self.make(3, xb, yd, 0),
            self.make(4, xb, sd),
            self.make(5, yb, xd, 1),
            self.make(6, yb, sd),
            self.make(7, db, sd),
        ]

    def start(self):
        for number in (0, 1, 2):
            self.c[number].start()

    def neighbours(self):
        self.c[0].wait_recv()
        self.c[3].start()
        self.c[4].start()
        self.c[1].wait_recv()
        self.c[5].start()
        self.c[6].start()

    def far(self):
        self.c[3].wait_recv()
        self.c[5].wait_recv()
        self.c[7].start()

    def wait_sib(self):
        self.c[2].wait_recv()

    def wait_sib_neighbours(self):
        self.c[4].wait_recv()
        self.c[6].wait_recv()

    def wait_sib_far(self):
        self.c[7].wait_recv()

    def finish(self):
        for copy in self.c:
            copy.wait_send()


class Scatter:
    def __init__(self, place, wire, buf, r1, r2, r3, rows=None):
        self.p, self.w, self.buf = place, wire, buf
        self.r1, self.r2, self.r3 = r1, r2, r3
        self.rows = rows or buf.shape[1]
        self.parts = halves(self.rows)
        self.first = wire.take(10)
        p = place
        self.sib = [p.block(1, q & 1, q >> 1) for q in range(4)]
        self.mine = [p.block(0, q & 1, q >> 1) for q in range(4)]
        xd, yd, sd = p.device(0, 1, 0), p.device(0, 0, 1), p.device(1, 0, 0)
        f, w = self.first, wire
        lo, hi = self.parts
        whole = pl.ds(0, self.rows)
        self.s1 = [w.copy(f + q, buf.at[self.sib[q], whole], r1.at[q], sd) for q in range(4)]
        self.s2 = [
            w.copy(f + 4, buf.at[self.mine[3], lo], r2.at[0, pl.ds(0, lo.size)], xd),
            w.copy(f + 5, buf.at[self.mine[3], hi], r2.at[1, pl.ds(0, hi.size)], yd),
        ]
        self.s3 = [
            w.copy(f + 6, buf.at[self.mine[1], lo], r3.at[0, lo], xd),
            w.copy(f + 7, buf.at[self.mine[1], hi], r3.at[0, hi], xd),
            w.copy(f + 8, buf.at[self.mine[2], lo], r3.at[1, lo], yd),
            w.copy(f + 9, buf.at[self.mine[2], hi], r3.at[1, hi], yd),
        ]

    def send_sib(self, q):
        self.s1[q].start()

    def add_sib(self, q):
        self.s1[q].wait_recv()
        add_into(self.buf.at[self.mine[q], pl.ds(0, self.rows)], self.r1.at[q])

    def send_far(self):
        self.add_sib(3)
        self.s2[0].start()
        self.s2[1].start()

    def send_near(self):
        self.add_sib(1)
        self.s3[0].start()
        self.add_sib(2)
        self.s3[3].start()

    def relay(self):
        lo, hi = self.parts
        self.s2[1].wait_recv()
        add_into(self.buf.at[self.mine[1], hi], self.r2.at[1, pl.ds(0, hi.size)])
        self.s3[1].start()
        self.s2[0].wait_recv()
        add_into(self.buf.at[self.mine[2], lo], self.r2.at[0, pl.ds(0, lo.size)])
        self.s3[2].start()
        self.add_sib(0)

    def result(self, out):
        for copy in self.s3:
            copy.wait_recv()
        rows = self.rows
        step = 16

        @pl.loop(0, rows // step)
        def _(i):
            at = pl.ds(pl.multiple_of(i * step, step), step)
            total = self.buf[self.mine[0], at].astype(F32) + self.r3[0, at].astype(F32) + self.r3[1, at].astype(F32)
            out[at] = total.astype(out.dtype)

    def finish(self):
        for copy in self.s1 + self.s2 + self.s3:
            copy.wait_send()


def add_into(ref, other):
    step = 16

    @pl.loop(0, ref.shape[0] // step)
    def _(i):
        at = pl.ds(pl.multiple_of(i * step, step), step)
        ref[at] = (ref[at].astype(F32) + other[at].astype(F32)).astype(ref.dtype)


def scatter_scratch(rows, width):
    return [
        pltpu.VMEM((4, rows, width), BF16),
        pltpu.VMEM((2, halves(rows)[1].size, width), BF16),
        pltpu.VMEM((2, rows, width), BF16),
    ]


def to_all(place, wire, make):
    first = wire.take(7)
    copies = []
    for number, rel in enumerate(RELATIVE[1:]):
        src, dst = make(rel)
        copies.append(wire.copy(first + number, src, dst, place.device(*rel)))
        copies[-1].start()
    return copies


def wait_recv(copies):
    for copy in copies:
        copy.wait_recv()


def wait_send(copies):
    for copy in copies:
        copy.wait_send()


def params(collective_id):
    return pltpu.CompilerParams(
        collective_id=collective_id, has_side_effects=True, vmem_limit_bytes=62 * 2**20
    )


VMEM = pl.BlockSpec(memory_space=pltpu.VMEM)

def gelu_parts(pre):
    square = pre * pre
    inner = jnp.tanh(GELU_A * pre * (1.0 + GELU_B * square))
    act = 0.5 * pre * (1.0 + inner)
    slope = 0.5 * (1.0 + inner) + 0.5 * pre * (1.0 - inner * inner) * (GELU_A * (1.0 + 3.0 * GELU_B * square))
    return act, slope


def local(src, dst, sem):
    return pltpu.make_async_copy(src, dst, sem)


def own_tokens(kept_ref, length, s):
    rows = lax.broadcasted_iota(jnp.int32, (length, kept_ref.shape[1]), 0)
    return jnp.where(rows == kept_ref[s : s + 1, :], 1.0, 0.0).astype(BF16)


def normed(v):
    cent = v - jnp.mean(v, -1, keepdims=True)
    inv = lax.rsqrt(jnp.mean(cent * cent, -1, keepdims=True) + EPS)
    return cent * inv, inv


def norm_back(grad, hat, inv):
    return inv * (grad - jnp.mean(grad, -1, keepdims=True) - hat * jnp.mean(grad * hat, -1, keepdims=True))


STEP = 32


def by_rows(samples, keep, fn):
    @pl.loop(0, samples * keep // STEP)
    def _(i):
        fn(lax.div(i, keep // STEP), pl.ds(pl.multiple_of(i * STEP, STEP), STEP))


SCALE = HEAD_DIM ** (-0.5)


def probabilities(q, k):
    scores = dot(q, k, (0, 0)) * SCALE
    exps = jnp.exp(scores - jnp.max(scores, -1, keepdims=True))
    return exps / jnp.sum(exps, -1, keepdims=True)


def arrival(p, t):
    dc = jnp.where((t == 1) | (t == 4) | (t == 5) | (t == 7), 1, 0)
    dx = jnp.where((t == 2) | (t == 4) | (t >= 6), 1, 0)
    dy = jnp.where((t == 3) | (t >= 5), 1, 0)
    c, x, y = lax.rem(p.c + dc, 2), lax.rem(p.x + dx, 2), lax.rem(p.y + dy, 2)
    return y * 4 + x * 2 + c


MSG_PROJ, MSG_FC2, MSG_QV, MSG_ROWS = 8, 16, 24, 40


def sample_weight(place, counts_ref, samples, s):
    count = jnp.full((1, 128), counts_ref[0], jnp.int32)
    used = count > place.z * samples + s
    return (jnp.where(used, 1.0, 0.0) / count.astype(F32))[:, 0:1]


def forward_kernel(samples, labels_ref, bands_ref, counts_ref, wq_ref, wp_ref, bias_ref, kept_ref, lat_ref, cot_ref, class_ref,
                   time_ref, ada_ref, bada_ref, w1_ref, b1_ref, w2_ref,
                   w_out, act_out, units_out, att_out, h1_out, mixed_out, proj_out, g1_out, g2_out, gb1_out, dh2_out, mod_out,
                   cond_out, vec_out, ids_out,
                   w_all, msg_all, cond_all, mod_in, mod_send, mod, h1, units, att, proj, mixed, vec, h2_all, dm_all, act, dpre,
                   pbuf, p1, p2, p3, acc, send, recv, sems):
    p = Place()
    wire = Wire(send, recv)
    greet(plane(p))
    g = p.g
    length = lat_ref.shape[1]
    keep = kept_ref.shape[1]
    rows, width = h1.shape
    pair = 2 * HEAD_DIM
    lanes = lax.broadcasted_iota(jnp.int32, (1, msg_all.shape[2]), 1)
    msg_all[g, 0:8] = jnp.zeros((8, msg_all.shape[2]), F32)
    for s in range(samples):
        line = jnp.where(lanes == 0, labels_ref[s], 0) + jnp.where(lanes == 1, bands_ref[s], 0)
        msg_all[g, s : s + 1, :] = line.astype(F32)
    msg_all[g, 8:MSG_ROWS] = jnp.zeros((MSG_ROWS - 8, msg_all.shape[2]), F32)
    for row in range(4):
        at = MSG_PROJ + 8 * row
        msg_all[g, at : at + 1, :] = bias_ref[row : row + 1, :]
    msgs = to_all(p, wire, lambda rel: (msg_all.at[g], msg_all.at[g]))
    w_all[g, 0 : 3 * pair] = wq_ref[...]
    w_all[g, 3 * pair : 4 * pair] = wp_ref[...]
    weights = Gather(p, wire, w_all)
    weights.start()
    main = Gather(p, wire, h2_all)
    back = Gather(p, wire, dm_all)
    sums = Scatter(p, wire, pbuf, p1, p2, p3)

    for s in range(samples):
        hot = own_tokens(kept_ref, length, s)
        at = pl.ds(s * keep, keep)
        mixed[at] = dot(hot, lat_ref[s], (0, 0))
        proj[at] = dot(hot, cot_ref[s], (0, 0)) * sample_weight(p, counts_ref, samples, s)

    wait_recv(msgs)
    labels = jnp.concatenate([msg_all[j, 0:samples, 0:1] for j in range(8)], 0)
    bands = jnp.concatenate([msg_all[j, 0:samples, 1:2] for j in range(8)], 0)

    def one_hot(ids, size):
        lanes = lax.broadcasted_iota(jnp.int32, (ids.shape[0], size), 1).astype(F32)
        return jnp.where(lanes == ids, 1.0, 0.0).astype(BF16)

    of_band = dot(one_hot(bands, time_ref.shape[0]), time_ref[...], (1, 0))
    cond_all[g] = of_band + dot(one_hot(labels, class_ref.shape[1]), class_ref[...], (1, 1))
    ids_out[...] = jnp.zeros_like(ids_out)
    ids_out[:, 0:1] = labels
    ids_out[:, 1:2] = bands
    conds = to_all(p, wire, lambda rel: (cond_all.at[g], cond_all.at[g]))
    wait_recv(conds)
    value = jnp.concatenate([cond_all[j] for j in range(8)], 1)
    value = (value * jax.nn.sigmoid(value)).astype(BF16)
    mods = dot(value, ada_ref[...], (1, 1)) + bada_ref[...]
    mod_send[...] = jnp.zeros_like(mod_send)
    for j in range(8):
        mod_send[j, 0:samples, :] = mods[samples * j : samples * (j + 1), :]
    mod_in[g] = mod_send[g]
    modc = to_all(p, wire, lambda rel: (mod_send.at[p.block(*rel)], mod_in.at[g]))
    vec[...] = jnp.zeros_like(vec)
    for row, at in ((0, MSG_PROJ), (1, MSG_FC2)):
        vec[row : row + 1, :] = jnp.concatenate([msg_all[j, at : at + 1, :] for j in range(8)], 1)
    wait_recv(modc)
    mod[...] = jnp.zeros_like(mod)
    for s in range(samples):
        line = jnp.concatenate([mod_in[j, s : s + 1, :] for j in range(8)], 1)
        for v in range(6):
            mod[s, v : v + 1, :] = line[:, v * width : (v + 1) * width]

    def first(s, at):
        hat, inv = normed(mixed[at])
        h1[at] = (hat * (1.0 + mod[s, 1:2, :]) + mod[s, 0:1, :]).astype(BF16)
        dm_all[g, at] = (mod[s, 5:6, :] * proj[at]).astype(BF16)

    by_rows(samples, keep, first)

    ones = jnp.ones((8, rows), BF16)

    @pl.loop(0, 8)
    def _(t):
        @pl.when(t == 1)
        def _():
            weights.wait_sib()

        @pl.when(t == 2)
        def _():
            weights.neighbours()
            back.start()

        @pl.when(t == 4)
        def _():
            weights.wait_sib_neighbours()

        @pl.when(t == 6)
        def _():
            weights.far()

        @pl.when(t == 7)
        def _():
            weights.wait_sib_far()

        block = arrival(p, t)
        for i in range(3):
            chunk = block * 3 + i
            bias_at = jnp.where(chunk >= 16, chunk - 8, chunk)
            keys = (chunk >= 8) & (chunk < 16)
            line = msg_all[lax.div(bias_at, 2), pl.ds(pl.multiple_of(MSG_QV + 8 * lax.rem(bias_at, 2), 8), 8), :]
            line = line * jnp.where(keys, 0.0, 1.0)
            value = dot(w_all[block, i * pair : (i + 1) * pair, :], h1[...], (1, 1))
            value = value + dot(line.astype(BF16), ones, (0, 0))
            units[2 * chunk] = value[:HEAD_DIM].astype(BF16)
            units[2 * chunk + 1] = value[HEAD_DIM:].astype(BF16)

    outs = [
        local(w_all, w_out, sems.at[0]),
        local(units, units_out, sems.at[1]),
        local(h1, h1_out, sems.at[2]),
        local(mod, mod_out, sems.at[3]),
        local(cond_all, cond_out, sems.at[4]),
        local(vec, vec_out, sems.at[5]),
        local(att, att_out, sems.at[6]),
        local(proj, proj_out, sems.at[7]),
        local(mixed, mixed_out, sems.at[8]),
        local(act, act_out, sems.at[9]),
    ]
    for copy in outs[:6]:
        copy.start()
    proj[...] = jnp.zeros_like(proj)

    @pl.loop(0, 8)
    def _(u):
        @pl.when(u == 6)
        def _():
            back.neighbours()

        for s in range(samples):
            lanes = pl.ds(s * keep, keep)
            pieces = []
            for e in range(2):
                probs = probabilities(units[2 * u + e, :, lanes], units[16 + 2 * u + e, :, lanes])
                pieces.append(dot(units[32 + 2 * u + e, :, lanes], probs.astype(BF16), (1, 1)))
            att[u, :, lanes] = jnp.concatenate(pieces, 0).astype(BF16)
        proj[...] += dot(att[u], w_all[u, pl.ds(3 * pair, pair), :], (0, 0))

    def second(s, at):
        proj[at] = proj[at] + vec[0:1, :]
        mixed[at] = mixed[at] + mod[s, 2:3, :] * proj[at]
        hat, inv = normed(mixed[at])
        h2_all[g, at] = (hat * (1.0 + mod[s, 4:5, :]) + mod[s, 3:4, :]).astype(BF16)

    by_rows(samples, keep, second)
    main.start()
    back.far()
    for copy in outs[6:9]:
        copy.start()

    gb1_out[...] = jnp.zeros_like(gb1_out)

    def hidden(block):
        pre = dot(h2_all[block], w1_ref[...], (1, 1)) + b1_ref[...]
        value, slope = gelu_parts(pre)
        act[block] = value.astype(BF16)
        low = (dot(dm_all[block], w2_ref[...], (1, 1)) * slope).astype(BF16)
        dpre[block] = low
        gb1_out[...] += jnp.sum(low.astype(F32), 0, keepdims=True)
        pbuf[block] = dot(low, w1_ref[...], (1, 0)).astype(BF16)

    @pl.loop(0, 8)
    def _(t):
        @pl.when(t == 1)
        def _():
            main.wait_sib()
            back.wait_sib()

        @pl.when(t == 2)
        def _():
            main.neighbours()
            back.wait_sib_neighbours()
            back.wait_sib_far()

        @pl.when(t == 4)
        def _():
            main.wait_sib_neighbours()

        @pl.when(t == 6)
        def _():
            main.far()

        @pl.when(t == 7)
        def _():
            main.wait_sib_far()

        hidden(arrival(p, t))
        for at, q in ((1, 0), (4, 1), (5, 2), (7, 3)):

            @pl.when(t == at)
            def _(q=q):
                sums.send_sib(q)

    outs[9].start()
    sums.send_far()
    sums.send_near()

    tile = acc.shape[1]
    for left, right, out in ((dpre, h2_all, g1_out), (act, dm_all, g2_out)):
        for n in range(width // tile):
            at = pl.ds(n * tile, tile)
            acc[...] = jnp.zeros_like(acc)

            @pl.loop(0, 8)
            def _(block, left=left, right=right, at=at):
                acc[...] += dot(left[block], right[block, :, at], (0, 0))

            out[:, at] = acc[...].astype(BF16)
        if left is dpre:
            sums.relay()
    sums.result(dh2_out)
    for piece in (weights, main, back, sums):
        piece.finish()
    for copies in (msgs, conds, modc):
        wait_send(copies)
    for copy in outs:
        copy.wait()


ANY = pl.BlockSpec(memory_space=pl.ANY)


SMEM = pl.BlockSpec(memory_space=pltpu.SMEM)


def forward(samples, labels, bands, counts, wq, wp, bias, kept, lat, cot, class_table, time_table, w_ada, b_ada, w1, b1, w2):
    keep, width = kept.shape[1], wq.shape[1]
    rows, hidden, count = samples * keep, w1.shape[0], 8 * samples
    shape = jax.ShapeDtypeStruct
    mods = (8, 8, w_ada.shape[0])
    cond = (8, count, class_table.shape[0])
    w = (8, wq.shape[0] + wp.shape[0], width)
    return pl.pallas_call(
        functools.partial(forward_kernel, samples),
        out_shape=[
            shape(w, BF16),
            shape((8, rows, hidden), BF16),
            shape((48, HEAD_DIM, rows), BF16),
            shape((8, 2 * HEAD_DIM, rows), BF16),
            shape((rows, width), BF16),
            shape((rows, width), F32),
            shape((rows, width), F32),
            shape((hidden, width), BF16),
            shape((hidden, width), BF16),
            shape((1, hidden), F32),
            shape((rows, width), F32),
            shape((samples, 8, width), F32),
            shape(cond, F32),
            shape((8, width), F32),
            shape((count, 128), F32),
        ],
        in_specs=[SMEM] * 3 + [VMEM] * 13,
        out_specs=[ANY] * 7 + [VMEM] * 4 + [ANY] * 3 + [VMEM],
        scratch_shapes=[
            pltpu.VMEM(w, BF16),
            pltpu.VMEM((8, MSG_ROWS, wp.shape[0]), F32),
            pltpu.VMEM(cond, F32),
            pltpu.VMEM(mods, F32),
            pltpu.VMEM(mods, F32),
            pltpu.VMEM((samples, 8, width), F32),
            pltpu.VMEM((rows, width), BF16),
            pltpu.VMEM((48, HEAD_DIM, rows), BF16),
            pltpu.VMEM((8, 2 * HEAD_DIM, rows), BF16),
            pltpu.VMEM((rows, width), F32),
            pltpu.VMEM((rows, width), F32),
            pltpu.VMEM((8, width), F32),
            pltpu.VMEM((8, rows, width), BF16),
            pltpu.VMEM((8, rows, width), BF16),
            pltpu.VMEM((8, rows, hidden), BF16),
            pltpu.VMEM((8, rows, hidden), BF16),
            pltpu.VMEM((8, rows, width), BF16),
            *scatter_scratch(rows, width),
            pltpu.VMEM((hidden, width // 3), F32),
            pltpu.SemaphoreType.DMA((55,)),
            pltpu.SemaphoreType.DMA((55,)),
            pltpu.SemaphoreType.DMA((10,)),
        ],
        compiler_params=params(1),
    )(labels, bands, counts, wq, wp, bias, kept, lat, cot, class_table, time_table, w_ada, b_ada, w1, b1, w2)


CHUNK = 144


def backward_kernel(samples, planes, counts_ref, w_hbm, act_hbm, units_hbm, att_hbm, h1_ref, mixed_ref, proj_ref, g1_ref, g2_ref, gb1_ref,
                    dh2_ref, mod_ref, cond_ref, vec_ref, ids_ref, kept_ref, lat_ref, cot_ref, ada_ref, w2_ref,
                    out, block_out, lat_out, dmod_z, dcond_z, cvec_z, sum_z, ids_z,
                    wt, wp, act, units, att, h1_all, dx2, dproj, dq, dq_all, from_end, gq, gp, qr1, qr2, qr3, pr1, pr2, pr3,
                    mlp, dh1, grad, dmod_send, dmod_in, dc_send, dc_in, bundle, bundles, send, recv, sems):
    p = Place()
    wire = Wire(send, recv)
    others = [(p.g, (p.z + k) % planes) for k in range(1, planes)]
    greet(plane(p) + others)
    g, z = p.g, p.z
    length = lat_ref.shape[1]
    keep = kept_ref.shape[1]
    rows, width = dx2.shape
    pair = 2 * HEAD_DIM
    loads = [
        local(w_hbm.at[:, pl.ds(3 * pair, pair)], wp, sems.at[0]),
        local(units_hbm, units, sems.at[1]),
        local(att_hbm, att, sems.at[2]),
        local(w_hbm.at[:, pl.ds(0, 3 * pair)], wt, sems.at[3]),
        local(act_hbm, act, sems.at[4]),
    ]
    for copy in loads:
        copy.start()

    sources = []
    for ref in (g1_ref, g2_ref, gp, gq):
        for start in range(0, ref.shape[0], CHUNK):
            sources.append(ref.at[pl.ds(start, CHUNK)])
    count = len(sources)
    up, across, down = wire.take(count), wire.take(count), wire.take(count)
    inner, outer, partner = 1 + z // 3, (z - 1) * 3, 3 - z
    at_end = (z == 0) | (z == planes - 1)
    ups = [wire.copy(up + k, sources[k], from_end.at[k], (g, inner)) for k in range(count)]
    acrosses = [wire.copy(across + k, from_end.at[k], out.at[k], (g, partner)) for k in range(count)]
    downs = [wire.copy(down + k, out.at[k], out.at[k], (g, outer)) for k in range(count)]

    def chain_send(*numbers):
        @pl.when(at_end)
        def _():
            for k in numbers:
                ups[k].start()

    def chain(*numbers):
        @pl.when(jnp.logical_not(at_end))
        def _():
            for k in numbers:
                if k < count:
                    ups[k].wait_recv()
                    add_into(from_end.at[k], sources[k])
                    acrosses[k].start()
                if k > 0:
                    acrosses[k - 1].wait_recv()
                    add_into(out.at[k - 1], from_end.at[k - 1])
                    downs[k - 1].start()

    chain_send(*range(8))

    tokens = Gather(p, wire, h1_all)
    h1_all[g] = h1_ref[...]
    tokens.start()

    value = cond_ref[...]
    cvec_z[z] = (value * jax.nn.sigmoid(value)).astype(BF16)
    ids_z[z] = ids_ref[...]
    first = wire.take(2 * (planes - 1))
    cvecs = [wire.copy(first + k, cvec_z.at[z], cvec_z.at[z], device) for k, device in enumerate(others)]
    first += planes - 1
    cvecs += [wire.copy(first + k, ids_z.at[z], ids_z.at[z], device) for k, device in enumerate(others)]
    for copy in cvecs:
        copy.start()

    for s in range(samples):
        hot = own_tokens(kept_ref, length, s)
        grad[pl.ds(s * keep, keep)] = dot(hot, cot_ref[s], (0, 0)) * sample_weight(p, counts_ref, samples, s)
    bundle[...] = jnp.zeros_like(bundle)

    def add_row(row, value):
        bundle[pl.ds(row, 1), :] += jnp.sum(value, 0, keepdims=True)

    SUM_PROJ, SUM_FC2 = 6 * samples, 6 * samples + 1

    def second(s, at):
        hat, inv = normed(mixed_ref[at])
        up_grad = dh2_ref[at]
        value = grad[at] + norm_back(up_grad * (1.0 + mod_ref[s, 4:5, :]), hat, inv)
        dx2[at] = value
        low = (mod_ref[s, 2:3, :] * value).astype(BF16)
        dproj[at] = low
        add_row(s * 6 + 3, up_grad)
        add_row(s * 6 + 4, up_grad * hat)
        add_row(s * 6 + 2, value * proj_ref[at])
        add_row(SUM_PROJ, low.astype(F32))
        add_row(SUM_FC2, (mod_ref[s, 5:6, :] * grad[at]).astype(BF16).astype(F32))

    by_rows(samples, keep, second)
    for copy in loads[:3]:
        copy.wait()

    @pl.loop(0, 8)
    def _(u):
        datt = dot(wp[u], dproj[...], (1, 1))
        wp[u] = dot(att[u], dproj[...], (1, 0)).astype(BF16)
        lists = ([], [], [])
        for s in range(samples):
            lanes = pl.ds(s * keep, keep)
            parts = ([], [], [])
            for e in range(2):
                q, k, v = (units[16 * i + 2 * u + e, :, lanes] for i in range(3))
                da = datt[e * HEAD_DIM : (e + 1) * HEAD_DIM, s * keep : (s + 1) * keep].astype(BF16)
                probs = probabilities(q, k)
                dprobs = dot(da, v, (0, 0))
                dscores = probs * (dprobs - jnp.sum(dprobs * probs, -1, keepdims=True))
                dscores = dscores.astype(BF16)
                parts[0].append(dot(k, dscores, (1, 1)) * SCALE)
                parts[1].append(dot(q, dscores, (1, 0)) * SCALE)
                parts[2].append(dot(da, probs.astype(BF16), (1, 0)))
            for i in range(3):
                lists[i].append(jnp.concatenate(parts[i], 0).astype(BF16))
        for i in range(3):
            chunk = 8 * i + u
            at = pl.ds(pl.multiple_of(lax.rem(chunk, 3) * pair, 16), pair)
            for s in range(samples):
                dq[lax.div(chunk, 3), at, pl.ds(s * keep, keep)] = lists[i][s]

        @pl.when(u == 3)
        def _():
            tokens.neighbours()
            chain(0)

        @pl.when(u == 7)
        def _():
            tokens.far()
            chain(1)

    dq_all[g] = dq[g]
    moves = to_all(p, wire, lambda rel: (dq.at[p.block(*rel)], dq_all.at[g]))
    projs = Scatter(p, wire, wp, pr1, pr2, pr3)
    for q in (3, 1, 2, 0):
        projs.send_sib(q)
    chain(2)

    loads[3].wait()
    dh1[...] = jnp.zeros_like(dh1)

    @pl.loop(0, 8)
    def _(j):
        dh1[...] += dot(dq[j], wt[j], (0, 0))

    projs.send_far()
    projs.send_near()
    chain(3)

    loads[4].wait()
    outs = Scatter(p, wire, wt, qr1, qr2, qr3, rows)

    @pl.loop(0, 8)
    def _(t):
        block = arrival(p, 7 - t)
        wt[block, pl.ds(0, rows)] = jnp.dot(act[block], w2_ref[...], preferred_element_type=F32).astype(BF16)
        for at, q in ((1, 0), (4, 1), (5, 2), (7, 3)):

            @pl.when(t == 7 - at)
            def _(q=q):
                outs.send_sib(q)

    projs.relay()
    outs.send_far()
    outs.send_near()
    chain(4)
    projs.result(gp)
    chain_send(8)

    for s in range(samples):
        hot = own_tokens(kept_ref, length, s)
        mlp[pl.ds(s * keep, keep)] = dot(hot, lat_ref[s], (0, 0))

    def back_first(s, at):
        hat, inv = normed(mlp[at])
        up_grad = dh1[at]
        dx = dx2[at] + norm_back(up_grad * (1.0 + mod_ref[s, 1:2, :]), hat, inv)
        add_row(s * 6, up_grad)
        add_row(s * 6 + 1, up_grad * hat)
        dproj[at] = dx.astype(BF16)

    by_rows(samples, keep, back_first)
    for s in range(samples):
        hot = own_tokens(kept_ref, length, s)
        is_kept = jnp.sum(hot.astype(F32), 1, keepdims=True) > 0.5
        spread = dot(hot, dproj[pl.ds(s * keep, keep)], (1, 0))
        weighted = cot_ref[s].astype(F32) * sample_weight(p, counts_ref, samples, s)
        lat_out[s] = jnp.where(is_kept, spread, weighted).astype(BF16)
    chain(5)

    tokens.wait_sib()
    tokens.wait_sib_neighbours()
    tokens.wait_sib_far()
    wait_recv(moves)
    for i in range(3):
        at = pl.ds(i * pair, pair)
        dh1[0:pair] = jnp.zeros((pair, width), F32)

        @pl.loop(0, 8)
        def _(j, at=at):
            dh1[0:pair] += dot(dq_all[j, at, :], h1_all[j], (1, 0))

        gq[at] = dh1[0:pair].astype(BF16)
        chain_send(9 + i)
    chain(6)

    outs.relay()
    outs.result(mlp)

    def end(s, at):
        value = mlp[at] + vec_ref[1:2, :]
        add_row(s * 6 + 5, grad[at] * value)
        dproj[at] = (mixed_ref[at] + mod_ref[s, 5:6, :] * value).astype(BF16)

    by_rows(samples, keep, end)
    chain(7)

    cols = ada_ref.shape[0]
    dmod_send[...] = jnp.zeros_like(dmod_send)
    for s in range(samples):
        line = jnp.concatenate([bundle[s * 6 + v : s * 6 + v + 1, :] for v in range(6)], 1)
        line = line.astype(BF16).astype(F32)
        for j in range(8):
            dmod_send[j, s : s + 1, :] = line[:, j * cols : (j + 1) * cols]
    dmod_in[g] = dmod_send[g]
    dmods = to_all(p, wire, lambda rel: (dmod_send.at[p.block(*rel)], dmod_in.at[g]))
    bundles[g, 0:8, :] = jnp.zeros((8, width), F32)
    bundles[g, 0:2, :] = bundle[SUM_PROJ : SUM_PROJ + 2, :]
    ones = jnp.ones((8, rows), BF16)
    for j in range(8):
        line = dot(ones, dq[j], (1, 1))
        bundles[g, 8 + j : 9 + j, 0 : 3 * pair] = line[0:1, :]
    sums = to_all(p, wire, lambda rel: (bundles.at[g], bundles.at[g]))

    for s in range(samples):
        hot = own_tokens(kept_ref, length, s)
        is_kept = jnp.sum(hot.astype(F32), 1, keepdims=True) > 0.5
        spread = dot(hot, dproj[pl.ds(s * keep, keep)], (1, 0))
        block_out[s] = jnp.where(is_kept, spread, lat_ref[s].astype(F32)).astype(BF16)

    wait_recv(dmods)
    part = jnp.concatenate([dmod_in[j, 0:samples, :] for j in range(8)], 0)
    dmod_z[z] = part
    first = wire.take(planes - 1)
    dmodz = [wire.copy(first + k, dmod_z.at[z], dmod_z.at[z], device) for k, device in enumerate(others)]
    for copy in dmodz:
        copy.start()
    dcvec = dot(part.astype(BF16), ada_ref[...], (1, 0))
    depth = cond_ref.shape[2]
    for j in range(8):
        dc_send[j] = dcvec[:, j * depth : (j + 1) * depth]
    dc_in[g] = dc_send[g]
    dcs = to_all(p, wire, lambda rel: (dc_send.at[p.block(*rel)], dc_in.at[g]))
    wait_recv(sums)
    sum_z[z] = sum(bundles[j] for j in range(8))
    sum_z[z, 2:3, 0 : gb1_ref.shape[1]] = gb1_ref[...]
    first = wire.take(planes - 1)
    sumz = [wire.copy(first + k, sum_z.at[z], sum_z.at[z], device) for k, device in enumerate(others)]
    for copy in sumz:
        copy.start()
    wait_recv(dcs)
    cond = cond_ref[g]
    gate = jax.nn.sigmoid(cond)
    dcond_z[z] = sum(dc_in[j] for j in range(8)) * (gate * (1.0 + cond * (1.0 - gate)))
    first = wire.take(planes - 1)
    dconds = [wire.copy(first + k, dcond_z.at[z], dcond_z.at[z], device) for k, device in enumerate(others)]
    for copy in dconds:
        copy.start()

    chain(*range(8, count + 1))

    @pl.when(jnp.logical_not(at_end))
    def _():
        for k in range(count):
            acrosses[k].wait_send()
            downs[k].wait_send()

    @pl.when(at_end)
    def _():
        for k in range(count):
            downs[k].wait_recv()
            ups[k].wait_send()

    for copies in (cvecs, dmodz, sumz, dconds):
        wait_recv(copies)
    for copies in (moves, dmods, sums, dcs, cvecs, dmodz, sumz, dconds):
        wait_send(copies)
    for piece in (tokens, projs, outs):
        piece.finish()


def backward(samples, planes, counts, w, act, units, att, h1, mixed, proj, g1, g2, gb1, dh2, mod, cond, vec, ids, kept, lat, cot,
             w_ada, w2):
    keep, width = kept.shape[1], h1.shape[1]
    rows, per = samples * keep, 8 * samples
    pair = 2 * HEAD_DIM
    wq, wp = 3 * pair, pair
    count = (g1.shape[0] + g2.shape[0] + wq + wp) // CHUNK
    shape = jax.ShapeDtypeStruct
    cols, depth = w_ada.shape[0], cond.shape[2]
    sems = 3 * count + 8 + 5 * (planes - 1) + 7 + 10 + 10 + 7 + 7 + 7
    return pl.pallas_call(
        functools.partial(backward_kernel, samples, planes),
        out_shape=[
            shape((count, CHUNK, width), BF16),
            shape(lat.shape, BF16),
            shape(lat.shape, BF16),
            shape((planes, per, cols), F32),
            shape((planes, per, depth), F32),
            shape((planes, 8, per, depth), BF16),
            shape((planes, 16, width), F32),
            shape((planes,) + ids.shape, F32),
        ],
        in_specs=[SMEM] + [ANY] * 4 + [VMEM] * 16,
        out_specs=[VMEM] * 8,
        scratch_shapes=[
            pltpu.VMEM((8, wq, width), BF16),
            pltpu.VMEM((8, wp, width), BF16),
            pltpu.VMEM(act.shape, BF16),
            pltpu.VMEM(units.shape, BF16),
            pltpu.VMEM(att.shape, BF16),
            pltpu.VMEM((8, rows, width), BF16),
            pltpu.VMEM((rows, width), F32),
            pltpu.VMEM((rows, width), BF16),
            pltpu.VMEM((8, wq, rows), BF16),
            pltpu.VMEM((8, wq, rows), BF16),
            pltpu.VMEM((count, CHUNK, width), BF16),
            pltpu.VMEM((wq, width), BF16),
            pltpu.VMEM((wp, width), BF16),
            *scatter_scratch(rows, width),
            *scatter_scratch(wp, width),
            pltpu.VMEM((rows, width), F32),
            pltpu.VMEM((rows, width), F32),
            pltpu.VMEM((rows, width), F32),
            pltpu.VMEM((8, 8, cols), F32),
            pltpu.VMEM((8, 8, cols), F32),
            pltpu.VMEM((8, per, depth), F32),
            pltpu.VMEM((8, per, depth), F32),
            pltpu.VMEM((16, width), F32),
            pltpu.VMEM((8, 16, width), F32),
            pltpu.SemaphoreType.DMA((sems,)),
            pltpu.SemaphoreType.DMA((sems,)),
            pltpu.SemaphoreType.DMA((5,)),
        ],
        compiler_params=params(2),
    )(counts, w, act, units, att, h1, mixed, proj, g1, g2, gb1, dh2, mod, cond, vec, ids, kept, lat, cot, w_ada, w2)


def plane_body(planes, latents, cotangent, bands, labels, kept, band_counts, time_table, class_table, w_ada, b_ada, w_qkv,
               qv_bias, w_proj, b_proj, w_fc1, b_fc1, w_fc2, b_fc2):
    samples, length, width = latents.shape
    g = lax.axis_index("grp")
    wq = w_qkv.shape[1]
    wp = w_proj.shape[0]
    hidden = w_fc1.shape[1]
    per = 8 * samples

    bias = jnp.concatenate([b_proj, b_fc2, qv_bias]).astype(F32).reshape(4, wp)
    (w, act, units, att, h1, mixed, proj, g1, g2, gb1, dh2, mod, cond, vec, ids) = forward(
        samples, labels, bands, band_counts, w_qkv.T, w_proj, bias, kept, latents, cotangent, class_table.T, time_table, w_ada.T,
        b_ada.astype(F32)[None], w_fc1.T, b_fc1.astype(F32)[None], w_fc2
    )
    totals, block_out, latents_grad, dmod_z, dcond_z, cvec_z, sum_z, ids_z = backward(
        samples, planes, band_counts, w, act, units, att, h1, mixed, proj, g1, g2, gb1, dh2, mod, cond, vec, ids, kept, latents,
        cotangent, w_ada.T, w_fc2
    )
    totals = totals.reshape(-1, width)
    at = 0
    pieces = []
    for size in (hidden, hidden, wp, wq):
        pieces.append(totals[at : at + size].astype(F32))
        at += size
    cvec_z = cvec_z.transpose(0, 2, 1, 3).reshape(planes * per, width)
    mod_z = dmod_z.reshape(planes * per, -1).astype(BF16)
    ada_grad = jnp.einsum("se,sd->ed", mod_z, cvec_z, preferred_element_type=F32).T
    ada_bias_grad = jnp.sum(mod_z.astype(F32), 0)
    sums = jnp.sum(sum_z, 0)
    part = lambda v, size: lax.dynamic_slice_in_dim(v, g * size, size, 0)
    qkv_sums = sums[8:, :wq].reshape(-1)
    qv_grad = part(jnp.concatenate([qkv_sums[:width], qkv_sums[2 * width :]]), qv_bias.shape[0])
    dcond = dcond_z.reshape(planes * per, -1)
    ids_z = ids_z.reshape(planes * per, -1)
    hot_class = (jnp.arange(class_table.shape[0], dtype=F32)[None, :] == ids_z[:, 0:1]).astype(F32)
    hot_time = (jnp.arange(time_table.shape[0], dtype=F32)[:, None] == ids_z[:, 1][None, :]).astype(F32)
    return (
        block_out,
        latents_grad,
        jnp.dot(hot_time, dcond, precision=HIGH),
        jnp.einsum("se,sc->ec", dcond, hot_class, precision=HIGH).T,
        ada_grad,
        ada_bias_grad,
        pieces[3].T,
        qv_grad,
        pieces[2],
        part(sums[0], b_proj.shape[0]),
        pieces[0].T,
        sums[2, :hidden],
        pieces[1],
        part(sums[1], b_fc2.shape[0]),
    )


def solution(mesh):
    planes = mesh.shape["dp"]
    small = mesh.shape["grp"] == 8 and planes == 4
    return jax.shard_map(
        functools.partial(plane_body, planes) if small else body,
        mesh=mesh,
        in_specs=(
            P(("grp", "dp"), None, None),
            P(("grp", "dp"), None, None),
            P(("grp", "dp")),
            P(("grp", "dp")),
            P(("grp", "dp"), None),
            P("grp"),
            P(None, "grp"),
            P(None, "grp"),
            P(None, "grp"),
            P("grp"),
            P(None, "grp"),
            P("grp"),
            P("grp", None),
            P("grp"),
            P(None, "grp"),
            P("grp"),
            P("grp", None),
            P("grp"),
        ),
        out_specs=(
            P(("grp", "dp"), None, None),
            P(("grp", "dp"), None, None),
            P(None, "grp"),
            P(None, "grp"),
            P(None, "grp"),
            P("grp"),
            P(None, "grp"),
            P("grp"),
            P("grp", None),
            P("grp"),
            P(None, "grp"),
            P("grp"),
            P("grp", None),
            P("grp"),
        ),
        check_vma=False,
    )
```

```python
import functools

import jax
import jax.numpy as jnp
from jax import lax
from jax.experimental import pallas as pl
from jax.experimental.pallas import tpu as pltpu
from jax.sharding import PartitionSpec as P

HEADS = 16
HEAD_DIM = 72


EPS = 1e-06
HIGH = lax.Precision.HIGHEST


def modulate(values, shift, scale):
    mean = jnp.mean(values, -1, keepdims=True)
    cent = values - mean
    var = jnp.mean(cent * cent, -1, keepdims=True)
    return cent * lax.rsqrt(var + EPS) * (1.0 + scale[:, None, :]) + shift[:, None, :]


def product(left, right):
    return jnp.einsum("btd,de->bte", left, right, preferred_element_type=jnp.float32)


def weight_term(left, right):
    return jnp.einsum("btd,bte->de", left, right, preferred_element_type=jnp.float32)


def core(weights, tokens, mod):
    w_qkv, qv_bias, w_proj, b_proj, w_fc1, b_fc1, w_fc2, b_fc2 = weights
    count, length, width = tokens.shape
    shift1, scale1, gate1, shift2, scale2, gate2 = jnp.split(mod, 6, -1)
    h1 = modulate(tokens, shift1, scale1).astype(jnp.bfloat16)
    bias = jnp.concatenate(
        [
            qv_bias[:width].astype(jnp.float32),
            jnp.zeros((width,), jnp.float32),
            qv_bias[width:].astype(jnp.float32),
        ]
    )
    qkv = (product(h1, w_qkv) + bias).astype(jnp.bfloat16)
    query = qkv[..., :width].reshape(count, length, HEADS, HEAD_DIM)
    keys = qkv[..., width : 2 * width].reshape(count, length, HEADS, HEAD_DIM)
    values = qkv[..., 2 * width :].reshape(count, length, HEADS, HEAD_DIM)
    scores = jnp.einsum(
        "bqhd,bkhd->bhqk", query, keys, preferred_element_type=jnp.float32
    ) * HEAD_DIM ** (-0.5)
    total = jax.scipy.special.logsumexp(scores, axis=-1, keepdims=True)
    probs_full = jnp.exp(scores - total)
    probs = probs_full.astype(jnp.bfloat16)
    att = (
        jnp.einsum("bhqk,bkhd->bqhd", probs, values, preferred_element_type=jnp.float32)
        .reshape(count, length, width)
        .astype(jnp.bfloat16)
    )
    proj = product(att, w_proj) + b_proj.astype(jnp.float32)
    mixed = tokens + gate1[:, None, :] * proj
    h2 = modulate(mixed, shift2, scale2).astype(jnp.bfloat16)
    pre = product(h2, w_fc1) + b_fc1.astype(jnp.float32)
    act = jax.nn.gelu(pre, approximate=True).astype(jnp.bfloat16)
    mlp = product(act, w_fc2) + b_fc2.astype(jnp.float32)
    result = mixed + gate2[:, None, :] * mlp
    saved = (h1, query, keys, values, probs_full, probs, att, proj, mixed, h2, pre, act, mlp)
    return (result, saved)


def body(
    latents,
    cotangent,
    bands,
    labels,
    kept,
    band_counts,
    time_table,
    class_table,
    w_ada,
    b_ada,
    w_qkv,
    qv_bias,
    w_proj,
    b_proj,
    w_fc1,
    b_fc1,
    w_fc2,
    b_fc2,
):
    gathered = (
        lax.all_gather(time_table, "grp", axis=1, tiled=True),
        lax.all_gather(class_table, "grp", axis=1, tiled=True),
        lax.all_gather(w_ada, "grp", axis=1, tiled=True),
        lax.all_gather(b_ada, "grp", axis=0, tiled=True),
        lax.all_gather(w_qkv, "grp", axis=1, tiled=True),
        lax.all_gather(qv_bias, "grp", axis=0, tiled=True),
        lax.all_gather(w_proj, "grp", axis=0, tiled=True),
        lax.all_gather(b_proj, "grp", axis=0, tiled=True),
        lax.all_gather(w_fc1, "grp", axis=1, tiled=True),
        lax.all_gather(b_fc1, "grp", axis=0, tiled=True),
        lax.all_gather(w_fc2, "grp", axis=0, tiled=True),
        lax.all_gather(b_fc2, "grp", axis=0, tiled=True),
    )
    time_full, class_full, ada_full, ada_bias = (gathered[0], gathered[1], gathered[2], gathered[3])
    samples = latents.shape[0]
    width = latents.shape[2]
    slot = lax.axis_index("dp") * samples + jnp.arange(samples, dtype=jnp.int32)
    group_count = band_counts[0]
    weight = jnp.where(slot < group_count, 1.0, 0.0).astype(jnp.float32) / group_count.astype(
        jnp.float32
    )
    band_hot = (bands[:, None] == jnp.arange(time_full.shape[0], dtype=jnp.int32)[None, :]).astype(
        jnp.float32
    )
    class_hot = (
        labels[:, None] == jnp.arange(class_full.shape[0], dtype=jnp.int32)[None, :]
    ).astype(jnp.float32)
    cond = jnp.dot(band_hot, time_full.astype(jnp.float32), precision=HIGH) + jnp.dot(
        class_hot, class_full.astype(jnp.float32), precision=HIGH
    )
    cvec = jax.nn.silu(cond).astype(jnp.bfloat16)
    mod = jnp.dot(cvec, ada_full, preferred_element_type=jnp.float32) + ada_bias.astype(jnp.float32)
    rows = jnp.arange(samples, dtype=jnp.int32)[:, None]
    tokens = jnp.take_along_axis(latents, kept[:, :, None], 1).astype(jnp.float32)
    result, unused = core(tuple(gathered[4:]), tokens, mod)
    block_out = latents.at[rows, kept].set(result.astype(jnp.bfloat16))
    fetched = (
        lax.all_gather(w_ada, "grp", axis=1, tiled=True),
        lax.all_gather(w_qkv, "grp", axis=1, tiled=True),
        lax.all_gather(qv_bias, "grp", axis=0, tiled=True),
        lax.all_gather(w_proj, "grp", axis=0, tiled=True),
        lax.all_gather(b_proj, "grp", axis=0, tiled=True),
        lax.all_gather(w_fc1, "grp", axis=1, tiled=True),
        lax.all_gather(b_fc1, "grp", axis=0, tiled=True),
        lax.all_gather(w_fc2, "grp", axis=0, tiled=True),
        lax.all_gather(b_fc2, "grp", axis=0, tiled=True),
    )
    ada_full = fetched[0]
    back = tuple(fetched[1:])
    qkv_full, unused_bias, proj_full, unused_pbias, fc1_full, unused_b1, fc2_full, unused_b2 = back
    result, saved = core(back, tokens, mod)
    h1, query, keys, values, probs_full, probs, att, proj, mixed, h2, pre, act, mlp = saved
    shift1, scale1, gate1, shift2, scale2, gate2 = jnp.split(mod, 6, -1)
    weighted = cotangent.astype(jnp.float32) * weight[:, None, None]
    grad_out = jnp.take_along_axis(weighted, kept[:, :, None], 1)
    grad_mlp = (gate2[:, None, :] * grad_out).astype(jnp.bfloat16)
    grad_gate2 = jnp.sum(grad_out * mlp, 1)
    fc2_grad = weight_term(act, grad_mlp)
    fc2_bias_grad = jnp.sum(grad_mlp.astype(jnp.float32), (0, 1))
    grad_act = jnp.einsum("bte,de->btd", grad_mlp, fc2_full, preferred_element_type=jnp.float32)
    unused_pre, gelu_back = jax.vjp(lambda value: jax.nn.gelu(value, approximate=True), pre)
    grad_pre = gelu_back(grad_act)[0].astype(jnp.bfloat16)
    fc1_grad = weight_term(h2, grad_pre)
    fc1_bias_grad = jnp.sum(grad_pre.astype(jnp.float32), (0, 1))
    grad_h2 = jnp.einsum("bte,de->btd", grad_pre, fc1_full, preferred_element_type=jnp.float32)
    unused_h2, norm_back = jax.vjp(modulate, mixed, shift2, scale2)
    grad_mixed, grad_shift2, grad_scale2 = norm_back(grad_h2)
    grad_mixed = grad_mixed + grad_out
    grad_proj = (gate1[:, None, :] * grad_mixed).astype(jnp.bfloat16)
    grad_gate1 = jnp.sum(grad_mixed * proj, 1)
    proj_grad = weight_term(att, grad_proj)
    proj_bias_grad = jnp.sum(grad_proj.astype(jnp.float32), (0, 1))
    grad_att = jnp.einsum(
        "bte,de->btd", grad_proj, proj_full, preferred_element_type=jnp.float32
    ).astype(jnp.bfloat16)
    grad_heads = grad_att.reshape(query.shape)
    grad_values = jnp.einsum(
        "bhqk,bqhd->bkhd", probs, grad_heads, preferred_element_type=jnp.float32
    )
    grad_probs = jnp.einsum(
        "bqhd,bkhd->bhqk", grad_heads, values, preferred_element_type=jnp.float32
    )
    grad_scores = probs_full * (grad_probs - jnp.sum(grad_probs * probs_full, -1, keepdims=True))
    grad_scores = grad_scores.astype(jnp.bfloat16)
    grad_query = jnp.einsum(
        "bhqk,bkhd->bqhd", grad_scores, keys, preferred_element_type=jnp.float32
    ) * HEAD_DIM ** (-0.5)
    grad_keys = jnp.einsum(
        "bhqk,bqhd->bkhd", grad_scores, query, preferred_element_type=jnp.float32
    ) * HEAD_DIM ** (-0.5)
    count, length = (tokens.shape[0], tokens.shape[1])
    grad_qkv = jnp.concatenate(
        [
            grad_query.reshape(count, length, width),
            grad_keys.reshape(count, length, width),
            grad_values.reshape(count, length, width),
        ],
        -1,
    ).astype(jnp.bfloat16)
    qkv_grad = weight_term(h1, grad_qkv)
    qkv_sums = jnp.sum(grad_qkv.astype(jnp.float32), (0, 1))
    qv_bias_grad = jnp.concatenate([qkv_sums[:width], qkv_sums[2 * width :]])
    grad_h1 = jnp.einsum("bte,de->btd", grad_qkv, qkv_full, preferred_element_type=jnp.float32)
    unused_h1, first_back = jax.vjp(modulate, tokens, shift1, scale1)
    grad_tokens, grad_shift1, grad_scale1 = first_back(grad_h1)
    grad_tokens = grad_tokens + grad_mixed
    latents_grad = weighted.at[rows, kept].set(grad_tokens).astype(jnp.bfloat16)
    grad_mod = jnp.concatenate(
        [grad_shift1, grad_scale1, grad_gate1, grad_shift2, grad_scale2, grad_gate2], -1
    ).astype(jnp.bfloat16)
    ada_grad = jnp.dot(cvec.T, grad_mod, preferred_element_type=jnp.float32)
    ada_bias_grad = jnp.sum(grad_mod.astype(jnp.float32), 0)
    grad_cvec = jnp.dot(grad_mod, ada_full.T, preferred_element_type=jnp.float32)
    unused_cond, silu_back = jax.vjp(jax.nn.silu, cond)
    grad_cond = silu_back(grad_cvec)[0]
    time_grad = jnp.dot(band_hot.T, grad_cond, precision=HIGH)
    class_grad = jnp.dot(class_hot.T, grad_cond, precision=HIGH)
    shares = (
        lax.psum_scatter(time_grad, "grp", scatter_dimension=1, tiled=True),
        lax.psum_scatter(class_grad, "grp", scatter_dimension=1, tiled=True),
        lax.psum_scatter(ada_grad, "grp", scatter_dimension=1, tiled=True),
        lax.psum_scatter(ada_bias_grad, "grp", scatter_dimension=0, tiled=True),
        lax.psum_scatter(qkv_grad, "grp", scatter_dimension=1, tiled=True),
        lax.psum_scatter(qv_bias_grad, "grp", scatter_dimension=0, tiled=True),
        lax.psum_scatter(proj_grad, "grp", scatter_dimension=0, tiled=True),
        lax.psum_scatter(proj_bias_grad, "grp", scatter_dimension=0, tiled=True),
        lax.psum_scatter(fc1_grad, "grp", scatter_dimension=1, tiled=True),
        lax.psum_scatter(fc1_bias_grad, "grp", scatter_dimension=0, tiled=True),
        lax.psum_scatter(fc2_grad, "grp", scatter_dimension=0, tiled=True),
        lax.psum_scatter(fc2_bias_grad, "grp", scatter_dimension=0, tiled=True),
    )
    totals = (
        lax.psum(shares[0].astype(jnp.bfloat16), "dp").astype(jnp.float32),
        lax.psum(shares[1].astype(jnp.bfloat16), "dp").astype(jnp.float32),
        lax.psum(shares[2].astype(jnp.bfloat16), "dp").astype(jnp.float32),
        lax.psum(shares[3].astype(jnp.bfloat16), "dp").astype(jnp.float32),
        lax.psum(shares[4].astype(jnp.bfloat16), "dp").astype(jnp.float32),
        lax.psum(shares[5].astype(jnp.bfloat16), "dp").astype(jnp.float32),
        lax.psum(shares[6].astype(jnp.bfloat16), "dp").astype(jnp.float32),
        lax.psum(shares[7].astype(jnp.bfloat16), "dp").astype(jnp.float32),
        lax.psum(shares[8].astype(jnp.bfloat16), "dp").astype(jnp.float32),
        lax.psum(shares[9].astype(jnp.bfloat16), "dp").astype(jnp.float32),
        lax.psum(shares[10].astype(jnp.bfloat16), "dp").astype(jnp.float32),
        lax.psum(shares[11].astype(jnp.bfloat16), "dp").astype(jnp.float32),
    )
    return (
        block_out,
        latents_grad,
        totals[0],
        totals[1],
        totals[2],
        totals[3],
        totals[4],
        totals[5],
        totals[6],
        totals[7],
        totals[8],
        totals[9],
        totals[10],
        totals[11],
    )


MESH = pl.DeviceIdType.MESH
F32 = jnp.float32
BF16 = jnp.bfloat16
GELU_A = 0.7978845608028654
GELU_B = 0.044715


def dot(left, right, dims):
    return lax.dot_general(left, right, ((dims[:1], dims[1:]), ((), ())), preferred_element_type=F32)


class Place:
    def __init__(self):
        self.g = lax.axis_index("grp")
        self.z = lax.axis_index("dp")
        self.c = self.g % 2
        self.x = (self.g // 2) % 2
        self.y = self.g // 4

    def block(self, dc, dx, dy):
        c = 1 - self.c if dc else self.c
        x = 1 - self.x if dx else self.x
        y = 1 - self.y if dy else self.y
        return y * 4 + x * 2 + c

    def device(self, dc, dx, dy):
        return (self.block(dc, dx, dy), self.z)


RELATIVE = [(r & 1, (r >> 1) & 1, r >> 2) for r in range(8)]


class Wire:
    def __init__(self, send, recv):
        self.send, self.recv, self.used = send, recv, 0

    def take(self, count):
        first = self.used
        self.used += count
        return first

    def copy(self, number, src, dst, device):
        return pltpu.make_async_remote_copy(
            src_ref=src,
            dst_ref=dst,
            send_sem=self.send.at[number],
            recv_sem=self.recv.at[number],
            device_id=device,
            device_id_type=MESH,
        )


def halves(rows):
    cut = rows // 32 * 16
    return pl.ds(0, cut), pl.ds(cut, rows - cut)


def greet(devices):
    barrier = pltpu.get_barrier_semaphore()
    for device in devices:
        pl.semaphore_signal(barrier, inc=1, device_id=device, device_id_type=MESH)
    pl.semaphore_wait(barrier, len(devices))


def plane(place):
    return [place.device(*rel) for rel in RELATIVE[1:]]


class Gather:
    def __init__(self, place, wire, buf, start=0, rows=None, origin=None):
        p = place
        rows = rows or buf.shape[1]
        lo, hi = halves(rows)
        parts = (pl.ds(start, rows), pl.ds(start, lo.size), pl.ds(start + lo.size, hi.size))
        first = wire.take(8)

        def make(number, block, device, part=0):
            ref = buf.at[block, parts[part]]
            src = origin if number < 3 and origin is not None else ref
            return wire.copy(first + number, src, ref, device)

        own, xb, yb, db = p.g, p.block(0, 1, 0), p.block(0, 0, 1), p.block(0, 1, 1)
        xd, yd, sd = p.device(0, 1, 0), p.device(0, 0, 1), p.device(1, 0, 0)
        self.c = [
            make(0, own, xd),
            make(1, own, yd),
            make(2, own, sd),
            make(3, xb, yd, 1),
            make(4, xb, sd),
            make(5, yb, xd, 2),
            make(6, yb, sd),
            make(7, db, sd),
        ]

    def start(self):
        for number in (0, 1, 2):
            self.c[number].start()

    def arrived(self):
        self.c[0].wait_recv()
        self.c[1].wait_recv()
        self.c[4].start()
        self.c[6].start()

    def forward(self):
        self.c[3].start()
        self.c[5].start()

    def neighbours(self):
        self.arrived()
        self.forward()

    def far(self):
        self.c[3].wait_recv()
        self.c[5].wait_recv()
        self.c[7].start()

    def wait_sib(self):
        self.c[2].wait_recv()

    def wait_sib_neighbours(self):
        self.c[4].wait_recv()
        self.c[6].wait_recv()

    def wait_sib_far(self):
        self.c[7].wait_recv()

    def finish(self):
        for copy in self.c:
            copy.wait_send()


class Scatter:
    def __init__(self, place, wire, buf, r1, r2, r3, rows=None):
        self.p, self.w, self.buf = place, wire, buf
        self.r1, self.r2, self.r3 = r1, r2, r3
        self.rows = rows or buf.shape[1]
        self.parts = halves(self.rows)
        self.first = wire.take(10)
        p = place
        self.sib = [p.block(1, q & 1, q >> 1) for q in range(4)]
        self.mine = [p.block(0, q & 1, q >> 1) for q in range(4)]
        xd, yd, sd = p.device(0, 1, 0), p.device(0, 0, 1), p.device(1, 0, 0)
        f, w = self.first, wire
        lo, hi = self.parts
        whole = pl.ds(0, self.rows)
        self.s1 = [w.copy(f + q, buf.at[self.sib[q], whole], r1.at[q, whole], sd) for q in range(4)]
        self.s2 = [
            w.copy(f + 4, buf.at[self.mine[3], lo], r2.at[0, pl.ds(0, lo.size)], xd),
            w.copy(f + 5, buf.at[self.mine[3], hi], r2.at[1, pl.ds(0, hi.size)], yd),
        ]
        self.s3 = [
            w.copy(f + 6, buf.at[self.mine[1], lo], r3.at[0, lo], xd),
            w.copy(f + 7, buf.at[self.mine[1], hi], r3.at[0, hi], xd),
            w.copy(f + 8, buf.at[self.mine[2], lo], r3.at[1, lo], yd),
            w.copy(f + 9, buf.at[self.mine[2], hi], r3.at[1, hi], yd),
        ]

    def send_sib(self, q):
        self.s1[q].start()

    def add_sib(self, q):
        self.s1[q].wait_recv()
        add_into(self.buf.at[self.mine[q], pl.ds(0, self.rows)], self.r1.at[q, pl.ds(0, self.rows)])

    def send_far(self):
        self.add_sib(3)
        self.s2[0].start()
        self.s2[1].start()

    def send_near(self):
        self.add_sib(1)
        self.s3[0].start()
        self.add_sib(2)
        self.s3[3].start()

    def relay(self):
        lo, hi = self.parts
        self.s2[1].wait_recv()
        add_into(self.buf.at[self.mine[1], hi], self.r2.at[1, pl.ds(0, hi.size)])
        self.s3[1].start()
        self.s2[0].wait_recv()
        add_into(self.buf.at[self.mine[2], lo], self.r2.at[0, pl.ds(0, lo.size)])
        self.s3[2].start()
        self.add_sib(0)

    def result(self, out):
        for copy in self.s3:
            copy.wait_recv()
        rows = self.rows
        step = 16

        @pl.loop(0, rows // step)
        def _(i):
            at = pl.ds(pl.multiple_of(i * step, step), step)
            total = self.buf[self.mine[0], at].astype(F32) + self.r3[0, at].astype(F32) + self.r3[1, at].astype(F32)
            out[at] = total.astype(out.dtype)

    def finish(self):
        for copy in self.s1 + self.s2 + self.s3:
            copy.wait_send()


def add_into(ref, other):
    step = 16

    @pl.loop(0, ref.shape[0] // step)
    def _(i):
        at = pl.ds(pl.multiple_of(i * step, step), step)
        ref[at] = (ref[at].astype(F32) + other[at].astype(F32)).astype(ref.dtype)


def scatter_scratch(rows, width):
    return [
        pltpu.VMEM((4, rows, width), BF16),
        pltpu.VMEM((2, halves(rows)[1].size, width), BF16),
        pltpu.VMEM((2, rows, width), BF16),
    ]


def to_all(place, wire, make):
    first = wire.take(7)
    copies = []
    for number, rel in enumerate(RELATIVE[1:]):
        src, dst = make(rel)
        copies.append(wire.copy(first + number, src, dst, place.device(*rel)))
        copies[-1].start()
    return copies


def wait_recv(copies):
    for copy in copies:
        copy.wait_recv()


def wait_send(copies):
    for copy in copies:
        copy.wait_send()


def params(collective_id):
    return pltpu.CompilerParams(
        collective_id=collective_id, has_side_effects=True, vmem_limit_bytes=63 * 2**20
    )


VMEM = pl.BlockSpec(memory_space=pltpu.VMEM)

def gelu_parts(pre):
    square = pre * pre
    inner = jnp.tanh(GELU_A * pre * (1.0 + GELU_B * square))
    act = 0.5 * pre * (1.0 + inner)
    slope = 0.5 * (1.0 + inner) + 0.5 * pre * (1.0 - inner * inner) * (GELU_A * (1.0 + 3.0 * GELU_B * square))
    return act, slope


def local(src, dst, sem):
    return pltpu.make_async_copy(src, dst, sem)


def own_tokens(kept_ref, length, s):
    rows = lax.broadcasted_iota(jnp.int32, (length, kept_ref.shape[1]), 0)
    return jnp.where(rows == kept_ref[s : s + 1, :], 1.0, 0.0).astype(BF16)


def normed(v):
    cent = v - jnp.mean(v, -1, keepdims=True)
    inv = lax.rsqrt(jnp.mean(cent * cent, -1, keepdims=True) + EPS)
    return cent * inv, inv


def norm_back(grad, hat, inv):
    return inv * (grad - jnp.mean(grad, -1, keepdims=True) - hat * jnp.mean(grad * hat, -1, keepdims=True))


STEP = 32


def by_rows(samples, keep, fn):
    @pl.loop(0, samples * keep // STEP)
    def _(i):
        fn(lax.div(i, keep // STEP), pl.ds(pl.multiple_of(i * STEP, STEP), STEP))


SCALE = HEAD_DIM ** (-0.5)


def probabilities(q, k):
    scores = dot(q, k, (0, 0)) * SCALE
    exps = jnp.exp(scores - jnp.max(scores, -1, keepdims=True))
    return exps / jnp.sum(exps, -1, keepdims=True)


def arrival(p, t):
    dc = jnp.where((t == 1) | (t == 4) | (t == 5) | (t == 7), 1, 0)
    dx = jnp.where((t == 2) | (t == 4) | (t >= 6), 1, 0)
    dy = jnp.where((t == 3) | (t >= 5), 1, 0)
    c, x, y = lax.rem(p.c + dc, 2), lax.rem(p.x + dx, 2), lax.rem(p.y + dy, 2)
    return y * 4 + x * 2 + c


MSG_PROJ, MSG_FC2, MSG_QV, MSG_ROWS = 0, 8, 16, 32


def sample_weight(place, counts_ref, samples, s):
    count = jnp.full((1, 128), counts_ref[0], jnp.int32)
    used = count > place.z * samples + s
    return (jnp.where(used, 1.0, 0.0) / count.astype(F32))[:, 0:1]


ANY = pl.BlockSpec(memory_space=pl.ANY)
SMEM = pl.BlockSpec(memory_space=pltpu.SMEM)
CHUNK = 144


def block_kernel(samples, planes, labels_ref, bands_ref, counts_ref, wq_hbm, wp_hbm, w1_hbm, w2_hbm, ada_hbm, lat_hbm, cot_hbm,
                 bias_ref, kept_ref, class_ref, time_ref, bada_ref, b1_ref,
                 out_hbm, block_hbm, latg_hbm, wq_keep, dmod_z, dcond_z, cvec_z, sum_z, ids_z,
                 wq, wp, w1, w2, h1_all, h2_all, dm_all, act, dpre, p1, p2, p3, units, att, mixed, proj, grad, dx2, tmp, rest,
                 dproj, dq, dq_all, from_end, out, g1, g2, gq, gp, gb1, ids_all, msg_all, cond_all, mod_in, mod_send, mod, vec,
                 dc_send, dc_in, bundle, bundles, send, recv, credits, sems, out_sems):
    p = Place()
    wire = Wire(send, recv)
    g, z = p.g, p.z
    others = [(g, (z + k) % planes) for k in range(1, planes)]
    greet(plane(p) + others)
    length = lat_hbm.shape[1]
    keep = kept_ref.shape[1]
    rows, width = mixed.shape
    pair = 2 * HEAD_DIM
    hidden_units = act.shape[2]
    ada_rest = ada_hbm.shape[0] - hidden_units

    loads = {}
    for number, (name, src, dst) in enumerate((
        ("wq", wq_hbm, wq.at[g]),
        ("wp", wp_hbm, wp.at[g]),
        ("lat", lat_hbm, h2_all.at[pl.ds(0, samples)]),
        ("cot", cot_hbm, h2_all.at[pl.ds(samples, samples)]),
        ("ada1", ada_hbm.at[pl.ds(0, hidden_units)], w1),
        ("ada2", ada_hbm.at[pl.ds(hidden_units, ada_rest)], w2.at[pl.ds(0, ada_rest)]),
        ("w1", w1_hbm, w1),
        ("w2", w2_hbm, w2),
        ("keep", wq, wq_keep),
        ("again", wq_keep, wq),
        ("ada1b", ada_hbm.at[pl.ds(0, hidden_units)], w1),
        ("ada2b", ada_hbm.at[pl.ds(hidden_units, ada_rest)], w2.at[pl.ds(0, ada_rest)]),
        ("latb", lat_hbm, wq.at[pl.ds(0, samples), pl.ds(0, length)]),
        ("cotb", cot_hbm, wq.at[pl.ds(samples, samples), pl.ds(0, length)]),
        ("block", wq.at[pl.ds(0, samples), pl.ds(0, length)], block_hbm),
        ("latg", wq.at[pl.ds(samples, samples), pl.ds(0, length)], latg_hbm),
    )):
        loads[name] = local(src, dst, sems.at[number])
    odd = z % 2
    there = (g, z + 1 - 2 * odd)
    ahead, behind = 2 * pair * odd, 2 * pair * (1 - odd)
    gather_a = Gather(p, wire, wq, ahead, pair, wq_hbm.at[pl.ds(ahead, pair)])
    gather_m = Gather(p, wire, wq, pair, pair, wq_hbm.at[pl.ds(pair, pair)])
    first = wire.take(7)
    near = [p.block(0, 1, 0), p.block(0, 0, 1), p.block(0, 1, 1)]
    sd = p.device(1, 0, 0)
    across_z = [wire.copy(first + i, wq.at[b, pl.ds(ahead, pair)], wq.at[b, pl.ds(ahead, pair)], there) for i, b in enumerate(near)]
    own_sib = wire.copy(first + 3, wq_hbm.at[pl.ds(behind, pair)], wq.at[g, pl.ds(behind, pair)], sd)
    from_z = [wire.copy(first + 4 + i, wq.at[b, pl.ds(behind, pair)], wq.at[b, pl.ds(behind, pair)], sd) for i, b in enumerate(near)]
    outward = Gather(p, wire, wp, origin=wp_hbm)
    main = Gather(p, wire, h2_all)
    back = Gather(p, wire, dm_all)
    tokens = Gather(p, wire, h1_all)
    sums = Scatter(p, wire, wq, p1, p2, p3, rows)
    outs = Scatter(p, wire, h2_all, dm_all.at[pl.ds(0, 4)], dm_all.at[pl.ds(4, 2)], dm_all.at[pl.ds(6, 2)])
    projs = Scatter(p, wire, wp, p1, p2, p3)
    sources = [ref.at[pl.ds(start, CHUNK)] for ref in (g1, g2, gq, gp) for start in range(0, ref.shape[0], CHUNK)]
    count = len(sources)
    up, across, down = wire.take(count), wire.take(count), wire.take(count)
    inner, outer, partner = 1 + z // 3, (z - 1) * 3, 3 - z
    at_end = (z == 0) | (z == planes - 1)
    ups = [wire.copy(up + k, sources[k], from_end.at[k], (g, inner)) for k in range(count)]
    acrosses = [wire.copy(across + k, from_end.at[k], out.at[k], (g, partner)) for k in range(count)]
    downs = [wire.copy(down + k, out.at[k], out.at[k], (g, outer)) for k in range(count)]
    results = [local(out.at[k], out_hbm.at[k], out_sems.at[k]) for k in range(count)]

    def chain_send(*numbers):
        @pl.when(at_end)
        def _():
            for k in numbers:
                ups[k].start()

    def chain(*numbers):
        @pl.when(jnp.logical_not(at_end))
        def _():
            for k in numbers:
                if k < count:
                    ups[k].wait_recv()
                    add_into(from_end.at[k], sources[k])
                    acrosses[k].start()
                if k > 0:
                    acrosses[k - 1].wait_recv()
                    add_into(out.at[k - 1], from_end.at[k - 1])
                    downs[k - 1].start()
                    results[k - 1].start()

    def to_planes(ref):
        first = wire.take(planes - 1)
        copies = [wire.copy(first + k, ref.at[z], ref.at[z], device) for k, device in enumerate(others)]
        for copy in copies:
            copy.start()
        return copies

    neighbours = [p.device(1, 0, 0), p.device(0, 1, 0), p.device(0, 0, 1)]

    def grant(number):
        for i, device in enumerate(neighbours):
            pl.semaphore_signal(credits.at[number, i], inc=1, device_id=device, device_id_type=MESH)

    def granted(number):
        for i in range(3):
            pl.semaphore_wait(credits.at[number, i], 1)

    lanes = lax.broadcasted_iota(jnp.int32, (1, 128), 1)
    ids_all[g] = jnp.zeros((8, 128), F32)
    for s in range(samples):
        line = jnp.where(lanes == 0, labels_ref[s], 0) + jnp.where(lanes == 1, bands_ref[s], 0)
        ids_all[g, s : s + 1, :] = line.astype(F32)
    idc = to_all(p, wire, lambda rel: (ids_all.at[g], ids_all.at[g]))
    gather_a.start()
    for name in ("lat", "cot", "ada1", "ada2", "wq", "wp"):
        loads[name].start()
    msg_all[g] = jnp.zeros(msg_all.shape[1:], F32)
    for row in range(4):
        at = MSG_PROJ + 8 * row
        msg_all[g, at : at + 1, :] = bias_ref[row : row + 1, :]

    wait_recv(idc)
    labels = jnp.concatenate([ids_all[j, 0:samples, 0:1] for j in range(8)], 0)
    bands = jnp.concatenate([ids_all[j, 0:samples, 1:2] for j in range(8)], 0)

    def one_hot(ids, size):
        lanes = lax.broadcasted_iota(jnp.int32, (ids.shape[0], size), 1).astype(F32)
        return jnp.where(lanes == ids, 1.0, 0.0).astype(BF16)

    of_band = dot(one_hot(bands, time_ref.shape[0]), time_ref[...], (1, 0))
    cond_all[g] = of_band + dot(one_hot(labels, class_ref.shape[1]), class_ref[...], (1, 1))
    conds = to_all(p, wire, lambda rel: (cond_all.at[g], cond_all.at[g]))
    ids_z[z] = jnp.zeros(ids_z.shape[1:], F32)
    ids_z[z, :, 0:1] = labels
    ids_z[z, :, 1:2] = bands
    gather_m.start()
    own_sib.start()

    loads["lat"].wait()
    loads["cot"].wait()
    for s in range(samples):
        hot = own_tokens(kept_ref, length, s)
        at = pl.ds(s * keep, keep)
        mixed[at] = dot(hot, h2_all[s], (0, 0))
        grad[at] = dot(hot, h2_all[samples + s], (0, 0)) * sample_weight(p, counts_ref, samples, s)

    gather_a.arrived()
    across_z[0].start()
    across_z[1].start()
    zs = [to_planes(ids_z)]
    wait_recv(conds)
    value = cond_all[...]
    value = value * jax.nn.sigmoid(value)
    cvec_z[z] = value.astype(BF16)
    zs.append(to_planes(cvec_z))
    value = jnp.concatenate([value[j] for j in range(8)], 1).astype(BF16)
    loads["ada1"].wait()
    loads["ada2"].wait()
    mods = [dot(value, w1[...], (1, 1)), dot(value, w2[0:ada_rest], (1, 1))]
    mods = jnp.concatenate(mods, 1) + bada_ref[...]
    mod_send[...] = jnp.zeros_like(mod_send)
    for j in range(8):
        mod_send[j, 0:samples, :] = mods[samples * j : samples * (j + 1), :]
    mod_in[g] = mod_send[g]
    modc = to_all(p, wire, lambda rel: (mod_send.at[p.block(*rel)], mod_in.at[g]))
    msgs = to_all(p, wire, lambda rel: (msg_all.at[g], msg_all.at[g]))
    gather_a.forward()
    loads["w1"].start()
    loads["w2"].start()
    wait_recv(modc)
    mod[...] = jnp.zeros_like(mod)
    for s in range(samples):
        line = jnp.concatenate([mod_in[j, s : s + 1, :] for j in range(8)], 1)
        for v in range(6):
            mod[s, v : v + 1, :] = line[:, v * width : (v + 1) * width]

    def first_norm(s, at):
        hat, inv = normed(mixed[at])
        h1_all[g, at] = (hat * (1.0 + mod[s, 1:2, :]) + mod[s, 0:1, :]).astype(BF16)
        dm_all[g, at] = (mod[s, 5:6, :] * grad[at]).astype(BF16)

    gather_m.neighbours()
    outward.start()
    by_rows(samples, keep, first_norm)
    wait_recv(msgs)
    vec[...] = jnp.zeros_like(vec)
    for row, at in ((0, MSG_PROJ), (1, MSG_FC2)):
        vec[row : row + 1, :] = jnp.concatenate([msg_all[j, at : at + 1, :] for j in range(8)], 1)

    ones = jnp.ones((8, rows), BF16)
    loads["wq"].wait()

    @pl.loop(0, 24)
    def _(n):
        for base, gather in ((0, gather_a), (8, gather_m)):

            @pl.when(n == base + 1)
            def _(gather=gather):
                gather.wait_sib()

            @pl.when(n == base + 4)
            def _(gather=gather):
                gather.wait_sib_neighbours()

            @pl.when(n == base + 6)
            def _(gather=gather, base=base):
                gather.far()
                if base == 0:
                    across_z[2].start()

            @pl.when(n == base + 7)
            def _(gather=gather):
                gather.wait_sib_far()

        @pl.when(n == 17)
        def _():
            own_sib.wait_recv()

        @pl.when(n == 18)
        def _():
            for i in range(2):
                across_z[i].wait_recv()
                from_z[i].start()

        @pl.when(n == 20)
        def _():
            for i in range(2):
                from_z[i].wait_recv()
            outward.neighbours()
            back.start()

        @pl.when(n == 22)
        def _():
            across_z[2].wait_recv()
            from_z[2].start()

        @pl.when(n == 23)
        def _():
            from_z[2].wait_recv()

        phase = lax.div(n, 8)
        block = arrival(p, lax.rem(n, 8))
        third = jnp.where(phase == 0, 2 * odd, jnp.where(phase == 1, 1, 2 - 2 * odd))
        chunk = block * 3 + third
        bias_at = jnp.where(chunk >= 16, chunk - 8, chunk)
        keys = (chunk >= 8) & (chunk < 16)
        line = msg_all[lax.div(bias_at, 2), pl.ds(pl.multiple_of(MSG_QV + 8 * lax.rem(bias_at, 2), 8), 8), :]
        line = line * jnp.where(keys, 0.0, 1.0)
        value = dot(wq[block, pl.ds(pl.multiple_of(third * pair, 16), pair), :], h1_all[g], (1, 1))
        value = value + dot(line.astype(BF16), ones, (0, 0))
        units[2 * chunk] = value[:HEAD_DIM].astype(BF16)
        units[2 * chunk + 1] = value[HEAD_DIM:].astype(BF16)

    loads["keep"].start()

    @pl.loop(0, 8)
    def _(u):
        @pl.when(u == 1)
        def _():
            outward.far()

        for s in range(samples):
            lanes = pl.ds(s * keep, keep)
            pieces = []
            for e in range(2):
                probs = probabilities(units[2 * u + e, :, lanes], units[16 + 2 * u + e, :, lanes])
                pieces.append(dot(units[32 + 2 * u + e, :, lanes], probs.astype(BF16), (1, 1)))
            att[u, :, lanes] = jnp.concatenate(pieces, 0).astype(BF16)

    loads["wp"].wait()
    outward.wait_sib()
    outward.wait_sib_neighbours()
    outward.wait_sib_far()
    proj[...] = jnp.zeros_like(proj)

    @pl.loop(0, 8)
    def _(u):
        proj[...] += dot(att[u], wp[u], (0, 0))

    def second_norm(s, at):
        proj[at] = proj[at] + vec[0:1, :]
        mixed[at] = mixed[at] + mod[s, 2:3, :] * proj[at]
        hat, inv = normed(mixed[at])
        h2_all[g, at] = (hat * (1.0 + mod[s, 4:5, :]) + mod[s, 3:4, :]).astype(BF16)

    back.neighbours()
    by_rows(samples, keep, second_norm)
    main.start()
    back.far()
    gb1[...] = jnp.zeros_like(gb1)
    for piece in (gather_a, gather_m):
        piece.finish()
    wait_send(across_z + from_z + [own_sib])
    loads["w1"].wait()
    loads["w2"].wait()
    loads["keep"].wait()

    def hidden(block):
        pre = dot(h2_all[block], w1[...], (1, 1)) + b1_ref[...]
        value, slope = gelu_parts(pre)
        act[block] = value.astype(BF16)
        low = (dot(dm_all[block], w2[...], (1, 1)) * slope).astype(BF16)
        dpre[block] = low
        gb1[...] += jnp.sum(low.astype(F32), 0, keepdims=True)
        wq[block, pl.ds(0, rows)] = dot(low, w1[...], (1, 0)).astype(BF16)

    @pl.loop(0, 8)
    def _(t):
        @pl.when(t == 1)
        def _():
            main.wait_sib()
            back.wait_sib()

        @pl.when(t == 2)
        def _():
            main.neighbours()
            back.wait_sib_neighbours()
            back.wait_sib_far()

        @pl.when(t == 4)
        def _():
            main.wait_sib_neighbours()

        @pl.when(t == 6)
        def _():
            sums.send_near()
            main.far()

        @pl.when(t == 7)
        def _():
            main.wait_sib_far()

        hidden(arrival(p, t))
        for at, q in ((1, 0), (4, 1), (5, 2), (7, 3)):

            @pl.when(t == at)
            def _(q=q):
                sums.send_sib(q)

    sums.send_far()

    def weight_grad(left, right, target):
        pieces = [(dx2, 0, 256), (tmp, 256, 256), (rest, 512, hidden_units - 512)]
        for ref, start, size in pieces:
            ref[0:size] = jnp.zeros((size, width), F32)

        @pl.loop(0, 4)
        def _(i):
            two = pl.ds(2 * i, 2)
            values = right[two].reshape(2 * rows, width)
            for ref, start, size in pieces:
                part = left[two, :, pl.ds(start, size)].reshape(2 * rows, size)
                ref[0:size] += dot(part, values, (0, 0))

        for ref, start, size in pieces:
            target[pl.ds(start, size)] = ref[0:size].astype(BF16)

    weight_grad(dpre, h2_all, g1)
    chain_send(0, 1, 2, 3)
    sums.relay()
    main.finish()
    tokens.start()
    weight_grad(act, dm_all, g2)
    chain_send(4, 5, 6, 7)
    back.finish()
    grant(0)
    sums.result(tmp)
    sums.finish()
    grant(1)
    loads["again"].start()
    chain(0)

    bundle[...] = jnp.zeros_like(bundle)

    def add_row(row, value):
        bundle[pl.ds(row, 1), :] += jnp.sum(value, 0, keepdims=True)

    SUM_PROJ, SUM_FC2 = 6 * samples, 6 * samples + 1

    def second_back(s, at):
        hat, inv = normed(mixed[at])
        up_grad = tmp[at]
        value = grad[at] + norm_back(up_grad * (1.0 + mod[s, 4:5, :]), hat, inv)
        dx2[at] = value
        low = (mod[s, 2:3, :] * value).astype(BF16)
        dproj[at] = low
        add_row(s * 6 + 3, up_grad)
        add_row(s * 6 + 4, up_grad * hat)
        add_row(s * 6 + 2, value * proj[at])
        add_row(SUM_PROJ, low.astype(F32))
        add_row(SUM_FC2, (mod[s, 5:6, :] * grad[at]).astype(BF16).astype(F32))

    by_rows(samples, keep, second_back)
    outward.finish()

    @pl.loop(0, 8)
    def _(u):
        datt = dot(wp[u], dproj[...], (1, 1))
        wp[u] = dot(att[u], dproj[...], (1, 0)).astype(BF16)
        lists = ([], [], [])
        for s in range(samples):
            lanes = pl.ds(s * keep, keep)
            parts = ([], [], [])
            for e in range(2):
                q, k, v = (units[16 * i + 2 * u + e, :, lanes] for i in range(3))
                da = datt[e * HEAD_DIM : (e + 1) * HEAD_DIM, s * keep : (s + 1) * keep].astype(BF16)
                probs = probabilities(q, k)
                dprobs = dot(da, v, (0, 0))
                dscores = probs * (dprobs - jnp.sum(dprobs * probs, -1, keepdims=True))
                dscores = dscores.astype(BF16)
                parts[0].append(dot(k, dscores, (1, 1)) * SCALE)
                parts[1].append(dot(q, dscores, (1, 0)) * SCALE)
                parts[2].append(dot(da, probs.astype(BF16), (1, 0)))
            for i in range(3):
                lists[i].append(jnp.concatenate(parts[i], 0).astype(BF16))
        for i in range(3):
            chunk = 8 * i + u
            at = pl.ds(pl.multiple_of(lax.rem(chunk, 3) * pair, 16), pair)
            for s in range(samples):
                dq[lax.div(chunk, 3), at, pl.ds(s * keep, keep)] = lists[i][s]

        @pl.when(u == 1)
        def _():
            chain(1)

        @pl.when(u == 4)
        def _():
            tokens.neighbours()
            chain(2)

    dq_all[g] = dq[g]
    moves = to_all(p, wire, lambda rel: (dq.at[p.block(*rel)], dq_all.at[g]))
    granted(1)
    for q in (3, 1, 2, 0):
        projs.send_sib(q)
    tokens.far()
    chain(3)

    loads["again"].wait()
    proj[...] = jnp.zeros_like(proj)

    @pl.loop(0, 8)
    def _(j):
        proj[...] += dot(dq[j], wq[j], (0, 0))

    loads["latb"].start()
    loads["cotb"].start()
    chain(4)

    granted(0)

    @pl.loop(0, 8)
    def _(t):
        block = arrival(p, 7 - t)
        h2_all[block] = jnp.dot(act[block], w2[...], preferred_element_type=F32).astype(BF16)
        for at, q in ((1, 0), (4, 1), (5, 2), (7, 3)):

            @pl.when(t == 7 - at)
            def _(q=q):
                outs.send_sib(q)

    loads["ada1b"].start()
    loads["ada2b"].start()
    tokens.wait_sib()
    tokens.wait_sib_neighbours()
    tokens.wait_sib_far()
    chain(5)

    wait_recv(moves)
    projs.send_far()
    projs.send_near()
    for i in range(3):
        at = pl.ds(i * pair, pair)
        tmp[0:pair] = jnp.zeros((pair, width), F32)

        @pl.loop(0, 8)
        def _(j, at=at):
            tmp[0:pair] += dot(dq_all[j, at, :], h1_all[j], (1, 0))

        gq[at] = tmp[0:pair].astype(BF16)
        chain_send(8 + i)
        if i == 1:
            chain(6)
    projs.relay()
    outs.send_far()
    outs.send_near()
    chain(7)

    loads["latb"].wait()
    loads["cotb"].wait()
    for s in range(samples):
        hot = own_tokens(kept_ref, length, s)
        tmp[pl.ds(s * keep, keep)] = dot(hot, wq[s, pl.ds(0, length)], (0, 0))

    def first_back(s, at):
        hat, inv = normed(tmp[at])
        up_grad = proj[at]
        dx = dx2[at] + norm_back(up_grad * (1.0 + mod[s, 1:2, :]), hat, inv)
        add_row(s * 6, up_grad)
        add_row(s * 6 + 1, up_grad * hat)
        dproj[at] = dx.astype(BF16)

    by_rows(samples, keep, first_back)
    projs.result(gp)
    chain_send(11)

    def place_tokens(s):
        hot = own_tokens(kept_ref, length, s)
        is_kept = jnp.sum(hot.astype(F32), 1, keepdims=True) > 0.5
        return is_kept, dot(hot, dproj[pl.ds(s * keep, keep)], (1, 0))

    for s in range(samples):
        is_kept, spread = place_tokens(s)
        at = (samples + s, pl.ds(0, length))
        weighted = wq[at].astype(F32) * sample_weight(p, counts_ref, samples, s)
        wq[at] = jnp.where(is_kept, spread, weighted).astype(BF16)
    loads["latg"].start()
    chain(8)
    outs.relay()
    chain(9)
    chain(10)
    outs.result(tmp)

    def end(s, at):
        value = tmp[at] + vec[1:2, :]
        add_row(s * 6 + 5, grad[at] * value)
        dproj[at] = (mixed[at] + mod[s, 5:6, :] * value).astype(BF16)

    by_rows(samples, keep, end)

    cols = ada_hbm.shape[0]
    wait_send(modc)
    mod_send[...] = jnp.zeros_like(mod_send)
    for s in range(samples):
        line = jnp.concatenate([bundle[s * 6 + v : s * 6 + v + 1, :] for v in range(6)], 1)
        line = line.astype(BF16).astype(F32)
        for j in range(8):
            mod_send[j, s : s + 1, :] = line[:, j * cols : (j + 1) * cols]
    mod_in[g] = mod_send[g]
    dmods = to_all(p, wire, lambda rel: (mod_send.at[p.block(*rel)], mod_in.at[g]))
    bundles[g, 0:8, :] = jnp.zeros((8, width), F32)
    bundles[g, 0:2, :] = bundle[SUM_PROJ : SUM_PROJ + 2, :]
    for j in range(8):
        line = dot(ones, dq[j], (1, 1))
        bundles[g, 8 + j : 9 + j, 0 : 3 * pair] = line[0:1, :]
    small = to_all(p, wire, lambda rel: (bundles.at[g], bundles.at[g]))

    for s in range(samples):
        is_kept, spread = place_tokens(s)
        at = (s, pl.ds(0, length))
        wq[at] = jnp.where(is_kept, spread, wq[at].astype(F32)).astype(BF16)
    loads["block"].start()
    loads["ada1b"].wait()
    loads["ada2b"].wait()
    wait_recv(dmods)
    part = jnp.concatenate([mod_in[j, 0:samples, :] for j in range(8)], 0)
    dmod_z[z] = part
    zs.append(to_planes(dmod_z))
    part = part.astype(BF16)
    dcvec = dot(part[:, :hidden_units], w1[...], (1, 0)) + dot(part[:, hidden_units:], w2[0:ada_rest], (1, 0))
    depth = cond_all.shape[2]
    for j in range(8):
        dc_send[j] = dcvec[:, j * depth : (j + 1) * depth]
    dc_in[g] = dc_send[g]
    dcs = to_all(p, wire, lambda rel: (dc_send.at[p.block(*rel)], dc_in.at[g]))
    wait_recv(small)
    sum_z[z] = sum(bundles[j] for j in range(8))
    sum_z[z, 2:3, 0:hidden_units] = gb1[...]
    zs.append(to_planes(sum_z))
    chain(11)
    wait_recv(dcs)
    cond = cond_all[g]
    gate = jax.nn.sigmoid(cond)
    dcond_z[z] = sum(dc_in[j] for j in range(8)) * (gate * (1.0 + cond * (1.0 - gate)))
    zs.append(to_planes(dcond_z))
    chain(12)

    @pl.when(jnp.logical_not(at_end))
    def _():
        for k in range(count):
            acrosses[k].wait_send()
            downs[k].wait_send()
            results[k].wait()

    @pl.when(at_end)
    def _():
        for k in range(count):
            downs[k].wait_recv()
            results[k].start()
        for k in range(count):
            ups[k].wait_send()
            results[k].wait()

    for copies in zs:
        wait_recv(copies)
        wait_send(copies)
    for copies in (idc, msgs, conds, moves, dmods, small, dcs):
        wait_send(copies)
    for piece in (tokens, projs, outs):
        piece.finish()
    loads["latg"].wait()
    loads["block"].wait()


def run_block(samples, planes, labels, bands, counts, wq, wp, w1, w2, w_ada, lat, cot, bias, kept, class_table, time_table, b_ada,
              b1):
    keep, width = kept.shape[1], wq.shape[1]
    rows, hidden, per = samples * keep, w1.shape[0], 8 * samples
    cols, depth = w_ada.shape[0], class_table.shape[0]
    count = (2 * hidden + wq.shape[0] + wp.shape[0]) // CHUNK
    shape, room = jax.ShapeDtypeStruct, pltpu.VMEM
    blocks = room((8, rows, width), BF16)
    plain = room((rows, width), F32)
    copies = 8 * 6 + 7 + 3 * 10 + 3 * count + 8 * 7 + 5 * (planes - 1)
    return pl.pallas_call(
        functools.partial(block_kernel, samples, planes),
        out_shape=[
            shape((count, CHUNK, width), BF16),
            shape(lat.shape, BF16),
            shape(lat.shape, BF16),
            shape((8,) + wq.shape, BF16),
            shape((planes, per, cols), F32),
            shape((planes, per, depth), F32),
            shape((planes, 8, per, depth), BF16),
            shape((planes, 16, width), F32),
            shape((planes, per, 128), F32),
        ],
        in_specs=[SMEM] * 3 + [ANY] * 7 + [VMEM] * 6,
        out_specs=[ANY] * 4 + [VMEM] * 5,
        scratch_shapes=[
            room((8,) + wq.shape, BF16),
            room((8,) + wp.shape, BF16),
            room(w1.shape, BF16),
            room(w2.shape, BF16),
            blocks,
            blocks,
            blocks,
            room((8, rows, hidden), BF16),
            room((8, rows, hidden), BF16),
            *scatter_scratch(rows, width),
            room((48, HEAD_DIM, rows), BF16),
            room((8, 2 * HEAD_DIM, rows), BF16),
            plain,
            plain,
            plain,
            plain,
            plain,
            room((hidden - 512, width), F32),
            room((rows, width), BF16),
            room((8, wq.shape[0], rows), BF16),
            room((8, wq.shape[0], rows), BF16),
            room((count, CHUNK, width), BF16),
            room((count, CHUNK, width), BF16),
            room(w1.shape, BF16),
            room(w1.shape, BF16),
            room(wq.shape, BF16),
            room(wp.shape, BF16),
            room((1, hidden), F32),
            room((8, 8, 128), F32),
            room((8, MSG_ROWS, wp.shape[0]), F32),
            room((8, per, depth), F32),
            room((8, 8, cols), F32),
            room((8, 8, cols), F32),
            room((samples, 8, width), F32),
            room((8, width), F32),
            room((8, per, depth), F32),
            room((8, per, depth), F32),
            room((16, width), F32),
            room((8, 16, width), F32),
            pltpu.SemaphoreType.DMA((copies,)),
            pltpu.SemaphoreType.DMA((copies,)),
            pltpu.SemaphoreType.REGULAR((2, 3)),
            pltpu.SemaphoreType.DMA((16,)),
            pltpu.SemaphoreType.DMA((count,)),
        ],
        compiler_params=params(1),
    )(labels, bands, counts, wq, wp, w1, w2, w_ada, lat, cot, bias, kept, class_table, time_table, b_ada, b1)


def plane_body(planes, latents, cotangent, bands, labels, kept, band_counts, time_table, class_table, w_ada, b_ada, w_qkv,
               qv_bias, w_proj, b_proj, w_fc1, b_fc1, w_fc2, b_fc2):
    samples, length, width = latents.shape
    g = lax.axis_index("grp")
    wq = w_qkv.shape[1]
    wp = w_proj.shape[0]
    hidden = w_fc1.shape[1]
    per = 8 * samples

    bias = jnp.concatenate([b_proj, b_fc2, qv_bias]).astype(F32).reshape(4, wp)
    totals, block_out, latents_grad, unused_weights, dmod_z, dcond_z, cvec_z, sum_z, ids_z = run_block(
        samples, planes, labels, bands, band_counts, w_qkv.T, w_proj, w_fc1.T, w_fc2, w_ada.T, latents, cotangent, bias, kept,
        class_table.T, time_table, b_ada.astype(F32)[None], b_fc1.astype(F32)[None]
    )
    totals = totals.reshape(-1, width)
    at = 0
    pieces = []
    for size in (hidden, hidden, wq, wp):
        pieces.append(totals[at : at + size].astype(F32))
        at += size
    cvec_z = cvec_z.transpose(0, 2, 1, 3).reshape(planes * per, width)
    mod_z = dmod_z.reshape(planes * per, -1).astype(BF16)
    ada_grad = jnp.einsum("se,sd->ed", mod_z, cvec_z, preferred_element_type=F32).T
    ada_bias_grad = jnp.sum(mod_z.astype(F32), 0)
    sums = jnp.sum(sum_z, 0)
    part = lambda v, size: lax.dynamic_slice_in_dim(v, g * size, size, 0)
    qkv_sums = sums[8:, :wq].reshape(-1)
    qv_grad = part(jnp.concatenate([qkv_sums[:width], qkv_sums[2 * width :]]), qv_bias.shape[0])
    dcond = dcond_z.reshape(planes * per, -1)
    ids_z = ids_z.reshape(planes * per, -1)
    hot_class = (jnp.arange(class_table.shape[0], dtype=F32)[None, :] == ids_z[:, 0:1]).astype(F32)
    hot_time = (jnp.arange(time_table.shape[0], dtype=F32)[:, None] == ids_z[:, 1][None, :]).astype(F32)
    return (
        block_out,
        latents_grad,
        jnp.dot(hot_time, dcond, precision=HIGH),
        jnp.einsum("se,sc->ec", dcond, hot_class, precision=HIGH).T,
        ada_grad,
        ada_bias_grad,
        pieces[2].T,
        qv_grad,
        pieces[3],
        part(sums[0], b_proj.shape[0]),
        pieces[0].T,
        sums[2, :hidden],
        pieces[1],
        part(sums[1], b_fc2.shape[0]),
    )


def solution(mesh):
    planes = mesh.shape["dp"]
    small = mesh.shape["grp"] == 8 and planes == 4
    return jax.shard_map(
        functools.partial(plane_body, planes) if small else body,
        mesh=mesh,
        in_specs=(
            P(("grp", "dp"), None, None),
            P(("grp", "dp"), None, None),
            P(("grp", "dp")),
            P(("grp", "dp")),
            P(("grp", "dp"), None),
            P("grp"),
            P(None, "grp"),
            P(None, "grp"),
            P(None, "grp"),
            P("grp"),
            P(None, "grp"),
            P("grp"),
            P("grp", None),
            P("grp"),
            P(None, "grp"),
            P("grp"),
            P("grp", None),
            P("grp"),
        ),
        out_specs=(
            P(("grp", "dp"), None, None),
            P(("grp", "dp"), None, None),
            P(None, "grp"),
            P(None, "grp"),
            P(None, "grp"),
            P("grp"),
            P(None, "grp"),
            P("grp"),
            P("grp", None),
            P("grp"),
            P(None, "grp"),
            P("grp"),
            P("grp", None),
            P("grp"),
        ),
        check_vma=False,
    )
```

```python
import functools

import jax
import jax.numpy as jnp
from jax import lax
from jax.experimental import pallas as pl
from jax.experimental.pallas import tpu as pltpu
from jax.sharding import PartitionSpec as P

HEADS = 16
HEAD_DIM = 72


EPS = 1e-06
HIGH = lax.Precision.HIGHEST


def modulate(values, shift, scale):
    mean = jnp.mean(values, -1, keepdims=True)
    cent = values - mean
    var = jnp.mean(cent * cent, -1, keepdims=True)
    return cent * lax.rsqrt(var + EPS) * (1.0 + scale[:, None, :]) + shift[:, None, :]


def product(left, right):
    return jnp.einsum("btd,de->bte", left, right, preferred_element_type=jnp.float32)


def weight_term(left, right):
    return jnp.einsum("btd,bte->de", left, right, preferred_element_type=jnp.float32)


def core(weights, tokens, mod):
    w_qkv, qv_bias, w_proj, b_proj, w_fc1, b_fc1, w_fc2, b_fc2 = weights
    count, length, width = tokens.shape
    shift1, scale1, gate1, shift2, scale2, gate2 = jnp.split(mod, 6, -1)
    h1 = modulate(tokens, shift1, scale1).astype(jnp.bfloat16)
    bias = jnp.concatenate(
        [
            qv_bias[:width].astype(jnp.float32),
            jnp.zeros((width,), jnp.float32),
            qv_bias[width:].astype(jnp.float32),
        ]
    )
    qkv = (product(h1, w_qkv) + bias).astype(jnp.bfloat16)
    query = qkv[..., :width].reshape(count, length, HEADS, HEAD_DIM)
    keys = qkv[..., width : 2 * width].reshape(count, length, HEADS, HEAD_DIM)
    values = qkv[..., 2 * width :].reshape(count, length, HEADS, HEAD_DIM)
    scores = jnp.einsum(
        "bqhd,bkhd->bhqk", query, keys, preferred_element_type=jnp.float32
    ) * HEAD_DIM ** (-0.5)
    total = jax.scipy.special.logsumexp(scores, axis=-1, keepdims=True)
    probs_full = jnp.exp(scores - total)
    probs = probs_full.astype(jnp.bfloat16)
    att = (
        jnp.einsum("bhqk,bkhd->bqhd", probs, values, preferred_element_type=jnp.float32)
        .reshape(count, length, width)
        .astype(jnp.bfloat16)
    )
    proj = product(att, w_proj) + b_proj.astype(jnp.float32)
    mixed = tokens + gate1[:, None, :] * proj
    h2 = modulate(mixed, shift2, scale2).astype(jnp.bfloat16)
    pre = product(h2, w_fc1) + b_fc1.astype(jnp.float32)
    act = jax.nn.gelu(pre, approximate=True).astype(jnp.bfloat16)
    mlp = product(act, w_fc2) + b_fc2.astype(jnp.float32)
    result = mixed + gate2[:, None, :] * mlp
    saved = (h1, query, keys, values, probs_full, probs, att, proj, mixed, h2, pre, act, mlp)
    return (result, saved)


def body(
    latents,
    cotangent,
    bands,
    labels,
    kept,
    band_counts,
    time_table,
    class_table,
    w_ada,
    b_ada,
    w_qkv,
    qv_bias,
    w_proj,
    b_proj,
    w_fc1,
    b_fc1,
    w_fc2,
    b_fc2,
):
    gathered = (
        lax.all_gather(time_table, "grp", axis=1, tiled=True),
        lax.all_gather(class_table, "grp", axis=1, tiled=True),
        lax.all_gather(w_ada, "grp", axis=1, tiled=True),
        lax.all_gather(b_ada, "grp", axis=0, tiled=True),
        lax.all_gather(w_qkv, "grp", axis=1, tiled=True),
        lax.all_gather(qv_bias, "grp", axis=0, tiled=True),
        lax.all_gather(w_proj, "grp", axis=0, tiled=True),
        lax.all_gather(b_proj, "grp", axis=0, tiled=True),
        lax.all_gather(w_fc1, "grp", axis=1, tiled=True),
        lax.all_gather(b_fc1, "grp", axis=0, tiled=True),
        lax.all_gather(w_fc2, "grp", axis=0, tiled=True),
        lax.all_gather(b_fc2, "grp", axis=0, tiled=True),
    )
    time_full, class_full, ada_full, ada_bias = (gathered[0], gathered[1], gathered[2], gathered[3])
    samples = latents.shape[0]
    width = latents.shape[2]
    slot = lax.axis_index("dp") * samples + jnp.arange(samples, dtype=jnp.int32)
    group_count = band_counts[0]
    weight = jnp.where(slot < group_count, 1.0, 0.0).astype(jnp.float32) / group_count.astype(
        jnp.float32
    )
    band_hot = (bands[:, None] == jnp.arange(time_full.shape[0], dtype=jnp.int32)[None, :]).astype(
        jnp.float32
    )
    class_hot = (
        labels[:, None] == jnp.arange(class_full.shape[0], dtype=jnp.int32)[None, :]
    ).astype(jnp.float32)
    cond = jnp.dot(band_hot, time_full.astype(jnp.float32), precision=HIGH) + jnp.dot(
        class_hot, class_full.astype(jnp.float32), precision=HIGH
    )
    cvec = jax.nn.silu(cond).astype(jnp.bfloat16)
    mod = jnp.dot(cvec, ada_full, preferred_element_type=jnp.float32) + ada_bias.astype(jnp.float32)
    rows = jnp.arange(samples, dtype=jnp.int32)[:, None]
    tokens = jnp.take_along_axis(latents, kept[:, :, None], 1).astype(jnp.float32)
    result, unused = core(tuple(gathered[4:]), tokens, mod)
    block_out = latents.at[rows, kept].set(result.astype(jnp.bfloat16))
    fetched = (
        lax.all_gather(w_ada, "grp", axis=1, tiled=True),
        lax.all_gather(w_qkv, "grp", axis=1, tiled=True),
        lax.all_gather(qv_bias, "grp", axis=0, tiled=True),
        lax.all_gather(w_proj, "grp", axis=0, tiled=True),
        lax.all_gather(b_proj, "grp", axis=0, tiled=True),
        lax.all_gather(w_fc1, "grp", axis=1, tiled=True),
        lax.all_gather(b_fc1, "grp", axis=0, tiled=True),
        lax.all_gather(w_fc2, "grp", axis=0, tiled=True),
        lax.all_gather(b_fc2, "grp", axis=0, tiled=True),
    )
    ada_full = fetched[0]
    back = tuple(fetched[1:])
    qkv_full, unused_bias, proj_full, unused_pbias, fc1_full, unused_b1, fc2_full, unused_b2 = back
    result, saved = core(back, tokens, mod)
    h1, query, keys, values, probs_full, probs, att, proj, mixed, h2, pre, act, mlp = saved
    shift1, scale1, gate1, shift2, scale2, gate2 = jnp.split(mod, 6, -1)
    weighted = cotangent.astype(jnp.float32) * weight[:, None, None]
    grad_out = jnp.take_along_axis(weighted, kept[:, :, None], 1)
    grad_mlp = (gate2[:, None, :] * grad_out).astype(jnp.bfloat16)
    grad_gate2 = jnp.sum(grad_out * mlp, 1)
    fc2_grad = weight_term(act, grad_mlp)
    fc2_bias_grad = jnp.sum(grad_mlp.astype(jnp.float32), (0, 1))
    grad_act = jnp.einsum("bte,de->btd", grad_mlp, fc2_full, preferred_element_type=jnp.float32)
    unused_pre, gelu_back = jax.vjp(lambda value: jax.nn.gelu(value, approximate=True), pre)
    grad_pre = gelu_back(grad_act)[0].astype(jnp.bfloat16)
    fc1_grad = weight_term(h2, grad_pre)
    fc1_bias_grad = jnp.sum(grad_pre.astype(jnp.float32), (0, 1))
    grad_h2 = jnp.einsum("bte,de->btd", grad_pre, fc1_full, preferred_element_type=jnp.float32)
    unused_h2, norm_back = jax.vjp(modulate, mixed, shift2, scale2)
    grad_mixed, grad_shift2, grad_scale2 = norm_back(grad_h2)
    grad_mixed = grad_mixed + grad_out
    grad_proj = (gate1[:, None, :] * grad_mixed).astype(jnp.bfloat16)
    grad_gate1 = jnp.sum(grad_mixed * proj, 1)
    proj_grad = weight_term(att, grad_proj)
    proj_bias_grad = jnp.sum(grad_proj.astype(jnp.float32), (0, 1))
    grad_att = jnp.einsum(
        "bte,de->btd", grad_proj, proj_full, preferred_element_type=jnp.float32
    ).astype(jnp.bfloat16)
    grad_heads = grad_att.reshape(query.shape)
    grad_values = jnp.einsum(
        "bhqk,bqhd->bkhd", probs, grad_heads, preferred_element_type=jnp.float32
    )
    grad_probs = jnp.einsum(
        "bqhd,bkhd->bhqk", grad_heads, values, preferred_element_type=jnp.float32
    )
    grad_scores = probs_full * (grad_probs - jnp.sum(grad_probs * probs_full, -1, keepdims=True))
    grad_scores = grad_scores.astype(jnp.bfloat16)
    grad_query = jnp.einsum(
        "bhqk,bkhd->bqhd", grad_scores, keys, preferred_element_type=jnp.float32
    ) * HEAD_DIM ** (-0.5)
    grad_keys = jnp.einsum(
        "bhqk,bqhd->bkhd", grad_scores, query, preferred_element_type=jnp.float32
    ) * HEAD_DIM ** (-0.5)
    count, length = (tokens.shape[0], tokens.shape[1])
    grad_qkv = jnp.concatenate(
        [
            grad_query.reshape(count, length, width),
            grad_keys.reshape(count, length, width),
            grad_values.reshape(count, length, width),
        ],
        -1,
    ).astype(jnp.bfloat16)
    qkv_grad = weight_term(h1, grad_qkv)
    qkv_sums = jnp.sum(grad_qkv.astype(jnp.float32), (0, 1))
    qv_bias_grad = jnp.concatenate([qkv_sums[:width], qkv_sums[2 * width :]])
    grad_h1 = jnp.einsum("bte,de->btd", grad_qkv, qkv_full, preferred_element_type=jnp.float32)
    unused_h1, first_back = jax.vjp(modulate, tokens, shift1, scale1)
    grad_tokens, grad_shift1, grad_scale1 = first_back(grad_h1)
    grad_tokens = grad_tokens + grad_mixed
    latents_grad = weighted.at[rows, kept].set(grad_tokens).astype(jnp.bfloat16)
    grad_mod = jnp.concatenate(
        [grad_shift1, grad_scale1, grad_gate1, grad_shift2, grad_scale2, grad_gate2], -1
    ).astype(jnp.bfloat16)
    ada_grad = jnp.dot(cvec.T, grad_mod, preferred_element_type=jnp.float32)
    ada_bias_grad = jnp.sum(grad_mod.astype(jnp.float32), 0)
    grad_cvec = jnp.dot(grad_mod, ada_full.T, preferred_element_type=jnp.float32)
    unused_cond, silu_back = jax.vjp(jax.nn.silu, cond)
    grad_cond = silu_back(grad_cvec)[0]
    time_grad = jnp.dot(band_hot.T, grad_cond, precision=HIGH)
    class_grad = jnp.dot(class_hot.T, grad_cond, precision=HIGH)
    shares = (
        lax.psum_scatter(time_grad, "grp", scatter_dimension=1, tiled=True),
        lax.psum_scatter(class_grad, "grp", scatter_dimension=1, tiled=True),
        lax.psum_scatter(ada_grad, "grp", scatter_dimension=1, tiled=True),
        lax.psum_scatter(ada_bias_grad, "grp", scatter_dimension=0, tiled=True),
        lax.psum_scatter(qkv_grad, "grp", scatter_dimension=1, tiled=True),
        lax.psum_scatter(qv_bias_grad, "grp", scatter_dimension=0, tiled=True),
        lax.psum_scatter(proj_grad, "grp", scatter_dimension=0, tiled=True),
        lax.psum_scatter(proj_bias_grad, "grp", scatter_dimension=0, tiled=True),
        lax.psum_scatter(fc1_grad, "grp", scatter_dimension=1, tiled=True),
        lax.psum_scatter(fc1_bias_grad, "grp", scatter_dimension=0, tiled=True),
        lax.psum_scatter(fc2_grad, "grp", scatter_dimension=0, tiled=True),
        lax.psum_scatter(fc2_bias_grad, "grp", scatter_dimension=0, tiled=True),
    )
    totals = (
        lax.psum(shares[0].astype(jnp.bfloat16), "dp").astype(jnp.float32),
        lax.psum(shares[1].astype(jnp.bfloat16), "dp").astype(jnp.float32),
        lax.psum(shares[2].astype(jnp.bfloat16), "dp").astype(jnp.float32),
        lax.psum(shares[3].astype(jnp.bfloat16), "dp").astype(jnp.float32),
        lax.psum(shares[4].astype(jnp.bfloat16), "dp").astype(jnp.float32),
        lax.psum(shares[5].astype(jnp.bfloat16), "dp").astype(jnp.float32),
        lax.psum(shares[6].astype(jnp.bfloat16), "dp").astype(jnp.float32),
        lax.psum(shares[7].astype(jnp.bfloat16), "dp").astype(jnp.float32),
        lax.psum(shares[8].astype(jnp.bfloat16), "dp").astype(jnp.float32),
        lax.psum(shares[9].astype(jnp.bfloat16), "dp").astype(jnp.float32),
        lax.psum(shares[10].astype(jnp.bfloat16), "dp").astype(jnp.float32),
        lax.psum(shares[11].astype(jnp.bfloat16), "dp").astype(jnp.float32),
    )
    return (
        block_out,
        latents_grad,
        totals[0],
        totals[1],
        totals[2],
        totals[3],
        totals[4],
        totals[5],
        totals[6],
        totals[7],
        totals[8],
        totals[9],
        totals[10],
        totals[11],
    )


MESH = pl.DeviceIdType.MESH
F32 = jnp.float32
BF16 = jnp.bfloat16
GELU_A = 0.7978845608028654
GELU_B = 0.044715


def dot(left, right, dims):
    return lax.dot_general(left, right, ((dims[:1], dims[1:]), ((), ())), preferred_element_type=F32)


class Place:
    def __init__(self):
        self.g = lax.axis_index("grp")
        self.z = lax.axis_index("dp")
        self.c = self.g % 2
        self.x = (self.g // 2) % 2
        self.y = self.g // 4

    def block(self, dc, dx, dy):
        c = 1 - self.c if dc else self.c
        x = 1 - self.x if dx else self.x
        y = 1 - self.y if dy else self.y
        return y * 4 + x * 2 + c

    def device(self, dc, dx, dy):
        return (self.block(dc, dx, dy), self.z)


RELATIVE = [(r & 1, (r >> 1) & 1, r >> 2) for r in range(8)]


class Wire:
    def __init__(self, send, recv):
        self.send, self.recv, self.sends, self.recvs = send, recv, 0, 0

    def take(self, recvs, sends=1):
        first = (self.sends, self.recvs)
        self.sends += sends
        self.recvs += recvs
        return first

    def copy(self, send, recv, src, dst, device):
        return pltpu.make_async_remote_copy(
            src_ref=src,
            dst_ref=dst,
            send_sem=self.send.at[send],
            recv_sem=self.recv.at[recv],
            device_id=device,
            device_id_type=MESH,
        )


def halves(rows):
    cut = rows // 32 * 16
    return pl.ds(0, cut), pl.ds(cut, rows - cut)


def greet(devices):
    barrier = pltpu.get_barrier_semaphore()
    for device in devices:
        pl.semaphore_signal(barrier, inc=1, device_id=device, device_id_type=MESH)
    pl.semaphore_wait(barrier, len(devices))


def plane(place):
    return [place.device(*rel) for rel in RELATIVE[1:]]


class Gather:
    def __init__(self, place, wire, buf, start=0, rows=None, origin=None):
        p = place
        rows = rows or buf.shape[1]
        lo, hi = halves(rows)
        parts = (pl.ds(start, rows), pl.ds(start, lo.size), pl.ds(start + lo.size, hi.size))
        send, recv = wire.take(8)

        def make(number, block, device, part=0):
            ref = buf.at[block, parts[part]]
            src = origin if number < 3 and origin is not None else ref
            return wire.copy(send, recv + number, src, ref, device)

        own, xb, yb, db = p.g, p.block(0, 1, 0), p.block(0, 0, 1), p.block(0, 1, 1)
        xd, yd, sd = p.device(0, 1, 0), p.device(0, 0, 1), p.device(1, 0, 0)
        self.c = [
            make(0, own, xd),
            make(1, own, yd),
            make(2, own, sd),
            make(3, xb, yd, 1),
            make(4, xb, sd),
            make(5, yb, xd, 2),
            make(6, yb, sd),
            make(7, db, sd),
        ]
        seven = buf.at[pl.ds(0, 7), parts[0]]
        self.sent = wire.copy(send, recv, seven, seven, sd)

    def start(self):
        for number in (0, 1, 2):
            self.c[number].start()

    def arrived(self):
        self.c[0].wait_recv()
        self.c[1].wait_recv()
        self.c[4].start()
        self.c[6].start()

    def forward(self):
        self.c[3].start()
        self.c[5].start()

    def neighbours(self):
        self.arrived()
        self.forward()

    def far(self):
        self.c[3].wait_recv()
        self.c[5].wait_recv()
        self.c[7].start()

    def wait_sib(self):
        self.c[2].wait_recv()

    def wait_sib_neighbours(self):
        self.c[4].wait_recv()
        self.c[6].wait_recv()

    def wait_sib_far(self):
        self.c[7].wait_recv()

    def finish(self):
        self.sent.wait_send()


class OverZ:
    def __init__(self, place, wire, buf, hbm, there, ahead, behind, rows):
        p = place
        near = [p.block(0, 1, 0), p.block(0, 0, 1), p.block(0, 1, 1)]
        sd = p.device(1, 0, 0)
        sem, recv = wire.take(7)
        send, take = pl.ds(ahead, rows), pl.ds(behind, rows)
        self.out = [wire.copy(sem, recv + i, buf.at[b, send], buf.at[b, send], there) for i, b in enumerate(near)]
        self.on = [wire.copy(sem, recv + 3 + i, buf.at[b, take], buf.at[b, take], sd) for i, b in enumerate(near)]
        self.own = wire.copy(sem, recv + 6, hbm.at[take], buf.at[p.g, take], sd)
        seven = buf.at[pl.ds(0, 7), send]
        self.sent = wire.copy(sem, recv, seven, seven, sd)

    def pass_on(self, *numbers):
        for i in numbers:
            self.out[i].wait_recv()
            self.on[i].start()

    def arrived(self, *numbers):
        for i in numbers:
            self.on[i].wait_recv()

    def finish(self):
        self.sent.wait_send()


class Scatter:
    def __init__(self, place, wire, buf, r1, r2, r3, rows=None):
        self.p, self.w, self.buf = place, wire, buf
        self.r1, self.r2, self.r3 = r1, r2, r3
        self.rows = rows = rows or buf.shape[1]
        p, w = place, wire
        self.sib = [p.block(1, q & 1, q >> 1) for q in range(4)]
        self.mine = [p.block(0, q & 1, q >> 1) for q in range(4)]
        xd, yd, sd = p.device(0, 1, 0), p.device(0, 0, 1), p.device(1, 0, 0)
        sem, recv = wire.take(14)
        whole = pl.ds(0, rows)
        lo, hi = halves(rows)
        self.parts = [[pl.ds(half.start + cut.start, cut.size) for cut in halves(half.size)] for half in (lo, hi)]
        self.s1 = [w.copy(sem, recv + q, buf.at[self.sib[q], whole], r1.at[q, whole], sd) for q in range(4)]
        self.s2, self.s3 = [], []
        for way, device in ((0, xd), (1, yd)):
            for i, part in enumerate(self.parts[way]):
                number = recv + 4 + 2 * way + i
                self.s2.append(w.copy(sem, number, buf.at[self.mine[3], part], r2.at[way, pl.ds(part.start - self.parts[way][0].start, part.size)], device))
        for way, device in ((0, xd), (1, yd)):
            direct = (lo, hi)[way]
            for i, part in enumerate([direct] + self.parts[1 - way]):
                number = recv + 8 + 3 * way + i
                self.s3.append(w.copy(sem, number, buf.at[self.mine[1 + way], part], r3.at[way, part], device))
        seven = buf.at[pl.ds(0, 7), whole]
        self.sent = wire.copy(sem, recv, seven, seven, sd)

    def send_sib(self, q):
        self.s1[q].start()

    def add_sib(self, q):
        self.s1[q].wait_recv()
        add_into(self.buf.at[self.mine[q], pl.ds(0, self.rows)], self.r1.at[q, pl.ds(0, self.rows)])

    def send_far(self):
        self.add_sib(3)
        for number in (0, 2, 1, 3):
            self.s2[number].start()

    def send_near(self):
        self.add_sib(1)
        self.s3[0].start()
        self.add_sib(2)
        self.s3[3].start()

    def relay(self):
        for i in range(2):
            for way in range(2):
                self.s2[2 * way + i].wait_recv()
                part = self.parts[way][i]
                came = self.r2.at[way, pl.ds(part.start - self.parts[way][0].start, part.size)]
                add_into(self.buf.at[self.mine[2 - way], part], came)
                self.s3[3 * (1 - way) + 1 + i].start()
        self.add_sib(0)

    def result(self, out):
        for copy in self.s3:
            copy.wait_recv()
        step = 16

        @pl.loop(0, self.rows // step)
        def _(i):
            at = pl.ds(pl.multiple_of(i * step, step), step)
            total = self.buf[self.mine[0], at].astype(F32) + self.r3[0, at].astype(F32) + self.r3[1, at].astype(F32)
            out[at] = total.astype(out.dtype)

    def finish(self):
        self.sent.wait_send()


def add_into(ref, other):
    step = 16

    @pl.loop(0, ref.shape[0] // step)
    def _(i):
        at = pl.ds(pl.multiple_of(i * step, step), step)
        ref[at] = (ref[at].astype(F32) + other[at].astype(F32)).astype(ref.dtype)


def scatter_scratch(rows, width):
    return [
        pltpu.VMEM((4, rows, width), BF16),
        pltpu.VMEM((2, halves(rows)[1].size, width), BF16),
        pltpu.VMEM((2, rows, width), BF16),
    ]


class Together:
    def __init__(self, wire, buf, pairs, device):
        send, recv = wire.take(1)
        count = len(pairs)
        for src, dst, target in pairs:
            wire.copy(send, recv, src, dst, target).start()
        all_blocks = buf.at[pl.ds(0, count)]
        self.all = wire.copy(send, recv, all_blocks, all_blocks, device)


def to_all(place, wire, buf, make):
    pairs = [(make(rel), buf.at[place.g], place.device(*rel)) for rel in RELATIVE[1:]]
    return Together(wire, buf, pairs, place.device(1, 0, 0))


def wait_recv(copies):
    copies.all.wait_recv()


def wait_send(copies):
    copies.all.wait_send()


def params(collective_id):
    return pltpu.CompilerParams(
        collective_id=collective_id, has_side_effects=True, vmem_limit_bytes=63 * 2**20
    )


VMEM = pl.BlockSpec(memory_space=pltpu.VMEM)

def gelu_parts(pre):
    square = pre * pre
    inner = jnp.tanh(GELU_A * pre * (1.0 + GELU_B * square))
    act = 0.5 * pre * (1.0 + inner)
    slope = 0.5 * (1.0 + inner) + 0.5 * pre * (1.0 - inner * inner) * (GELU_A * (1.0 + 3.0 * GELU_B * square))
    return act, slope


def local(src, dst, sem):
    return pltpu.make_async_copy(src, dst, sem)


def own_tokens(kept_ref, length, s):
    rows = lax.broadcasted_iota(jnp.int32, (length, kept_ref.shape[1]), 0)
    return jnp.where(rows == kept_ref[s : s + 1, :], 1.0, 0.0).astype(BF16)


def normed(v):
    cent = v - jnp.mean(v, -1, keepdims=True)
    inv = lax.rsqrt(jnp.mean(cent * cent, -1, keepdims=True) + EPS)
    return cent * inv, inv


def norm_back(grad, hat, inv):
    return inv * (grad - jnp.mean(grad, -1, keepdims=True) - hat * jnp.mean(grad * hat, -1, keepdims=True))


STEP = 32


def by_rows(samples, keep, fn):
    @pl.loop(0, samples * keep // STEP)
    def _(i):
        fn(lax.div(i, keep // STEP), pl.ds(pl.multiple_of(i * STEP, STEP), STEP))


SCALE = HEAD_DIM ** (-0.5)


def probabilities(q, k):
    scores = dot(q, k, (0, 0)) * SCALE
    exps = jnp.exp(scores - jnp.max(scores, -1, keepdims=True))
    return exps / jnp.sum(exps, -1, keepdims=True)


def arrival(p, t, last=7):
    dc = jnp.where((t == 1) | (t == 4) | (t == 5) | (t == last), 1, 0)
    dx = jnp.where((t == 2) | (t == 4) | (t >= 6), 1, 0)
    dy = jnp.where((t == 3) | (t >= 5), 1, 0)
    c, x, y = lax.rem(p.c + dc, 2), lax.rem(p.x + dx, 2), lax.rem(p.y + dy, 2)
    return y * 4 + x * 2 + c


def sample_weight(place, counts_ref, samples, s):
    count = jnp.full((1, 128), counts_ref[0], jnp.int32)
    used = count > place.z * samples + s
    return (jnp.where(used, 1.0, 0.0) / count.astype(F32))[:, 0:1]


ANY = pl.BlockSpec(memory_space=pltpu.HBM)
SMEM = pl.BlockSpec(memory_space=pltpu.SMEM)
PIECE = 48


def block_kernel(samples, planes, labels_ref, bands_ref, counts_ref, wq_hbm, wp_hbm, w1_hbm, w2_hbm, ada_hbm, lat_hbm, cot_hbm,
                 bp_ref, b2_ref, qv_ref, bada_ref, b1_ref, kept_ref, class_ref, time_ref,
                 out_hbm, y_hbm, dx_hbm, wq_keep, dmod_hbm, dcond_hbm, cvec_hbm, sum_hbm, ids_hbm,
                 dmod_z, dcond_z, cvec_z, sum_z, ids_z,
                 wq, wp, w1, w2, h1_all, h2_all, dm_all, act, dpre, p1, p2, p3, units, att, mixed, proj, grad, dx2, tmp, rest,
                 dproj, dq, dq_all, from_end, out, grads, gb1, ids_all, msg_all, cond_all, mod_in, mod_send, mod, vec,
                 dc_send, dc_in, bundle, share_send, share_in, send, recv, credits, sems):
    p = Place()
    wire = Wire(send, recv)
    g, z = p.g, p.z
    others = [(g, (z + k) % planes) for k in range(1, planes)]
    greet(plane(p) + others)
    length = lat_hbm.shape[1]
    keep = kept_ref.shape[1]
    rows, width = mixed.shape
    pair = 2 * HEAD_DIM
    hidden_units = act.shape[2]
    ada_rest = ada_hbm.shape[0] - hidden_units

    loads = {}
    for number, (name, src, dst) in enumerate((
        ("wq", wq_hbm, wq.at[g]),
        ("wp", wp_hbm, wp.at[g]),
        ("lat", lat_hbm, h2_all.at[pl.ds(0, samples)]),
        ("cot", cot_hbm, h2_all.at[pl.ds(samples, samples)]),
        ("ada1", ada_hbm.at[pl.ds(0, hidden_units)], w1),
        ("ada2", ada_hbm.at[pl.ds(hidden_units, ada_rest)], w2.at[pl.ds(0, ada_rest)]),
        ("w1", w1_hbm, w1),
        ("w2", w2_hbm, w2),
        ("keep", wq, wq_keep),
        ("again", wq_keep, wq),
        ("ada1b", ada_hbm.at[pl.ds(0, hidden_units)], w1),
        ("ada2b", ada_hbm.at[pl.ds(hidden_units, ada_rest)], w2.at[pl.ds(0, ada_rest)]),
        ("latb", lat_hbm, wq.at[pl.ds(0, samples), pl.ds(0, length)]),
        ("dx", dproj, dx_hbm),
        ("y", dproj, y_hbm),
        ("dmod", dmod_z, dmod_hbm),
        ("dcond", dcond_z, dcond_hbm),
        ("cvec", cvec_z, cvec_hbm),
        ("sum", sum_z, sum_hbm),
        ("ids", ids_z, ids_hbm),
    )):
        loads[name] = local(src, dst, sems.at[number])
    odd = z % 2
    there = (g, z + 1 - 2 * odd)
    gather_a = Gather(p, wire, wq, 2 * pair * odd, pair, wq_hbm.at[pl.ds(2 * pair * odd, pair)])
    gather_m = Gather(p, wire, wq, pair, pair, wq_hbm.at[pl.ds(pair, pair)])
    qkv_z = OverZ(p, wire, wq, wq_hbm, there, 2 * pair * odd, 2 * pair * (1 - odd), pair)
    inside = pair // 32 * 16 + 16
    beyond = pair - inside
    outward = Gather(p, wire, wp, beyond * odd, inside, wp_hbm.at[pl.ds(beyond * odd, inside)])
    proj_z = OverZ(p, wire, wp, wp_hbm, there, inside * odd, inside * (1 - odd), beyond)
    main = Gather(p, wire, h2_all)
    back = Gather(p, wire, dm_all)
    tokens = Gather(p, wire, h1_all)
    sums = Scatter(p, wire, wq, p1, p2, p3, rows)
    outs = Scatter(p, wire, h2_all, dm_all.at[pl.ds(0, 4)], dm_all.at[pl.ds(4, 2)], dm_all.at[pl.ds(6, 2)])
    projs = Scatter(p, wire, wp, p1, p2, p3)
    part_of = lambda start, size: grads.at[pl.ds(start, size)]
    g1, g2 = part_of(0, hidden_units), part_of(hidden_units, hidden_units)
    gq, gp = part_of(2 * hidden_units, 3 * pair), part_of(2 * hidden_units + 3 * pair, pair)
    count = grads.shape[0] // PIECE
    (up, up_r), (across, across_r), (down, down_r) = [wire.take(count) for way in range(3)]
    inner, outer, partner = 1 + z // 3, (z - 1) * 3, 3 - z
    at_end = (z == 0) | (z == planes - 1)
    rows_of = lambda ref, k: ref.at[pl.ds(pl.multiple_of(k * PIECE, 16), PIECE)]
    go_up = lambda k: wire.copy(up, up_r + k, rows_of(grads, k), rows_of(from_end, k), (g, inner))
    go_across = lambda k: wire.copy(across, across_r + k, rows_of(from_end, k), rows_of(out, k), (g, partner))
    go_down = lambda k: wire.copy(down, down_r + k, rows_of(out, k), rows_of(out, k), (g, outer))
    to_hbm = lambda k: local(rows_of(out, k), rows_of(out_hbm, k), sems.at[20])

    def chain_send(first, last):
        @pl.when(at_end)
        def _():
            for k in range(first, last):
                go_up(k).start()

    def chain_up(k):
        @pl.when(jnp.logical_not(at_end))
        def _():
            go_up(k).wait_recv()
            add_into(rows_of(from_end, k), rows_of(grads, k))
            go_across(k).start()

    def chain_down(k):
        @pl.when(jnp.logical_not(at_end))
        def _():
            go_across(k).wait_recv()
            add_into(rows_of(out, k), rows_of(from_end, k))
            go_down(k).start()
            to_hbm(k).start()

    def chain(k, lag=3):
        chain_up(k)
        chain_down(k - lag)

    def to_planes(ref):
        return Together(wire, ref, [(ref.at[z], ref.at[z], device) for device in others], others[0])

    neighbours = [p.device(1, 0, 0), p.device(0, 1, 0), p.device(0, 0, 1)]

    def grant(number):
        for i, device in enumerate(neighbours):
            pl.semaphore_signal(credits.at[number, i], inc=1, device_id=device, device_id_type=MESH)

    def granted(number):
        for i in range(3):
            pl.semaphore_wait(credits.at[number, i], 1)

    lanes = lax.broadcasted_iota(jnp.int32, (1, 128), 1)
    for s in range(samples):
        line = jnp.where(lanes == 0, labels_ref[s], 0) + jnp.where(lanes == 1, bands_ref[s], 0)
        ids_all[g, s : s + 1, :] = line.astype(F32)
    line_of = lambda ref: ref[...].astype(F32).reshape(1, ref.shape[0])
    b_ada, b1, qv = line_of(bada_ref), line_of(b1_ref), line_of(qv_ref)
    for row, line in enumerate((line_of(bp_ref), line_of(b2_ref), qv[:, :pair], qv[:, pair:])):
        msg_all[g, row : row + 1, :] = line
    idc = to_all(p, wire, ids_all, lambda rel: ids_all.at[g])
    gather_a.start()
    msgs = to_all(p, wire, msg_all, lambda rel: msg_all.at[g])
    for name in ("lat", "cot", "ada1", "ada2", "wq", "wp"):
        loads[name].start()

    wait_recv(idc)
    labels = jnp.concatenate([ids_all[j, 0:samples, 0:1] for j in range(8)], 0)
    bands = jnp.concatenate([ids_all[j, 0:samples, 1:2] for j in range(8)], 0)

    def one_hot(ids, size):
        lanes = lax.broadcasted_iota(jnp.int32, (ids.shape[0], size), 1).astype(F32)
        return jnp.where(lanes == ids, 1.0, 0.0).astype(BF16)

    of_band = dot(one_hot(bands, time_ref.shape[0]), time_ref[...], (1, 0))
    cond_all[g] = of_band + dot(one_hot(labels, class_ref.shape[1]), class_ref[...], (1, 1))
    conds = to_all(p, wire, cond_all, lambda rel: cond_all.at[g])
    ids_z[z] = jnp.zeros(ids_z.shape[1:], F32)
    ids_z[z, :, 0:1] = labels
    ids_z[z, :, 1:2] = bands


    loads["lat"].wait()
    loads["cot"].wait()
    for s in range(samples):
        hot = own_tokens(kept_ref, length, s)
        at = pl.ds(s * keep, keep)
        mixed[at] = dot(hot, h2_all[s], (0, 0))
        grad[at] = dot(hot, h2_all[samples + s], (0, 0)) * sample_weight(p, counts_ref, samples, s)

    gather_a.neighbours()
    qkv_z.out[0].start()
    qkv_z.out[1].start()
    wait_recv(conds)
    value = jnp.concatenate([cond_all[j] for j in range(8)], 1)
    value = (value * jax.nn.sigmoid(value)).astype(BF16)
    cvec_z[z] = value
    loads["ada1"].wait()
    loads["ada2"].wait()
    mods = [dot(value, w1[...], (1, 1)), dot(value, w2[0:ada_rest], (1, 1))]
    mods = jnp.concatenate(mods, 1) + b_ada
    for j in range(8):
        mod_send[j] = mods[samples * j : samples * (j + 1), :]
    mod_in[g] = mod_send[g]
    modc = to_all(p, wire, mod_in, lambda rel: mod_send.at[p.block(*rel)])
    gather_m.start()
    qkv_z.own.start()
    loads["w1"].start()
    loads["w2"].start()
    gather_a.far()
    qkv_z.out[2].start()
    wait_recv(modc)
    mod[...] = jnp.zeros_like(mod)
    for s in range(samples):
        line = jnp.concatenate([mod_in[j, s : s + 1, :] for j in range(8)], 1)
        for v in range(6):
            mod[s, v : v + 1, :] = line[:, v * width : (v + 1) * width]

    def first_norm(s, at):
        hat, inv = normed(mixed[at])
        h1_all[g, at] = (hat * (1.0 + mod[s, 1:2, :]) + mod[s, 0:1, :]).astype(BF16)
        dm_all[g, at] = (mod[s, 5:6, :] * grad[at]).astype(BF16)

    by_rows(samples, keep, first_norm)
    wait_recv(msgs)
    vec[...] = jnp.zeros_like(vec)
    for row in range(2):
        vec[row : row + 1, :] = jnp.concatenate([msg_all[j, row : row + 1, :] for j in range(8)], 1)

    ones = jnp.ones((8, rows), BF16)
    loads["wq"].wait()

    @pl.loop(0, 24)
    def _(n):
        for base, gather in ((0, gather_a), (8, gather_m)):

            @pl.when(n == base + 1)
            def _(gather=gather):
                gather.wait_sib()

            @pl.when(n == base + 4)
            def _(gather=gather):
                gather.wait_sib_neighbours()

            if base:

                @pl.when(n == base + 6)
                def _(gather=gather):
                    gather.far()

            @pl.when(n == base + 7)
            def _(gather=gather):
                gather.wait_sib_far()

        @pl.when(n == 6)
        def _():
            gather_m.neighbours()
            outward.start()
            proj_z.own.start()

        @pl.when(n == 16)
        def _():
            outward.neighbours()
            back.start()
            proj_z.out[0].start()
            proj_z.out[1].start()

        @pl.when(n == 17)
        def _():
            qkv_z.own.wait_recv()

        @pl.when(n == 18)
        def _():
            qkv_z.pass_on(0, 1)

        @pl.when(n == 20)
        def _():
            qkv_z.arrived(0, 1)

        @pl.when(n == 22)
        def _():
            qkv_z.pass_on(2)

        @pl.when(n == 23)
        def _():
            qkv_z.arrived(2)

        phase = lax.div(n, 8)
        block = arrival(p, lax.rem(n, 8))
        third = jnp.where(phase == 0, 2 * odd, jnp.where(phase == 1, 1, 2 - 2 * odd))
        chunk = block * 3 + third
        bias_at = jnp.where(chunk >= 16, chunk - 8, chunk)
        keys = (chunk >= 8) & (chunk < 16)
        line = msg_all[lax.div(bias_at, 2), pl.ds(2 + lax.rem(bias_at, 2), 1), :] * jnp.where(keys, 0.0, 1.0)
        line = jnp.concatenate([line, jnp.zeros((7, pair), F32)], 0)
        value = dot(wq[block, pl.ds(pl.multiple_of(third * pair, 16), pair), :], h1_all[g], (1, 1))
        value = value + dot(line.astype(BF16), ones, (0, 0))
        units[2 * chunk] = value[:HEAD_DIM].astype(BF16)
        units[2 * chunk + 1] = value[HEAD_DIM:].astype(BF16)

    loads["keep"].start()
    zs = [to_planes(ids_z), to_planes(cvec_z)]

    @pl.loop(0, 8)
    def _(u):
        @pl.when(u == 3)
        def _():
            outward.far()
            proj_z.out[2].start()

        for s in range(samples):
            lanes = pl.ds(s * keep, keep)
            pieces = []
            for e in range(2):
                probs = probabilities(units[2 * u + e, :, lanes], units[16 + 2 * u + e, :, lanes])
                pieces.append(dot(units[32 + 2 * u + e, :, lanes], probs.astype(BF16), (1, 1)))
            att[u, :, lanes] = jnp.concatenate(pieces, 0).astype(BF16)

    back.neighbours()
    loads["wp"].wait()
    outward.wait_sib()
    outward.wait_sib_neighbours()
    outward.wait_sib_far()
    proj_z.own.wait_recv()
    proj_z.pass_on(0, 1, 2)
    proj_z.arrived(0, 1, 2)
    proj[...] = jnp.zeros_like(proj)

    @pl.loop(0, 8)
    def _(u):
        proj[...] += dot(att[u], wp[u], (0, 0))

    def second_norm(s, at):
        proj[at] = proj[at] + vec[0:1, :]
        mixed[at] = mixed[at] + mod[s, 2:3, :] * proj[at]
        hat, inv = normed(mixed[at])
        h2_all[g, at] = (hat * (1.0 + mod[s, 4:5, :]) + mod[s, 3:4, :]).astype(BF16)

    by_rows(samples, keep, second_norm)
    main.start()
    back.far()
    gb1[...] = jnp.zeros_like(gb1)
    for piece in (gather_a, gather_m, qkv_z):
        piece.finish()
    loads["w1"].wait()
    loads["w2"].wait()
    loads["keep"].wait()

    def hidden(block):
        pre = dot(h2_all[block], w1[...], (1, 1)) + b1
        value, slope = gelu_parts(pre)
        act[block] = value.astype(BF16)
        low = (dot(dm_all[block], w2[...], (1, 1)) * slope).astype(BF16)
        dpre[block] = low
        gb1[...] += jnp.sum(low.astype(F32), 0, keepdims=True)
        wq[block, pl.ds(0, rows)] = dot(low, w1[...], (1, 0)).astype(BF16)

    @pl.loop(0, 8)
    def _(t):
        @pl.when(t == 1)
        def _():
            main.wait_sib()
            back.wait_sib()

        @pl.when(t == 2)
        def _():
            main.neighbours()
            back.wait_sib_neighbours()
            back.wait_sib_far()

        @pl.when(t == 4)
        def _():
            main.wait_sib_neighbours()

        @pl.when(t == 6)
        def _():
            main.far()
            sums.send_near()
            main.wait_sib_far()

        hidden(arrival(p, t, 6))
        for at, q in ((1, 0), (4, 1), (5, 2), (6, 3)):

            @pl.when(t == at)
            def _(q=q):
                sums.send_sib(q)

    sums.send_far()

    def weight_grad(left, right, base, between):
        for ref, start, size in ((dx2, 0, 256), (tmp, 256, 256), (rest, 512, hidden_units - 512)):
            ref[0:size] = jnp.zeros((size, width), F32)

            @pl.loop(0, 4)
            def _(i):
                two = pl.ds(2 * i, 2)
                part = left[two, :, pl.ds(start, size)].reshape(2 * rows, size)
                ref[0:size] += dot(part, right[two].reshape(2 * rows, width), (0, 0))

            grads[base + start : base + start + size] = ref[0:size].astype(BF16)
            chain_send(-(-(base + start) // PIECE) if start == 0 else (base + start) // PIECE, (base + start + size) // PIECE)
            between(start)

    weight_grad(dpre, h2_all, 0, lambda start: None)
    sums.relay()
    main.finish()
    tokens.start()
    chain_up(0)
    weight_grad(act, dm_all, hidden_units, lambda start: chain_up(1 + start // 256))
    chain_down(0)
    back.finish()
    grant(0)
    sums.result(tmp)
    sums.finish()
    grant(1)
    loads["again"].start()

    bundle[...] = jnp.zeros_like(bundle)

    def add_row(row, value):
        bundle[pl.ds(row, 1), :] += jnp.sum(value, 0, keepdims=True)

    SUM_PROJ, SUM_FC2 = 6 * samples, 6 * samples + 1

    def second_back(s, at):
        hat, inv = normed(mixed[at])
        up_grad = tmp[at]
        value = grad[at] + norm_back(up_grad * (1.0 + mod[s, 4:5, :]), hat, inv)
        dx2[at] = value
        low = (mod[s, 2:3, :] * value).astype(BF16)
        dproj[at] = low
        add_row(s * 6 + 3, up_grad)
        add_row(s * 6 + 4, up_grad * hat)
        add_row(s * 6 + 2, value * proj[at])
        add_row(SUM_PROJ, low.astype(F32))
        add_row(SUM_FC2, (mod[s, 5:6, :] * grad[at]).astype(BF16).astype(F32))

    chain_up(4)
    by_rows(samples, keep, second_back)
    chain_down(1)
    chain_up(5)
    chain_down(2)
    outward.finish()
    proj_z.finish()

    @pl.loop(0, 8)
    def _(u):
        datt = dot(wp[u], dproj[...], (1, 1))
        wp[u] = dot(att[u], dproj[...], (1, 0)).astype(BF16)
        lists = ([], [], [])
        for s in range(samples):
            lanes = pl.ds(s * keep, keep)
            parts = ([], [], [])
            for e in range(2):
                q, k, v = (units[16 * i + 2 * u + e, :, lanes] for i in range(3))
                da = datt[e * HEAD_DIM : (e + 1) * HEAD_DIM, s * keep : (s + 1) * keep].astype(BF16)
                probs = probabilities(q, k)
                dprobs = dot(da, v, (0, 0))
                dscores = probs * (dprobs - jnp.sum(dprobs * probs, -1, keepdims=True))
                dscores = dscores.astype(BF16)
                parts[0].append(dot(k, dscores, (1, 1)) * SCALE)
                parts[1].append(dot(q, dscores, (1, 0)) * SCALE)
                parts[2].append(dot(da, probs.astype(BF16), (1, 0)))
            for i in range(3):
                lists[i].append(jnp.concatenate(parts[i], 0).astype(BF16))
        for i in range(3):
            chunk = 8 * i + u
            at = pl.ds(pl.multiple_of(lax.rem(chunk, 3) * pair, 16), pair)
            for s in range(samples):
                dq[lax.div(chunk, 3), at, pl.ds(s * keep, keep)] = lists[i][s]

        @pl.when(u == 4)
        def _():
            tokens.neighbours()

        chain(6 + u)

    dq_all[g] = dq[g]
    moves = to_all(p, wire, dq_all, lambda rel: dq.at[p.block(*rel)])
    granted(1)
    for q in (3, 1, 2, 0):
        projs.send_sib(q)
    tokens.far()

    loads["again"].wait()
    proj[...] = jnp.zeros_like(proj)

    @pl.loop(0, 8)
    def _(j):
        proj[...] += dot(dq[j], wq[j], (0, 0))
        for at in range(2):

            @pl.when(j == 4 * at + 3)
            def _(at=at):
                chain(14 + at)

    loads["latb"].start()

    granted(0)

    @pl.loop(0, 8)
    def _(t):
        block = arrival(p, 7 - t)
        h2_all[block] = jnp.dot(act[block], w2[...], preferred_element_type=F32).astype(BF16)

        for at in range(2):

            @pl.when(t == 4 * at + 3)
            def _(at=at):
                chain(16 + at)

        for at, q in ((1, 0), (4, 1), (5, 2), (7, 3)):

            @pl.when(t == 7 - at)
            def _(q=q):
                outs.send_sib(q)

    loads["ada1b"].start()
    loads["ada2b"].start()
    tokens.wait_sib()
    tokens.wait_sib_neighbours()
    tokens.wait_sib_far()
    for k in range(18, 22):
        chain(k)

    wait_recv(moves)
    projs.send_far()
    projs.send_near()
    for i in range(3):
        at = pl.ds(i * pair, pair)
        tmp[0:pair] = jnp.zeros((pair, width), F32)

        @pl.loop(0, 8)
        def _(j, at=at):
            tmp[0:pair] += dot(dq_all[j, at, :], h1_all[j], (1, 0))

        gq[at] = tmp[0:pair].astype(BF16)
        chain_send(24 + 3 * i, 27 + 3 * i)
        chain(22 + i)
    projs.relay()
    outs.send_far()
    outs.send_near()
    chain(25)

    loads["latb"].wait()
    for s in range(samples):
        hot = own_tokens(kept_ref, length, s)
        tmp[pl.ds(s * keep, keep)] = dot(hot, wq[s, pl.ds(0, length)], (0, 0))

    def first_back(s, at):
        hat, inv = normed(tmp[at])
        up_grad = proj[at]
        dx = dx2[at] + norm_back(up_grad * (1.0 + mod[s, 1:2, :]), hat, inv)
        add_row(s * 6, up_grad)
        add_row(s * 6 + 1, up_grad * hat)
        dproj[at] = dx.astype(BF16)

    by_rows(samples, keep, first_back)
    chain(26)
    projs.result(gp)
    chain_send(33, 36)
    loads["dx"].start()
    chain(27)
    chain(28)
    outs.relay()
    for k in range(29, 35):
        chain(k)
    outs.result(tmp)
    chain(35)

    def end(s, at):
        value = tmp[at] + vec[1:2, :]
        add_row(s * 6 + 5, grad[at] * value)
        dproj[at] = (mixed[at] + mod[s, 5:6, :] * value).astype(BF16)

    loads["dx"].wait()
    by_rows(samples, keep, end)
    loads["y"].start()

    cols = ada_hbm.shape[0]
    wait_send(modc)
    for s in range(samples):
        line = jnp.concatenate([bundle[s * 6 + v : s * 6 + v + 1, :] for v in range(6)], 1)
        for j in range(8):
            mod_send[j, s : s + 1, :] = line[:, j * cols : (j + 1) * cols].astype(BF16).astype(F32)
    mod_in[g] = mod_send[g]
    dmods = to_all(p, wire, mod_in, lambda rel: mod_send.at[p.block(*rel)])
    lines = [dot(ones, dq[j], (1, 1))[0:1, :] for j in range(8)]
    for j in range(8):
        for row, at in ((0, SUM_PROJ), (1, SUM_FC2)):
            share_send[j, row : row + 1, :] = bundle[at : at + 1, j * pair : (j + 1) * pair]
        for e in range(2):
            u = 2 * j + e + (8 if j >= 4 else 0)
            share_send[j, 2 + e : 3 + e, :] = lines[u // 3][:, u % 3 * pair : (u % 3 + 1) * pair]
    share_in[g] = share_send[g]
    small = to_all(p, wire, share_in, lambda rel: share_send.at[p.block(*rel)])
    chain_down(33)
    loads["ada1b"].wait()
    loads["ada2b"].wait()
    wait_recv(dmods)
    part = jnp.concatenate([mod_in[j] for j in range(8)], 0).astype(BF16)
    dmod_z[z] = part
    zs.append(to_planes(dmod_z))
    dcvec = dot(part[:, :hidden_units], w1[...], (1, 0)) + dot(part[:, hidden_units:], w2[0:ada_rest], (1, 0))
    depth = cond_all.shape[2]
    for j in range(8):
        dc_send[j] = dcvec[:, j * depth : (j + 1) * depth]
    dc_in[g] = dc_send[g]
    dcs = to_all(p, wire, dc_in, lambda rel: dc_send.at[p.block(*rel)])
    chain_down(34)
    wait_recv(small)
    sum_z[z, 0:4, :] = sum(share_in[j] for j in range(8))
    for i in range(hidden_units // pair):
        sum_z[z, 4 + i : 5 + i, :] = gb1[:, i * pair : (i + 1) * pair]
    zs.append(to_planes(sum_z))
    chain_down(35)
    wait_recv(dcs)
    cond = cond_all[g]
    gate = jax.nn.sigmoid(cond)
    dcond_z[z] = sum(dc_in[j] for j in range(8)) * (gate * (1.0 + cond * (1.0 - gate)))
    zs.append(to_planes(dcond_z))

    whole = lambda sem, ref: wire.copy(sem, up_r, ref, ref, (g, partner))

    @pl.when(jnp.logical_not(at_end))
    def _():
        whole(across, out).wait_send()
        whole(down, out).wait_send()

    @pl.when(at_end)
    def _():
        @pl.loop(0, count)
        def _(k):
            go_down(k).wait_recv()
            to_hbm(k).start()

        whole(up, out).wait_send()

    local(out, out_hbm, sems.at[20]).wait()
    for copies in zs:
        wait_recv(copies)
    for name in ("ids", "cvec", "dmod", "sum", "dcond"):
        loads[name].start()
    for copies in zs:
        wait_send(copies)
    for copies in (idc, msgs, conds, moves, dmods, small, dcs):
        wait_send(copies)
    for piece in (tokens, projs, outs):
        piece.finish()
    for name in ("y", "ids", "cvec", "dmod", "sum", "dcond"):
        loads[name].wait()


def run_block(samples, planes, labels, bands, counts, wq, wp, w1, w2, w_ada, lat, cot, biases, kept, class_table, time_table):
    keep, width = kept.shape[1], wq.shape[1]
    rows, hidden, per = samples * keep, w1.shape[0], 8 * samples
    cols, depth = w_ada.shape[0], class_table.shape[0]
    total = 2 * hidden + wq.shape[0] + wp.shape[0]
    count = total // PIECE
    shape, room = jax.ShapeDtypeStruct, pltpu.VMEM
    blocks = room((8, rows, width), BF16)
    plain = room((rows, width), F32)
    over_z = [
        ((planes, per, cols), BF16),
        ((planes, per, depth), F32),
        ((planes, per, width), BF16),
        ((planes, 4 + hidden // depth, depth), F32),
        ((planes, per, 128), F32),
    ]
    sends, recvs = 6 + 2 + 3 + 3 + 8 + 5, 8 * 6 + 2 * 7 + 3 * 14 + 3 * count + 8 + 5
    return pl.pallas_call(
        functools.partial(block_kernel, samples, planes),
        out_shape=[
            shape((total, width), BF16),
            shape((rows, width), BF16),
            shape((rows, width), BF16),
            shape((8,) + wq.shape, BF16),
            *[shape(dims, kind) for dims, kind in over_z],
        ],
        in_specs=[SMEM] * 3 + [ANY] * 7 + [VMEM] * 8,
        out_specs=[ANY] * 9,
        scratch_shapes=[
            *[room(dims, kind) for dims, kind in over_z],
            room((8,) + wq.shape, BF16),
            room((8,) + wp.shape, BF16),
            room(w1.shape, BF16),
            room(w2.shape, BF16),
            blocks,
            blocks,
            blocks,
            room((8, rows, hidden), BF16),
            room((8, rows, hidden), BF16),
            *scatter_scratch(rows, width),
            room((48, HEAD_DIM, rows), BF16),
            room((8, 2 * HEAD_DIM, rows), BF16),
            plain,
            plain,
            plain,
            plain,
            plain,
            room((hidden - 512, width), F32),
            room((rows, width), BF16),
            room((8, wq.shape[0], rows), BF16),
            room((8, wq.shape[0], rows), BF16),
            room((total, width), BF16),
            room((total, width), BF16),
            room((total, width), BF16),
            room((1, hidden), F32),
            room((8, samples, 128), F32),
            room((8, 4, wp.shape[0]), F32),
            room((8, per, depth), F32),
            room((8, samples, cols), F32),
            room((8, samples, cols), F32),
            room((samples, 8, width), F32),
            room((8, width), F32),
            room((8, per, depth), F32),
            room((8, per, depth), F32),
            room((16, width), F32),
            room((8, 4, wp.shape[0]), F32),
            room((8, 4, wp.shape[0]), F32),
            pltpu.SemaphoreType.DMA((sends,)),
            pltpu.SemaphoreType.DMA((recvs,)),
            pltpu.SemaphoreType.REGULAR((2, 3)),
            pltpu.SemaphoreType.DMA((21,)),
        ],
        compiler_params=params(1),
    )(labels, bands, counts, wq, wp, w1, w2, w_ada, lat, cot, *biases, kept, class_table, time_table)


def outputs_kernel(samples, planes, counts_ref, totals_hbm, y_hbm, dx_hbm, lat_hbm, cot_hbm, kept_hbm, dmod_hbm, dcond_hbm,
                   cvec_hbm, sum_hbm, ids_hbm,
                   block_hbm, latg_hbm, g1_hbm, g2_hbm, gq_hbm, gp_hbm, ada_hbm, time_hbm, class_hbm, bada_hbm, qv_hbm, bp_hbm,
                   b1_hbm, b2_hbm,
                   kept_ref, dmod_ref, dcond_ref, cvec_ref, sum_ref, ids_ref, time_out, class_out, bada_out, qv_out, bp_out,
                   b1_out, b2_out, totals, wide, ada, tokens, both, sems_in, sems):
    p = Place()
    length = lat_hbm.shape[1]
    keep = kept_ref.shape[1]
    chunk = 144
    count, width = totals.shape[0] // chunk, totals.shape[1]
    per = 8 * samples
    chunks = [pl.ds(k * chunk, chunk) for k in range(count)]
    ins = [local(totals_hbm.at[at], totals.at[at], sems_in.at[k]) for k, at in enumerate(chunks)]
    ins += [
        local(y_hbm, tokens.at[0], sems_in.at[count]),
        local(dx_hbm, tokens.at[1], sems_in.at[count + 1]),
        local(lat_hbm, both.at[0], sems_in.at[count + 2]),
        local(cot_hbm, both.at[1], sems_in.at[count + 3]),
    ]
    pairs = ((dmod_hbm, dmod_ref), (cvec_hbm, cvec_ref), (kept_hbm, kept_ref), (dcond_hbm, dcond_ref), (sum_hbm, sum_ref), (ids_hbm, ids_ref))
    small = [local(src, dst, sems_in.at[count + 4 + i]) for i, (src, dst) in enumerate(pairs)]
    for copy in small + ins[count:] + ins[:count]:
        copy.start()
    done = []

    def send(src, dst):
        done.append(local(src, dst, sems.at[len(done)]))
        done[-1].start()

    for copy in small:
        copy.wait()
    cvec = jnp.concatenate([cvec_ref[k] for k in range(planes)], 0)
    dmod = jnp.concatenate([dmod_ref[k] for k in range(planes)], 0)
    cols = ada.shape[0]
    for start in range(0, cols, 256):
        size = min(256, cols - start)
        ada[start : start + size] = dot(dmod[:, start : start + size], cvec, (0, 0))
        send(ada.at[pl.ds(start, size)], ada_hbm.at[pl.ds(start, size)])
    bada_out[...] = jnp.sum(dmod.astype(F32), 0)
    send(bada_out, bada_hbm)

    for copy in ins[count:]:
        copy.wait()
    for s in range(samples):
        hot = own_tokens(kept_ref, length, s)
        is_kept = jnp.sum(hot.astype(F32), 1, keepdims=True) > 0.5
        at = pl.ds(s * keep, keep)
        both[0, s] = jnp.where(is_kept, dot(hot, tokens[0, at], (1, 0)), both[0, s].astype(F32)).astype(BF16)
        weighted = both[1, s].astype(F32) * sample_weight(p, counts_ref, samples, s)
        both[1, s] = jnp.where(is_kept, dot(hot, tokens[1, at], (1, 0)), weighted).astype(BF16)
    send(both.at[0], block_hbm)
    send(both.at[1], latg_hbm)

    k = 0
    for out in (g1_hbm, g2_hbm, gq_hbm, gp_hbm):
        for start in range(0, out.shape[0], chunk):
            ins[k].wait()
            wide[chunks[k]] = totals[chunks[k]].astype(F32)
            send(wide.at[chunks[k]], out.at[pl.ds(start, chunk)])
            k += 1

    dcond = jnp.concatenate([dcond_ref[k] for k in range(planes)], 0)
    ids = jnp.concatenate([ids_ref[k] for k in range(planes)], 0)

    def one_hot(column, size):
        lanes = lax.broadcasted_iota(jnp.int32, (planes * per, size), 1).astype(F32)
        return jnp.where(lanes == ids[:, column : column + 1], 1.0, 0.0)

    def exact(left, right):
        return lax.dot_general(left, right, (((0,), (0,)), ((), ())), precision=HIGH, preferred_element_type=F32)

    time_out[...] = exact(one_hot(1, time_out.shape[0]), dcond)
    send(time_out, time_hbm)
    class_out[...] = exact(dcond, one_hot(0, class_out.shape[1]))
    send(class_out, class_hbm)
    sums = sum(sum_ref[k] for k in range(planes))
    joined = lambda start, stop: jnp.concatenate([sums[i : i + 1, :] for i in range(start, stop)], 1)
    places = ((bp_out, bp_hbm, 0, 1), (b2_out, b2_hbm, 1, 2), (qv_out, qv_hbm, 2, 4), (b1_out, b1_hbm, 4, sums.shape[0]))
    for out, hbm, start, stop in places:
        out[...] = joined(start, stop).reshape(out.shape[0])
        send(out, hbm)
    for copy in done:
        copy.wait()


def place_outputs(samples, planes, counts, totals, y, dx, lat, cot, kept, dmod, dcond, cvec, sums, ids, hidden, wq, wp, classes, bands):
    count, width = totals.shape[0] // 144, totals.shape[1]
    cols, depth = dmod.shape[2], dcond.shape[2]
    shape, room = jax.ShapeDtypeStruct, pltpu.VMEM
    wide = lambda size: shape((size, width), F32)
    return pl.pallas_call(
        functools.partial(outputs_kernel, samples, planes),
        out_shape=[
            shape(lat.shape, BF16),
            shape(lat.shape, BF16),
            wide(hidden),
            wide(hidden),
            wide(wq),
            wide(wp),
            wide(cols),
            shape((bands, depth), F32),
            shape((depth, classes), F32),
            shape((cols,), F32),
            shape((2 * wp,), F32),
            shape((wp,), F32),
            shape((hidden,), F32),
            shape((wp,), F32),
        ],
        in_specs=[SMEM] + [ANY] * 11,
        out_specs=[ANY] * 14,
        scratch_shapes=[
            room(kept.shape, jnp.int32),
            room(dmod.shape, BF16),
            room(dcond.shape, F32),
            room(cvec.shape, BF16),
            room(sums.shape, F32),
            room(ids.shape, F32),
            room((bands, depth), F32),
            room((depth, classes), F32),
            room((cols,), F32),
            room((2 * wp,), F32),
            room((wp,), F32),
            room((hidden,), F32),
            room((wp,), F32),
            room(totals.shape, BF16),
            room(totals.shape, F32),
            room((cols, width), F32),
            room((2,) + y.shape, BF16),
            room((2,) + lat.shape, BF16),
            pltpu.SemaphoreType.DMA((count + 10,)),
            pltpu.SemaphoreType.DMA((count + 9 + -(-cols // 256),)),
        ],
        compiler_params=pltpu.CompilerParams(vmem_limit_bytes=63 * 2**20),
    )(counts, totals, y, dx, lat, cot, kept, dmod, dcond, cvec, sums, ids)


def plane_body(planes, latents, cotangent, bands, labels, kept, band_counts, time_table, class_table, w_ada, b_ada, w_qkv,
               qv_bias, w_proj, b_proj, w_fc1, b_fc1, w_fc2, b_fc2):
    samples, length, width = latents.shape
    wq = w_qkv.shape[1]
    wp = w_proj.shape[0]
    hidden = w_fc1.shape[1]

    totals, y, dx, unused_weights, dmod, dcond, cvec, sums, ids = run_block(
        samples, planes, labels, bands, band_counts, w_qkv.T, w_proj, w_fc1.T, w_fc2, w_ada.T, latents, cotangent,
        (b_proj, b_fc2, qv_bias, b_ada, b_fc1), kept, class_table.T, time_table
    )
    block_out, latents_grad, g1, g2, gq, gp, ada, time, classes, bada, qv, bp, b1, b2 = place_outputs(
        samples, planes, band_counts, totals, y, dx, latents, cotangent, kept, dmod, dcond, cvec, sums, ids, hidden, wq, wp,
        class_table.shape[0], time_table.shape[0]
    )
    return (block_out, latents_grad, time, classes.T, ada.T, bada, gq.T, qv, gp, bp, g1.T, b1, g2, b2)


def solution(mesh):
    planes = mesh.shape["dp"]
    small = mesh.shape["grp"] == 8 and planes == 4
    return jax.shard_map(
        functools.partial(plane_body, planes) if small else body,
        mesh=mesh,
        in_specs=(
            P(("grp", "dp"), None, None),
            P(("grp", "dp"), None, None),
            P(("grp", "dp")),
            P(("grp", "dp")),
            P(("grp", "dp"), None),
            P("grp"),
            P(None, "grp"),
            P(None, "grp"),
            P(None, "grp"),
            P("grp"),
            P(None, "grp"),
            P("grp"),
            P("grp", None),
            P("grp"),
            P(None, "grp"),
            P("grp"),
            P("grp", None),
            P("grp"),
        ),
        out_specs=(
            P(("grp", "dp"), None, None),
            P(("grp", "dp"), None, None),
            P(None, "grp"),
            P(None, "grp"),
            P(None, "grp"),
            P("grp"),
            P(None, "grp"),
            P("grp"),
            P("grp", None),
            P("grp"),
            P(None, "grp"),
            P("grp"),
            P("grp", None),
            P("grp"),
        ),
        check_vma=False,
    )
```

```python
import functools

import jax
import jax.numpy as jnp
from jax import lax
from jax.experimental import pallas as pl
from jax.experimental.pallas import tpu as pltpu
from jax.sharding import PartitionSpec as P

HEADS = 16
HEAD_DIM = 72


EPS = 1e-06
HIGH = lax.Precision.HIGHEST


def modulate(values, shift, scale):
    mean = jnp.mean(values, -1, keepdims=True)
    cent = values - mean
    var = jnp.mean(cent * cent, -1, keepdims=True)
    return cent * lax.rsqrt(var + EPS) * (1.0 + scale[:, None, :]) + shift[:, None, :]


def product(left, right):
    return jnp.einsum("btd,de->bte", left, right, preferred_element_type=jnp.float32)


def weight_term(left, right):
    return jnp.einsum("btd,bte->de", left, right, preferred_element_type=jnp.float32)


def core(weights, tokens, mod):
    w_qkv, qv_bias, w_proj, b_proj, w_fc1, b_fc1, w_fc2, b_fc2 = weights
    count, length, width = tokens.shape
    shift1, scale1, gate1, shift2, scale2, gate2 = jnp.split(mod, 6, -1)
    h1 = modulate(tokens, shift1, scale1).astype(jnp.bfloat16)
    bias = jnp.concatenate(
        [
            qv_bias[:width].astype(jnp.float32),
            jnp.zeros((width,), jnp.float32),
            qv_bias[width:].astype(jnp.float32),
        ]
    )
    qkv = (product(h1, w_qkv) + bias).astype(jnp.bfloat16)
    query = qkv[..., :width].reshape(count, length, HEADS, HEAD_DIM)
    keys = qkv[..., width : 2 * width].reshape(count, length, HEADS, HEAD_DIM)
    values = qkv[..., 2 * width :].reshape(count, length, HEADS, HEAD_DIM)
    scores = jnp.einsum(
        "bqhd,bkhd->bhqk", query, keys, preferred_element_type=jnp.float32
    ) * HEAD_DIM ** (-0.5)
    total = jax.scipy.special.logsumexp(scores, axis=-1, keepdims=True)
    probs_full = jnp.exp(scores - total)
    probs = probs_full.astype(jnp.bfloat16)
    att = (
        jnp.einsum("bhqk,bkhd->bqhd", probs, values, preferred_element_type=jnp.float32)
        .reshape(count, length, width)
        .astype(jnp.bfloat16)
    )
    proj = product(att, w_proj) + b_proj.astype(jnp.float32)
    mixed = tokens + gate1[:, None, :] * proj
    h2 = modulate(mixed, shift2, scale2).astype(jnp.bfloat16)
    pre = product(h2, w_fc1) + b_fc1.astype(jnp.float32)
    act = jax.nn.gelu(pre, approximate=True).astype(jnp.bfloat16)
    mlp = product(act, w_fc2) + b_fc2.astype(jnp.float32)
    result = mixed + gate2[:, None, :] * mlp
    saved = (h1, query, keys, values, probs_full, probs, att, proj, mixed, h2, pre, act, mlp)
    return (result, saved)


def body(
    latents,
    cotangent,
    bands,
    labels,
    kept,
    band_counts,
    time_table,
    class_table,
    w_ada,
    b_ada,
    w_qkv,
    qv_bias,
    w_proj,
    b_proj,
    w_fc1,
    b_fc1,
    w_fc2,
    b_fc2,
):
    gathered = (
        lax.all_gather(time_table, "grp", axis=1, tiled=True),
        lax.all_gather(class_table, "grp", axis=1, tiled=True),
        lax.all_gather(w_ada, "grp", axis=1, tiled=True),
        lax.all_gather(b_ada, "grp", axis=0, tiled=True),
        lax.all_gather(w_qkv, "grp", axis=1, tiled=True),
        lax.all_gather(qv_bias, "grp", axis=0, tiled=True),
        lax.all_gather(w_proj, "grp", axis=0, tiled=True),
        lax.all_gather(b_proj, "grp", axis=0, tiled=True),
        lax.all_gather(w_fc1, "grp", axis=1, tiled=True),
        lax.all_gather(b_fc1, "grp", axis=0, tiled=True),
        lax.all_gather(w_fc2, "grp", axis=0, tiled=True),
        lax.all_gather(b_fc2, "grp", axis=0, tiled=True),
    )
    time_full, class_full, ada_full, ada_bias = (gathered[0], gathered[1], gathered[2], gathered[3])
    samples = latents.shape[0]
    width = latents.shape[2]
    slot = lax.axis_index("dp") * samples + jnp.arange(samples, dtype=jnp.int32)
    group_count = band_counts[0]
    weight = jnp.where(slot < group_count, 1.0, 0.0).astype(jnp.float32) / group_count.astype(
        jnp.float32
    )
    band_hot = (bands[:, None] == jnp.arange(time_full.shape[0], dtype=jnp.int32)[None, :]).astype(
        jnp.float32
    )
    class_hot = (
        labels[:, None] == jnp.arange(class_full.shape[0], dtype=jnp.int32)[None, :]
    ).astype(jnp.float32)
    cond = jnp.dot(band_hot, time_full.astype(jnp.float32), precision=HIGH) + jnp.dot(
        class_hot, class_full.astype(jnp.float32), precision=HIGH
    )
    cvec = jax.nn.silu(cond).astype(jnp.bfloat16)
    mod = jnp.dot(cvec, ada_full, preferred_element_type=jnp.float32) + ada_bias.astype(jnp.float32)
    rows = jnp.arange(samples, dtype=jnp.int32)[:, None]
    tokens = jnp.take_along_axis(latents, kept[:, :, None], 1).astype(jnp.float32)
    result, unused = core(tuple(gathered[4:]), tokens, mod)
    block_out = latents.at[rows, kept].set(result.astype(jnp.bfloat16))
    fetched = (
        lax.all_gather(w_ada, "grp", axis=1, tiled=True),
        lax.all_gather(w_qkv, "grp", axis=1, tiled=True),
        lax.all_gather(qv_bias, "grp", axis=0, tiled=True),
        lax.all_gather(w_proj, "grp", axis=0, tiled=True),
        lax.all_gather(b_proj, "grp", axis=0, tiled=True),
        lax.all_gather(w_fc1, "grp", axis=1, tiled=True),
        lax.all_gather(b_fc1, "grp", axis=0, tiled=True),
        lax.all_gather(w_fc2, "grp", axis=0, tiled=True),
        lax.all_gather(b_fc2, "grp", axis=0, tiled=True),
    )
    ada_full = fetched[0]
    back = tuple(fetched[1:])
    qkv_full, unused_bias, proj_full, unused_pbias, fc1_full, unused_b1, fc2_full, unused_b2 = back
    result, saved = core(back, tokens, mod)
    h1, query, keys, values, probs_full, probs, att, proj, mixed, h2, pre, act, mlp = saved
    shift1, scale1, gate1, shift2, scale2, gate2 = jnp.split(mod, 6, -1)
    weighted = cotangent.astype(jnp.float32) * weight[:, None, None]
    grad_out = jnp.take_along_axis(weighted, kept[:, :, None], 1)
    grad_mlp = (gate2[:, None, :] * grad_out).astype(jnp.bfloat16)
    grad_gate2 = jnp.sum(grad_out * mlp, 1)
    fc2_grad = weight_term(act, grad_mlp)
    fc2_bias_grad = jnp.sum(grad_mlp.astype(jnp.float32), (0, 1))
    grad_act = jnp.einsum("bte,de->btd", grad_mlp, fc2_full, preferred_element_type=jnp.float32)
    unused_pre, gelu_back = jax.vjp(lambda value: jax.nn.gelu(value, approximate=True), pre)
    grad_pre = gelu_back(grad_act)[0].astype(jnp.bfloat16)
    fc1_grad = weight_term(h2, grad_pre)
    fc1_bias_grad = jnp.sum(grad_pre.astype(jnp.float32), (0, 1))
    grad_h2 = jnp.einsum("bte,de->btd", grad_pre, fc1_full, preferred_element_type=jnp.float32)
    unused_h2, norm_back = jax.vjp(modulate, mixed, shift2, scale2)
    grad_mixed, grad_shift2, grad_scale2 = norm_back(grad_h2)
    grad_mixed = grad_mixed + grad_out
    grad_proj = (gate1[:, None, :] * grad_mixed).astype(jnp.bfloat16)
    grad_gate1 = jnp.sum(grad_mixed * proj, 1)
    proj_grad = weight_term(att, grad_proj)
    proj_bias_grad = jnp.sum(grad_proj.astype(jnp.float32), (0, 1))
    grad_att = jnp.einsum(
        "bte,de->btd", grad_proj, proj_full, preferred_element_type=jnp.float32
    ).astype(jnp.bfloat16)
    grad_heads = grad_att.reshape(query.shape)
    grad_values = jnp.einsum(
        "bhqk,bqhd->bkhd", probs, grad_heads, preferred_element_type=jnp.float32
    )
    grad_probs = jnp.einsum(
        "bqhd,bkhd->bhqk", grad_heads, values, preferred_element_type=jnp.float32
    )
    grad_scores = probs_full * (grad_probs - jnp.sum(grad_probs * probs_full, -1, keepdims=True))
    grad_scores = grad_scores.astype(jnp.bfloat16)
    grad_query = jnp.einsum(
        "bhqk,bkhd->bqhd", grad_scores, keys, preferred_element_type=jnp.float32
    ) * HEAD_DIM ** (-0.5)
    grad_keys = jnp.einsum(
        "bhqk,bqhd->bkhd", grad_scores, query, preferred_element_type=jnp.float32
    ) * HEAD_DIM ** (-0.5)
    count, length = (tokens.shape[0], tokens.shape[1])
    grad_qkv = jnp.concatenate(
        [
            grad_query.reshape(count, length, width),
            grad_keys.reshape(count, length, width),
            grad_values.reshape(count, length, width),
        ],
        -1,
    ).astype(jnp.bfloat16)
    qkv_grad = weight_term(h1, grad_qkv)
    qkv_sums = jnp.sum(grad_qkv.astype(jnp.float32), (0, 1))
    qv_bias_grad = jnp.concatenate([qkv_sums[:width], qkv_sums[2 * width :]])
    grad_h1 = jnp.einsum("bte,de->btd", grad_qkv, qkv_full, preferred_element_type=jnp.float32)
    unused_h1, first_back = jax.vjp(modulate, tokens, shift1, scale1)
    grad_tokens, grad_shift1, grad_scale1 = first_back(grad_h1)
    grad_tokens = grad_tokens + grad_mixed
    latents_grad = weighted.at[rows, kept].set(grad_tokens).astype(jnp.bfloat16)
    grad_mod = jnp.concatenate(
        [grad_shift1, grad_scale1, grad_gate1, grad_shift2, grad_scale2, grad_gate2], -1
    ).astype(jnp.bfloat16)
    ada_grad = jnp.dot(cvec.T, grad_mod, preferred_element_type=jnp.float32)
    ada_bias_grad = jnp.sum(grad_mod.astype(jnp.float32), 0)
    grad_cvec = jnp.dot(grad_mod, ada_full.T, preferred_element_type=jnp.float32)
    unused_cond, silu_back = jax.vjp(jax.nn.silu, cond)
    grad_cond = silu_back(grad_cvec)[0]
    time_grad = jnp.dot(band_hot.T, grad_cond, precision=HIGH)
    class_grad = jnp.dot(class_hot.T, grad_cond, precision=HIGH)
    shares = (
        lax.psum_scatter(time_grad, "grp", scatter_dimension=1, tiled=True),
        lax.psum_scatter(class_grad, "grp", scatter_dimension=1, tiled=True),
        lax.psum_scatter(ada_grad, "grp", scatter_dimension=1, tiled=True),
        lax.psum_scatter(ada_bias_grad, "grp", scatter_dimension=0, tiled=True),
        lax.psum_scatter(qkv_grad, "grp", scatter_dimension=1, tiled=True),
        lax.psum_scatter(qv_bias_grad, "grp", scatter_dimension=0, tiled=True),
        lax.psum_scatter(proj_grad, "grp", scatter_dimension=0, tiled=True),
        lax.psum_scatter(proj_bias_grad, "grp", scatter_dimension=0, tiled=True),
        lax.psum_scatter(fc1_grad, "grp", scatter_dimension=1, tiled=True),
        lax.psum_scatter(fc1_bias_grad, "grp", scatter_dimension=0, tiled=True),
        lax.psum_scatter(fc2_grad, "grp", scatter_dimension=0, tiled=True),
        lax.psum_scatter(fc2_bias_grad, "grp", scatter_dimension=0, tiled=True),
    )
    totals = (
        lax.psum(shares[0].astype(jnp.bfloat16), "dp").astype(jnp.float32),
        lax.psum(shares[1].astype(jnp.bfloat16), "dp").astype(jnp.float32),
        lax.psum(shares[2].astype(jnp.bfloat16), "dp").astype(jnp.float32),
        lax.psum(shares[3].astype(jnp.bfloat16), "dp").astype(jnp.float32),
        lax.psum(shares[4].astype(jnp.bfloat16), "dp").astype(jnp.float32),
        lax.psum(shares[5].astype(jnp.bfloat16), "dp").astype(jnp.float32),
        lax.psum(shares[6].astype(jnp.bfloat16), "dp").astype(jnp.float32),
        lax.psum(shares[7].astype(jnp.bfloat16), "dp").astype(jnp.float32),
        lax.psum(shares[8].astype(jnp.bfloat16), "dp").astype(jnp.float32),
        lax.psum(shares[9].astype(jnp.bfloat16), "dp").astype(jnp.float32),
        lax.psum(shares[10].astype(jnp.bfloat16), "dp").astype(jnp.float32),
        lax.psum(shares[11].astype(jnp.bfloat16), "dp").astype(jnp.float32),
    )
    return (
        block_out,
        latents_grad,
        totals[0],
        totals[1],
        totals[2],
        totals[3],
        totals[4],
        totals[5],
        totals[6],
        totals[7],
        totals[8],
        totals[9],
        totals[10],
        totals[11],
    )


MESH = pl.DeviceIdType.MESH
F32 = jnp.float32
BF16 = jnp.bfloat16
GELU_A = 0.7978845608028654
GELU_B = 0.044715


def dot(left, right, dims):
    return lax.dot_general(left, right, ((dims[:1], dims[1:]), ((), ())), preferred_element_type=F32)


class Place:
    def __init__(self):
        self.g = lax.axis_index("grp")
        self.z = lax.axis_index("dp")
        self.c = self.g % 2
        self.x = (self.g // 2) % 2
        self.y = self.g // 4

    def block(self, dc, dx, dy):
        c = 1 - self.c if dc else self.c
        x = 1 - self.x if dx else self.x
        y = 1 - self.y if dy else self.y
        return y * 4 + x * 2 + c

    def device(self, dc, dx, dy):
        return (self.block(dc, dx, dy), self.z)


RELATIVE = [(r & 1, (r >> 1) & 1, r >> 2) for r in range(8)]


class Wire:
    def __init__(self, send, recv):
        self.send, self.recv, self.sends, self.recvs = send, recv, 0, 0

    def take(self, recvs, sends=1):
        first = (self.sends, self.recvs)
        self.sends += sends
        self.recvs += recvs
        return first

    def copy(self, send, recv, src, dst, device):
        return pltpu.make_async_remote_copy(
            src_ref=src,
            dst_ref=dst,
            send_sem=self.send.at[send],
            recv_sem=self.recv.at[recv],
            device_id=device,
            device_id_type=MESH,
        )


def halves(rows):
    cut = rows // 32 * 16
    return pl.ds(0, cut), pl.ds(cut, rows - cut)


def greet(devices):
    barrier = pltpu.get_barrier_semaphore()
    for device in devices:
        pl.semaphore_signal(barrier, inc=1, device_id=device, device_id_type=MESH)
    pl.semaphore_wait(barrier, len(devices))


def plane(place):
    return [place.device(*rel) for rel in RELATIVE[1:]]


class Gather:
    def __init__(self, place, wire, buf, start=0, rows=None, origin=None):
        p = place
        rows = rows or buf.shape[1]
        lo, hi = halves(rows)
        parts = (pl.ds(start, rows), pl.ds(start, lo.size), pl.ds(start + lo.size, hi.size))
        send, recv = wire.take(8)

        def make(number, block, device, part=0):
            ref = buf.at[block, parts[part]]
            src = origin if number < 3 and origin is not None else ref
            return wire.copy(send, recv + number, src, ref, device)

        own, xb, yb, db = p.g, p.block(0, 1, 0), p.block(0, 0, 1), p.block(0, 1, 1)
        xd, yd, sd = p.device(0, 1, 0), p.device(0, 0, 1), p.device(1, 0, 0)
        self.c = [
            make(0, own, xd),
            make(1, own, yd),
            make(2, own, sd),
            make(3, xb, yd, 1),
            make(4, xb, sd),
            make(5, yb, xd, 2),
            make(6, yb, sd),
            make(7, db, sd),
        ]
        seven = buf.at[pl.ds(0, 7), parts[0]]
        self.sent = wire.copy(send, recv, seven, seven, sd)

    def start(self):
        for number in (0, 1, 2):
            self.c[number].start()

    def arrived(self):
        self.c[0].wait_recv()
        self.c[1].wait_recv()
        self.c[4].start()
        self.c[6].start()

    def forward(self):
        self.c[3].start()
        self.c[5].start()

    def neighbours(self):
        self.arrived()
        self.forward()

    def far(self):
        self.c[3].wait_recv()
        self.c[5].wait_recv()
        self.c[7].start()

    def wait_sib(self):
        self.c[2].wait_recv()

    def wait_sib_neighbours(self):
        self.c[4].wait_recv()
        self.c[6].wait_recv()

    def wait_sib_far(self):
        self.c[7].wait_recv()

    def finish(self):
        self.sent.wait_send()


class Halves:
    def __init__(self, place, wire, buf):
        self.lo, self.hi = [Gather(place, wire, buf, part.start, part.size) for part in halves(buf.shape[1])]

    def start(self):
        for number in (0, 1, 2):
            self.lo.c[number].start()
        for number in (0, 1, 2):
            self.hi.c[number].start()

    def far(self):
        self.lo.far()
        self.hi.far()

    def wait_sib(self):
        self.lo.wait_sib()
        self.hi.wait_sib()

    def wait_sib_neighbours(self):
        self.lo.wait_sib_neighbours()
        self.hi.wait_sib_neighbours()

    def wait_sib_far(self):
        self.lo.wait_sib_far()
        self.hi.wait_sib_far()

    def finish(self):
        self.lo.finish()
        self.hi.finish()


class OverZ:
    def __init__(self, place, wire, buf, hbm, there, ahead, behind, rows):
        p = place
        near = [p.block(0, 1, 0), p.block(0, 0, 1), p.block(0, 1, 1)]
        sd = p.device(1, 0, 0)
        sem, recv = wire.take(7)
        send, take = pl.ds(ahead, rows), pl.ds(behind, rows)
        self.out = [wire.copy(sem, recv + i, buf.at[b, send], buf.at[b, send], there) for i, b in enumerate(near)]
        self.on = [wire.copy(sem, recv + 3 + i, buf.at[b, take], buf.at[b, take], sd) for i, b in enumerate(near)]
        self.own = wire.copy(sem, recv + 6, hbm.at[take], buf.at[p.g, take], sd)
        seven = buf.at[pl.ds(0, 7), send]
        self.sent = wire.copy(sem, recv, seven, seven, sd)

    def pass_on(self, *numbers):
        for i in numbers:
            self.out[i].wait_recv()
            self.on[i].start()

    def arrived(self, *numbers):
        for i in numbers:
            self.on[i].wait_recv()

    def finish(self):
        self.sent.wait_send()


class Scatter:
    def __init__(self, place, wire, buf, r1, r2, r3, rows=None):
        self.p, self.w, self.buf = place, wire, buf
        self.r1, self.r2, self.r3 = r1, r2, r3
        self.rows = rows = rows or buf.shape[1]
        p, w = place, wire
        self.sib = [p.block(1, q & 1, q >> 1) for q in range(4)]
        self.mine = [p.block(0, q & 1, q >> 1) for q in range(4)]
        xd, yd, sd = p.device(0, 1, 0), p.device(0, 0, 1), p.device(1, 0, 0)
        sem, recv = wire.take(15)
        whole = pl.ds(0, rows)
        lo, hi = halves(rows)
        self.parts = [[pl.ds(half.start + cut.start, cut.size) for cut in halves(half.size)] for half in (lo, hi)]
        self.s1 = [w.copy(sem, recv + q, buf.at[self.sib[q], whole], r1.at[q, whole], sd) for q in range(3)]
        self.far_sib = [w.copy(sem, recv + 3 + 11 * i, buf.at[self.sib[3], half], r1.at[3, half], sd) for i, half in enumerate((lo, hi))]
        self.lo_hi = (lo, hi)
        self.s2, self.s3 = [], []
        for way, device in ((0, xd), (1, yd)):
            for i, part in enumerate(self.parts[way]):
                number = recv + 4 + 2 * way + i
                self.s2.append(w.copy(sem, number, buf.at[self.mine[3], part], r2.at[way, pl.ds(part.start - self.parts[way][0].start, part.size)], device))
        for way, device in ((0, xd), (1, yd)):
            direct = (lo, hi)[way]
            for i, part in enumerate([direct] + self.parts[1 - way]):
                number = recv + 8 + 3 * way + i
                self.s3.append(w.copy(sem, number, buf.at[self.mine[1 + way], part], r3.at[way, part], device))
        seven = buf.at[pl.ds(0, 7), whole]
        self.sent = wire.copy(sem, recv, seven, seven, sd)

    def send_sib(self, q):
        for copy in self.far_sib if q == 3 else [self.s1[q]]:
            copy.start()

    def add_sib(self, q):
        if q == 3:
            for copy, half in zip(self.far_sib, self.lo_hi):
                copy.wait_recv()
                add_into(self.buf.at[self.mine[3], half], self.r1.at[3, half])
            return
        self.s1[q].wait_recv()
        add_into(self.buf.at[self.mine[q], pl.ds(0, self.rows)], self.r1.at[q, pl.ds(0, self.rows)])

    def send_far(self):
        self.add_sib(3)
        for number in (0, 2, 1, 3):
            self.s2[number].start()

    def send_near(self):
        self.add_sib(1)
        self.s3[0].start()
        self.add_sib(2)
        self.s3[3].start()

    def relay(self, i):
        for way in range(2):
            self.s2[2 * way + i].wait_recv()
            part = self.parts[way][i]
            came = self.r2.at[way, pl.ds(part.start - self.parts[way][0].start, part.size)]
            add_into(self.buf.at[self.mine[2 - way], part], came)
            self.s3[3 * (1 - way) + 1 + i].start()
        if i == 1:
            self.add_sib(0)

    def result(self, out):
        for copy in self.s3:
            copy.wait_recv()
        step = 16

        @pl.loop(0, self.rows // step)
        def _(i):
            at = pl.ds(pl.multiple_of(i * step, step), step)
            total = self.buf[self.mine[0], at].astype(F32) + self.r3[0, at].astype(F32) + self.r3[1, at].astype(F32)
            out[at] = total.astype(out.dtype)

    def finish(self):
        self.sent.wait_send()


def add_into(ref, other):
    step = 16

    @pl.loop(0, ref.shape[0] // step)
    def _(i):
        at = pl.ds(pl.multiple_of(i * step, step), step)
        ref[at] = (ref[at].astype(F32) + other[at].astype(F32)).astype(ref.dtype)


def scatter_scratch(rows, width):
    return [
        pltpu.VMEM((4, rows, width), BF16),
        pltpu.VMEM((2, halves(rows)[1].size, width), BF16),
        pltpu.VMEM((2, rows, width), BF16),
    ]


class Together:
    def __init__(self, wire, buf, pairs, device):
        send, recv = wire.take(1)
        count = len(pairs)
        for src, dst, target in pairs:
            wire.copy(send, recv, src, dst, target).start()
        all_blocks = buf.at[pl.ds(0, count)]
        self.all = wire.copy(send, recv, all_blocks, all_blocks, device)


def to_all(place, wire, buf, make):
    pairs = [(make(rel), buf.at[place.g], place.device(*rel)) for rel in RELATIVE[1:]]
    return Together(wire, buf, pairs, place.device(1, 0, 0))


def wait_recv(copies):
    copies.all.wait_recv()


def wait_send(copies):
    copies.all.wait_send()


def params(collective_id):
    return pltpu.CompilerParams(
        collective_id=collective_id, has_side_effects=True, vmem_limit_bytes=63 * 2**20
    )


VMEM = pl.BlockSpec(memory_space=pltpu.VMEM)

def gelu_parts(pre):
    square = pre * pre
    inner = jnp.tanh(GELU_A * pre * (1.0 + GELU_B * square))
    act = 0.5 * pre * (1.0 + inner)
    slope = 0.5 * (1.0 + inner) + 0.5 * pre * (1.0 - inner * inner) * (GELU_A * (1.0 + 3.0 * GELU_B * square))
    return act, slope


def local(src, dst, sem):
    return pltpu.make_async_copy(src, dst, sem)


def own_tokens(kept_ref, length, s):
    rows = lax.broadcasted_iota(jnp.int32, (length, kept_ref.shape[1]), 0)
    return jnp.where(rows == kept_ref[s : s + 1, :], 1.0, 0.0).astype(BF16)


def normed(v):
    cent = v - jnp.mean(v, -1, keepdims=True)
    inv = lax.rsqrt(jnp.mean(cent * cent, -1, keepdims=True) + EPS)
    return cent * inv, inv


def norm_back(grad, hat, inv):
    return inv * (grad - jnp.mean(grad, -1, keepdims=True) - hat * jnp.mean(grad * hat, -1, keepdims=True))


STEP = 32


def by_rows(samples, keep, fn):
    @pl.loop(0, samples * keep // STEP)
    def _(i):
        fn(lax.div(i, keep // STEP), pl.ds(pl.multiple_of(i * STEP, STEP), STEP))


SCALE = HEAD_DIM ** (-0.5)


def probabilities(q, k):
    scores = dot(k, q, (0, 0)) * SCALE
    exps = jnp.exp(scores - jnp.max(scores, 0, keepdims=True))
    return exps / jnp.sum(exps, 0, keepdims=True)


def arrival(p, t, last=7):
    dc = jnp.where((t == 1) | (t == 4) | (t == 5) | (t == last), 1, 0)
    dx = jnp.where((t == 2) | (t == 4) | (t >= 6), 1, 0)
    dy = jnp.where((t == 3) | (t >= 5), 1, 0)
    c, x, y = lax.rem(p.c + dc, 2), lax.rem(p.x + dx, 2), lax.rem(p.y + dy, 2)
    return y * 4 + x * 2 + c


def sample_weight(place, counts_ref, samples, s):
    count = jnp.full((1, 128), counts_ref[0], jnp.int32)
    used = count > place.z * samples + s
    return (jnp.where(used, 1.0, 0.0) / count.astype(F32))[:, 0:1]


ANY = pl.BlockSpec(memory_space=pltpu.HBM)
SMEM = pl.BlockSpec(memory_space=pltpu.SMEM)
PIECE = 48


def block_kernel(samples, planes, labels_ref, bands_ref, counts_ref, wq_hbm, wp_hbm, w1_hbm, w2_hbm, ada_hbm, lat_hbm, cot_hbm,
                 bp_ref, b2_ref, qv_ref, bada_ref, b1_ref, kept_ref, class_ref, time_ref,
                 out_hbm, y_hbm, dx_hbm, wq_keep, dmod_hbm, dcond_hbm, cvec_hbm, sum_hbm, ids_hbm,
                 dmod_z, dcond_z, cvec_z, sum_z, ids_z,
                 wq, wp, w1, w2, h1_all, h2_all, dm_all, act, dpre, p1, p2, p3, units, att, mixed, proj, grad, dx2, tmp, rest,
                 dproj, dq, dq_all, from_end, out, grads, gb1, ids_all, msg_all, cond_all, mod_in, mod_send, mod, vec,
                 dc_send, dc_in, bundle, share_send, share_in, send, recv, credits, sems):
    p = Place()
    wire = Wire(send, recv)
    g, z = p.g, p.z
    others = [(g, (z + k) % planes) for k in range(1, planes)]
    greet(plane(p) + others)
    length = lat_hbm.shape[1]
    keep = kept_ref.shape[1]
    rows, width = mixed.shape
    pair = 2 * HEAD_DIM
    hidden_units = act.shape[2]
    ada_rest = ada_hbm.shape[0] - hidden_units

    loads = {}
    for number, (name, src, dst) in enumerate((
        ("wq", wq_hbm, wq.at[g]),
        ("wp", wp_hbm, wp.at[g]),
        ("lat", lat_hbm, h2_all.at[pl.ds(0, samples)]),
        ("cot", cot_hbm, h2_all.at[pl.ds(samples, samples)]),
        ("ada1", ada_hbm.at[pl.ds(0, hidden_units)], w1),
        ("ada2", ada_hbm.at[pl.ds(hidden_units, ada_rest)], w2.at[pl.ds(0, ada_rest)]),
        ("w1", w1_hbm, w1),
        ("w2", w2_hbm, w2),
        ("keep", wq, wq_keep),
        ("again", wq_keep, wq),
        ("ada1b", ada_hbm.at[pl.ds(0, hidden_units)], w1),
        ("ada2b", ada_hbm.at[pl.ds(hidden_units, ada_rest)], w2.at[pl.ds(0, ada_rest)]),
        ("latb", lat_hbm, wq.at[pl.ds(0, samples), pl.ds(0, length)]),
        ("dx", dproj, dx_hbm),
        ("y", dproj, y_hbm),
        ("dmod", dmod_z, dmod_hbm),
        ("dcond", dcond_z, dcond_hbm),
        ("cvec", cvec_z, cvec_hbm),
        ("sum", sum_z, sum_hbm),
        ("ids", ids_z, ids_hbm),
    )):
        loads[name] = local(src, dst, sems.at[number])
    odd = z % 2
    there = (g, z + 1 - 2 * odd)
    gather_a = Gather(p, wire, wq, 2 * pair * odd, pair, wq_hbm.at[pl.ds(2 * pair * odd, pair)])
    gather_m = Gather(p, wire, wq, pair, pair, wq_hbm.at[pl.ds(pair, pair)])
    qkv_z = OverZ(p, wire, wq, wq_hbm, there, 2 * pair * odd, 2 * pair * (1 - odd), pair)
    inside = pair // 32 * 16 + 16
    beyond = pair - inside
    outward = Gather(p, wire, wp, beyond * odd, inside, wp_hbm.at[pl.ds(beyond * odd, inside)])
    proj_z = OverZ(p, wire, wp, wp_hbm, there, inside * odd, inside * (1 - odd), beyond)
    main = Halves(p, wire, h2_all)
    back = Halves(p, wire, dm_all)
    tokens = Gather(p, wire, h1_all)
    sums = Scatter(p, wire, wq, p1, p2, p3, rows)
    outs = Scatter(p, wire, h2_all, dm_all.at[pl.ds(0, 4)], dm_all.at[pl.ds(4, 2)], dm_all.at[pl.ds(6, 2)])
    projs = Scatter(p, wire, wp, p1, p2, p3)
    part_of = lambda start, size: grads.at[pl.ds(start, size)]
    g1, g2 = part_of(0, hidden_units), part_of(hidden_units, hidden_units)
    gq, gp = part_of(2 * hidden_units, 3 * pair), part_of(2 * hidden_units + 3 * pair, pair)
    count = grads.shape[0] // PIECE
    (up, up_r), (across, across_r), (down, down_r) = [wire.take(count) for way in range(3)]
    inner, outer, partner = 1 + z // 3, (z - 1) * 3, 3 - z
    at_end = (z == 0) | (z == planes - 1)
    rows_of = lambda ref, k: ref.at[pl.ds(pl.multiple_of(k * PIECE, 16), PIECE)]
    go_up = lambda k: wire.copy(up, up_r + k, rows_of(grads, k), rows_of(from_end, k), (g, inner))
    go_across = lambda k: wire.copy(across, across_r + k, rows_of(from_end, k), rows_of(out, k), (g, partner))
    go_down = lambda k: wire.copy(down, down_r + k, rows_of(out, k), rows_of(out, k), (g, outer))
    to_hbm = lambda k: local(rows_of(out, k), rows_of(out_hbm, k), sems.at[20])

    def chain_send(first, last):
        @pl.when(at_end)
        def _():
            for k in range(first, last):
                go_up(k).start()

    def chain_up(k):
        @pl.when(jnp.logical_not(at_end))
        def _():
            go_up(k).wait_recv()
            add_into(rows_of(from_end, k), rows_of(grads, k))
            go_across(k).start()

    def chain_down(k):
        @pl.when(jnp.logical_not(at_end))
        def _():
            go_across(k).wait_recv()
            add_into(rows_of(out, k), rows_of(from_end, k))
            go_down(k).start()
            to_hbm(k).start()

    def chain(k, lag):
        chain_up(k)
        chain_down(k - lag)

    def to_planes(ref):
        return Together(wire, ref, [(ref.at[z], ref.at[z], device) for device in others], others[0])

    neighbours = [p.device(1, 0, 0), p.device(0, 1, 0), p.device(0, 0, 1)]

    def grant(number):
        for i, device in enumerate(neighbours):
            pl.semaphore_signal(credits.at[number, i], inc=1, device_id=device, device_id_type=MESH)

    def granted(number):
        for i in range(3):
            pl.semaphore_wait(credits.at[number, i], 1)

    lanes = lax.broadcasted_iota(jnp.int32, (1, 128), 1)
    for s in range(samples):
        line = jnp.where(lanes == 0, labels_ref[s], 0) + jnp.where(lanes == 1, bands_ref[s], 0)
        ids_all[g, s : s + 1, :] = line.astype(F32)
    line_of = lambda ref: ref[...].astype(F32).reshape(1, ref.shape[0])
    b_ada, b1, qv = line_of(bada_ref), line_of(b1_ref), line_of(qv_ref)
    for row, line in enumerate((line_of(bp_ref), line_of(b2_ref), qv[:, :pair], qv[:, pair:])):
        msg_all[g, row : row + 1, :] = line
    idc = to_all(p, wire, ids_all, lambda rel: ids_all.at[g])
    gather_a.start()
    msgs = to_all(p, wire, msg_all, lambda rel: msg_all.at[g])
    for name in ("lat", "cot", "ada1", "ada2", "wq", "wp"):
        loads[name].start()

    wait_recv(idc)
    labels = jnp.concatenate([ids_all[j, 0:samples, 0:1] for j in range(8)], 0)
    bands = jnp.concatenate([ids_all[j, 0:samples, 1:2] for j in range(8)], 0)

    def one_hot(ids, size):
        lanes = lax.broadcasted_iota(jnp.int32, (ids.shape[0], size), 1).astype(F32)
        return jnp.where(lanes == ids, 1.0, 0.0).astype(BF16)

    of_band = dot(one_hot(bands, time_ref.shape[0]), time_ref[...], (1, 0))
    cond_all[g] = of_band + dot(one_hot(labels, class_ref.shape[1]), class_ref[...], (1, 1))
    conds = to_all(p, wire, cond_all, lambda rel: cond_all.at[g])
    ids_z[z] = jnp.zeros(ids_z.shape[1:], F32)
    ids_z[z, :, 0:1] = labels
    ids_z[z, :, 1:2] = bands


    loads["lat"].wait()
    loads["cot"].wait()
    for s in range(samples):
        hot = own_tokens(kept_ref, length, s)
        at = pl.ds(s * keep, keep)
        mixed[at] = dot(hot, h2_all[s], (0, 0))
        grad[at] = dot(hot, h2_all[samples + s], (0, 0)) * sample_weight(p, counts_ref, samples, s)

    gather_a.neighbours()
    qkv_z.out[0].start()
    qkv_z.out[1].start()
    wait_recv(conds)
    value = jnp.concatenate([cond_all[j] for j in range(8)], 1)
    value = (value * jax.nn.sigmoid(value)).astype(BF16)
    cvec_z[z] = value
    loads["ada1"].wait()
    loads["ada2"].wait()
    mods = [dot(value, w1[...], (1, 1)), dot(value, w2[0:ada_rest], (1, 1))]
    mods = jnp.concatenate(mods, 1) + b_ada
    for j in range(8):
        mod_send[j] = mods[samples * j : samples * (j + 1), :]
    mod_in[g] = mod_send[g]
    modc = to_all(p, wire, mod_in, lambda rel: mod_send.at[p.block(*rel)])
    gather_m.start()
    qkv_z.own.start()
    loads["w1"].start()
    loads["w2"].start()
    outward.start()
    proj_z.own.start()
    gather_a.far()
    qkv_z.out[2].start()
    wait_recv(modc)
    mod[...] = jnp.zeros_like(mod)
    for s in range(samples):
        line = jnp.concatenate([mod_in[j, s : s + 1, :] for j in range(8)], 1)
        for v in range(6):
            mod[s, v : v + 1, :] = line[:, v * width : (v + 1) * width]

    def first_norm(s, at):
        hat, inv = normed(mixed[at])
        h1_all[g, at] = (hat * (1.0 + mod[s, 1:2, :]) + mod[s, 0:1, :]).astype(BF16)
        dm_all[g, at] = (mod[s, 5:6, :] * grad[at]).astype(BF16)

    by_rows(samples, keep, first_norm)
    wait_recv(msgs)
    vec[...] = jnp.zeros_like(vec)
    for row in range(2):
        vec[row : row + 1, :] = jnp.concatenate([msg_all[j, row : row + 1, :] for j in range(8)], 1)

    ones = jnp.ones((8, rows), BF16)
    loads["wq"].wait()

    @pl.loop(0, 24)
    def _(n):
        @pl.when(n == 1)
        def _():
            gather_a.wait_sib()

        @pl.when(n == 4)
        def _():
            gather_a.wait_sib_neighbours()

        @pl.when(n == 7)
        def _():
            gather_a.wait_sib_far()

        @pl.when(n == 9)
        def _():
            gather_m.wait_sib()

        @pl.when(n == 8)
        def _():
            gather_m.neighbours()

        @pl.when(n == 12)
        def _():
            gather_m.wait_sib_neighbours()

        @pl.when(n == 14)
        def _():
            outward.neighbours()
            proj_z.out[0].start()
            proj_z.out[1].start()
            back.start()

        @pl.when(n == 15)
        def _():
            qkv_z.own.wait_recv()
            qkv_z.pass_on(0, 1)

        @pl.when(n == 18)
        def _():
            qkv_z.arrived(0, 1)
            gather_m.far()

        @pl.when(n == 20)
        def _():
            qkv_z.pass_on(2)

        @pl.when(n == 21)
        def _():
            gather_m.wait_sib_far()

        @pl.when(n == 22)
        def _():
            outward.far()
            proj_z.out[2].start()

        @pl.when(n == 23)
        def _():
            qkv_z.arrived(2)

        phase = jnp.where(n < 8, 0, jnp.where((n < 14) | (n == 20) | (n == 21), 1, 2))
        turn = jnp.where(n < 8, n, jnp.where(n < 14, n - 8, jnp.where(n < 20, n - 14, jnp.where(n < 22, n - 14, n - 16))))
        block = arrival(p, turn)
        third = jnp.where(phase == 0, 2 * odd, jnp.where(phase == 1, 1, 2 - 2 * odd))
        chunk = block * 3 + third
        bias_at = jnp.where(chunk >= 16, chunk - 8, chunk)
        keys = (chunk >= 8) & (chunk < 16)
        line = msg_all[lax.div(bias_at, 2), pl.ds(2 + lax.rem(bias_at, 2), 1), :] * jnp.where(keys, 0.0, 1.0)
        line = jnp.concatenate([line, jnp.zeros((7, pair), F32)], 0)
        value = dot(wq[block, pl.ds(pl.multiple_of(third * pair, 16), pair), :], h1_all[g], (1, 1))
        value = value + dot(line.astype(BF16), ones, (0, 0))
        units[2 * chunk] = value[:HEAD_DIM].astype(BF16)
        units[2 * chunk + 1] = value[HEAD_DIM:].astype(BF16)

    loads["keep"].start()
    zs = [to_planes(ids_z), to_planes(cvec_z)]

    @pl.loop(0, 4)
    def _(i):
        for u in (2 * i, 2 * i + 1):
            for s in range(samples):
                lanes = pl.ds(s * keep, keep)
                pieces = []
                for e in range(2):
                    probs = probabilities(units[2 * u + e, :, lanes], units[16 + 2 * u + e, :, lanes])
                    pieces.append(dot(units[32 + 2 * u + e, :, lanes], probs.astype(BF16), (1, 0)))
                att[u, :, lanes] = jnp.concatenate(pieces, 0).astype(BF16)

    back.lo.neighbours()
    loads["wp"].wait()
    outward.wait_sib()
    outward.wait_sib_neighbours()
    outward.wait_sib_far()
    proj_z.own.wait_recv()
    proj_z.pass_on(0, 1, 2)
    back.hi.neighbours()
    proj_z.arrived(0, 1, 2)
    proj[...] = jnp.zeros_like(proj)

    @pl.loop(0, 8)
    def _(u):
        proj[...] += dot(att[u], wp[u], (0, 0))

    def second_norm(s, at):
        proj[at] = proj[at] + vec[0:1, :]
        mixed[at] = mixed[at] + mod[s, 2:3, :] * proj[at]
        hat, inv = normed(mixed[at])
        h2_all[g, at] = (hat * (1.0 + mod[s, 4:5, :]) + mod[s, 3:4, :]).astype(BF16)

    by_rows(samples, keep, second_norm)
    main.start()
    back.far()
    gb1[...] = jnp.zeros_like(gb1)
    for piece in (gather_a, gather_m, qkv_z):
        piece.finish()
    loads["w1"].wait()
    loads["w2"].wait()
    loads["keep"].wait()

    half_rows = rows // 2

    def hidden(places):
        both = lambda ref: jnp.concatenate([ref[block, at] for block, at in places], 0)
        pre = dot(both(h2_all), w1[...], (1, 1)) + b1
        value, slope = gelu_parts(pre)
        value = value.astype(BF16)
        low = (dot(both(dm_all), w2[...], (1, 1)) * slope).astype(BF16)
        gb1[...] += jnp.sum(low.astype(F32), 0, keepdims=True)
        share = dot(low, w1[...], (1, 0)).astype(BF16)
        for i, (block, at) in enumerate(places):
            part = slice(i * half_rows, (i + 1) * half_rows)
            act[block, at] = value[part]
            dpre[block, at] = low[part]
            wq[block, at] = share[part]

    @pl.loop(0, 8)
    def _(n):
        @pl.when(n == 1)
        def _():
            main.wait_sib()
            back.wait_sib()

        @pl.when(n == 2)
        def _():
            main.lo.neighbours()
            back.wait_sib_neighbours()
            back.wait_sib_far()

        @pl.when(n == 3)
        def _():
            main.lo.wait_sib_neighbours()

        @pl.when(n == 4)
        def _():
            main.hi.neighbours()

        @pl.when(n == 5)
        def _():
            main.hi.wait_sib_neighbours()

        @pl.when(n == 6)
        def _():
            main.lo.far()
            sums.send_near()
            main.lo.wait_sib_far()

        @pl.when(n == 7)
        def _():
            main.hi.far()
            main.hi.wait_sib_far()

        upper = (n == 4) | (n == 5) | (n == 7)
        turn = jnp.where(n < 2, n, jnp.where(n < 6, 2 + 2 * lax.rem(n, 2), 6))
        halves_at = (jnp.where(upper, 1, 0), jnp.where(upper | (n < 2), 1, 0))
        turns = (turn, jnp.where(n < 2, turn, turn + 1))
        hidden([(arrival(p, t, 6), pl.ds(pl.multiple_of(h * half_rows, 16), half_rows)) for t, h in zip(turns, halves_at)])

        @pl.when(n == 1)
        def _():
            sums.send_sib(0)

        @pl.when(n == 5)
        def _():
            sums.send_sib(1)
            sums.send_sib(2)

        @pl.when(n == 6)
        def _():
            sums.far_sib[0].start()

        @pl.when(n == 7)
        def _():
            sums.far_sib[1].start()

    sums.send_far()

    def weight_grad(left, right, base, between):
        for n, (start, size) in enumerate(((0, 128), (128, 256), (384, hidden_units - 384))):
            part = left[:, :, pl.ds(start, size)].reshape(8 * rows, size)
            grads[base + start : base + start + size] = dot(part, right[...].reshape(8 * rows, width), (0, 0)).astype(BF16)
            chain_send(-(-base // PIECE) if n == 0 else (base + start) // PIECE, (base + start + size) // PIECE)
            between(n)

    def output_blocks(first, last):
        @pl.loop(first, last)
        def _(block):
            h2_all[block] = jnp.dot(act[block], w2[...], preferred_element_type=F32).astype(BF16)

    def visit(n):
        if n == 0:
            chain_up(0)
            sums.relay(0)
        elif n == 1:
            chain_up(1)
            sums.relay(1)
            tokens.start()
            chain_up(2)
            chain_down(0)

    weight_grad(dpre, h2_all, 0, lambda n: None)
    weight_grad(act, dm_all, hidden_units, visit)
    main.finish()
    chain_up(3)
    chain_down(1)
    output_blocks(0, 3)
    chain_up(4)
    chain_down(2)
    back.finish()
    grant(0)
    sums.result(tmp)
    sums.finish()
    grant(1)
    loads["again"].start()

    bundle[...] = jnp.zeros_like(bundle)

    def add_row(row, value):
        bundle[pl.ds(row, 1), :] += jnp.sum(value, 0, keepdims=True)

    SUM_PROJ, SUM_FC2 = 6 * samples, 6 * samples + 1

    def second_back(s, at):
        @pl.when(at.start == rows // 2)
        def _():
            chain_up(5)
            chain_down(3)

        hat, inv = normed(mixed[at])
        up_grad = tmp[at]
        value = grad[at] + norm_back(up_grad * (1.0 + mod[s, 4:5, :]), hat, inv)
        dx2[at] = value
        low = (mod[s, 2:3, :] * value).astype(BF16)
        dproj[at] = low
        add_row(s * 6 + 3, up_grad)
        add_row(s * 6 + 4, up_grad * hat)
        add_row(s * 6 + 2, value * proj[at])
        add_row(SUM_PROJ, low.astype(F32))
        add_row(SUM_FC2, (mod[s, 5:6, :] * grad[at]).astype(BF16).astype(F32))

    by_rows(samples, keep, second_back)
    chain_down(4)
    outward.finish()
    proj_z.finish()

    def heads_back(u):
        datt = dot(wp[u], dproj[...], (1, 1))
        wp[u] = dot(att[u], dproj[...], (1, 0)).astype(BF16)
        lists = ([], [], [])
        for s in range(samples):
            lanes = pl.ds(s * keep, keep)
            parts = ([], [], [])
            for e in range(2):
                q, k, v = (units[16 * i + 2 * u + e, :, lanes] for i in range(3))
                da = datt[e * HEAD_DIM : (e + 1) * HEAD_DIM, s * keep : (s + 1) * keep].astype(BF16)
                probs = probabilities(q, k)
                dprobs = dot(v, da, (0, 0))
                dscores = probs * (dprobs - jnp.sum(dprobs * probs, 0, keepdims=True))
                dscores = dscores.astype(BF16)
                parts[0].append(dot(k, dscores, (1, 0)) * SCALE)
                parts[1].append(dot(q, dscores, (1, 1)) * SCALE)
                parts[2].append(dot(da, probs.astype(BF16), (1, 1)))
            for i in range(3):
                lists[i].append(jnp.concatenate(parts[i], 0).astype(BF16))
        for i in range(3):
            chunk = 8 * i + u
            at = pl.ds(pl.multiple_of(lax.rem(chunk, 3) * pair, 16), pair)
            for s in range(samples):
                dq[lax.div(chunk, 3), at, pl.ds(s * keep, keep)] = lists[i][s]

    visits = {
        (0, 0): ((6,), ()),
        (0, 1): ((7,), (5,)),
        (1, 1): ((8,), (6,)),
        (2, 0): ((9,), (7,)),
        (2, 1): ((10,), ()),
        (3, 0): ((), (8,)),
        (3, 1): ((11,), (9,)),
    }

    @pl.loop(0, 4)
    def _(i):
        for e in range(2):
            heads_back(2 * i + e)
            if e == 0:

                @pl.when(i == 2)
                def _():
                    tokens.neighbours()

            for (at, half), (ups, downs) in visits.items():
                if half == e:

                    @pl.when(i == at)
                    def _(ups=ups, downs=downs):
                        for k in ups:
                            chain_up(k)
                        for k in downs:
                            chain_down(k)

    dq_all[g] = dq[g]
    moves = to_all(p, wire, dq_all, lambda rel: dq.at[p.block(*rel)])
    granted(1)
    for q in (3, 1, 2, 0):
        projs.send_sib(q)

    loads["again"].wait()
    proj[...] = jnp.zeros_like(proj)

    @pl.loop(0, 8)
    def _(j):
        proj[...] += dot(dq[j], wq[j], (0, 0))
        for at, step, k in ((1, chain_up, 12), (3, chain_down, 10), (6, chain_up, 13)):

            @pl.when(j == at)
            def _(step=step, k=k):
                step(k)

    loads["latb"].start()

    chain_down(11)
    granted(0)
    output_blocks(3, 6)
    chain(14, 2)
    output_blocks(6, 8)
    for q in (3, 1, 2, 0):
        outs.send_sib(q)
    loads["ada1b"].start()
    loads["ada2b"].start()
    for k in range(15, 18):
        chain(k, 2)
    tokens.far()
    for k in range(18, 22):
        chain(k, 2)
    tokens.wait_sib()
    tokens.wait_sib_neighbours()
    tokens.wait_sib_far()

    wait_recv(moves)
    projs.send_far()
    projs.send_near()
    outs.send_far()
    chain(22, 2)
    for i in range(3):
        at = pl.ds(i * pair, pair)
        tmp[0:pair] = jnp.zeros((pair, width), F32)

        @pl.loop(0, 8)
        def _(j, at=at):
            tmp[0:pair] += dot(dq_all[j, at, :], h1_all[j], (1, 0))

        gq[at] = tmp[0:pair].astype(BF16)
        chain_send(24 + 3 * i, 27 + 3 * i)
        if i == 0:
            chain(23, 2)
            projs.relay(0)
            projs.relay(1)
            outs.send_near()
            chain(24, 2)
        elif i == 1:
            chain(25, 2)
            chain(26, 2)
        else:
            chain(27, 2)
            outs.relay(0)
            outs.relay(1)

    loads["latb"].wait()
    for s in range(samples):
        hot = own_tokens(kept_ref, length, s)
        tmp[pl.ds(s * keep, keep)] = dot(hot, wq[s, pl.ds(0, length)], (0, 0))

    def first_back(s, at):
        @pl.when(at.start == rows // 2)
        def _():
            chain(28, 2)

        hat, inv = normed(tmp[at])
        up_grad = proj[at]
        dx = dx2[at] + norm_back(up_grad * (1.0 + mod[s, 1:2, :]), hat, inv)
        add_row(s * 6, up_grad)
        add_row(s * 6 + 1, up_grad * hat)
        dproj[at] = dx.astype(BF16)

    by_rows(samples, keep, first_back)
    loads["dx"].start()
    chain(29, 2)
    chain(30, 2)
    chain(31, 2)
    projs.result(gp)
    chain_send(33, 36)
    for k in range(32, 35):
        chain(k, 2)
    outs.result(tmp)

    def end(s, at):
        value = tmp[at] + vec[1:2, :]
        add_row(s * 6 + 5, grad[at] * value)
        dproj[at] = (mixed[at] + mod[s, 5:6, :] * value).astype(BF16)

    loads["dx"].wait()
    by_rows(samples, keep, end)
    loads["y"].start()

    cols = ada_hbm.shape[0]
    wait_send(modc)
    for s in range(samples):
        line = jnp.concatenate([bundle[s * 6 + v : s * 6 + v + 1, :] for v in range(6)], 1)
        for j in range(8):
            mod_send[j, s : s + 1, :] = line[:, j * cols : (j + 1) * cols].astype(BF16).astype(F32)
    mod_in[g] = mod_send[g]
    dmods = to_all(p, wire, mod_in, lambda rel: mod_send.at[p.block(*rel)])
    lines = [dot(ones, dq[j], (1, 1))[0:1, :] for j in range(8)]
    for j in range(8):
        for row, at in ((0, SUM_PROJ), (1, SUM_FC2)):
            share_send[j, row : row + 1, :] = bundle[at : at + 1, j * pair : (j + 1) * pair]
        for e in range(2):
            u = 2 * j + e + (8 if j >= 4 else 0)
            share_send[j, 2 + e : 3 + e, :] = lines[u // 3][:, u % 3 * pair : (u % 3 + 1) * pair]
    share_in[g] = share_send[g]
    small = to_all(p, wire, share_in, lambda rel: share_send.at[p.block(*rel)])
    chain(35, 2)
    loads["ada1b"].wait()
    loads["ada2b"].wait()
    wait_recv(dmods)
    part = jnp.concatenate([mod_in[j] for j in range(8)], 0).astype(BF16)
    dmod_z[z] = part
    zs.append(to_planes(dmod_z))
    dcvec = dot(part[:, :hidden_units], w1[...], (1, 0)) + dot(part[:, hidden_units:], w2[0:ada_rest], (1, 0))
    depth = cond_all.shape[2]
    for j in range(8):
        dc_send[j] = dcvec[:, j * depth : (j + 1) * depth]
    dc_in[g] = dc_send[g]
    dcs = to_all(p, wire, dc_in, lambda rel: dc_send.at[p.block(*rel)])
    chain_down(34)
    wait_recv(small)
    sum_z[z, 0:4, :] = sum(share_in[j] for j in range(8))
    for i in range(hidden_units // pair):
        sum_z[z, 4 + i : 5 + i, :] = gb1[:, i * pair : (i + 1) * pair]
    zs.append(to_planes(sum_z))
    chain_down(35)
    wait_recv(dcs)
    cond = cond_all[g]
    gate = jax.nn.sigmoid(cond)
    dcond_z[z] = sum(dc_in[j] for j in range(8)) * (gate * (1.0 + cond * (1.0 - gate)))
    zs.append(to_planes(dcond_z))

    whole = lambda sem, ref: wire.copy(sem, up_r, ref, ref, (g, partner))

    @pl.when(jnp.logical_not(at_end))
    def _():
        whole(across, out).wait_send()
        whole(down, out).wait_send()

    @pl.when(at_end)
    def _():
        @pl.loop(0, count)
        def _(k):
            go_down(k).wait_recv()
            to_hbm(k).start()

        whole(up, out).wait_send()

    local(out, out_hbm, sems.at[20]).wait()
    for copies in zs:
        wait_recv(copies)
    for name in ("ids", "cvec", "dmod", "sum", "dcond"):
        loads[name].start()
    for copies in zs:
        wait_send(copies)
    for copies in (idc, msgs, conds, moves, dmods, small, dcs):
        wait_send(copies)
    for piece in (tokens, projs, outs):
        piece.finish()
    for name in ("y", "ids", "cvec", "dmod", "sum", "dcond"):
        loads[name].wait()


def run_block(samples, planes, labels, bands, counts, wq, wp, w1, w2, w_ada, lat, cot, biases, kept, class_table, time_table):
    keep, width = kept.shape[1], wq.shape[1]
    rows, hidden, per = samples * keep, w1.shape[0], 8 * samples
    cols, depth = w_ada.shape[0], class_table.shape[0]
    total = 2 * hidden + wq.shape[0] + wp.shape[0]
    count = total // PIECE
    shape, room = jax.ShapeDtypeStruct, pltpu.VMEM
    blocks = room((8, rows, width), BF16)
    plain = room((rows, width), F32)
    over_z = [
        ((planes, per, cols), BF16),
        ((planes, per, depth), F32),
        ((planes, per, width), BF16),
        ((planes, 4 + hidden // depth, depth), F32),
        ((planes, per, 128), F32),
    ]
    sends, recvs = 8 + 2 + 3 + 3 + 8 + 5, 8 * 8 + 2 * 7 + 3 * 15 + 3 * count + 8 + 5
    return pl.pallas_call(
        functools.partial(block_kernel, samples, planes),
        out_shape=[
            shape((total, width), BF16),
            shape((rows, width), BF16),
            shape((rows, width), BF16),
            shape((8,) + wq.shape, BF16),
            *[shape(dims, kind) for dims, kind in over_z],
        ],
        in_specs=[SMEM] * 3 + [ANY] * 7 + [VMEM] * 8,
        out_specs=[ANY] * 9,
        scratch_shapes=[
            *[room(dims, kind) for dims, kind in over_z],
            room((8,) + wq.shape, BF16),
            room((8,) + wp.shape, BF16),
            room(w1.shape, BF16),
            room(w2.shape, BF16),
            blocks,
            blocks,
            blocks,
            room((8, rows, hidden), BF16),
            room((8, rows, hidden), BF16),
            *scatter_scratch(rows, width),
            room((48, HEAD_DIM, rows), BF16),
            room((8, 2 * HEAD_DIM, rows), BF16),
            plain,
            plain,
            plain,
            plain,
            plain,
            room((hidden - 512, width), F32),
            room((rows, width), BF16),
            room((8, wq.shape[0], rows), BF16),
            room((8, wq.shape[0], rows), BF16),
            room((total, width), BF16),
            room((total, width), BF16),
            room((total, width), BF16),
            room((1, hidden), F32),
            room((8, samples, 128), F32),
            room((8, 4, wp.shape[0]), F32),
            room((8, per, depth), F32),
            room((8, samples, cols), F32),
            room((8, samples, cols), F32),
            room((samples, 8, width), F32),
            room((8, width), F32),
            room((8, per, depth), F32),
            room((8, per, depth), F32),
            room((16, width), F32),
            room((8, 4, wp.shape[0]), F32),
            room((8, 4, wp.shape[0]), F32),
            pltpu.SemaphoreType.DMA((sends,)),
            pltpu.SemaphoreType.DMA((recvs,)),
            pltpu.SemaphoreType.REGULAR((2, 3)),
            pltpu.SemaphoreType.DMA((21,)),
        ],
        compiler_params=params(1),
    )(labels, bands, counts, wq, wp, w1, w2, w_ada, lat, cot, *biases, kept, class_table, time_table)


def outputs_kernel(samples, planes, counts_ref, totals_hbm, y_hbm, dx_hbm, lat_hbm, cot_hbm, kept_hbm, dmod_hbm, dcond_hbm,
                   cvec_hbm, sum_hbm, ids_hbm,
                   block_hbm, latg_hbm, g1_hbm, g2_hbm, gq_hbm, gp_hbm, ada_hbm, time_hbm, class_hbm, bada_hbm, qv_hbm, bp_hbm,
                   b1_hbm, b2_hbm,
                   kept_ref, dmod_ref, dcond_ref, cvec_ref, sum_ref, ids_ref, time_out, class_out, bada_out, qv_out, bp_out,
                   b1_out, b2_out, totals, wide, ada, tokens, both, sems_in, sems):
    p = Place()
    length = lat_hbm.shape[1]
    keep = kept_ref.shape[1]
    chunk = 144
    count, width = totals.shape[0] // chunk, totals.shape[1]
    per = 8 * samples
    chunks = [pl.ds(k * chunk, chunk) for k in range(count)]
    ins = [local(totals_hbm.at[at], totals.at[at], sems_in.at[k]) for k, at in enumerate(chunks)]
    ins += [
        local(y_hbm, tokens.at[0], sems_in.at[count]),
        local(dx_hbm, tokens.at[1], sems_in.at[count + 1]),
        local(lat_hbm, both.at[0], sems_in.at[count + 2]),
        local(cot_hbm, both.at[1], sems_in.at[count + 3]),
    ]
    pairs = ((dmod_hbm, dmod_ref), (cvec_hbm, cvec_ref), (kept_hbm, kept_ref), (dcond_hbm, dcond_ref), (sum_hbm, sum_ref), (ids_hbm, ids_ref))
    small = [local(src, dst, sems_in.at[count + 4 + i]) for i, (src, dst) in enumerate(pairs)]
    for copy in small + ins[count:] + ins[:count]:
        copy.start()
    done = []

    def send(src, dst):
        done.append(local(src, dst, sems.at[len(done)]))
        done[-1].start()

    for copy in small:
        copy.wait()
    cvec = jnp.concatenate([cvec_ref[k] for k in range(planes)], 0)
    dmod = jnp.concatenate([dmod_ref[k] for k in range(planes)], 0)
    cols = ada.shape[0]
    for start in range(0, cols, 256):
        size = min(256, cols - start)
        ada[start : start + size] = dot(dmod[:, start : start + size], cvec, (0, 0))
        send(ada.at[pl.ds(start, size)], ada_hbm.at[pl.ds(start, size)])
    bada_out[...] = jnp.sum(dmod.astype(F32), 0)
    send(bada_out, bada_hbm)

    for copy in ins[count:]:
        copy.wait()
    for s in range(samples):
        hot = own_tokens(kept_ref, length, s)
        is_kept = jnp.sum(hot.astype(F32), 1, keepdims=True) > 0.5
        at = pl.ds(s * keep, keep)
        both[0, s] = jnp.where(is_kept, dot(hot, tokens[0, at], (1, 0)), both[0, s].astype(F32)).astype(BF16)
        weighted = both[1, s].astype(F32) * sample_weight(p, counts_ref, samples, s)
        both[1, s] = jnp.where(is_kept, dot(hot, tokens[1, at], (1, 0)), weighted).astype(BF16)
    send(both.at[0], block_hbm)
    send(both.at[1], latg_hbm)

    k = 0
    for out in (g1_hbm, g2_hbm, gq_hbm, gp_hbm):
        for start in range(0, out.shape[0], chunk):
            ins[k].wait()
            wide[chunks[k]] = totals[chunks[k]].astype(F32)
            send(wide.at[chunks[k]], out.at[pl.ds(start, chunk)])
            k += 1

    dcond = jnp.concatenate([dcond_ref[k] for k in range(planes)], 0)
    ids = jnp.concatenate([ids_ref[k] for k in range(planes)], 0)

    def one_hot(column, size):
        lanes = lax.broadcasted_iota(jnp.int32, (planes * per, size), 1).astype(F32)
        return jnp.where(lanes == ids[:, column : column + 1], 1.0, 0.0)

    def exact(left, right):
        return lax.dot_general(left, right, (((0,), (0,)), ((), ())), precision=HIGH, preferred_element_type=F32)

    time_out[...] = exact(one_hot(1, time_out.shape[0]), dcond)
    send(time_out, time_hbm)
    class_out[...] = exact(dcond, one_hot(0, class_out.shape[1]))
    send(class_out, class_hbm)
    sums = sum(sum_ref[k] for k in range(planes))
    joined = lambda start, stop: jnp.concatenate([sums[i : i + 1, :] for i in range(start, stop)], 1)
    places = ((bp_out, bp_hbm, 0, 1), (b2_out, b2_hbm, 1, 2), (qv_out, qv_hbm, 2, 4), (b1_out, b1_hbm, 4, sums.shape[0]))
    for out, hbm, start, stop in places:
        out[...] = joined(start, stop).reshape(out.shape[0])
        send(out, hbm)
    for copy in done:
        copy.wait()


def place_outputs(samples, planes, counts, totals, y, dx, lat, cot, kept, dmod, dcond, cvec, sums, ids, hidden, wq, wp, classes, bands):
    count, width = totals.shape[0] // 144, totals.shape[1]
    cols, depth = dmod.shape[2], dcond.shape[2]
    shape, room = jax.ShapeDtypeStruct, pltpu.VMEM
    wide = lambda size: shape((size, width), F32)
    return pl.pallas_call(
        functools.partial(outputs_kernel, samples, planes),
        out_shape=[
            shape(lat.shape, BF16),
            shape(lat.shape, BF16),
            wide(hidden),
            wide(hidden),
            wide(wq),
            wide(wp),
            wide(cols),
            shape((bands, depth), F32),
            shape((depth, classes), F32),
            shape((cols,), F32),
            shape((2 * wp,), F32),
            shape((wp,), F32),
            shape((hidden,), F32),
            shape((wp,), F32),
        ],
        in_specs=[SMEM] + [ANY] * 11,
        out_specs=[ANY] * 14,
        scratch_shapes=[
            room(kept.shape, jnp.int32),
            room(dmod.shape, BF16),
            room(dcond.shape, F32),
            room(cvec.shape, BF16),
            room(sums.shape, F32),
            room(ids.shape, F32),
            room((bands, depth), F32),
            room((depth, classes), F32),
            room((cols,), F32),
            room((2 * wp,), F32),
            room((wp,), F32),
            room((hidden,), F32),
            room((wp,), F32),
            room(totals.shape, BF16),
            room(totals.shape, F32),
            room((cols, width), F32),
            room((2,) + y.shape, BF16),
            room((2,) + lat.shape, BF16),
            pltpu.SemaphoreType.DMA((count + 10,)),
            pltpu.SemaphoreType.DMA((count + 9 + -(-cols // 256),)),
        ],
        compiler_params=pltpu.CompilerParams(vmem_limit_bytes=63 * 2**20),
    )(counts, totals, y, dx, lat, cot, kept, dmod, dcond, cvec, sums, ids)


def plane_body(planes, latents, cotangent, bands, labels, kept, band_counts, time_table, class_table, w_ada, b_ada, w_qkv,
               qv_bias, w_proj, b_proj, w_fc1, b_fc1, w_fc2, b_fc2):
    samples, length, width = latents.shape
    wq = w_qkv.shape[1]
    wp = w_proj.shape[0]
    hidden = w_fc1.shape[1]

    totals, y, dx, unused_weights, dmod, dcond, cvec, sums, ids = run_block(
        samples, planes, labels, bands, band_counts, w_qkv.T, w_proj, w_fc1.T, w_fc2, w_ada.T, latents, cotangent,
        (b_proj, b_fc2, qv_bias, b_ada, b_fc1), kept, class_table.T, time_table
    )
    block_out, latents_grad, g1, g2, gq, gp, ada, time, classes, bada, qv, bp, b1, b2 = place_outputs(
        samples, planes, band_counts, totals, y, dx, latents, cotangent, kept, dmod, dcond, cvec, sums, ids, hidden, wq, wp,
        class_table.shape[0], time_table.shape[0]
    )
    return (block_out, latents_grad, time, classes.T, ada.T, bada, gq.T, qv, gp, bp, g1.T, b1, g2, b2)


def solution(mesh):
    planes = mesh.shape["dp"]
    small = mesh.shape["grp"] == 8 and planes == 4
    return jax.shard_map(
        functools.partial(plane_body, planes) if small else body,
        mesh=mesh,
        in_specs=(
            P(("grp", "dp"), None, None),
            P(("grp", "dp"), None, None),
            P(("grp", "dp")),
            P(("grp", "dp")),
            P(("grp", "dp"), None),
            P("grp"),
            P(None, "grp"),
            P(None, "grp"),
            P(None, "grp"),
            P("grp"),
            P(None, "grp"),
            P("grp"),
            P("grp", None),
            P("grp"),
            P(None, "grp"),
            P("grp"),
            P("grp", None),
            P("grp"),
        ),
        out_specs=(
            P(("grp", "dp"), None, None),
            P(("grp", "dp"), None, None),
            P(None, "grp"),
            P(None, "grp"),
            P(None, "grp"),
            P("grp"),
            P(None, "grp"),
            P("grp"),
            P("grp", None),
            P("grp"),
            P(None, "grp"),
            P("grp"),
            P("grp", None),
            P("grp"),
        ),
        check_vma=False,
    )
```

```python
import functools

import jax
import jax.numpy as jnp
from jax import lax
from jax.experimental import pallas as pl
from jax.experimental.pallas import tpu as pltpu
from jax.sharding import PartitionSpec as P

HEADS = 16
HEAD_DIM = 72


EPS = 1e-06
HIGH = lax.Precision.HIGHEST


def modulate(values, shift, scale):
    mean = jnp.mean(values, -1, keepdims=True)
    cent = values - mean
    var = jnp.mean(cent * cent, -1, keepdims=True)
    return cent * lax.rsqrt(var + EPS) * (1.0 + scale[:, None, :]) + shift[:, None, :]


def product(left, right):
    return jnp.einsum("btd,de->bte", left, right, preferred_element_type=jnp.float32)


def weight_term(left, right):
    return jnp.einsum("btd,bte->de", left, right, preferred_element_type=jnp.float32)


def core(weights, tokens, mod):
    w_qkv, qv_bias, w_proj, b_proj, w_fc1, b_fc1, w_fc2, b_fc2 = weights
    count, length, width = tokens.shape
    shift1, scale1, gate1, shift2, scale2, gate2 = jnp.split(mod, 6, -1)
    h1 = modulate(tokens, shift1, scale1).astype(jnp.bfloat16)
    bias = jnp.concatenate(
        [
            qv_bias[:width].astype(jnp.float32),
            jnp.zeros((width,), jnp.float32),
            qv_bias[width:].astype(jnp.float32),
        ]
    )
    qkv = (product(h1, w_qkv) + bias).astype(jnp.bfloat16)
    query = qkv[..., :width].reshape(count, length, HEADS, HEAD_DIM)
    keys = qkv[..., width : 2 * width].reshape(count, length, HEADS, HEAD_DIM)
    values = qkv[..., 2 * width :].reshape(count, length, HEADS, HEAD_DIM)
    scores = jnp.einsum(
        "bqhd,bkhd->bhqk", query, keys, preferred_element_type=jnp.float32
    ) * HEAD_DIM ** (-0.5)
    total = jax.scipy.special.logsumexp(scores, axis=-1, keepdims=True)
    probs_full = jnp.exp(scores - total)
    probs = probs_full.astype(jnp.bfloat16)
    att = (
        jnp.einsum("bhqk,bkhd->bqhd", probs, values, preferred_element_type=jnp.float32)
        .reshape(count, length, width)
        .astype(jnp.bfloat16)
    )
    proj = product(att, w_proj) + b_proj.astype(jnp.float32)
    mixed = tokens + gate1[:, None, :] * proj
    h2 = modulate(mixed, shift2, scale2).astype(jnp.bfloat16)
    pre = product(h2, w_fc1) + b_fc1.astype(jnp.float32)
    act = jax.nn.gelu(pre, approximate=True).astype(jnp.bfloat16)
    mlp = product(act, w_fc2) + b_fc2.astype(jnp.float32)
    result = mixed + gate2[:, None, :] * mlp
    saved = (h1, query, keys, values, probs_full, probs, att, proj, mixed, h2, pre, act, mlp)
    return (result, saved)


def body(
    latents,
    cotangent,
    bands,
    labels,
    kept,
    band_counts,
    time_table,
    class_table,
    w_ada,
    b_ada,
    w_qkv,
    qv_bias,
    w_proj,
    b_proj,
    w_fc1,
    b_fc1,
    w_fc2,
    b_fc2,
):
    gathered = (
        lax.all_gather(time_table, "grp", axis=1, tiled=True),
        lax.all_gather(class_table, "grp", axis=1, tiled=True),
        lax.all_gather(w_ada, "grp", axis=1, tiled=True),
        lax.all_gather(b_ada, "grp", axis=0, tiled=True),
        lax.all_gather(w_qkv, "grp", axis=1, tiled=True),
        lax.all_gather(qv_bias, "grp", axis=0, tiled=True),
        lax.all_gather(w_proj, "grp", axis=0, tiled=True),
        lax.all_gather(b_proj, "grp", axis=0, tiled=True),
        lax.all_gather(w_fc1, "grp", axis=1, tiled=True),
        lax.all_gather(b_fc1, "grp", axis=0, tiled=True),
        lax.all_gather(w_fc2, "grp", axis=0, tiled=True),
        lax.all_gather(b_fc2, "grp", axis=0, tiled=True),
    )
    time_full, class_full, ada_full, ada_bias = (gathered[0], gathered[1], gathered[2], gathered[3])
    samples = latents.shape[0]
    width = latents.shape[2]
    slot = lax.axis_index("dp") * samples + jnp.arange(samples, dtype=jnp.int32)
    group_count = band_counts[0]
    weight = jnp.where(slot < group_count, 1.0, 0.0).astype(jnp.float32) / group_count.astype(
        jnp.float32
    )
    band_hot = (bands[:, None] == jnp.arange(time_full.shape[0], dtype=jnp.int32)[None, :]).astype(
        jnp.float32
    )
    class_hot = (
        labels[:, None] == jnp.arange(class_full.shape[0], dtype=jnp.int32)[None, :]
    ).astype(jnp.float32)
    cond = jnp.dot(band_hot, time_full.astype(jnp.float32), precision=HIGH) + jnp.dot(
        class_hot, class_full.astype(jnp.float32), precision=HIGH
    )
    cvec = jax.nn.silu(cond).astype(jnp.bfloat16)
    mod = jnp.dot(cvec, ada_full, preferred_element_type=jnp.float32) + ada_bias.astype(jnp.float32)
    rows = jnp.arange(samples, dtype=jnp.int32)[:, None]
    tokens = jnp.take_along_axis(latents, kept[:, :, None], 1).astype(jnp.float32)
    result, unused = core(tuple(gathered[4:]), tokens, mod)
    block_out = latents.at[rows, kept].set(result.astype(jnp.bfloat16))
    fetched = (
        lax.all_gather(w_ada, "grp", axis=1, tiled=True),
        lax.all_gather(w_qkv, "grp", axis=1, tiled=True),
        lax.all_gather(qv_bias, "grp", axis=0, tiled=True),
        lax.all_gather(w_proj, "grp", axis=0, tiled=True),
        lax.all_gather(b_proj, "grp", axis=0, tiled=True),
        lax.all_gather(w_fc1, "grp", axis=1, tiled=True),
        lax.all_gather(b_fc1, "grp", axis=0, tiled=True),
        lax.all_gather(w_fc2, "grp", axis=0, tiled=True),
        lax.all_gather(b_fc2, "grp", axis=0, tiled=True),
    )
    ada_full = fetched[0]
    back = tuple(fetched[1:])
    qkv_full, unused_bias, proj_full, unused_pbias, fc1_full, unused_b1, fc2_full, unused_b2 = back
    result, saved = core(back, tokens, mod)
    h1, query, keys, values, probs_full, probs, att, proj, mixed, h2, pre, act, mlp = saved
    shift1, scale1, gate1, shift2, scale2, gate2 = jnp.split(mod, 6, -1)
    weighted = cotangent.astype(jnp.float32) * weight[:, None, None]
    grad_out = jnp.take_along_axis(weighted, kept[:, :, None], 1)
    grad_mlp = (gate2[:, None, :] * grad_out).astype(jnp.bfloat16)
    grad_gate2 = jnp.sum(grad_out * mlp, 1)
    fc2_grad = weight_term(act, grad_mlp)
    fc2_bias_grad = jnp.sum(grad_mlp.astype(jnp.float32), (0, 1))
    grad_act = jnp.einsum("bte,de->btd", grad_mlp, fc2_full, preferred_element_type=jnp.float32)
    unused_pre, gelu_back = jax.vjp(lambda value: jax.nn.gelu(value, approximate=True), pre)
    grad_pre = gelu_back(grad_act)[0].astype(jnp.bfloat16)
    fc1_grad = weight_term(h2, grad_pre)
    fc1_bias_grad = jnp.sum(grad_pre.astype(jnp.float32), (0, 1))
    grad_h2 = jnp.einsum("bte,de->btd", grad_pre, fc1_full, preferred_element_type=jnp.float32)
    unused_h2, norm_back = jax.vjp(modulate, mixed, shift2, scale2)
    grad_mixed, grad_shift2, grad_scale2 = norm_back(grad_h2)
    grad_mixed = grad_mixed + grad_out
    grad_proj = (gate1[:, None, :] * grad_mixed).astype(jnp.bfloat16)
    grad_gate1 = jnp.sum(grad_mixed * proj, 1)
    proj_grad = weight_term(att, grad_proj)
    proj_bias_grad = jnp.sum(grad_proj.astype(jnp.float32), (0, 1))
    grad_att = jnp.einsum(
        "bte,de->btd", grad_proj, proj_full, preferred_element_type=jnp.float32
    ).astype(jnp.bfloat16)
    grad_heads = grad_att.reshape(query.shape)
    grad_values = jnp.einsum(
        "bhqk,bqhd->bkhd", probs, grad_heads, preferred_element_type=jnp.float32
    )
    grad_probs = jnp.einsum(
        "bqhd,bkhd->bhqk", grad_heads, values, preferred_element_type=jnp.float32
    )
    grad_scores = probs_full * (grad_probs - jnp.sum(grad_probs * probs_full, -1, keepdims=True))
    grad_scores = grad_scores.astype(jnp.bfloat16)
    grad_query = jnp.einsum(
        "bhqk,bkhd->bqhd", grad_scores, keys, preferred_element_type=jnp.float32
    ) * HEAD_DIM ** (-0.5)
    grad_keys = jnp.einsum(
        "bhqk,bqhd->bkhd", grad_scores, query, preferred_element_type=jnp.float32
    ) * HEAD_DIM ** (-0.5)
    count, length = (tokens.shape[0], tokens.shape[1])
    grad_qkv = jnp.concatenate(
        [
            grad_query.reshape(count, length, width),
            grad_keys.reshape(count, length, width),
            grad_values.reshape(count, length, width),
        ],
        -1,
    ).astype(jnp.bfloat16)
    qkv_grad = weight_term(h1, grad_qkv)
    qkv_sums = jnp.sum(grad_qkv.astype(jnp.float32), (0, 1))
    qv_bias_grad = jnp.concatenate([qkv_sums[:width], qkv_sums[2 * width :]])
    grad_h1 = jnp.einsum("bte,de->btd", grad_qkv, qkv_full, preferred_element_type=jnp.float32)
    unused_h1, first_back = jax.vjp(modulate, tokens, shift1, scale1)
    grad_tokens, grad_shift1, grad_scale1 = first_back(grad_h1)
    grad_tokens = grad_tokens + grad_mixed
    latents_grad = weighted.at[rows, kept].set(grad_tokens).astype(jnp.bfloat16)
    grad_mod = jnp.concatenate(
        [grad_shift1, grad_scale1, grad_gate1, grad_shift2, grad_scale2, grad_gate2], -1
    ).astype(jnp.bfloat16)
    ada_grad = jnp.dot(cvec.T, grad_mod, preferred_element_type=jnp.float32)
    ada_bias_grad = jnp.sum(grad_mod.astype(jnp.float32), 0)
    grad_cvec = jnp.dot(grad_mod, ada_full.T, preferred_element_type=jnp.float32)
    unused_cond, silu_back = jax.vjp(jax.nn.silu, cond)
    grad_cond = silu_back(grad_cvec)[0]
    time_grad = jnp.dot(band_hot.T, grad_cond, precision=HIGH)
    class_grad = jnp.dot(class_hot.T, grad_cond, precision=HIGH)
    shares = (
        lax.psum_scatter(time_grad, "grp", scatter_dimension=1, tiled=True),
        lax.psum_scatter(class_grad, "grp", scatter_dimension=1, tiled=True),
        lax.psum_scatter(ada_grad, "grp", scatter_dimension=1, tiled=True),
        lax.psum_scatter(ada_bias_grad, "grp", scatter_dimension=0, tiled=True),
        lax.psum_scatter(qkv_grad, "grp", scatter_dimension=1, tiled=True),
        lax.psum_scatter(qv_bias_grad, "grp", scatter_dimension=0, tiled=True),
        lax.psum_scatter(proj_grad, "grp", scatter_dimension=0, tiled=True),
        lax.psum_scatter(proj_bias_grad, "grp", scatter_dimension=0, tiled=True),
        lax.psum_scatter(fc1_grad, "grp", scatter_dimension=1, tiled=True),
        lax.psum_scatter(fc1_bias_grad, "grp", scatter_dimension=0, tiled=True),
        lax.psum_scatter(fc2_grad, "grp", scatter_dimension=0, tiled=True),
        lax.psum_scatter(fc2_bias_grad, "grp", scatter_dimension=0, tiled=True),
    )
    totals = (
        lax.psum(shares[0].astype(jnp.bfloat16), "dp").astype(jnp.float32),
        lax.psum(shares[1].astype(jnp.bfloat16), "dp").astype(jnp.float32),
        lax.psum(shares[2].astype(jnp.bfloat16), "dp").astype(jnp.float32),
        lax.psum(shares[3].astype(jnp.bfloat16), "dp").astype(jnp.float32),
        lax.psum(shares[4].astype(jnp.bfloat16), "dp").astype(jnp.float32),
        lax.psum(shares[5].astype(jnp.bfloat16), "dp").astype(jnp.float32),
        lax.psum(shares[6].astype(jnp.bfloat16), "dp").astype(jnp.float32),
        lax.psum(shares[7].astype(jnp.bfloat16), "dp").astype(jnp.float32),
        lax.psum(shares[8].astype(jnp.bfloat16), "dp").astype(jnp.float32),
        lax.psum(shares[9].astype(jnp.bfloat16), "dp").astype(jnp.float32),
        lax.psum(shares[10].astype(jnp.bfloat16), "dp").astype(jnp.float32),
        lax.psum(shares[11].astype(jnp.bfloat16), "dp").astype(jnp.float32),
    )
    return (
        block_out,
        latents_grad,
        totals[0],
        totals[1],
        totals[2],
        totals[3],
        totals[4],
        totals[5],
        totals[6],
        totals[7],
        totals[8],
        totals[9],
        totals[10],
        totals[11],
    )


MESH = pl.DeviceIdType.MESH
F32 = jnp.float32
BF16 = jnp.bfloat16
GELU_A = 0.7978845608028654
GELU_B = 0.044715


def dot(left, right, dims):
    return lax.dot_general(left, right, ((dims[:1], dims[1:]), ((), ())), preferred_element_type=F32)


class Place:
    def __init__(self):
        self.g = lax.axis_index("grp")
        self.z = lax.axis_index("dp")
        self.c = self.g % 2
        self.x = (self.g // 2) % 2
        self.y = self.g // 4

    def block(self, dc, dx, dy):
        c = 1 - self.c if dc else self.c
        x = 1 - self.x if dx else self.x
        y = 1 - self.y if dy else self.y
        return y * 4 + x * 2 + c

    def device(self, dc, dx, dy):
        return (self.block(dc, dx, dy), self.z)


RELATIVE = [(r & 1, (r >> 1) & 1, r >> 2) for r in range(8)]


class Wire:
    def __init__(self, send, recv):
        self.send, self.recv, self.sends, self.recvs = send, recv, 0, 0

    def take(self, recvs, sends=1):
        first = (self.sends, self.recvs)
        self.sends += sends
        self.recvs += recvs
        return first

    def copy(self, send, recv, src, dst, device):
        return pltpu.make_async_remote_copy(
            src_ref=src,
            dst_ref=dst,
            send_sem=self.send.at[send],
            recv_sem=self.recv.at[recv],
            device_id=device,
            device_id_type=MESH,
        )


def halves(rows):
    cut = rows // 32 * 16
    return pl.ds(0, cut), pl.ds(cut, rows - cut)


def greet(devices):
    barrier = pltpu.get_barrier_semaphore()
    for device in devices:
        pl.semaphore_signal(barrier, inc=1, device_id=device, device_id_type=MESH)
    pl.semaphore_wait(barrier, len(devices))


def plane(place):
    return [place.device(*rel) for rel in RELATIVE[1:]]


class Gather:
    def __init__(self, place, wire, buf, start=0, rows=None, origin=None):
        p = place
        rows = rows or buf.shape[1]
        lo, hi = halves(rows)
        parts = (pl.ds(start, rows), pl.ds(start, lo.size), pl.ds(start + lo.size, hi.size))
        send, recv = wire.take(8)

        def make(number, block, device, part=0):
            ref = buf.at[block, parts[part]]
            src = origin if number < 3 and origin is not None else ref
            return wire.copy(send, recv + number, src, ref, device)

        own, xb, yb, db = p.g, p.block(0, 1, 0), p.block(0, 0, 1), p.block(0, 1, 1)
        xd, yd, sd = p.device(0, 1, 0), p.device(0, 0, 1), p.device(1, 0, 0)
        self.c = [
            make(0, own, xd),
            make(1, own, yd),
            make(2, own, sd),
            make(3, xb, yd, 1),
            make(4, xb, sd),
            make(5, yb, xd, 2),
            make(6, yb, sd),
            make(7, db, sd),
        ]
        seven = buf.at[pl.ds(0, 7), parts[0]]
        self.sent = wire.copy(send, recv, seven, seven, sd)

    def start(self):
        for number in (0, 1, 2):
            self.c[number].start()

    def arrived(self):
        self.c[0].wait_recv()
        self.c[1].wait_recv()
        self.c[4].start()
        self.c[6].start()

    def forward(self):
        self.c[3].start()
        self.c[5].start()

    def neighbours(self):
        self.arrived()
        self.forward()

    def far(self):
        self.c[3].wait_recv()
        self.c[5].wait_recv()
        self.c[7].start()

    def wait_sib(self):
        self.c[2].wait_recv()

    def wait_sib_neighbours(self):
        self.c[4].wait_recv()
        self.c[6].wait_recv()

    def wait_sib_far(self):
        self.c[7].wait_recv()

    def finish(self):
        self.sent.wait_send()


class Halves:
    def __init__(self, place, wire, buf):
        self.lo, self.hi = [Gather(place, wire, buf, part.start, part.size) for part in halves(buf.shape[1])]

    def start(self):
        for number in (0, 1, 2):
            self.lo.c[number].start()
        for number in (0, 1, 2):
            self.hi.c[number].start()

    def far(self):
        self.lo.far()
        self.hi.far()

    def wait_sib(self):
        self.lo.wait_sib()
        self.hi.wait_sib()

    def wait_sib_neighbours(self):
        self.lo.wait_sib_neighbours()
        self.hi.wait_sib_neighbours()

    def wait_sib_far(self):
        self.lo.wait_sib_far()
        self.hi.wait_sib_far()

    def finish(self):
        self.lo.finish()
        self.hi.finish()


class OverZ:
    def __init__(self, place, wire, buf, hbm, there, ahead, behind, rows):
        p = place
        near = [p.block(0, 1, 0), p.block(0, 0, 1), p.block(0, 1, 1)]
        sd = p.device(1, 0, 0)
        sem, recv = wire.take(7)
        send, take = pl.ds(ahead, rows), pl.ds(behind, rows)
        self.out = [wire.copy(sem, recv + i, buf.at[b, send], buf.at[b, send], there) for i, b in enumerate(near)]
        self.on = [wire.copy(sem, recv + 3 + i, buf.at[b, take], buf.at[b, take], sd) for i, b in enumerate(near)]
        self.own = wire.copy(sem, recv + 6, hbm.at[take], buf.at[p.g, take], sd)
        seven = buf.at[pl.ds(0, 7), send]
        self.sent = wire.copy(sem, recv, seven, seven, sd)

    def pass_on(self, *numbers):
        for i in numbers:
            self.out[i].wait_recv()
            self.on[i].start()

    def arrived(self, *numbers):
        for i in numbers:
            self.on[i].wait_recv()

    def finish(self):
        self.sent.wait_send()


class Scatter:
    def __init__(self, place, wire, buf, r1, r2, r3, rows=None):
        self.p, self.w, self.buf = place, wire, buf
        self.r1, self.r2, self.r3 = r1, r2, r3
        self.rows = rows = rows or buf.shape[1]
        p, w = place, wire
        self.sib = [p.block(1, q & 1, q >> 1) for q in range(4)]
        self.mine = [p.block(0, q & 1, q >> 1) for q in range(4)]
        xd, yd, sd = p.device(0, 1, 0), p.device(0, 0, 1), p.device(1, 0, 0)
        sem, recv = wire.take(18)
        whole = pl.ds(0, rows)
        lo, hi = halves(rows)
        self.parts = [[pl.ds(half.start + cut.start, cut.size) for cut in halves(half.size)] for half in (lo, hi)]
        self.lo_hi = (lo, hi)
        self.s1 = [
            [w.copy(sem, recv + 10 + 2 * q + i, buf.at[self.sib[q], part], r1.at[q, part], sd) for i, part in enumerate((lo, hi))]
            for q in range(4)
        ]
        self.s2, self.s3 = [], []
        for way, device in ((0, xd), (1, yd)):
            for i, part in enumerate(self.parts[way]):
                number = recv + 2 * way + i
                self.s2.append(w.copy(sem, number, buf.at[self.mine[3], part], r2.at[way, pl.ds(part.start - self.parts[way][0].start, part.size)], device))
        for way, device in ((0, xd), (1, yd)):
            direct = (lo, hi)[way]
            for i, part in enumerate([direct] + self.parts[1 - way]):
                number = recv + 4 + 3 * way + i
                self.s3.append(w.copy(sem, number, buf.at[self.mine[1 + way], part], r3.at[way, part], device))
        seven = buf.at[pl.ds(0, 7), whole]
        self.sent = wire.copy(sem, recv, seven, seven, sd)

    def send_sib(self, q, halves_of=(0, 1)):
        for i in halves_of:
            self.s1[q][i].start()

    def add_sib(self, q, halves_of=(0, 1)):
        for i in halves_of:
            self.s1[q][i].wait_recv()
            add_into(self.buf.at[self.mine[q], self.lo_hi[i]], self.r1.at[q, self.lo_hi[i]])

    def send_far(self):
        self.add_sib(3)
        for number in (0, 2, 1, 3):
            self.s2[number].start()

    def near(self, way):
        self.add_sib(1 + way, (way,))
        self.s3[3 * way].start()

    def send_near(self):
        self.near(0)
        self.near(1)

    def relay(self, i):
        if i == 0:
            self.add_sib(1, (1,))
            self.add_sib(2, (0,))
        for way in range(2):
            self.s2[2 * way + i].wait_recv()
            part = self.parts[way][i]
            came = self.r2.at[way, pl.ds(part.start - self.parts[way][0].start, part.size)]
            add_into(self.buf.at[self.mine[2 - way], part], came)
            self.s3[3 * (1 - way) + 1 + i].start()
        if i == 1:
            self.add_sib(0)

    def result(self, out):
        for copy in self.s3:
            copy.wait_recv()
        step = 16

        @pl.loop(0, self.rows // step)
        def _(i):
            at = pl.ds(pl.multiple_of(i * step, step), step)
            total = self.buf[self.mine[0], at].astype(F32) + self.r3[0, at].astype(F32) + self.r3[1, at].astype(F32)
            out[at] = total.astype(out.dtype)

    def finish(self):
        self.sent.wait_send()


def add_into(ref, other):
    step = 16

    @pl.loop(0, ref.shape[0] // step)
    def _(i):
        at = pl.ds(pl.multiple_of(i * step, step), step)
        ref[at] = (ref[at].astype(F32) + other[at].astype(F32)).astype(ref.dtype)


def scatter_scratch(rows, width):
    return [
        pltpu.VMEM((4, rows, width), BF16),
        pltpu.VMEM((2, halves(rows)[1].size, width), BF16),
        pltpu.VMEM((2, rows, width), BF16),
    ]


class Together:
    def __init__(self, wire, buf, pairs, device):
        send, recv = wire.take(1)
        count = len(pairs)
        for src, dst, target in pairs:
            wire.copy(send, recv, src, dst, target).start()
        all_blocks = buf.at[pl.ds(0, count)]
        self.all = wire.copy(send, recv, all_blocks, all_blocks, device)


def to_all(place, wire, buf, make):
    pairs = [(make(rel), buf.at[place.g], place.device(*rel)) for rel in RELATIVE[1:]]
    return Together(wire, buf, pairs, place.device(1, 0, 0))


def wait_recv(copies):
    copies.all.wait_recv()


def wait_send(copies):
    copies.all.wait_send()


def params(collective_id):
    return pltpu.CompilerParams(
        collective_id=collective_id, has_side_effects=True, vmem_limit_bytes=63 * 2**20
    )


VMEM = pl.BlockSpec(memory_space=pltpu.VMEM)

def gelu_parts(pre):
    square = pre * pre
    half = 0.5 + 0.5 * jnp.tanh(pre * (GELU_A + GELU_A * GELU_B * square))
    act = pre * half
    slope = half + (act - act * half) * (2.0 * GELU_A + 6.0 * GELU_A * GELU_B * square)
    return act, slope


def local(src, dst, sem):
    return pltpu.make_async_copy(src, dst, sem)


def own_tokens(kept_ref, length, s):
    rows = lax.broadcasted_iota(jnp.int32, (length, kept_ref.shape[1]), 0)
    return jnp.where(rows == kept_ref[s : s + 1, :], 1.0, 0.0).astype(BF16)


def normed(v):
    cent = v - jnp.mean(v, -1, keepdims=True)
    inv = lax.rsqrt(jnp.mean(cent * cent, -1, keepdims=True) + EPS)
    return cent * inv, inv


def norm_back(grad, hat, inv):
    return inv * (grad - jnp.mean(grad, -1, keepdims=True) - hat * jnp.mean(grad * hat, -1, keepdims=True))


STEP = 32


def by_rows(samples, keep, fn):
    @pl.loop(0, samples * keep // STEP)
    def _(i):
        fn(lax.div(i, keep // STEP), pl.ds(pl.multiple_of(i * STEP, STEP), STEP))


SCALE = HEAD_DIM ** (-0.5)


def probabilities(q, k):
    scores = dot(k, q, (0, 0)) * SCALE
    exps = jnp.exp(scores - jnp.max(scores, 0, keepdims=True))
    return exps / jnp.sum(exps, 0, keepdims=True)


def arrival(p, t, last=7):
    dc = jnp.where((t == 1) | (t == 4) | (t == 5) | (t == last), 1, 0)
    dx = jnp.where((t == 2) | (t == 4) | (t >= 6), 1, 0)
    dy = jnp.where((t == 3) | (t >= 5), 1, 0)
    c, x, y = lax.rem(p.c + dc, 2), lax.rem(p.x + dx, 2), lax.rem(p.y + dy, 2)
    return y * 4 + x * 2 + c


def sample_weight(place, counts_ref, samples, s):
    count = jnp.full((1, 128), counts_ref[0], jnp.int32)
    used = count > place.z * samples + s
    return (jnp.where(used, 1.0, 0.0) / count.astype(F32))[:, 0:1]


ANY = pl.BlockSpec(memory_space=pltpu.HBM)
SMEM = pl.BlockSpec(memory_space=pltpu.SMEM)
PIECE = 48


def block_kernel(samples, planes, labels_ref, bands_ref, counts_ref, wq_hbm, wp_hbm, w1_hbm, w2_hbm, ada_hbm, lat_hbm, cot_hbm,
                 bp_ref, b2_ref, qv_ref, bada_ref, b1_ref, kept_ref, class_ref, time_ref,
                 out_hbm, y_hbm, dx_hbm, wq_keep, dmod_hbm, dcond_hbm, cvec_hbm, sum_hbm, ids_hbm,
                 dmod_z, dcond_z, cvec_z, sum_z, ids_z,
                 wq, wp, w1, w2, h1_all, h2_all, dm_all, act, dpre, p1, p2, p3, units, att, mixed, proj, grad, dx2, tmp, rest,
                 dproj, dq, dq_all, from_end, out, grads, gb1, ids_all, msg_all, cond_all, mod_in, mod_send, mod, vec,
                 dc_send, dc_in, bundle, share_send, share_in, send, recv, credits, sems):
    p = Place()
    wire = Wire(send, recv)
    g, z = p.g, p.z
    others = [(g, (z + k) % planes) for k in range(1, planes)]
    greet(plane(p) + others)
    length = lat_hbm.shape[1]
    keep = kept_ref.shape[1]
    rows, width = mixed.shape
    pair = 2 * HEAD_DIM
    hidden_units = act.shape[2]
    ada_rest = ada_hbm.shape[0] - hidden_units

    loads = {}
    for number, (name, src, dst) in enumerate((
        ("wq", wq_hbm, wq.at[g]),
        ("wp", wp_hbm, wp.at[g]),
        ("lat", lat_hbm, h2_all.at[pl.ds(0, samples)]),
        ("cot", cot_hbm, h2_all.at[pl.ds(samples, samples)]),
        ("ada1", ada_hbm.at[pl.ds(0, hidden_units)], w1),
        ("ada2", ada_hbm.at[pl.ds(hidden_units, ada_rest)], w2.at[pl.ds(0, ada_rest)]),
        ("w1", w1_hbm, w1),
        ("w2", w2_hbm, w2),
        ("keep", wq, wq_keep),
        ("again", wq_keep, wq),
        ("ada1b", ada_hbm.at[pl.ds(0, hidden_units)], w1),
        ("ada2b", ada_hbm.at[pl.ds(hidden_units, ada_rest)], w2.at[pl.ds(0, ada_rest)]),
        ("latb", lat_hbm, wq.at[pl.ds(0, samples), pl.ds(0, length)]),
        ("dx", dproj, dx_hbm),
        ("y", dproj, y_hbm),
        ("dmod", dmod_z, dmod_hbm),
        ("dcond", dcond_z, dcond_hbm),
        ("cvec", cvec_z, cvec_hbm),
        ("sum", sum_z, sum_hbm),
        ("ids", ids_z, ids_hbm),
    )):
        loads[name] = local(src, dst, sems.at[number])
    odd = z % 2
    there = (g, z + 1 - 2 * odd)
    gather_a = Gather(p, wire, wq, 2 * pair * odd, pair, wq_hbm.at[pl.ds(2 * pair * odd, pair)])
    gather_m = Gather(p, wire, wq, pair, pair, wq_hbm.at[pl.ds(pair, pair)])
    qkv_z = OverZ(p, wire, wq, wq_hbm, there, 2 * pair * odd, 2 * pair * (1 - odd), pair)
    inside = pair // 32 * 16 + 16
    beyond = pair - inside
    outward = Gather(p, wire, wp, beyond * odd, inside, wp_hbm.at[pl.ds(beyond * odd, inside)])
    proj_z = OverZ(p, wire, wp, wp_hbm, there, inside * odd, inside * (1 - odd), beyond)
    main = Halves(p, wire, h2_all)
    back = Halves(p, wire, dm_all)
    tokens = Halves(p, wire, h1_all)
    sums = Scatter(p, wire, wq, p1, p2, p3, rows)
    outs = Scatter(p, wire, h2_all, dm_all.at[pl.ds(0, 4)], dm_all.at[pl.ds(4, 2)], dm_all.at[pl.ds(6, 2)])
    projs = Scatter(p, wire, wp, p1, p2, p3)
    part_of = lambda start, size: grads.at[pl.ds(start, size)]
    g1, g2 = part_of(0, hidden_units), part_of(hidden_units, hidden_units)
    gq, gp = part_of(2 * hidden_units, 3 * pair), part_of(2 * hidden_units + 3 * pair, pair)
    count = grads.shape[0] // PIECE
    (up, up_r), (across, across_r), (down, _) = [wire.take(recvs) for recvs in (count, count, 0)]
    inner, outer, partner = 1 + z // 3, (z - 1) * 3, 3 - z
    at_end = (z == 0) | (z == planes - 1)
    rows_of = lambda ref, k: ref.at[pl.ds(pl.multiple_of(k * PIECE, 16), PIECE)]
    go_up = lambda k: wire.copy(up, up_r + k, rows_of(grads, k), rows_of(from_end, k), (g, inner))
    go_across = lambda k: wire.copy(across, across_r + k, rows_of(from_end, k), rows_of(out, k), (g, partner))
    go_down = lambda k: wire.copy(down, up_r + k, rows_of(out, k), rows_of(out, k), (g, outer))
    to_hbm = lambda k: local(rows_of(out, k), rows_of(out_hbm, k), sems.at[20])

    def chain_send(first, last):
        @pl.when(at_end)
        def _():
            for k in range(first, last):
                go_up(k).start()

    def chain_up(k):
        @pl.when(jnp.logical_not(at_end))
        def _():
            go_up(k).wait_recv()
            add_into(rows_of(from_end, k), rows_of(grads, k))
            go_across(k).start()

    def chain_down(k):
        @pl.when(jnp.logical_not(at_end))
        def _():
            go_across(k).wait_recv()
            add_into(rows_of(out, k), rows_of(from_end, k))
            go_down(k).start()
            to_hbm(k).start()

    def chain(k, lag):
        chain_up(k)
        chain_down(k - lag)

    def to_planes(ref):
        return Together(wire, ref, [(ref.at[z], ref.at[z], device) for device in others], others[0])

    neighbours = [p.device(1, 0, 0), p.device(0, 1, 0), p.device(0, 0, 1)]

    def grant(number):
        for i, device in enumerate(neighbours):
            pl.semaphore_signal(credits.at[number, i], inc=1, device_id=device, device_id_type=MESH)

    def granted(number):
        for i in range(3):
            pl.semaphore_wait(credits.at[number, i], 1)

    lanes = lax.broadcasted_iota(jnp.int32, (1, 128), 1)
    for s in range(samples):
        line = jnp.where(lanes == 0, labels_ref[s], 0) + jnp.where(lanes == 1, bands_ref[s], 0)
        ids_all[g, s : s + 1, :] = line.astype(F32)
    line_of = lambda ref: ref[...].astype(F32).reshape(1, ref.shape[0])
    b_ada, b1, qv = line_of(bada_ref), line_of(b1_ref), line_of(qv_ref)
    for row, line in enumerate((line_of(bp_ref), line_of(b2_ref), qv[:, :pair], qv[:, pair:])):
        msg_all[g, row : row + 1, :] = line
    idc = to_all(p, wire, ids_all, lambda rel: ids_all.at[g])
    gather_a.start()
    msgs = to_all(p, wire, msg_all, lambda rel: msg_all.at[g])
    for name in ("lat", "cot", "ada1", "ada2", "wq", "wp"):
        loads[name].start()

    wait_recv(idc)
    labels = jnp.concatenate([ids_all[j, 0:samples, 0:1] for j in range(8)], 0)
    bands = jnp.concatenate([ids_all[j, 0:samples, 1:2] for j in range(8)], 0)

    def one_hot(ids, size):
        lanes = lax.broadcasted_iota(jnp.int32, (ids.shape[0], size), 1).astype(F32)
        return jnp.where(lanes == ids, 1.0, 0.0).astype(BF16)

    of_band = dot(one_hot(bands, time_ref.shape[0]), time_ref[...], (1, 0))
    cond_all[g] = of_band + dot(one_hot(labels, class_ref.shape[1]), class_ref[...], (1, 1))
    conds = to_all(p, wire, cond_all, lambda rel: cond_all.at[g])
    ids_z[z] = jnp.zeros(ids_z.shape[1:], F32)
    ids_z[z, :, 0:1] = labels
    ids_z[z, :, 1:2] = bands


    loads["lat"].wait()
    loads["cot"].wait()
    for s in range(samples):
        hot = own_tokens(kept_ref, length, s)
        at = pl.ds(s * keep, keep)
        mixed[at] = dot(hot, h2_all[s], (0, 0))
        grad[at] = dot(hot, h2_all[samples + s], (0, 0)) * sample_weight(p, counts_ref, samples, s)

    gather_a.neighbours()
    qkv_z.out[0].start()
    qkv_z.out[1].start()
    wait_recv(conds)
    value = jnp.concatenate([cond_all[j] for j in range(8)], 1)
    value = (value * jax.nn.sigmoid(value)).astype(BF16)
    cvec_z[z] = value
    loads["ada1"].wait()
    loads["ada2"].wait()
    mods = [dot(value, w1[...], (1, 1)), dot(value, w2[0:ada_rest], (1, 1))]
    mods = jnp.concatenate(mods, 1) + b_ada
    for j in range(8):
        mod_send[j] = mods[samples * j : samples * (j + 1), :]
    mod_in[g] = mod_send[g]
    modc = to_all(p, wire, mod_in, lambda rel: mod_send.at[p.block(*rel)])
    gather_m.start()
    qkv_z.own.start()
    loads["w1"].start()
    loads["w2"].start()
    outward.start()
    proj_z.own.start()
    gather_a.far()
    qkv_z.out[2].start()
    wait_recv(modc)
    mod[...] = jnp.zeros_like(mod)
    for s in range(samples):
        line = jnp.concatenate([mod_in[j, s : s + 1, :] for j in range(8)], 1)
        for v in range(6):
            mod[s, v : v + 1, :] = line[:, v * width : (v + 1) * width]

    def first_norm(s, at):
        hat, inv = normed(mixed[at])
        h1_all[g, at] = (hat * (1.0 + mod[s, 1:2, :]) + mod[s, 0:1, :]).astype(BF16)
        dm_all[g, at] = (mod[s, 5:6, :] * grad[at]).astype(BF16)

    by_rows(samples, keep, first_norm)
    wait_recv(msgs)
    vec[...] = jnp.zeros_like(vec)
    for row in range(2):
        vec[row : row + 1, :] = jnp.concatenate([msg_all[j, row : row + 1, :] for j in range(8)], 1)

    ones = jnp.ones((8, rows), BF16)
    loads["wq"].wait()

    @pl.loop(0, 24)
    def _(n):
        @pl.when(n == 1)
        def _():
            gather_a.wait_sib()

        @pl.when(n == 4)
        def _():
            gather_a.wait_sib_neighbours()

        @pl.when(n == 7)
        def _():
            gather_a.wait_sib_far()

        @pl.when(n == 9)
        def _():
            gather_m.wait_sib()

        @pl.when(n == 8)
        def _():
            gather_m.neighbours()

        @pl.when(n == 12)
        def _():
            gather_m.wait_sib_neighbours()

        @pl.when(n == 14)
        def _():
            outward.neighbours()
            proj_z.out[0].start()
            proj_z.out[1].start()
            back.start()

        @pl.when(n == 15)
        def _():
            qkv_z.own.wait_recv()
            qkv_z.pass_on(0, 1)

        @pl.when(n == 18)
        def _():
            qkv_z.arrived(0, 1)
            gather_m.far()

        @pl.when(n == 20)
        def _():
            qkv_z.pass_on(2)

        @pl.when(n == 21)
        def _():
            gather_m.wait_sib_far()

        @pl.when(n == 22)
        def _():
            outward.far()
            proj_z.out[2].start()

        @pl.when(n == 23)
        def _():
            qkv_z.arrived(2)

        phase = jnp.where(n < 8, 0, jnp.where((n < 14) | (n == 20) | (n == 21), 1, 2))
        turn = jnp.where(n < 8, n, jnp.where(n < 14, n - 8, jnp.where(n < 20, n - 14, jnp.where(n < 22, n - 14, n - 16))))
        block = arrival(p, turn)
        third = jnp.where(phase == 0, 2 * odd, jnp.where(phase == 1, 1, 2 - 2 * odd))
        chunk = block * 3 + third
        bias_at = jnp.where(chunk >= 16, chunk - 8, chunk)
        keys = (chunk >= 8) & (chunk < 16)
        line = msg_all[lax.div(bias_at, 2), pl.ds(2 + lax.rem(bias_at, 2), 1), :] * jnp.where(keys, 0.0, 1.0)
        line = jnp.concatenate([line, jnp.zeros((7, pair), F32)], 0)
        value = dot(wq[block, pl.ds(pl.multiple_of(third * pair, 16), pair), :], h1_all[g], (1, 1))
        value = value + dot(line.astype(BF16), ones, (0, 0))
        units[2 * chunk] = value[:HEAD_DIM].astype(BF16)
        units[2 * chunk + 1] = value[HEAD_DIM:].astype(BF16)

    loads["keep"].start()
    zs = [to_planes(ids_z), to_planes(cvec_z)]

    @pl.loop(0, 4)
    def _(i):
        for u in (2 * i, 2 * i + 1):
            for s in range(samples):
                lanes = pl.ds(s * keep, keep)
                pieces = []
                for e in range(2):
                    probs = probabilities(units[2 * u + e, :, lanes], units[16 + 2 * u + e, :, lanes])
                    pieces.append(dot(units[32 + 2 * u + e, :, lanes], probs.astype(BF16), (1, 0)))
                att[u, :, lanes] = jnp.concatenate(pieces, 0).astype(BF16)

    back.lo.neighbours()
    loads["wp"].wait()
    outward.wait_sib()
    outward.wait_sib_neighbours()
    outward.wait_sib_far()
    proj_z.own.wait_recv()
    proj_z.pass_on(0, 1, 2)
    back.hi.neighbours()
    proj_z.arrived(0, 1, 2)
    proj[...] = jnp.zeros_like(proj)

    @pl.loop(0, 8)
    def _(u):
        proj[...] += dot(att[u], wp[u], (0, 0))

    def second_norm(s, at):
        proj[at] = proj[at] + vec[0:1, :]
        mixed[at] = mixed[at] + mod[s, 2:3, :] * proj[at]
        hat, inv = normed(mixed[at])
        h2_all[g, at] = (hat * (1.0 + mod[s, 4:5, :]) + mod[s, 3:4, :]).astype(BF16)

    by_rows(samples, keep, second_norm)
    main.start()
    back.far()
    gb1[...] = jnp.zeros_like(gb1)
    for piece in (gather_a, gather_m, qkv_z):
        piece.finish()
    loads["w1"].wait()
    loads["w2"].wait()
    loads["keep"].wait()

    half_rows = rows // 2

    def hidden(places):
        both = lambda ref: jnp.concatenate([ref[block, at] for block, at in places], 0)
        pre = dot(both(h2_all), w1[...], (1, 1)) + b1
        value, slope = gelu_parts(pre)
        value = value.astype(BF16)
        low = (dot(both(dm_all), w2[...], (1, 1)) * slope).astype(BF16)
        gb1[...] += jnp.sum(low.astype(F32), 0, keepdims=True)
        share = dot(low, w1[...], (1, 0)).astype(BF16)
        for i, (block, at) in enumerate(places):
            part = slice(i * half_rows, (i + 1) * half_rows)
            act[block, at] = value[part]
            dpre[block, at] = low[part]
            wq[block, at] = share[part]

    @pl.loop(0, 8)
    def _(n):
        @pl.when(n == 1)
        def _():
            main.wait_sib()
            back.wait_sib()

        @pl.when(n == 2)
        def _():
            main.lo.neighbours()
            back.wait_sib_neighbours()
            back.wait_sib_far()

        @pl.when(n == 3)
        def _():
            main.lo.wait_sib_neighbours()

        @pl.when(n == 4)
        def _():
            main.hi.neighbours()

        @pl.when(n == 5)
        def _():
            main.hi.wait_sib_neighbours()

        @pl.when(n == 6)
        def _():
            main.lo.far()
            sums.send_sib(2, (1,))
            sums.send_sib(1, (1,))
            sums.near(0)
            main.lo.wait_sib_far()

        @pl.when(n == 7)
        def _():
            main.hi.far()
            sums.near(1)
            main.hi.wait_sib_far()

        upper = (n == 4) | (n == 5) | (n == 7)
        turn = jnp.where(n < 2, n, jnp.where(n < 6, 2 + 2 * lax.rem(n, 2), 6))
        halves_at = (jnp.where(upper, 1, 0), jnp.where(upper | (n < 2), 1, 0))
        turns = (turn, jnp.where(n < 2, turn, turn + 1))
        hidden([(arrival(p, t, 6), pl.ds(pl.multiple_of(h * half_rows, 16), half_rows)) for t, h in zip(turns, halves_at)])

        @pl.when(n == 1)
        def _():
            sums.send_sib(0)

        @pl.when(n == 3)
        def _():
            sums.send_sib(1, (0,))
            sums.send_sib(2, (0,))

        @pl.when(n == 6)
        def _():
            sums.send_sib(3, (0,))

        @pl.when(n == 7)
        def _():
            sums.send_sib(3, (1,))

    sums.send_far()

    def weight_grad(left, right, base, between):
        for n, (start, size) in enumerate(((0, 128), (128, 256), (384, hidden_units - 384))):
            part = left[:, :, pl.ds(start, size)].reshape(8 * rows, size)
            grads[base + start : base + start + size] = dot(part, right[...].reshape(8 * rows, width), (0, 0)).astype(BF16)
            chain_send(-(-base // PIECE) if n == 0 else (base + start) // PIECE, (base + start + size) // PIECE)
            between(n)

    def output_blocks(first, last):
        @pl.loop(first, last)
        def _(block):
            h2_all[block] = jnp.dot(act[block], w2[...], preferred_element_type=F32).astype(BF16)

    def visit(n):
        if n == 0:
            chain_up(0)
            sums.relay(0)
        elif n == 1:
            chain_up(1)
            sums.relay(1)
            tokens.start()
            chain_up(2)
            chain_down(0)

    weight_grad(dpre, h2_all, 0, lambda n: None)
    weight_grad(act, dm_all, hidden_units, visit)
    main.finish()
    chain_up(3)
    chain_down(1)
    output_blocks(0, 3)
    chain_up(4)
    chain_down(2)
    back.finish()
    grant(0)
    sums.result(tmp)
    sums.finish()
    grant(1)
    loads["again"].start()

    bundle[...] = jnp.zeros_like(bundle)

    def add_row(row, value):
        bundle[pl.ds(row, 1), :] += jnp.sum(value, 0, keepdims=True)

    SUM_PROJ, SUM_FC2 = 6 * samples, 6 * samples + 1

    def second_back(s, at):
        @pl.when(at.start == rows // 2)
        def _():
            chain_up(5)
            chain_down(3)

        hat, inv = normed(mixed[at])
        up_grad = tmp[at]
        value = grad[at] + norm_back(up_grad * (1.0 + mod[s, 4:5, :]), hat, inv)
        dx2[at] = value
        low = (mod[s, 2:3, :] * value).astype(BF16)
        dproj[at] = low
        add_row(s * 6 + 3, up_grad)
        add_row(s * 6 + 4, up_grad * hat)
        add_row(s * 6 + 2, value * proj[at])
        add_row(SUM_PROJ, low.astype(F32))
        add_row(SUM_FC2, (mod[s, 5:6, :] * grad[at]).astype(BF16).astype(F32))

    by_rows(samples, keep, second_back)
    chain_down(4)
    outward.finish()
    proj_z.finish()

    def heads_back(u):
        datt = dot(wp[u], dproj[...], (1, 1))
        wp[u] = dot(att[u], dproj[...], (1, 0)).astype(BF16)
        lists = ([], [], [])
        for s in range(samples):
            lanes = pl.ds(s * keep, keep)
            parts = ([], [], [])
            for e in range(2):
                q, k, v = (units[16 * i + 2 * u + e, :, lanes] for i in range(3))
                da = datt[e * HEAD_DIM : (e + 1) * HEAD_DIM, s * keep : (s + 1) * keep].astype(BF16)
                probs = probabilities(q, k)
                dprobs = dot(v, da, (0, 0))
                dscores = probs * (dprobs - jnp.sum(dprobs * probs, 0, keepdims=True))
                dscores = dscores.astype(BF16)
                parts[0].append(dot(k, dscores, (1, 0)) * SCALE)
                parts[1].append(dot(q, dscores, (1, 1)) * SCALE)
                parts[2].append(dot(da, probs.astype(BF16), (1, 1)))
            for i in range(3):
                lists[i].append(jnp.concatenate(parts[i], 0).astype(BF16))
        for i in range(3):
            chunk = 8 * i + u
            at = pl.ds(pl.multiple_of(lax.rem(chunk, 3) * pair, 16), pair)
            for s in range(samples):
                dq[lax.div(chunk, 3), at, pl.ds(s * keep, keep)] = lists[i][s]

    visits = {
        (0, 0): ((6,), ()),
        (0, 1): ((7,), (5,)),
        (1, 1): ((8,), (6,)),
        (2, 0): ((9,), (7,)),
        (2, 1): ((10,), ()),
        (3, 0): ((), (8,)),
        (3, 1): ((11,), (9,)),
    }

    @pl.loop(0, 4)
    def _(i):
        for e in range(2):
            heads_back(2 * i + e)
            if e == 1:

                @pl.when(i == 1)
                def _():
                    tokens.lo.neighbours()

                @pl.when(i == 2)
                def _():
                    tokens.hi.neighbours()

            for (at, half), (ups, downs) in visits.items():
                if half == e:

                    @pl.when(i == at)
                    def _(ups=ups, downs=downs):
                        for k in ups:
                            chain_up(k)
                        for k in downs:
                            chain_down(k)

    dq_all[g] = dq[g]
    moves = to_all(p, wire, dq_all, lambda rel: dq.at[p.block(*rel)])
    granted(1)
    for q in (3, 1, 2, 0):
        projs.send_sib(q)

    loads["again"].wait()
    proj[...] = jnp.zeros_like(proj)

    @pl.loop(0, 8)
    def _(j):
        proj[...] += dot(dq[j], wq[j], (0, 0))
        for at, step, k in ((1, chain_up, 12), (3, chain_down, 10), (6, chain_up, 13)):

            @pl.when(j == at)
            def _(step=step, k=k):
                step(k)

    loads["latb"].start()

    projs.send_far()
    projs.send_near()
    chain_down(11)
    granted(0)
    output_blocks(3, 6)
    chain(14, 2)
    output_blocks(6, 8)
    for q in (3, 1, 2, 0):
        outs.send_sib(q)
    loads["ada1b"].start()
    loads["ada2b"].start()
    for k in range(15, 18):
        chain(k, 2)
    tokens.far()
    for k in range(18, 22):
        chain(k, 2)
    outs.send_far()
    tokens.wait_sib()
    tokens.wait_sib_neighbours()
    tokens.wait_sib_far()

    wait_recv(moves)
    chain(22, 2)
    for i in range(3):
        at = pl.ds(i * pair, pair)
        tmp[0:pair] = jnp.zeros((pair, width), F32)

        @pl.loop(0, 8)
        def _(j, at=at):
            tmp[0:pair] += dot(dq_all[j, at, :], h1_all[j], (1, 0))

        gq[at] = tmp[0:pair].astype(BF16)
        chain_send(24 + 3 * i, 27 + 3 * i)
        if i == 0:
            chain(23, 2)
            projs.relay(0)
            projs.relay(1)
            outs.send_near()
            chain(24, 2)
        elif i == 1:
            chain(25, 2)
            chain(26, 2)
        else:
            chain(27, 2)

    loads["latb"].wait()
    for s in range(samples):
        hot = own_tokens(kept_ref, length, s)
        tmp[pl.ds(s * keep, keep)] = dot(hot, wq[s, pl.ds(0, length)], (0, 0))

    def first_back(s, at):
        @pl.when(at.start == rows // 2)
        def _():
            chain(28, 2)

        hat, inv = normed(tmp[at])
        up_grad = proj[at]
        dx = dx2[at] + norm_back(up_grad * (1.0 + mod[s, 1:2, :]), hat, inv)
        add_row(s * 6, up_grad)
        add_row(s * 6 + 1, up_grad * hat)
        dproj[at] = dx.astype(BF16)

    by_rows(samples, keep, first_back)
    loads["dx"].start()
    chain(29, 2)
    outs.relay(0)
    outs.relay(1)
    chain(30, 2)
    projs.result(gp)
    chain_send(33, 36)
    chain(31, 2)
    outs.result(tmp)

    def end(s, at):
        value = tmp[at] + vec[1:2, :]
        add_row(s * 6 + 5, grad[at] * value)
        dproj[at] = (mixed[at] + mod[s, 5:6, :] * value).astype(BF16)

    loads["dx"].wait()
    by_rows(samples, keep, end)
    loads["y"].start()

    cols = ada_hbm.shape[0]
    wait_send(modc)
    for s in range(samples):
        line = jnp.concatenate([bundle[s * 6 + v : s * 6 + v + 1, :] for v in range(6)], 1)
        for j in range(8):
            mod_send[j, s : s + 1, :] = line[:, j * cols : (j + 1) * cols].astype(BF16).astype(F32)
    mod_in[g] = mod_send[g]
    dmods = to_all(p, wire, mod_in, lambda rel: mod_send.at[p.block(*rel)])
    lines = [dot(ones, dq[j], (1, 1))[0:1, :] for j in range(8)]
    for j in range(8):
        for row, at in ((0, SUM_PROJ), (1, SUM_FC2)):
            share_send[j, row : row + 1, :] = bundle[at : at + 1, j * pair : (j + 1) * pair]
        for e in range(2):
            u = 2 * j + e + (8 if j >= 4 else 0)
            share_send[j, 2 + e : 3 + e, :] = lines[u // 3][:, u % 3 * pair : (u % 3 + 1) * pair]
    share_in[g] = share_send[g]
    small = to_all(p, wire, share_in, lambda rel: share_send.at[p.block(*rel)])
    chain(32, 2)
    chain(33, 2)
    loads["ada1b"].wait()
    loads["ada2b"].wait()
    wait_recv(dmods)
    part = jnp.concatenate([mod_in[j] for j in range(8)], 0).astype(BF16)
    dmod_z[z] = part
    dcvec = dot(part[:, :hidden_units], w1[...], (1, 0)) + dot(part[:, hidden_units:], w2[0:ada_rest], (1, 0))
    depth = cond_all.shape[2]
    for j in range(8):
        dc_send[j] = dcvec[:, j * depth : (j + 1) * depth]
    dc_in[g] = dc_send[g]
    dcs = to_all(p, wire, dc_in, lambda rel: dc_send.at[p.block(*rel)])
    zs.append(to_planes(dmod_z))
    chain(34, 2)
    wait_recv(small)
    sum_z[z, 0:4, :] = sum(share_in[j] for j in range(8))
    for i in range(hidden_units // pair):
        sum_z[z, 4 + i : 5 + i, :] = gb1[:, i * pair : (i + 1) * pair]
    zs.append(to_planes(sum_z))
    chain(35, 2)
    wait_recv(dcs)
    cond = cond_all[g]
    gate = jax.nn.sigmoid(cond)
    dcond_z[z] = sum(dc_in[j] for j in range(8)) * (gate * (1.0 + cond * (1.0 - gate)))
    zs.append(to_planes(dcond_z))

    chain_down(34)
    chain_down(35)
    whole = lambda sem, ref: wire.copy(sem, up_r, ref, ref, (g, partner))

    @pl.when(jnp.logical_not(at_end))
    def _():
        whole(across, out).wait_send()
        whole(down, out).wait_send()

    @pl.when(at_end)
    def _():
        @pl.loop(0, count)
        def _(k):
            go_down(k).wait_recv()
            to_hbm(k).start()

        whole(up, out).wait_send()

    local(out, out_hbm, sems.at[20]).wait()
    for copies in zs:
        wait_recv(copies)
    for name in ("ids", "cvec", "dmod", "sum", "dcond"):
        loads[name].start()
    for copies in zs:
        wait_send(copies)
    for copies in (idc, msgs, conds, moves, dmods, small, dcs):
        wait_send(copies)
    for piece in (tokens, projs, outs):
        piece.finish()
    for name in ("y", "ids", "cvec", "dmod", "sum", "dcond"):
        loads[name].wait()


def run_block(samples, planes, labels, bands, counts, wq, wp, w1, w2, w_ada, lat, cot, biases, kept, class_table, time_table):
    keep, width = kept.shape[1], wq.shape[1]
    rows, hidden, per = samples * keep, w1.shape[0], 8 * samples
    cols, depth = w_ada.shape[0], class_table.shape[0]
    total = 2 * hidden + wq.shape[0] + wp.shape[0]
    count = total // PIECE
    shape, room = jax.ShapeDtypeStruct, pltpu.VMEM
    blocks = room((8, rows, width), BF16)
    plain = room((rows, width), F32)
    over_z = [
        ((planes, per, cols), BF16),
        ((planes, per, depth), F32),
        ((planes, per, width), BF16),
        ((planes, 4 + hidden // depth, depth), F32),
        ((planes, per, 128), F32),
    ]
    sends, recvs = 9 + 2 + 3 + 3 + 8 + 5, 8 * 9 + 2 * 7 + 3 * 18 + 2 * count + 8 + 5
    return pl.pallas_call(
        functools.partial(block_kernel, samples, planes),
        out_shape=[
            shape((total, width), BF16),
            shape((rows, width), BF16),
            shape((rows, width), BF16),
            shape((8,) + wq.shape, BF16),
            *[shape(dims, kind) for dims, kind in over_z],
        ],
        in_specs=[SMEM] * 3 + [ANY] * 7 + [VMEM] * 8,
        out_specs=[ANY] * 9,
        scratch_shapes=[
            *[room(dims, kind) for dims, kind in over_z],
            room((8,) + wq.shape, BF16),
            room((8,) + wp.shape, BF16),
            room(w1.shape, BF16),
            room(w2.shape, BF16),
            blocks,
            blocks,
            blocks,
            room((8, rows, hidden), BF16),
            room((8, rows, hidden), BF16),
            *scatter_scratch(rows, width),
            room((48, HEAD_DIM, rows), BF16),
            room((8, 2 * HEAD_DIM, rows), BF16),
            plain,
            plain,
            plain,
            plain,
            plain,
            room((hidden - 512, width), F32),
            room((rows, width), BF16),
            room((8, wq.shape[0], rows), BF16),
            room((8, wq.shape[0], rows), BF16),
            room((total, width), BF16),
            room((total, width), BF16),
            room((total, width), BF16),
            room((1, hidden), F32),
            room((8, samples, 128), F32),
            room((8, 4, wp.shape[0]), F32),
            room((8, per, depth), F32),
            room((8, samples, cols), F32),
            room((8, samples, cols), F32),
            room((samples, 8, width), F32),
            room((8, width), F32),
            room((8, per, depth), F32),
            room((8, per, depth), F32),
            room((16, width), F32),
            room((8, 4, wp.shape[0]), F32),
            room((8, 4, wp.shape[0]), F32),
            pltpu.SemaphoreType.DMA((sends,)),
            pltpu.SemaphoreType.DMA((recvs,)),
            pltpu.SemaphoreType.REGULAR((2, 3)),
            pltpu.SemaphoreType.DMA((21,)),
        ],
        compiler_params=params(1),
    )(labels, bands, counts, wq, wp, w1, w2, w_ada, lat, cot, *biases, kept, class_table, time_table)


def outputs_kernel(samples, planes, counts_ref, totals_hbm, y_hbm, dx_hbm, lat_hbm, cot_hbm, kept_hbm, dmod_hbm, dcond_hbm,
                   cvec_hbm, sum_hbm, ids_hbm,
                   block_hbm, latg_hbm, g1_hbm, g2_hbm, gq_hbm, gp_hbm, ada_hbm, time_hbm, class_hbm, bada_hbm, qv_hbm, bp_hbm,
                   b1_hbm, b2_hbm,
                   kept_ref, dmod_ref, dcond_ref, cvec_ref, sum_ref, ids_ref, time_out, class_out, bada_out, qv_out, bp_out,
                   b1_out, b2_out, totals, wide, ada, tokens, both, sems_in, sems):
    p = Place()
    length = lat_hbm.shape[1]
    keep = kept_ref.shape[1]
    chunk = 144
    count, width = totals.shape[0] // chunk, totals.shape[1]
    per = 8 * samples
    chunks = [pl.ds(k * chunk, chunk) for k in range(count)]
    ins = [local(totals_hbm.at[at], totals.at[at], sems_in.at[k]) for k, at in enumerate(chunks)]
    ins += [
        local(y_hbm, tokens.at[0], sems_in.at[count]),
        local(dx_hbm, tokens.at[1], sems_in.at[count + 1]),
        local(lat_hbm, both.at[0], sems_in.at[count + 2]),
        local(cot_hbm, both.at[1], sems_in.at[count + 3]),
    ]
    pairs = ((dmod_hbm, dmod_ref), (cvec_hbm, cvec_ref), (kept_hbm, kept_ref), (dcond_hbm, dcond_ref), (sum_hbm, sum_ref), (ids_hbm, ids_ref))
    small = [local(src, dst, sems_in.at[count + 4 + i]) for i, (src, dst) in enumerate(pairs)]
    for copy in small + ins[count:] + ins[:count]:
        copy.start()
    done = []

    def send(src, dst):
        done.append(local(src, dst, sems.at[len(done)]))
        done[-1].start()

    for copy in small:
        copy.wait()
    cvec = jnp.concatenate([cvec_ref[k] for k in range(planes)], 0)
    dmod = jnp.concatenate([dmod_ref[k] for k in range(planes)], 0)
    cols = ada.shape[0]
    for start in range(0, cols, 256):
        size = min(256, cols - start)
        ada[start : start + size] = dot(dmod[:, start : start + size], cvec, (0, 0))
        send(ada.at[pl.ds(start, size)], ada_hbm.at[pl.ds(start, size)])
    bada_out[...] = jnp.sum(dmod.astype(F32), 0)
    send(bada_out, bada_hbm)

    dcond = jnp.concatenate([dcond_ref[k] for k in range(planes)], 0)
    ids = jnp.concatenate([ids_ref[k] for k in range(planes)], 0)

    def one_hot(column, size):
        lanes = lax.broadcasted_iota(jnp.int32, (planes * per, size), 1).astype(F32)
        return jnp.where(lanes == ids[:, column : column + 1], 1.0, 0.0)

    def exact(left, right):
        return lax.dot_general(left, right, (((0,), (0,)), ((), ())), precision=HIGH, preferred_element_type=F32)

    time_out[...] = exact(one_hot(1, time_out.shape[0]), dcond)
    send(time_out, time_hbm)
    class_out[...] = exact(dcond, one_hot(0, class_out.shape[1]))
    send(class_out, class_hbm)
    sums = sum(sum_ref[k] for k in range(planes))
    joined = lambda start, stop: jnp.concatenate([sums[i : i + 1, :] for i in range(start, stop)], 1)
    places = ((bp_out, bp_hbm, 0, 1), (b2_out, b2_hbm, 1, 2), (qv_out, qv_hbm, 2, 4), (b1_out, b1_hbm, 4, sums.shape[0]))
    for out, hbm, start, stop in places:
        out[...] = joined(start, stop).reshape(out.shape[0])
        send(out, hbm)

    for copy in ins[count:]:
        copy.wait()
    for s in range(samples):
        hot = own_tokens(kept_ref, length, s)
        is_kept = jnp.sum(hot.astype(F32), 1, keepdims=True) > 0.5
        at = pl.ds(s * keep, keep)
        both[0, s] = jnp.where(is_kept, dot(hot, tokens[0, at], (1, 0)), both[0, s].astype(F32)).astype(BF16)
        weighted = both[1, s].astype(F32) * sample_weight(p, counts_ref, samples, s)
        both[1, s] = jnp.where(is_kept, dot(hot, tokens[1, at], (1, 0)), weighted).astype(BF16)
    send(both.at[0], block_hbm)
    send(both.at[1], latg_hbm)

    k = 0
    for out in (g1_hbm, g2_hbm, gq_hbm, gp_hbm):
        for start in range(0, out.shape[0], chunk):
            ins[k].wait()
            wide[chunks[k]] = totals[chunks[k]].astype(F32)
            send(wide.at[chunks[k]], out.at[pl.ds(start, chunk)])
            k += 1

    for copy in done:
        copy.wait()


def place_outputs(samples, planes, counts, totals, y, dx, lat, cot, kept, dmod, dcond, cvec, sums, ids, hidden, wq, wp, classes, bands):
    count, width = totals.shape[0] // 144, totals.shape[1]
    cols, depth = dmod.shape[2], dcond.shape[2]
    shape, room = jax.ShapeDtypeStruct, pltpu.VMEM
    wide = lambda size: shape((size, width), F32)
    return pl.pallas_call(
        functools.partial(outputs_kernel, samples, planes),
        out_shape=[
            shape(lat.shape, BF16),
            shape(lat.shape, BF16),
            wide(hidden),
            wide(hidden),
            wide(wq),
            wide(wp),
            wide(cols),
            shape((bands, depth), F32),
            shape((depth, classes), F32),
            shape((cols,), F32),
            shape((2 * wp,), F32),
            shape((wp,), F32),
            shape((hidden,), F32),
            shape((wp,), F32),
        ],
        in_specs=[SMEM] + [ANY] * 11,
        out_specs=[ANY] * 14,
        scratch_shapes=[
            room(kept.shape, jnp.int32),
            room(dmod.shape, BF16),
            room(dcond.shape, F32),
            room(cvec.shape, BF16),
            room(sums.shape, F32),
            room(ids.shape, F32),
            room((bands, depth), F32),
            room((depth, classes), F32),
            room((cols,), F32),
            room((2 * wp,), F32),
            room((wp,), F32),
            room((hidden,), F32),
            room((wp,), F32),
            room(totals.shape, BF16),
            room(totals.shape, F32),
            room((cols, width), F32),
            room((2,) + y.shape, BF16),
            room((2,) + lat.shape, BF16),
            pltpu.SemaphoreType.DMA((count + 10,)),
            pltpu.SemaphoreType.DMA((count + 9 + -(-cols // 256),)),
        ],
        compiler_params=pltpu.CompilerParams(vmem_limit_bytes=63 * 2**20),
    )(counts, totals, y, dx, lat, cot, kept, dmod, dcond, cvec, sums, ids)


def plane_body(planes, latents, cotangent, bands, labels, kept, band_counts, time_table, class_table, w_ada, b_ada, w_qkv,
               qv_bias, w_proj, b_proj, w_fc1, b_fc1, w_fc2, b_fc2):
    samples, length, width = latents.shape
    wq = w_qkv.shape[1]
    wp = w_proj.shape[0]
    hidden = w_fc1.shape[1]

    totals, y, dx, unused_weights, dmod, dcond, cvec, sums, ids = run_block(
        samples, planes, labels, bands, band_counts, w_qkv.T, w_proj, w_fc1.T, w_fc2, w_ada.T, latents, cotangent,
        (b_proj, b_fc2, qv_bias, b_ada, b_fc1), kept, class_table.T, time_table
    )
    block_out, latents_grad, g1, g2, gq, gp, ada, time, classes, bada, qv, bp, b1, b2 = place_outputs(
        samples, planes, band_counts, totals, y, dx, latents, cotangent, kept, dmod, dcond, cvec, sums, ids, hidden, wq, wp,
        class_table.shape[0], time_table.shape[0]
    )
    return (block_out, latents_grad, time, classes.T, ada.T, bada, gq.T, qv, gp, bp, g1.T, b1, g2, b2)


def solution(mesh):
    planes = mesh.shape["dp"]
    small = mesh.shape["grp"] == 8 and planes == 4
    return jax.shard_map(
        functools.partial(plane_body, planes) if small else body,
        mesh=mesh,
        in_specs=(
            P(("grp", "dp"), None, None),
            P(("grp", "dp"), None, None),
            P(("grp", "dp")),
            P(("grp", "dp")),
            P(("grp", "dp"), None),
            P("grp"),
            P(None, "grp"),
            P(None, "grp"),
            P(None, "grp"),
            P("grp"),
            P(None, "grp"),
            P("grp"),
            P("grp", None),
            P("grp"),
            P(None, "grp"),
            P("grp"),
            P("grp", None),
            P("grp"),
        ),
        out_specs=(
            P(("grp", "dp"), None, None),
            P(("grp", "dp"), None, None),
            P(None, "grp"),
            P(None, "grp"),
            P(None, "grp"),
            P("grp"),
            P(None, "grp"),
            P("grp"),
            P("grp", None),
            P("grp"),
            P(None, "grp"),
            P("grp"),
            P("grp", None),
            P("grp"),
        ),
        check_vma=False,
    )
```

```python
import functools

import jax
import jax.numpy as jnp
from jax import lax
from jax.experimental import pallas as pl
from jax.experimental.pallas import tpu as pltpu
from jax.sharding import PartitionSpec as P

HEADS = 16
HEAD_DIM = 72


EPS = 1e-06
HIGH = lax.Precision.HIGHEST


def modulate(values, shift, scale):
    mean = jnp.mean(values, -1, keepdims=True)
    cent = values - mean
    var = jnp.mean(cent * cent, -1, keepdims=True)
    return cent * lax.rsqrt(var + EPS) * (1.0 + scale[:, None, :]) + shift[:, None, :]


def product(left, right):
    return jnp.einsum("btd,de->bte", left, right, preferred_element_type=jnp.float32)


def weight_term(left, right):
    return jnp.einsum("btd,bte->de", left, right, preferred_element_type=jnp.float32)


def core(weights, tokens, mod):
    w_qkv, qv_bias, w_proj, b_proj, w_fc1, b_fc1, w_fc2, b_fc2 = weights
    count, length, width = tokens.shape
    shift1, scale1, gate1, shift2, scale2, gate2 = jnp.split(mod, 6, -1)
    h1 = modulate(tokens, shift1, scale1).astype(jnp.bfloat16)
    bias = jnp.concatenate(
        [
            qv_bias[:width].astype(jnp.float32),
            jnp.zeros((width,), jnp.float32),
            qv_bias[width:].astype(jnp.float32),
        ]
    )
    qkv = (product(h1, w_qkv) + bias).astype(jnp.bfloat16)
    query = qkv[..., :width].reshape(count, length, HEADS, HEAD_DIM)
    keys = qkv[..., width : 2 * width].reshape(count, length, HEADS, HEAD_DIM)
    values = qkv[..., 2 * width :].reshape(count, length, HEADS, HEAD_DIM)
    scores = jnp.einsum(
        "bqhd,bkhd->bhqk", query, keys, preferred_element_type=jnp.float32
    ) * HEAD_DIM ** (-0.5)
    total = jax.scipy.special.logsumexp(scores, axis=-1, keepdims=True)
    probs_full = jnp.exp(scores - total)
    probs = probs_full.astype(jnp.bfloat16)
    att = (
        jnp.einsum("bhqk,bkhd->bqhd", probs, values, preferred_element_type=jnp.float32)
        .reshape(count, length, width)
        .astype(jnp.bfloat16)
    )
    proj = product(att, w_proj) + b_proj.astype(jnp.float32)
    mixed = tokens + gate1[:, None, :] * proj
    h2 = modulate(mixed, shift2, scale2).astype(jnp.bfloat16)
    pre = product(h2, w_fc1) + b_fc1.astype(jnp.float32)
    act = jax.nn.gelu(pre, approximate=True).astype(jnp.bfloat16)
    mlp = product(act, w_fc2) + b_fc2.astype(jnp.float32)
    result = mixed + gate2[:, None, :] * mlp
    saved = (h1, query, keys, values, probs_full, probs, att, proj, mixed, h2, pre, act, mlp)
    return (result, saved)


def body(
    latents,
    cotangent,
    bands,
    labels,
    kept,
    band_counts,
    time_table,
    class_table,
    w_ada,
    b_ada,
    w_qkv,
    qv_bias,
    w_proj,
    b_proj,
    w_fc1,
    b_fc1,
    w_fc2,
    b_fc2,
):
    gathered = (
        lax.all_gather(time_table, "grp", axis=1, tiled=True),
        lax.all_gather(class_table, "grp", axis=1, tiled=True),
        lax.all_gather(w_ada, "grp", axis=1, tiled=True),
        lax.all_gather(b_ada, "grp", axis=0, tiled=True),
        lax.all_gather(w_qkv, "grp", axis=1, tiled=True),
        lax.all_gather(qv_bias, "grp", axis=0, tiled=True),
        lax.all_gather(w_proj, "grp", axis=0, tiled=True),
        lax.all_gather(b_proj, "grp", axis=0, tiled=True),
        lax.all_gather(w_fc1, "grp", axis=1, tiled=True),
        lax.all_gather(b_fc1, "grp", axis=0, tiled=True),
        lax.all_gather(w_fc2, "grp", axis=0, tiled=True),
        lax.all_gather(b_fc2, "grp", axis=0, tiled=True),
    )
    time_full, class_full, ada_full, ada_bias = (gathered[0], gathered[1], gathered[2], gathered[3])
    samples = latents.shape[0]
    width = latents.shape[2]
    slot = lax.axis_index("dp") * samples + jnp.arange(samples, dtype=jnp.int32)
    group_count = band_counts[0]
    weight = jnp.where(slot < group_count, 1.0, 0.0).astype(jnp.float32) / group_count.astype(
        jnp.float32
    )
    band_hot = (bands[:, None] == jnp.arange(time_full.shape[0], dtype=jnp.int32)[None, :]).astype(
        jnp.float32
    )
    class_hot = (
        labels[:, None] == jnp.arange(class_full.shape[0], dtype=jnp.int32)[None, :]
    ).astype(jnp.float32)
    cond = jnp.dot(band_hot, time_full.astype(jnp.float32), precision=HIGH) + jnp.dot(
        class_hot, class_full.astype(jnp.float32), precision=HIGH
    )
    cvec = jax.nn.silu(cond).astype(jnp.bfloat16)
    mod = jnp.dot(cvec, ada_full, preferred_element_type=jnp.float32) + ada_bias.astype(jnp.float32)
    rows = jnp.arange(samples, dtype=jnp.int32)[:, None]
    tokens = jnp.take_along_axis(latents, kept[:, :, None], 1).astype(jnp.float32)
    result, unused = core(tuple(gathered[4:]), tokens, mod)
    block_out = latents.at[rows, kept].set(result.astype(jnp.bfloat16))
    fetched = (
        lax.all_gather(w_ada, "grp", axis=1, tiled=True),
        lax.all_gather(w_qkv, "grp", axis=1, tiled=True),
        lax.all_gather(qv_bias, "grp", axis=0, tiled=True),
        lax.all_gather(w_proj, "grp", axis=0, tiled=True),
        lax.all_gather(b_proj, "grp", axis=0, tiled=True),
        lax.all_gather(w_fc1, "grp", axis=1, tiled=True),
        lax.all_gather(b_fc1, "grp", axis=0, tiled=True),
        lax.all_gather(w_fc2, "grp", axis=0, tiled=True),
        lax.all_gather(b_fc2, "grp", axis=0, tiled=True),
    )
    ada_full = fetched[0]
    back = tuple(fetched[1:])
    qkv_full, unused_bias, proj_full, unused_pbias, fc1_full, unused_b1, fc2_full, unused_b2 = back
    result, saved = core(back, tokens, mod)
    h1, query, keys, values, probs_full, probs, att, proj, mixed, h2, pre, act, mlp = saved
    shift1, scale1, gate1, shift2, scale2, gate2 = jnp.split(mod, 6, -1)
    weighted = cotangent.astype(jnp.float32) * weight[:, None, None]
    grad_out = jnp.take_along_axis(weighted, kept[:, :, None], 1)
    grad_mlp = (gate2[:, None, :] * grad_out).astype(jnp.bfloat16)
    grad_gate2 = jnp.sum(grad_out * mlp, 1)
    fc2_grad = weight_term(act, grad_mlp)
    fc2_bias_grad = jnp.sum(grad_mlp.astype(jnp.float32), (0, 1))
    grad_act = jnp.einsum("bte,de->btd", grad_mlp, fc2_full, preferred_element_type=jnp.float32)
    unused_pre, gelu_back = jax.vjp(lambda value: jax.nn.gelu(value, approximate=True), pre)
    grad_pre = gelu_back(grad_act)[0].astype(jnp.bfloat16)
    fc1_grad = weight_term(h2, grad_pre)
    fc1_bias_grad = jnp.sum(grad_pre.astype(jnp.float32), (0, 1))
    grad_h2 = jnp.einsum("bte,de->btd", grad_pre, fc1_full, preferred_element_type=jnp.float32)
    unused_h2, norm_back = jax.vjp(modulate, mixed, shift2, scale2)
    grad_mixed, grad_shift2, grad_scale2 = norm_back(grad_h2)
    grad_mixed = grad_mixed + grad_out
    grad_proj = (gate1[:, None, :] * grad_mixed).astype(jnp.bfloat16)
    grad_gate1 = jnp.sum(grad_mixed * proj, 1)
    proj_grad = weight_term(att, grad_proj)
    proj_bias_grad = jnp.sum(grad_proj.astype(jnp.float32), (0, 1))
    grad_att = jnp.einsum(
        "bte,de->btd", grad_proj, proj_full, preferred_element_type=jnp.float32
    ).astype(jnp.bfloat16)
    grad_heads = grad_att.reshape(query.shape)
    grad_values = jnp.einsum(
        "bhqk,bqhd->bkhd", probs, grad_heads, preferred_element_type=jnp.float32
    )
    grad_probs = jnp.einsum(
        "bqhd,bkhd->bhqk", grad_heads, values, preferred_element_type=jnp.float32
    )
    grad_scores = probs_full * (grad_probs - jnp.sum(grad_probs * probs_full, -1, keepdims=True))
    grad_scores = grad_scores.astype(jnp.bfloat16)
    grad_query = jnp.einsum(
        "bhqk,bkhd->bqhd", grad_scores, keys, preferred_element_type=jnp.float32
    ) * HEAD_DIM ** (-0.5)
    grad_keys = jnp.einsum(
        "bhqk,bqhd->bkhd", grad_scores, query, preferred_element_type=jnp.float32
    ) * HEAD_DIM ** (-0.5)
    count, length = (tokens.shape[0], tokens.shape[1])
    grad_qkv = jnp.concatenate(
        [
            grad_query.reshape(count, length, width),
            grad_keys.reshape(count, length, width),
            grad_values.reshape(count, length, width),
        ],
        -1,
    ).astype(jnp.bfloat16)
    qkv_grad = weight_term(h1, grad_qkv)
    qkv_sums = jnp.sum(grad_qkv.astype(jnp.float32), (0, 1))
    qv_bias_grad = jnp.concatenate([qkv_sums[:width], qkv_sums[2 * width :]])
    grad_h1 = jnp.einsum("bte,de->btd", grad_qkv, qkv_full, preferred_element_type=jnp.float32)
    unused_h1, first_back = jax.vjp(modulate, tokens, shift1, scale1)
    grad_tokens, grad_shift1, grad_scale1 = first_back(grad_h1)
    grad_tokens = grad_tokens + grad_mixed
    latents_grad = weighted.at[rows, kept].set(grad_tokens).astype(jnp.bfloat16)
    grad_mod = jnp.concatenate(
        [grad_shift1, grad_scale1, grad_gate1, grad_shift2, grad_scale2, grad_gate2], -1
    ).astype(jnp.bfloat16)
    ada_grad = jnp.dot(cvec.T, grad_mod, preferred_element_type=jnp.float32)
    ada_bias_grad = jnp.sum(grad_mod.astype(jnp.float32), 0)
    grad_cvec = jnp.dot(grad_mod, ada_full.T, preferred_element_type=jnp.float32)
    unused_cond, silu_back = jax.vjp(jax.nn.silu, cond)
    grad_cond = silu_back(grad_cvec)[0]
    time_grad = jnp.dot(band_hot.T, grad_cond, precision=HIGH)
    class_grad = jnp.dot(class_hot.T, grad_cond, precision=HIGH)
    shares = (
        lax.psum_scatter(time_grad, "grp", scatter_dimension=1, tiled=True),
        lax.psum_scatter(class_grad, "grp", scatter_dimension=1, tiled=True),
        lax.psum_scatter(ada_grad, "grp", scatter_dimension=1, tiled=True),
        lax.psum_scatter(ada_bias_grad, "grp", scatter_dimension=0, tiled=True),
        lax.psum_scatter(qkv_grad, "grp", scatter_dimension=1, tiled=True),
        lax.psum_scatter(qv_bias_grad, "grp", scatter_dimension=0, tiled=True),
        lax.psum_scatter(proj_grad, "grp", scatter_dimension=0, tiled=True),
        lax.psum_scatter(proj_bias_grad, "grp", scatter_dimension=0, tiled=True),
        lax.psum_scatter(fc1_grad, "grp", scatter_dimension=1, tiled=True),
        lax.psum_scatter(fc1_bias_grad, "grp", scatter_dimension=0, tiled=True),
        lax.psum_scatter(fc2_grad, "grp", scatter_dimension=0, tiled=True),
        lax.psum_scatter(fc2_bias_grad, "grp", scatter_dimension=0, tiled=True),
    )
    totals = (
        lax.psum(shares[0].astype(jnp.bfloat16), "dp").astype(jnp.float32),
        lax.psum(shares[1].astype(jnp.bfloat16), "dp").astype(jnp.float32),
        lax.psum(shares[2].astype(jnp.bfloat16), "dp").astype(jnp.float32),
        lax.psum(shares[3].astype(jnp.bfloat16), "dp").astype(jnp.float32),
        lax.psum(shares[4].astype(jnp.bfloat16), "dp").astype(jnp.float32),
        lax.psum(shares[5].astype(jnp.bfloat16), "dp").astype(jnp.float32),
        lax.psum(shares[6].astype(jnp.bfloat16), "dp").astype(jnp.float32),
        lax.psum(shares[7].astype(jnp.bfloat16), "dp").astype(jnp.float32),
        lax.psum(shares[8].astype(jnp.bfloat16), "dp").astype(jnp.float32),
        lax.psum(shares[9].astype(jnp.bfloat16), "dp").astype(jnp.float32),
        lax.psum(shares[10].astype(jnp.bfloat16), "dp").astype(jnp.float32),
        lax.psum(shares[11].astype(jnp.bfloat16), "dp").astype(jnp.float32),
    )
    return (
        block_out,
        latents_grad,
        totals[0],
        totals[1],
        totals[2],
        totals[3],
        totals[4],
        totals[5],
        totals[6],
        totals[7],
        totals[8],
        totals[9],
        totals[10],
        totals[11],
    )


MESH = pl.DeviceIdType.MESH
F32 = jnp.float32
BF16 = jnp.bfloat16
GELU_A = 0.7978845608028654
GELU_B = 0.044715


def dot(left, right, dims):
    return lax.dot_general(left, right, ((dims[:1], dims[1:]), ((), ())), preferred_element_type=F32)


class Place:
    def __init__(self):
        self.g = lax.axis_index("grp")
        self.z = lax.axis_index("dp")
        self.c = self.g % 2
        self.x = (self.g // 2) % 2
        self.y = self.g // 4

    def block(self, dc, dx, dy):
        c = 1 - self.c if dc else self.c
        x = 1 - self.x if dx else self.x
        y = 1 - self.y if dy else self.y
        return y * 4 + x * 2 + c

    def device(self, dc, dx, dy):
        return (self.block(dc, dx, dy), self.z)


RELATIVE = [(r & 1, (r >> 1) & 1, r >> 2) for r in range(8)]


class Wire:
    def __init__(self, send, recv):
        self.send, self.recv, self.sends, self.recvs = send, recv, 0, 0

    def take(self, recvs, sends=1):
        first = (self.sends, self.recvs)
        self.sends += sends
        self.recvs += recvs
        return first

    def copy(self, send, recv, src, dst, device):
        return pltpu.make_async_remote_copy(
            src_ref=src,
            dst_ref=dst,
            send_sem=self.send.at[send],
            recv_sem=self.recv.at[recv],
            device_id=device,
            device_id_type=MESH,
        )


def halves(rows):
    cut = rows // 32 * 16
    return pl.ds(0, cut), pl.ds(cut, rows - cut)


def greet(devices):
    barrier = pltpu.get_barrier_semaphore()
    for device in devices:
        pl.semaphore_signal(barrier, inc=1, device_id=device, device_id_type=MESH)
    pl.semaphore_wait(barrier, len(devices))


def plane(place):
    return [place.device(*rel) for rel in RELATIVE[1:]]


class Gather:
    def __init__(self, place, wire, buf, start=0, rows=None, origin=None):
        p = place
        rows = rows or buf.shape[1]
        lo, hi = halves(rows)
        parts = (pl.ds(start, rows), pl.ds(start, lo.size), pl.ds(start + lo.size, hi.size))
        send, recv = wire.take(8)

        def make(number, block, device, part=0):
            ref = buf.at[block, parts[part]]
            src = origin if number < 3 and origin is not None else ref
            return wire.copy(send, recv + number, src, ref, device)

        own, xb, yb, db = p.g, p.block(0, 1, 0), p.block(0, 0, 1), p.block(0, 1, 1)
        xd, yd, sd = p.device(0, 1, 0), p.device(0, 0, 1), p.device(1, 0, 0)
        self.c = [
            make(0, own, xd),
            make(1, own, yd),
            make(2, own, sd),
            make(3, xb, yd, 1),
            make(4, xb, sd),
            make(5, yb, xd, 2),
            make(6, yb, sd),
            make(7, db, sd),
        ]
        seven = buf.at[pl.ds(0, 7), parts[0]]
        self.sent = wire.copy(send, recv, seven, seven, sd)

    def start(self):
        for number in (0, 1, 2):
            self.c[number].start()

    def arrived(self):
        self.c[0].wait_recv()
        self.c[1].wait_recv()
        self.c[4].start()
        self.c[6].start()

    def forward(self):
        self.c[3].start()
        self.c[5].start()

    def neighbours(self):
        self.arrived()
        self.forward()

    def far(self):
        self.c[3].wait_recv()
        self.c[5].wait_recv()
        self.c[7].start()

    def wait_sib(self):
        self.c[2].wait_recv()

    def wait_sib_neighbours(self):
        self.c[4].wait_recv()
        self.c[6].wait_recv()

    def wait_sib_far(self):
        self.c[7].wait_recv()

    def finish(self):
        self.sent.wait_send()


class Halves:
    def __init__(self, place, wire, buf):
        self.lo, self.hi = [Gather(place, wire, buf, part.start, part.size) for part in halves(buf.shape[1])]

    def start(self):
        for number in (0, 1, 2):
            self.lo.c[number].start()
        for number in (0, 1, 2):
            self.hi.c[number].start()

    def far(self):
        self.lo.far()
        self.hi.far()

    def wait_sib(self):
        self.lo.wait_sib()
        self.hi.wait_sib()

    def wait_sib_neighbours(self):
        self.lo.wait_sib_neighbours()
        self.hi.wait_sib_neighbours()

    def wait_sib_far(self):
        self.lo.wait_sib_far()
        self.hi.wait_sib_far()

    def finish(self):
        self.lo.finish()
        self.hi.finish()


class OverZ:
    def __init__(self, place, wire, buf, hbm, there, ahead, behind, rows):
        p = place
        near = [p.block(0, 1, 0), p.block(0, 0, 1), p.block(0, 1, 1)]
        sd = p.device(1, 0, 0)
        sem, recv = wire.take(7)
        send, take = pl.ds(ahead, rows), pl.ds(behind, rows)
        self.out = [wire.copy(sem, recv + i, buf.at[b, send], buf.at[b, send], there) for i, b in enumerate(near)]
        self.on = [wire.copy(sem, recv + 3 + i, buf.at[b, take], buf.at[b, take], sd) for i, b in enumerate(near)]
        self.own = wire.copy(sem, recv + 6, hbm.at[take], buf.at[p.g, take], sd)
        seven = buf.at[pl.ds(0, 7), send]
        self.sent = wire.copy(sem, recv, seven, seven, sd)

    def pass_on(self, *numbers):
        for i in numbers:
            self.out[i].wait_recv()
            self.on[i].start()

    def arrived(self, *numbers):
        for i in numbers:
            self.on[i].wait_recv()

    def finish(self):
        self.sent.wait_send()


class Scatter:
    def __init__(self, place, wire, buf, r1, r2, r3, rows=None):
        self.p, self.w, self.buf = place, wire, buf
        self.r1, self.r2, self.r3 = r1, r2, r3
        self.rows = rows = rows or buf.shape[1]
        p, w = place, wire
        self.sib = [p.block(1, q & 1, q >> 1) for q in range(4)]
        self.mine = [p.block(0, q & 1, q >> 1) for q in range(4)]
        xd, yd, sd = p.device(0, 1, 0), p.device(0, 0, 1), p.device(1, 0, 0)
        sem, recv = wire.take(18)
        whole = pl.ds(0, rows)
        lo, hi = halves(rows)
        self.parts = [[pl.ds(half.start + cut.start, cut.size) for cut in halves(half.size)] for half in (lo, hi)]
        self.lo_hi = (lo, hi)
        self.s1 = [
            [w.copy(sem, recv + 10 + 2 * q + i, buf.at[self.sib[q], part], r1.at[q, part], sd) for i, part in enumerate((lo, hi))]
            for q in range(4)
        ]
        self.s2, self.s3 = [], []
        for way, device in ((0, xd), (1, yd)):
            for i, part in enumerate(self.parts[way]):
                number = recv + 2 * way + i
                self.s2.append(w.copy(sem, number, buf.at[self.mine[3], part], r2.at[way, pl.ds(part.start - self.parts[way][0].start, part.size)], device))
        for way, device in ((0, xd), (1, yd)):
            direct = (lo, hi)[way]
            for i, part in enumerate([direct] + self.parts[1 - way]):
                number = recv + 4 + 3 * way + i
                self.s3.append(w.copy(sem, number, buf.at[self.mine[1 + way], part], r3.at[way, part], device))
        seven = buf.at[pl.ds(0, 7), whole]
        self.sent = wire.copy(sem, recv, seven, seven, sd)

    def send_sib(self, q, halves_of=(0, 1)):
        for i in halves_of:
            self.s1[q][i].start()

    def add_sib(self, q, halves_of=(0, 1)):
        for i in halves_of:
            self.s1[q][i].wait_recv()
            add_into(self.buf.at[self.mine[q], self.lo_hi[i]], self.r1.at[q, self.lo_hi[i]])

    def send_far(self):
        self.add_sib(3)
        for number in (0, 2, 1, 3):
            self.s2[number].start()

    def near(self, way):
        self.add_sib(1 + way, (way,))
        self.s3[3 * way].start()

    def send_near(self):
        self.near(0)
        self.near(1)

    def relay(self, i):
        if i == 0:
            self.add_sib(1, (1,))
            self.add_sib(2, (0,))
        for way in range(2):
            self.s2[2 * way + i].wait_recv()
            part = self.parts[way][i]
            came = self.r2.at[way, pl.ds(part.start - self.parts[way][0].start, part.size)]
            add_into(self.buf.at[self.mine[2 - way], part], came)
            self.s3[3 * (1 - way) + 1 + i].start()
        if i == 1:
            self.add_sib(0)

    def result(self, out):
        for copy in self.s3:
            copy.wait_recv()
        step = 16

        @pl.loop(0, self.rows // step)
        def _(i):
            at = pl.ds(pl.multiple_of(i * step, step), step)
            total = self.buf[self.mine[0], at].astype(F32) + self.r3[0, at].astype(F32) + self.r3[1, at].astype(F32)
            out[at] = total.astype(out.dtype)

    def finish(self):
        self.sent.wait_send()


def add_into(ref, other):
    step = 16

    @pl.loop(0, ref.shape[0] // step)
    def _(i):
        at = pl.ds(pl.multiple_of(i * step, step), step)
        ref[at] = (ref[at].astype(F32) + other[at].astype(F32)).astype(ref.dtype)


def scatter_scratch(rows, width):
    return [
        pltpu.VMEM((4, rows, width), BF16),
        pltpu.VMEM((2, halves(rows)[1].size, width), BF16),
        pltpu.VMEM((2, rows, width), BF16),
    ]


class Together:
    def __init__(self, wire, buf, pairs, device):
        send, recv = wire.take(1)
        count = len(pairs)
        for src, dst, target in pairs:
            wire.copy(send, recv, src, dst, target).start()
        all_blocks = buf.at[pl.ds(0, count)]
        self.all = wire.copy(send, recv, all_blocks, all_blocks, device)


def to_all(place, wire, buf, make):
    pairs = [(make(rel), buf.at[place.g], place.device(*rel)) for rel in RELATIVE[1:]]
    return Together(wire, buf, pairs, place.device(1, 0, 0))


def wait_recv(copies):
    copies.all.wait_recv()


def wait_send(copies):
    copies.all.wait_send()


def params(collective_id):
    return pltpu.CompilerParams(
        collective_id=collective_id, has_side_effects=True, vmem_limit_bytes=63 * 2**20
    )


VMEM = pl.BlockSpec(memory_space=pltpu.VMEM)

def gelu_parts(pre):
    square = pre * pre
    half = 0.5 + 0.5 * jnp.tanh(pre * (GELU_A + GELU_A * GELU_B * square))
    act = pre * half
    slope = half + (act - act * half) * (2.0 * GELU_A + 6.0 * GELU_A * GELU_B * square)
    return act, slope


def local(src, dst, sem):
    return pltpu.make_async_copy(src, dst, sem)


def own_tokens(kept_ref, length, s):
    rows = lax.broadcasted_iota(jnp.int32, (length, kept_ref.shape[1]), 0)
    return jnp.where(rows == kept_ref[s : s + 1, :], 1.0, 0.0).astype(BF16)


def normed(v):
    cent = v - jnp.mean(v, -1, keepdims=True)
    inv = lax.rsqrt(jnp.mean(cent * cent, -1, keepdims=True) + EPS)
    return cent * inv, inv


def norm_back(grad, hat, inv):
    return inv * (grad - jnp.mean(grad, -1, keepdims=True) - hat * jnp.mean(grad * hat, -1, keepdims=True))


STEP = 32


def by_rows(samples, keep, fn):
    @pl.loop(0, samples * keep // STEP)
    def _(i):
        fn(lax.div(i, keep // STEP), pl.ds(pl.multiple_of(i * STEP, STEP), STEP))


SCALE = HEAD_DIM ** (-0.5)


def probabilities(q, k):
    scores = dot(k, q, (0, 0)) * SCALE
    exps = jnp.exp(scores - jnp.max(scores, 0, keepdims=True))
    return exps / jnp.sum(exps, 0, keepdims=True)


def arrival(p, t, last=7):
    dc = jnp.where((t == 1) | (t == 4) | (t == 5) | (t == last), 1, 0)
    dx = jnp.where((t == 2) | (t == 4) | (t >= 6), 1, 0)
    dy = jnp.where((t == 3) | (t >= 5), 1, 0)
    c, x, y = lax.rem(p.c + dc, 2), lax.rem(p.x + dx, 2), lax.rem(p.y + dy, 2)
    return y * 4 + x * 2 + c


def sample_weight(place, counts_ref, samples, s):
    count = jnp.full((1, 128), counts_ref[0], jnp.int32)
    used = count > place.z * samples + s
    return (jnp.where(used, 1.0, 0.0) / count.astype(F32))[:, 0:1]


ANY = pl.BlockSpec(memory_space=pltpu.HBM)
SMEM = pl.BlockSpec(memory_space=pltpu.SMEM)
PIECE = 48


def block_kernel(samples, planes, labels_ref, bands_ref, counts_ref, wq_hbm, wp_hbm, w1_hbm, w2_hbm, ada_hbm, lat_hbm, cot_hbm,
                 bp_hbm, b2_hbm, qv_hbm, bada_hbm, b1_hbm, kept_hbm, class_hbm, time_hbm,
                 out_hbm, y_hbm, dx_hbm, wq_keep, dmod_hbm, dcond_hbm, cvec_hbm, sum_hbm, ids_hbm,
                 bp_ref, b2_ref, qv_ref, bada_ref, b1_ref, kept_ref, class_ref, time_ref,
                 dmod_z, dcond_z, cvec_z, sum_z, ids_z,
                 wq, wp, w1, w2, h1_all, h2_all, dm_all, act, dpre, p1, p2, p3, units, att, mixed, proj, grad, dx2, tmp, rest,
                 dproj, dq, dq_all, from_end, out, grads, gb1, ids_all, msg_all, cond_all, mod_in, mod_send, mod, vec,
                 dc_send, dc_in, bundle, share_send, share_in, send, recv, credits, sems):
    p = Place()
    wire = Wire(send, recv)
    g, z = p.g, p.z
    others = [(g, (z + k) % planes) for k in range(1, planes)]
    smalls = (
        (bp_hbm, bp_ref),
        (b2_hbm, b2_ref),
        (qv_hbm, qv_ref),
        (bada_hbm, bada_ref),
        (b1_hbm, b1_ref),
        (kept_hbm, kept_ref),
        (class_hbm, class_ref),
        (time_hbm, time_ref),
    )
    early = [local(src, dst, sems.at[21 + i]) for i, (src, dst) in enumerate(smalls)]
    for copy in early:
        copy.start()
    greet(plane(p) + others)
    for copy in early:
        copy.wait()
    length = lat_hbm.shape[1]
    keep = kept_ref.shape[1]
    rows, width = mixed.shape
    pair = 2 * HEAD_DIM
    hidden_units = act.shape[2]
    ada_rest = ada_hbm.shape[0] - hidden_units

    loads = {}
    for number, (name, src, dst) in enumerate((
        ("wq", wq_hbm, wq.at[g]),
        ("wp", wp_hbm, wp.at[g]),
        ("lat", lat_hbm, h2_all.at[pl.ds(0, samples)]),
        ("cot", cot_hbm, h2_all.at[pl.ds(samples, samples)]),
        ("ada1", ada_hbm.at[pl.ds(0, hidden_units)], w1),
        ("ada2", ada_hbm.at[pl.ds(hidden_units, ada_rest)], w2.at[pl.ds(0, ada_rest)]),
        ("w1", w1_hbm, w1),
        ("w2", w2_hbm, w2),
        ("keep", wq, wq_keep),
        ("again", wq_keep, wq),
        ("ada1b", ada_hbm.at[pl.ds(0, hidden_units)], w1),
        ("ada2b", ada_hbm.at[pl.ds(hidden_units, ada_rest)], w2.at[pl.ds(0, ada_rest)]),
        ("latb", lat_hbm, wq.at[pl.ds(0, samples), pl.ds(0, length)]),
        ("dx", dproj, dx_hbm),
        ("y", dproj, y_hbm),
        ("dmod", dmod_z, dmod_hbm),
        ("dcond", dcond_z, dcond_hbm),
        ("cvec", cvec_z, cvec_hbm),
        ("sum", sum_z, sum_hbm),
        ("ids", ids_z, ids_hbm),
    )):
        loads[name] = local(src, dst, sems.at[number])
    odd = z % 2
    there = (g, z + 1 - 2 * odd)
    gather_a = Gather(p, wire, wq, 2 * pair * odd, pair, wq_hbm.at[pl.ds(2 * pair * odd, pair)])
    gather_m = Gather(p, wire, wq, pair, pair, wq_hbm.at[pl.ds(pair, pair)])
    qkv_z = OverZ(p, wire, wq, wq_hbm, there, 2 * pair * odd, 2 * pair * (1 - odd), pair)
    inside = pair // 32 * 16 + 16
    beyond = pair - inside
    outward = Gather(p, wire, wp, beyond * odd, inside, wp_hbm.at[pl.ds(beyond * odd, inside)])
    proj_z = OverZ(p, wire, wp, wp_hbm, there, inside * odd, inside * (1 - odd), beyond)
    main = Halves(p, wire, h2_all)
    back = Halves(p, wire, dm_all)
    tokens = Halves(p, wire, h1_all)
    sums = Scatter(p, wire, wq, p1, p2, p3, rows)
    outs = Scatter(p, wire, h2_all, dm_all.at[pl.ds(0, 4)], dm_all.at[pl.ds(4, 2)], dm_all.at[pl.ds(6, 2)])
    projs = Scatter(p, wire, wp, p1, p2, p3)
    part_of = lambda start, size: grads.at[pl.ds(start, size)]
    g1, g2 = part_of(0, hidden_units), part_of(hidden_units, hidden_units)
    gq, gp = part_of(2 * hidden_units, 3 * pair), part_of(2 * hidden_units + 3 * pair, pair)
    count = grads.shape[0] // PIECE
    (up, up_r), (across, across_r), (down, _) = [wire.take(recvs) for recvs in (count, count, 0)]
    inner, outer, partner = 1 + z // 3, (z - 1) * 3, 3 - z
    at_end = (z == 0) | (z == planes - 1)
    rows_of = lambda ref, k: ref.at[pl.ds(pl.multiple_of(k * PIECE, 16), PIECE)]
    go_up = lambda k: wire.copy(up, up_r + k, rows_of(grads, k), rows_of(from_end, k), (g, inner))
    go_across = lambda k: wire.copy(across, across_r + k, rows_of(from_end, k), rows_of(out, k), (g, partner))
    go_down = lambda k: wire.copy(down, up_r + k, rows_of(out, k), rows_of(out, k), (g, outer))
    to_hbm = lambda k: local(rows_of(out, k), rows_of(out_hbm, k), sems.at[20])

    def chain_send(first, last):
        @pl.when(at_end)
        def _():
            for k in range(first, last):
                go_up(k).start()

    def chain_up(k):
        @pl.when(jnp.logical_not(at_end))
        def _():
            go_up(k).wait_recv()
            add_into(rows_of(from_end, k), rows_of(grads, k))
            go_across(k).start()

    def chain_down(k):
        @pl.when(jnp.logical_not(at_end))
        def _():
            go_across(k).wait_recv()
            add_into(rows_of(out, k), rows_of(from_end, k))
            go_down(k).start()
            to_hbm(k).start()

    def chain(k, lag):
        chain_up(k)
        chain_down(k - lag)

    def to_planes(ref):
        return Together(wire, ref, [(ref.at[z], ref.at[z], device) for device in others], others[0])

    neighbours = [p.device(1, 0, 0), p.device(0, 1, 0), p.device(0, 0, 1)]

    def grant(number):
        for i, device in enumerate(neighbours):
            pl.semaphore_signal(credits.at[number, i], inc=1, device_id=device, device_id_type=MESH)

    def granted(number):
        for i in range(3):
            pl.semaphore_wait(credits.at[number, i], 1)

    lanes = lax.broadcasted_iota(jnp.int32, (1, 128), 1)
    for s in range(samples):
        line = jnp.where(lanes == 0, labels_ref[s], 0) + jnp.where(lanes == 1, bands_ref[s], 0)
        ids_all[g, s : s + 1, :] = line.astype(F32)
    line_of = lambda ref: ref[...].astype(F32).reshape(1, ref.shape[0])
    b_ada, b1, qv = line_of(bada_ref), line_of(b1_ref), line_of(qv_ref)
    for row, line in enumerate((line_of(bp_ref), line_of(b2_ref), qv[:, :pair], qv[:, pair:])):
        msg_all[g, row : row + 1, :] = line
    idc = to_all(p, wire, ids_all, lambda rel: ids_all.at[g])
    gather_a.start()
    msgs = to_all(p, wire, msg_all, lambda rel: msg_all.at[g])
    for name in ("lat", "cot", "ada1", "ada2", "wq", "wp"):
        loads[name].start()

    wait_recv(idc)
    labels = jnp.concatenate([ids_all[j, 0:samples, 0:1] for j in range(8)], 0)
    bands = jnp.concatenate([ids_all[j, 0:samples, 1:2] for j in range(8)], 0)

    def one_hot(ids, size):
        lanes = lax.broadcasted_iota(jnp.int32, (ids.shape[0], size), 1).astype(F32)
        return jnp.where(lanes == ids, 1.0, 0.0).astype(BF16)

    of_band = dot(one_hot(bands, time_ref.shape[0]), time_ref[...], (1, 0))
    cond_all[g] = of_band + dot(one_hot(labels, class_ref.shape[1]), class_ref[...], (1, 1))
    conds = to_all(p, wire, cond_all, lambda rel: cond_all.at[g])
    ids_z[z] = jnp.zeros(ids_z.shape[1:], F32)
    ids_z[z, :, 0:1] = labels
    ids_z[z, :, 1:2] = bands


    loads["lat"].wait()
    loads["cot"].wait()
    for s in range(samples):
        hot = own_tokens(kept_ref, length, s)
        at = pl.ds(s * keep, keep)
        mixed[at] = dot(hot, h2_all[s], (0, 0))
        grad[at] = dot(hot, h2_all[samples + s], (0, 0)) * sample_weight(p, counts_ref, samples, s)

    gather_a.neighbours()
    qkv_z.out[0].start()
    qkv_z.out[1].start()
    wait_recv(conds)
    value = jnp.concatenate([cond_all[j] for j in range(8)], 1)
    value = (value * jax.nn.sigmoid(value)).astype(BF16)
    cvec_z[z] = value
    loads["ada1"].wait()
    loads["ada2"].wait()
    mods = [dot(value, w1[...], (1, 1)), dot(value, w2[0:ada_rest], (1, 1))]
    mods = jnp.concatenate(mods, 1) + b_ada
    for j in range(8):
        mod_send[j] = mods[samples * j : samples * (j + 1), :]
    mod_in[g] = mod_send[g]
    modc = to_all(p, wire, mod_in, lambda rel: mod_send.at[p.block(*rel)])
    gather_m.start()
    qkv_z.own.start()
    loads["w1"].start()
    loads["w2"].start()
    outward.start()
    proj_z.own.start()
    gather_a.far()
    qkv_z.out[2].start()
    wait_recv(modc)
    mod[...] = jnp.zeros_like(mod)
    for s in range(samples):
        line = jnp.concatenate([mod_in[j, s : s + 1, :] for j in range(8)], 1)
        for v in range(6):
            mod[s, v : v + 1, :] = line[:, v * width : (v + 1) * width]

    def first_norm(s, at):
        hat, inv = normed(mixed[at])
        h1_all[g, at] = (hat * (1.0 + mod[s, 1:2, :]) + mod[s, 0:1, :]).astype(BF16)
        dm_all[g, at] = (mod[s, 5:6, :] * grad[at]).astype(BF16)

    by_rows(samples, keep, first_norm)
    wait_recv(msgs)
    vec[...] = jnp.zeros_like(vec)
    for row in range(2):
        vec[row : row + 1, :] = jnp.concatenate([msg_all[j, row : row + 1, :] for j in range(8)], 1)

    ones = jnp.ones((8, rows), BF16)
    loads["wq"].wait()

    @pl.loop(0, 24)
    def _(n):
        @pl.when(n == 1)
        def _():
            gather_a.wait_sib()

        @pl.when(n == 4)
        def _():
            gather_a.wait_sib_neighbours()

        @pl.when(n == 7)
        def _():
            gather_a.wait_sib_far()

        @pl.when(n == 9)
        def _():
            gather_m.wait_sib()

        @pl.when(n == 8)
        def _():
            gather_m.neighbours()

        @pl.when(n == 12)
        def _():
            gather_m.wait_sib_neighbours()

        @pl.when(n == 14)
        def _():
            outward.neighbours()
            proj_z.out[0].start()
            proj_z.out[1].start()
            back.start()

        @pl.when(n == 15)
        def _():
            qkv_z.own.wait_recv()
            qkv_z.pass_on(0, 1)

        @pl.when(n == 18)
        def _():
            qkv_z.arrived(0, 1)
            gather_m.far()

        @pl.when(n == 20)
        def _():
            qkv_z.pass_on(2)

        @pl.when(n == 21)
        def _():
            gather_m.wait_sib_far()

        @pl.when(n == 22)
        def _():
            outward.far()
            proj_z.out[2].start()

        @pl.when(n == 23)
        def _():
            qkv_z.arrived(2)

        phase = jnp.where(n < 8, 0, jnp.where((n < 14) | (n == 20) | (n == 21), 1, 2))
        turn = jnp.where(n < 8, n, jnp.where(n < 14, n - 8, jnp.where(n < 20, n - 14, jnp.where(n < 22, n - 14, n - 16))))
        block = arrival(p, turn)
        third = jnp.where(phase == 0, 2 * odd, jnp.where(phase == 1, 1, 2 - 2 * odd))
        chunk = block * 3 + third
        bias_at = jnp.where(chunk >= 16, chunk - 8, chunk)
        keys = (chunk >= 8) & (chunk < 16)
        line = msg_all[lax.div(bias_at, 2), pl.ds(2 + lax.rem(bias_at, 2), 1), :] * jnp.where(keys, 0.0, 1.0)
        line = jnp.concatenate([line, jnp.zeros((7, pair), F32)], 0)
        value = dot(wq[block, pl.ds(pl.multiple_of(third * pair, 16), pair), :], h1_all[g], (1, 1))
        value = value + dot(line.astype(BF16), ones, (0, 0))
        units[2 * chunk] = value[:HEAD_DIM].astype(BF16)
        units[2 * chunk + 1] = value[HEAD_DIM:].astype(BF16)

    loads["keep"].start()
    zs = [to_planes(ids_z), to_planes(cvec_z)]

    @pl.loop(0, 4)
    def _(i):
        for u in (2 * i, 2 * i + 1):
            for s in range(samples):
                lanes = pl.ds(s * keep, keep)
                pieces = []
                for e in range(2):
                    probs = probabilities(units[2 * u + e, :, lanes], units[16 + 2 * u + e, :, lanes])
                    pieces.append(dot(units[32 + 2 * u + e, :, lanes], probs.astype(BF16), (1, 0)))
                att[u, :, lanes] = jnp.concatenate(pieces, 0).astype(BF16)

    back.lo.neighbours()
    loads["wp"].wait()
    outward.wait_sib()
    outward.wait_sib_neighbours()
    outward.wait_sib_far()
    proj_z.own.wait_recv()
    proj_z.pass_on(0, 1, 2)
    back.hi.neighbours()
    proj_z.arrived(0, 1, 2)
    proj[...] = jnp.zeros_like(proj)

    @pl.loop(0, 8)
    def _(u):
        proj[...] += dot(att[u], wp[u], (0, 0))

    def second_norm(s, at):
        proj[at] = proj[at] + vec[0:1, :]
        mixed[at] = mixed[at] + mod[s, 2:3, :] * proj[at]
        hat, inv = normed(mixed[at])
        h2_all[g, at] = (hat * (1.0 + mod[s, 4:5, :]) + mod[s, 3:4, :]).astype(BF16)

    by_rows(samples, keep, second_norm)
    main.start()
    back.far()
    gb1[...] = jnp.zeros_like(gb1)
    for piece in (gather_a, gather_m, qkv_z):
        piece.finish()
    loads["w1"].wait()
    loads["w2"].wait()
    loads["keep"].wait()

    half_rows = rows // 2

    def hidden(places):
        both = lambda ref: jnp.concatenate([ref[block, at] for block, at in places], 0)
        pre = dot(both(h2_all), w1[...], (1, 1)) + b1
        value, slope = gelu_parts(pre)
        value = value.astype(BF16)
        low = (dot(both(dm_all), w2[...], (1, 1)) * slope).astype(BF16)
        gb1[...] += jnp.sum(low.astype(F32), 0, keepdims=True)
        share = dot(low, w1[...], (1, 0)).astype(BF16)
        for i, (block, at) in enumerate(places):
            part = slice(i * half_rows, (i + 1) * half_rows)
            act[block, at] = value[part]
            dpre[block, at] = low[part]
            wq[block, at] = share[part]

    @pl.loop(0, 8)
    def _(n):
        @pl.when(n == 1)
        def _():
            main.wait_sib()
            back.wait_sib()

        @pl.when(n == 2)
        def _():
            main.lo.neighbours()
            back.wait_sib_neighbours()
            back.wait_sib_far()

        @pl.when(n == 3)
        def _():
            main.lo.wait_sib_neighbours()

        @pl.when(n == 4)
        def _():
            main.hi.neighbours()

        @pl.when(n == 5)
        def _():
            main.hi.wait_sib_neighbours()

        @pl.when(n == 6)
        def _():
            main.lo.far()
            sums.send_sib(2, (1,))
            sums.send_sib(1, (1,))
            sums.near(0)
            main.lo.wait_sib_far()

        @pl.when(n == 7)
        def _():
            main.hi.far()
            sums.near(1)
            main.hi.wait_sib_far()

        upper = (n == 4) | (n == 5) | (n == 7)
        turn = jnp.where(n < 2, n, jnp.where(n < 6, 2 + 2 * lax.rem(n, 2), 6))
        halves_at = (jnp.where(upper, 1, 0), jnp.where(upper | (n < 2), 1, 0))
        turns = (turn, jnp.where(n < 2, turn, turn + 1))
        hidden([(arrival(p, t, 6), pl.ds(pl.multiple_of(h * half_rows, 16), half_rows)) for t, h in zip(turns, halves_at)])

        @pl.when(n == 1)
        def _():
            sums.send_sib(0)

        @pl.when(n == 3)
        def _():
            sums.send_sib(1, (0,))
            sums.send_sib(2, (0,))

        @pl.when(n == 6)
        def _():
            sums.send_sib(3, (0,))

        @pl.when(n == 7)
        def _():
            sums.send_sib(3, (1,))

    def weight_grad(left, right, base, between):
        for n, (start, size) in enumerate(((0, 128), (128, 256), (384, hidden_units - 384))):
            part = left[:, :, pl.ds(start, size)].reshape(8 * rows, size)
            grads[base + start : base + start + size] = dot(part, right[...].reshape(8 * rows, width), (0, 0)).astype(BF16)
            chain_send(-(-base // PIECE) if n == 0 else (base + start) // PIECE, (base + start + size) // PIECE)
            between(n)

    def output_blocks(first, last):
        @pl.loop(first, last)
        def _(block):
            h2_all[block] = jnp.dot(act[block], w2[...], preferred_element_type=F32).astype(BF16)

    def visit(n):
        if n == 0:
            chain_up(0)
            sums.relay(0)
            chain_up(1)
        elif n == 1:
            chain_down(0)
            chain_up(2)
            sums.relay(1)
            tokens.start()

    weight_grad(dpre, h2_all, 0, lambda n: sums.send_far() if n == 0 else None)
    weight_grad(act, dm_all, hidden_units, visit)
    main.finish()
    chain_down(1)
    chain_up(3)
    output_blocks(0, 3)
    chain_up(4)
    chain_down(2)
    back.finish()
    grant(0)
    sums.result(tmp)
    sums.finish()
    grant(1)
    loads["again"].start()
    chain_down(3)
    chain_up(5)

    bundle[...] = jnp.zeros_like(bundle)

    def add_row(row, value):
        bundle[pl.ds(row, 1), :] += jnp.sum(value, 0, keepdims=True)

    SUM_PROJ, SUM_FC2 = 6 * samples, 6 * samples + 1

    def second_back(s, at):
        hat, inv = normed(mixed[at])
        up_grad = tmp[at]
        value = grad[at] + norm_back(up_grad * (1.0 + mod[s, 4:5, :]), hat, inv)
        dx2[at] = value
        low = (mod[s, 2:3, :] * value).astype(BF16)
        dproj[at] = low
        add_row(s * 6 + 3, up_grad)
        add_row(s * 6 + 4, up_grad * hat)
        add_row(s * 6 + 2, value * proj[at])
        add_row(SUM_PROJ, low.astype(F32))
        add_row(SUM_FC2, (mod[s, 5:6, :] * grad[at]).astype(BF16).astype(F32))

    by_rows(samples, keep, second_back)
    chain_up(6)
    chain_down(4)
    outward.finish()
    proj_z.finish()

    def heads_back(u):
        datt = dot(wp[u], dproj[...], (1, 1))
        wp[u] = dot(att[u], dproj[...], (1, 0)).astype(BF16)
        lists = ([], [], [])
        for s in range(samples):
            lanes = pl.ds(s * keep, keep)
            parts = ([], [], [])
            for e in range(2):
                q, k, v = (units[16 * i + 2 * u + e, :, lanes] for i in range(3))
                da = datt[e * HEAD_DIM : (e + 1) * HEAD_DIM, s * keep : (s + 1) * keep].astype(BF16)
                probs = probabilities(q, k)
                dprobs = dot(v, da, (0, 0))
                dscores = probs * (dprobs - jnp.sum(dprobs * probs, 0, keepdims=True))
                dscores = dscores.astype(BF16)
                parts[0].append(dot(k, dscores, (1, 0)) * SCALE)
                parts[1].append(dot(q, dscores, (1, 1)) * SCALE)
                parts[2].append(dot(da, probs.astype(BF16), (1, 1)))
            for i in range(3):
                lists[i].append(jnp.concatenate(parts[i], 0).astype(BF16))
        for i in range(3):
            chunk = 8 * i + u
            at = pl.ds(pl.multiple_of(lax.rem(chunk, 3) * pair, 16), pair)
            for s in range(samples):
                dq[lax.div(chunk, 3), at, pl.ds(s * keep, keep)] = lists[i][s]

    visits = {
        (0, 0): ((), (5,)),
        (0, 1): ((7,), ()),
        (1, 0): ((8,), (6,)),
        (1, 1): ((9,), ()),
        (2, 0): ((), (7,)),
        (2, 1): ((10,), (8,)),
        (3, 0): ((11,), ()),
        (3, 1): ((), (9,)),
    }

    @pl.loop(0, 4)
    def _(i):
        for e in range(2):
            heads_back(2 * i + e)
            if e == 1:

                @pl.when(i == 1)
                def _():
                    tokens.lo.neighbours()

                @pl.when(i == 2)
                def _():
                    tokens.hi.neighbours()

            for (at, half), (ups, downs) in visits.items():
                if half == e:

                    @pl.when(i == at)
                    def _(ups=ups, downs=downs):
                        for k in ups:
                            chain_up(k)
                        for k in downs:
                            chain_down(k)

    dq_all[g] = dq[g]
    moves = to_all(p, wire, dq_all, lambda rel: dq.at[p.block(*rel)])
    granted(1)
    for q in (3, 1, 2, 0):
        projs.send_sib(q)

    loads["again"].wait()
    proj[...] = jnp.zeros_like(proj)

    @pl.loop(0, 8)
    def _(j):
        proj[...] += dot(dq[j], wq[j], (0, 0))
        for at, step, k in ((1, chain_up, 12), (3, chain_down, 10), (6, chain_up, 13)):

            @pl.when(j == at)
            def _(step=step, k=k):
                step(k)

    loads["latb"].start()

    projs.send_far()
    projs.send_near()
    chain_down(11)
    granted(0)
    output_blocks(3, 6)
    chain(14, 2)
    output_blocks(6, 8)
    for q in (3, 1, 2, 0):
        outs.send_sib(q)
    loads["ada1b"].start()
    loads["ada2b"].start()
    for k in range(15, 18):
        chain(k, 2)
    tokens.far()
    for k in range(18, 22):
        chain(k, 2)
    outs.send_far()
    tokens.wait_sib()
    tokens.wait_sib_neighbours()
    tokens.wait_sib_far()

    wait_recv(moves)
    chain(22, 2)
    for i in range(3):
        at = pl.ds(i * pair, pair)
        tmp[0:pair] = jnp.zeros((pair, width), F32)

        @pl.loop(0, 8)
        def _(j, at=at):
            tmp[0:pair] += dot(dq_all[j, at, :], h1_all[j], (1, 0))

        gq[at] = tmp[0:pair].astype(BF16)
        chain_send(24 + 3 * i, 27 + 3 * i)
        if i == 0:
            chain(23, 2)
            projs.relay(0)
            projs.relay(1)
            outs.send_near()
            chain(24, 2)
        elif i == 1:
            chain(25, 2)
            chain(26, 2)
        else:
            chain(27, 2)

    loads["latb"].wait()
    for s in range(samples):
        hot = own_tokens(kept_ref, length, s)
        tmp[pl.ds(s * keep, keep)] = dot(hot, wq[s, pl.ds(0, length)], (0, 0))

    def first_back(s, at):
        @pl.when(at.start == rows // 2)
        def _():
            chain(28, 2)

        hat, inv = normed(tmp[at])
        up_grad = proj[at]
        dx = dx2[at] + norm_back(up_grad * (1.0 + mod[s, 1:2, :]), hat, inv)
        add_row(s * 6, up_grad)
        add_row(s * 6 + 1, up_grad * hat)
        dproj[at] = dx.astype(BF16)

    by_rows(samples, keep, first_back)
    loads["dx"].start()
    chain(29, 2)
    outs.relay(0)
    outs.relay(1)
    chain(30, 2)
    projs.result(gp)
    chain_send(33, 36)
    chain(31, 2)
    outs.result(tmp)

    def end(s, at):
        value = tmp[at] + vec[1:2, :]
        add_row(s * 6 + 5, grad[at] * value)
        dproj[at] = (mixed[at] + mod[s, 5:6, :] * value).astype(BF16)

    loads["dx"].wait()
    by_rows(samples, keep, end)
    loads["y"].start()

    cols = ada_hbm.shape[0]
    wait_send(modc)
    for s in range(samples):
        line = jnp.concatenate([bundle[s * 6 + v : s * 6 + v + 1, :] for v in range(6)], 1)
        for j in range(8):
            mod_send[j, s : s + 1, :] = line[:, j * cols : (j + 1) * cols].astype(BF16).astype(F32)
    mod_in[g] = mod_send[g]
    dmods = to_all(p, wire, mod_in, lambda rel: mod_send.at[p.block(*rel)])
    lines = [dot(ones, dq[j], (1, 1))[0:1, :] for j in range(8)]
    for j in range(8):
        for row, at in ((0, SUM_PROJ), (1, SUM_FC2)):
            share_send[j, row : row + 1, :] = bundle[at : at + 1, j * pair : (j + 1) * pair]
        for e in range(2):
            u = 2 * j + e + (8 if j >= 4 else 0)
            share_send[j, 2 + e : 3 + e, :] = lines[u // 3][:, u % 3 * pair : (u % 3 + 1) * pair]
    share_in[g] = share_send[g]
    small = to_all(p, wire, share_in, lambda rel: share_send.at[p.block(*rel)])
    chain(32, 2)
    chain(33, 2)
    loads["ada1b"].wait()
    loads["ada2b"].wait()
    wait_recv(dmods)
    part = jnp.concatenate([mod_in[j] for j in range(8)], 0).astype(BF16)
    dmod_z[z] = part
    dcvec = dot(part[:, :hidden_units], w1[...], (1, 0)) + dot(part[:, hidden_units:], w2[0:ada_rest], (1, 0))
    depth = cond_all.shape[2]
    for j in range(8):
        dc_send[j] = dcvec[:, j * depth : (j + 1) * depth]
    dc_in[g] = dc_send[g]
    dcs = to_all(p, wire, dc_in, lambda rel: dc_send.at[p.block(*rel)])
    zs.append(to_planes(dmod_z))
    chain(34, 2)
    wait_recv(small)
    sum_z[z, 0:4, :] = sum(share_in[j] for j in range(8))
    for i in range(hidden_units // pair):
        sum_z[z, 4 + i : 5 + i, :] = gb1[:, i * pair : (i + 1) * pair]
    zs.append(to_planes(sum_z))
    chain(35, 2)
    wait_recv(dcs)
    cond = cond_all[g]
    gate = jax.nn.sigmoid(cond)
    dcond_z[z] = sum(dc_in[j] for j in range(8)) * (gate * (1.0 + cond * (1.0 - gate)))
    zs.append(to_planes(dcond_z))

    chain_down(34)
    chain_down(35)
    whole = lambda sem, ref: wire.copy(sem, up_r, ref, ref, (g, partner))

    @pl.when(jnp.logical_not(at_end))
    def _():
        whole(across, out).wait_send()
        whole(down, out).wait_send()

    @pl.when(at_end)
    def _():
        @pl.loop(0, count)
        def _(k):
            go_down(k).wait_recv()
            to_hbm(k).start()

        whole(up, out).wait_send()

    local(out, out_hbm, sems.at[20]).wait()
    for copies in zs:
        wait_recv(copies)
    for name in ("ids", "cvec", "dmod", "sum", "dcond"):
        loads[name].start()
    for copies in zs:
        wait_send(copies)
    for copies in (idc, msgs, conds, moves, dmods, small, dcs):
        wait_send(copies)
    for piece in (tokens, projs, outs):
        piece.finish()
    for name in ("y", "ids", "cvec", "dmod", "sum", "dcond"):
        loads[name].wait()


def run_block(samples, planes, labels, bands, counts, wq, wp, w1, w2, w_ada, lat, cot, biases, kept, class_table, time_table):
    keep, width = kept.shape[1], wq.shape[1]
    rows, hidden, per = samples * keep, w1.shape[0], 8 * samples
    cols, depth = w_ada.shape[0], class_table.shape[0]
    total = 2 * hidden + wq.shape[0] + wp.shape[0]
    count = total // PIECE
    shape, room = jax.ShapeDtypeStruct, pltpu.VMEM
    blocks = room((8, rows, width), BF16)
    plain = room((rows, width), F32)
    over_z = [
        ((planes, per, cols), BF16),
        ((planes, per, depth), F32),
        ((planes, per, width), BF16),
        ((planes, 4 + hidden // depth, depth), F32),
        ((planes, per, 128), F32),
    ]
    sends, recvs = 9 + 2 + 3 + 3 + 8 + 5, 8 * 9 + 2 * 7 + 3 * 18 + 2 * count + 8 + 5
    return pl.pallas_call(
        functools.partial(block_kernel, samples, planes),
        out_shape=[
            shape((total, width), BF16),
            shape((rows, width), BF16),
            shape((rows, width), BF16),
            shape((8,) + wq.shape, BF16),
            *[shape(dims, kind) for dims, kind in over_z],
        ],
        in_specs=[SMEM] * 3 + [ANY] * 15,
        out_specs=[ANY] * 9,
        scratch_shapes=[
            *[room(array.shape, array.dtype) for array in (*biases, kept, class_table, time_table)],
            *[room(dims, kind) for dims, kind in over_z],
            room((8,) + wq.shape, BF16),
            room((8,) + wp.shape, BF16),
            room(w1.shape, BF16),
            room(w2.shape, BF16),
            blocks,
            blocks,
            blocks,
            room((8, rows, hidden), BF16),
            room((8, rows, hidden), BF16),
            *scatter_scratch(rows, width),
            room((48, HEAD_DIM, rows), BF16),
            room((8, 2 * HEAD_DIM, rows), BF16),
            plain,
            plain,
            plain,
            plain,
            plain,
            room((hidden - 512, width), F32),
            room((rows, width), BF16),
            room((8, wq.shape[0], rows), BF16),
            room((8, wq.shape[0], rows), BF16),
            room((total, width), BF16),
            room((total, width), BF16),
            room((total, width), BF16),
            room((1, hidden), F32),
            room((8, samples, 128), F32),
            room((8, 4, wp.shape[0]), F32),
            room((8, per, depth), F32),
            room((8, samples, cols), F32),
            room((8, samples, cols), F32),
            room((samples, 8, width), F32),
            room((8, width), F32),
            room((8, per, depth), F32),
            room((8, per, depth), F32),
            room((16, width), F32),
            room((8, 4, wp.shape[0]), F32),
            room((8, 4, wp.shape[0]), F32),
            pltpu.SemaphoreType.DMA((sends,)),
            pltpu.SemaphoreType.DMA((recvs,)),
            pltpu.SemaphoreType.REGULAR((2, 3)),
            pltpu.SemaphoreType.DMA((29,)),
        ],
        compiler_params=params(1),
    )(labels, bands, counts, wq, wp, w1, w2, w_ada, lat, cot, *biases, kept, class_table, time_table)


def outputs_kernel(samples, planes, counts_ref, totals_hbm, y_hbm, dx_hbm, lat_hbm, cot_hbm, kept_hbm, dmod_hbm, dcond_hbm,
                   cvec_hbm, sum_hbm, ids_hbm,
                   block_hbm, latg_hbm, g1_hbm, g2_hbm, gq_hbm, gp_hbm, ada_hbm, time_hbm, class_hbm, bada_hbm, qv_hbm, bp_hbm,
                   b1_hbm, b2_hbm,
                   kept_ref, dmod_ref, dcond_ref, cvec_ref, sum_ref, ids_ref, time_out, class_out, bada_out, qv_out, bp_out,
                   b1_out, b2_out, totals, wide, ada, tokens, both, sems_in, sems):
    p = Place()
    length = lat_hbm.shape[1]
    keep = kept_ref.shape[1]
    chunk = 144
    count, width = totals.shape[0] // chunk, totals.shape[1]
    per = 8 * samples
    chunks = [pl.ds(k * chunk, chunk) for k in range(count)]
    ins = [local(totals_hbm.at[at], totals.at[at], sems_in.at[k]) for k, at in enumerate(chunks)]
    ins += [
        local(y_hbm, tokens.at[0], sems_in.at[count]),
        local(dx_hbm, tokens.at[1], sems_in.at[count + 1]),
        local(lat_hbm, both.at[0], sems_in.at[count + 2]),
        local(cot_hbm, both.at[1], sems_in.at[count + 3]),
    ]
    pairs = ((dmod_hbm, dmod_ref), (cvec_hbm, cvec_ref), (kept_hbm, kept_ref), (dcond_hbm, dcond_ref), (sum_hbm, sum_ref), (ids_hbm, ids_ref))
    small = [local(src, dst, sems_in.at[count + 4 + i]) for i, (src, dst) in enumerate(pairs)]
    for copy in small + ins[count:] + ins[:count]:
        copy.start()
    done = []

    def send(src, dst):
        done.append(local(src, dst, sems.at[len(done)]))
        done[-1].start()

    for copy in small:
        copy.wait()
    cvec = jnp.concatenate([cvec_ref[k] for k in range(planes)], 0)
    dmod = jnp.concatenate([dmod_ref[k] for k in range(planes)], 0)
    cols = ada.shape[0]
    for start in range(0, cols, 256):
        size = min(256, cols - start)
        ada[start : start + size] = dot(dmod[:, start : start + size], cvec, (0, 0))
        send(ada.at[pl.ds(start, size)], ada_hbm.at[pl.ds(start, size)])
    bada_out[...] = jnp.sum(dmod.astype(F32), 0)
    send(bada_out, bada_hbm)

    dcond = jnp.concatenate([dcond_ref[k] for k in range(planes)], 0)
    ids = jnp.concatenate([ids_ref[k] for k in range(planes)], 0)

    def one_hot(column, size):
        lanes = lax.broadcasted_iota(jnp.int32, (planes * per, size), 1).astype(F32)
        return jnp.where(lanes == ids[:, column : column + 1], 1.0, 0.0)

    def exact(left, right):
        return lax.dot_general(left, right, (((0,), (0,)), ((), ())), precision=HIGH, preferred_element_type=F32)

    time_out[...] = exact(one_hot(1, time_out.shape[0]), dcond)
    send(time_out, time_hbm)
    class_out[...] = exact(dcond, one_hot(0, class_out.shape[1]))
    send(class_out, class_hbm)
    sums = sum(sum_ref[k] for k in range(planes))
    joined = lambda start, stop: jnp.concatenate([sums[i : i + 1, :] for i in range(start, stop)], 1)
    places = ((bp_out, bp_hbm, 0, 1), (b2_out, b2_hbm, 1, 2), (qv_out, qv_hbm, 2, 4), (b1_out, b1_hbm, 4, sums.shape[0]))
    for out, hbm, start, stop in places:
        out[...] = joined(start, stop).reshape(out.shape[0])
        send(out, hbm)

    for copy in ins[count:]:
        copy.wait()
    for s in range(samples):
        hot = own_tokens(kept_ref, length, s)
        is_kept = jnp.sum(hot.astype(F32), 1, keepdims=True) > 0.5
        at = pl.ds(s * keep, keep)
        both[0, s] = jnp.where(is_kept, dot(hot, tokens[0, at], (1, 0)), both[0, s].astype(F32)).astype(BF16)
        weighted = both[1, s].astype(F32) * sample_weight(p, counts_ref, samples, s)
        both[1, s] = jnp.where(is_kept, dot(hot, tokens[1, at], (1, 0)), weighted).astype(BF16)
    send(both.at[0], block_hbm)
    send(both.at[1], latg_hbm)

    k = 0
    for out in (g1_hbm, g2_hbm, gq_hbm, gp_hbm):
        for start in range(0, out.shape[0], chunk):
            ins[k].wait()
            wide[chunks[k]] = totals[chunks[k]].astype(F32)
            send(wide.at[chunks[k]], out.at[pl.ds(start, chunk)])
            k += 1

    for copy in done:
        copy.wait()


def place_outputs(samples, planes, counts, totals, y, dx, lat, cot, kept, dmod, dcond, cvec, sums, ids, hidden, wq, wp, classes, bands):
    count, width = totals.shape[0] // 144, totals.shape[1]
    cols, depth = dmod.shape[2], dcond.shape[2]
    shape, room = jax.ShapeDtypeStruct, pltpu.VMEM
    wide = lambda size: shape((size, width), F32)
    return pl.pallas_call(
        functools.partial(outputs_kernel, samples, planes),
        out_shape=[
            shape(lat.shape, BF16),
            shape(lat.shape, BF16),
            wide(hidden),
            wide(hidden),
            wide(wq),
            wide(wp),
            wide(cols),
            shape((bands, depth), F32),
            shape((depth, classes), F32),
            shape((cols,), F32),
            shape((2 * wp,), F32),
            shape((wp,), F32),
            shape((hidden,), F32),
            shape((wp,), F32),
        ],
        in_specs=[SMEM] + [ANY] * 11,
        out_specs=[ANY] * 14,
        scratch_shapes=[
            room(kept.shape, jnp.int32),
            room(dmod.shape, BF16),
            room(dcond.shape, F32),
            room(cvec.shape, BF16),
            room(sums.shape, F32),
            room(ids.shape, F32),
            room((bands, depth), F32),
            room((depth, classes), F32),
            room((cols,), F32),
            room((2 * wp,), F32),
            room((wp,), F32),
            room((hidden,), F32),
            room((wp,), F32),
            room(totals.shape, BF16),
            room(totals.shape, F32),
            room((cols, width), F32),
            room((2,) + y.shape, BF16),
            room((2,) + lat.shape, BF16),
            pltpu.SemaphoreType.DMA((count + 10,)),
            pltpu.SemaphoreType.DMA((count + 9 + -(-cols // 256),)),
        ],
        compiler_params=pltpu.CompilerParams(vmem_limit_bytes=63 * 2**20),
    )(counts, totals, y, dx, lat, cot, kept, dmod, dcond, cvec, sums, ids)


def plane_body(planes, latents, cotangent, bands, labels, kept, band_counts, time_table, class_table, w_ada, b_ada, w_qkv,
               qv_bias, w_proj, b_proj, w_fc1, b_fc1, w_fc2, b_fc2):
    samples, length, width = latents.shape
    wq = w_qkv.shape[1]
    wp = w_proj.shape[0]
    hidden = w_fc1.shape[1]

    totals, y, dx, unused_weights, dmod, dcond, cvec, sums, ids = run_block(
        samples, planes, labels, bands, band_counts, w_qkv.T, w_proj, w_fc1.T, w_fc2, w_ada.T, latents, cotangent,
        (b_proj, b_fc2, qv_bias, b_ada, b_fc1), kept, class_table.T, time_table
    )
    block_out, latents_grad, g1, g2, gq, gp, ada, time, classes, bada, qv, bp, b1, b2 = place_outputs(
        samples, planes, band_counts, totals, y, dx, latents, cotangent, kept, dmod, dcond, cvec, sums, ids, hidden, wq, wp,
        class_table.shape[0], time_table.shape[0]
    )
    return (block_out, latents_grad, time, classes.T, ada.T, bada, gq.T, qv, gp, bp, g1.T, b1, g2, b2)


def solution(mesh):
    planes = mesh.shape["dp"]
    small = mesh.shape["grp"] == 8 and planes == 4
    return jax.shard_map(
        functools.partial(plane_body, planes) if small else body,
        mesh=mesh,
        in_specs=(
            P(("grp", "dp"), None, None),
            P(("grp", "dp"), None, None),
            P(("grp", "dp")),
            P(("grp", "dp")),
            P(("grp", "dp"), None),
            P("grp"),
            P(None, "grp"),
            P(None, "grp"),
            P(None, "grp"),
            P("grp"),
            P(None, "grp"),
            P("grp"),
            P("grp", None),
            P("grp"),
            P(None, "grp"),
            P("grp"),
            P("grp", None),
            P("grp"),
        ),
        out_specs=(
            P(("grp", "dp"), None, None),
            P(("grp", "dp"), None, None),
            P(None, "grp"),
            P(None, "grp"),
            P(None, "grp"),
            P("grp"),
            P(None, "grp"),
            P("grp"),
            P("grp", None),
            P("grp"),
            P(None, "grp"),
            P("grp"),
            P("grp", None),
            P("grp"),
        ),
        check_vma=False,
    )
```
